32 devices in a mesh: groups: 2 (over x), blk: 16 (over z, y, core).
Axes of the slice: x: 2, y: 2, z: 4, core: 2. Of those that a mesh axis runs over, the one named last changes fastest.
Arguments:
- density: bfloat16 [256, 9, 128, 128], P(('groups', 'blk')), parts along dimension 0, may hold values from -0.25 to 0.25
- ao_values: bfloat16 [384, 4, 128, 256], P(('groups', 'blk')), parts along dimension 0, may hold values from -6 to 6
- kernel: bfloat16 [384, 256, 256], P(('groups', 'blk')), parts along dimension 0, may hold values from -0.375 to 0.375
- grid_weights: float32 [384, 256], P(('groups', 'blk')), parts along dimension 0, may hold values from 0.002 to 0.02
- centre: int32 [384], P(('groups', 'blk')), parts along dimension 0, may hold values from 2 to 125, as said below
- sig_offsets: int32 [384, 4], P(('groups', 'blk')), parts along dimension 0, may hold values from -2 to 2, as said below
- counts: int32 [384], P(('groups', 'blk')), parts along dimension 0, may hold values from 0 to 4, as said below
Outputs:
- exchange: float32 [256, 9, 128, 128], P(('groups', 'blk')), parts along dimension 0
The draws below stay inside these ranges and needn't reach their ends.
There are 2 independent parts, one for each index of `groups`. The reference program is written for one: setup_inputs(seed, part) draws one part's arguments, and reference() takes and returns one part's arrays. A program takes and returns all parts, laid end to end along the dimension named above; each array names one. Nothing has to cross between parts.
Inputs may be any that keep to these rules, and one draw needn't show every extreme that they name: `centre`: the batches in the rows of one blk device have their atom block among that device's 8 blocks; the device's first batch slot has the lowest such block that the range allows, its slot 10 the highest. `sig_offsets`: the 4 offsets of a batch are distinct; those of a device's first slot and of its slot 10 include -2 and 2. `counts`: the first batch slot and slot 10 of each blk device have 4 live blocks and its last slot none.
All inputs are finite; a program needn't handle non-finite values.
Results may differ from the reference program's by a relative error of at most 0.0041.
Values may be sent and summed in bfloat16 or wider, within the bound.
No kernel may reach another device: no remote copies, remote signals or barrier semaphores. Data moves between devices by JAX's collectives and lax.ppermute only.
A program may use at most 128 MiB of HBM per device.

```python
import math
import jax
import jax.numpy as jnp
from jax import lax

NB = 128
PTS = 256
REACH = 2
SIG = 4
BLK_DEV = 8
BATCH_DEV = 12
BAND = 9
NBLK = 128
NBATCH = 192


def draw_centre(key, part):
    key = jax.random.fold_in(key, 1)
    owner = jnp.arange(NBATCH, dtype=jnp.int32) // BATCH_DEV
    place = jnp.arange(NBATCH, dtype=jnp.int32) % BATCH_DEV
    first = owner * BLK_DEV
    lowest = jnp.maximum(first, REACH)
    highest = jnp.minimum(first + BLK_DEV - 1, NBLK - 1 - REACH)
    raw = jax.random.randint(key, (NBATCH,), 0, 65536, dtype=jnp.int32)
    picked = lowest + raw % (highest - lowest + 1)
    picked = jnp.where(place == 0, lowest, picked)
    picked = jnp.where(place == BATCH_DEV - 2, highest, picked)
    return picked.astype(jnp.int32)


def draw_sig_offsets(key, part):
    key = jax.random.fold_in(key, 2)
    width = 2 * REACH + 1
    position = jnp.arange(width, dtype=jnp.int32)
    place = jnp.arange(NBATCH, dtype=jnp.int32) % BATCH_DEV
    special = (place == 0) | (place == BATCH_DEV - 2)
    ends = (position == 0) | (position == width - 1)
    scores = jax.random.randint(key, (NBATCH, width), 0, 4096, dtype=jnp.int32) * width + position[None, :]
    scores = jnp.where(special[:, None] & ends[None, :], position[None, :] - width, scores)
    order = jnp.argsort(scores, axis=1)
    return (order[:, :SIG] - REACH).astype(jnp.int32)


def draw_counts(key, part):
    key = jax.random.fold_in(key, 3)
    raw = jax.random.randint(key, (NBATCH,), 0, SIG + 1, dtype=jnp.int32)
    place = jnp.arange(NBATCH, dtype=jnp.int32) % BATCH_DEV
    raw = jnp.where(place == 0, SIG, raw)
    raw = jnp.where(place == BATCH_DEV - 2, SIG, raw)
    raw = jnp.where(place == BATCH_DEV - 1, 0, raw)
    return raw.astype(jnp.int32)


def steps_of(rng, shape, cuts, smallest, high):
    def one(axis_at, blocks):
        heights = jax.random.uniform(jax.random.fold_in(jax.random.fold_in(rng, 6), axis_at), (blocks,), jnp.float32, smallest / len(cuts), high / len(cuts))
        return jnp.repeat(jnp.exp(heights), shape[axis_at] // blocks).reshape((-1,) + (1,) * (len(shape) - axis_at - 1))

    factor_of = one(*cuts[0])
    for cut in cuts[1:]:
        factor_of = factor_of * one(*cut)
    return factor_of


def scatter_about(own_key, dims, deviation, most, cuts=(), kind=jnp.bfloat16):
    result = jax.random.normal(own_key, dims, jnp.float32) * deviation
    if len(cuts) > 0:
        result = steps_of(own_key, dims, cuts, -0.22, 0.18) * result
    return jnp.clip(result, min=-most, max=most).astype(kind)


def setup_inputs(seed: int = 0, part: int = 0) -> dict:
    key_of = jax.random.split(jax.random.key(seed), 8)
    part_keys = jax.random.split(jax.random.fold_in(key_of[7], part), 8)
    density = scatter_about(part_keys[0], (NBLK, BAND, NB, NB), (SIG * NB) ** -0.5, 0.25, ((0, 16),))
    ao_values = scatter_about(part_keys[1], (NBATCH, SIG, NB, PTS), 1.0, 6.0, ((0, 16),))
    kernel = scatter_about(part_keys[2], (NBATCH, PTS, PTS), PTS ** -0.5, 0.375, ((0, 16),))
    grid_weights = jnp.clip(jnp.exp(math.log(0.02) - 2.30258502 * jax.random.uniform(part_keys[3], (NBATCH, PTS), jnp.float32) ** steps_of(part_keys[3], (NBATCH, PTS), ((0, 16),), -0.2, 0.2)), 0.002, 0.02)
    centre = draw_centre(jax.random.fold_in(jax.random.fold_in(key_of[7], part), 71), part)
    sig_offsets = draw_sig_offsets(jax.random.fold_in(jax.random.fold_in(key_of[7], part), 71), part)
    counts = draw_counts(jax.random.fold_in(jax.random.fold_in(key_of[7], part), 71), part)
    return {"density": density, "ao_values": ao_values, "kernel": kernel, "grid_weights": grid_weights, "centre": centre, "sig_offsets": sig_offsets, "counts": counts}


def reference(density, ao_values, kernel, grid_weights, centre, sig_offsets, counts):
    slots = jnp.arange(SIG, dtype=jnp.int32)

    def one_batch(total, item):
        values, potential, weights, middle, offsets, count = item
        blocks = (middle + offsets).astype(jnp.int32)
        live = slots < count
        panel = values * live[:, None, None].astype(values.dtype)
        bands = (blocks[None, :] - blocks[:, None] + 2 * REACH).astype(jnp.int32)
        tiles = density[blocks[:, None], bands]
        fpanel = jnp.einsum("kjab,jbg->kag", tiles.astype(jnp.float32), panel.astype(jnp.float32)).astype(jnp.bfloat16)
        gpanel = jnp.einsum("kag,gh->kah", fpanel.astype(jnp.float32), potential.astype(jnp.float32))
        hpanel = (gpanel * weights[None, None, :] * live[:, None, None].astype(jnp.float32)).astype(jnp.bfloat16)
        part = jnp.einsum("kag,jbg->kjab", panel.astype(jnp.float32), hpanel.astype(jnp.float32))
        total = total.at[blocks[:, None], bands].add(part)
        return total, None

    start = jnp.zeros(density.shape, jnp.float32)
    total, _ = lax.scan(one_batch, start, (ao_values, kernel, grid_weights, centre, sig_offsets, counts))
    return total
```

```python
import functools

import jax
import jax.numpy as jnp
from jax import lax
from jax.experimental import pallas as pl
from jax.experimental.pallas import tpu as pltpu
from jax.sharding import PartitionSpec as P

MIB = 1 << 20
SMEM_SPEC = pl.BlockSpec(memory_space=pltpu.SMEM)
VMEM_SPEC = pl.BlockSpec(memory_space=pltpu.VMEM)
ANY_SPEC = pl.BlockSpec(memory_space=pl.ANY)


class Geometry:
    def __init__(self, rows, band):
        self.rows, self.band = rows, band
        self.half = (band - 1) // 2
        self.reach = reach = self.half // 2
        self.own = rows * band
        self.low = [(rows - m, reach + m, band - reach - m) for m in range(reach, 0, -1)]
        self.high = [(m, 0, 3 * reach - m) for m in range(reach)]
        self.halo = sum(count for _, _, count in self.low)
        self.total = self.own + 2 * self.halo
        self.up_pack, self.down_pack = ([], [])
        for pack, segments in ((self.up_pack, self.low), (self.down_pack, self.high)):
            place = 0
            for row, start, count in segments:
                pack.append((row * band + start, place, count))
                place += count
        self.bases = {}
        place = self.own
        for index, (_, start, count) in enumerate(self.low):
            self.bases[index - reach] = place - start
            place += count
        for index, (_, start, count) in enumerate(self.high):
            self.bases[rows + index] = place - start
            place += count
        touched = set()
        for start, _, count in self.up_pack + self.down_pack:
            touched.update(range(start, start + count))
        self.quiet = []
        for index in range(self.own):
            if index in touched:
                continue
            if self.quiet and sum(self.quiet[-1]) == index:
                self.quiet[-1] = (self.quiet[-1][0], self.quiet[-1][1] + 1)
            else:
                self.quiet.append((index, 1))

    def base(self, row):
        value = row * self.band
        for at, base in self.bases.items():
            value = jnp.where(row == at, base, value)
        return value


def run_copies(copies):
    for copy in copies:
        copy.start()
    for copy in copies:
        copy.wait()


def pack_kernel(geo, index_ref, density_ref, first_ref, second_ref, sems):
    odd = index_ref[0] % 2 == 1

    def fill(up_ref, down_ref):
        copies = []
        for pack, ref in ((geo.up_pack, up_ref), (geo.down_pack, down_ref)):
            for start, place, count in pack:
                copies.append(
                    pltpu.make_async_copy(
                        density_ref.at[pl.ds(start, count)],
                        ref.at[pl.ds(place, count)],
                        sems.at[len(copies)],
                    )
                )
        run_copies(copies)

    @pl.when(jnp.logical_not(odd))
    def _():
        fill(first_ref, second_ref)

    @pl.when(odd)
    def _():
        fill(second_ref, first_ref)


def batch_rows(geo, index_ref, centre_ref, offsets_ref, counts_ref, b):
    first = index_ref[0] * geo.rows
    local = centre_ref[b] - first
    slots = offsets_ref.shape[0]
    offsets = [offsets_ref[k, b] for k in range(slots)]
    count = counts_ref[b]
    inside = jnp.bool_(True)
    for k in range(slots):
        row = local + offsets[k]
        inside = inside & ((k >= count) | ((row >= 0) & (row < geo.rows)))
    return local, offsets, count, inside


def add_batch(geo, b, live, local, offsets, tiles_ref, ao_ref, kernel_ref, weights_ref, acc_ref):
    nb = ao_ref.shape[2]
    pts = ao_ref.shape[3]
    bases = [geo.base(local + offsets[k]) for k in range(live)]
    places = [
        [bases[k] + offsets[j] - offsets[k] + geo.half for j in range(live)] for k in range(live)
    ]
    x = ao_ref[b, pl.ds(0, live)].reshape(live * nb, pts)
    tiles = jnp.concatenate(
        [
            jnp.concatenate([tiles_ref[places[k][j]] for j in range(live)], axis=1)
            for k in range(live)
        ],
        axis=0,
    )
    f = jnp.dot(tiles, x, preferred_element_type=jnp.float32).astype(jnp.bfloat16)
    g = jnp.dot(f, kernel_ref[b], preferred_element_type=jnp.float32)
    h = (g * weights_ref[pl.ds(b, 1), :]).astype(jnp.bfloat16)
    part = lax.dot_general(x, h, (((1,), (1,)), ((), ())), preferred_element_type=jnp.float32)
    for k in range(live):
        for j in range(live):
            acc_ref[places[k][j]] += part[k * nb : (k + 1) * nb, j * nb : (j + 1) * nb]


def each_batch(
    geo, inner, scalars, tiles_ref, ao_ref, kernel_ref, weights_ref, acc_ref, arrived=None
):
    slots = ao_ref.shape[1]

    def step(b, carry):
        local, offsets, count, inside = batch_rows(geo, *scalars, b)
        if arrived is not None:
            arrived(b)
        wanted = inside if inner else jnp.logical_not(inside)
        for live in range(1, slots + 1):

            @pl.when(wanted & (count == live))
            def _(live=live):
                add_batch(
                    geo, b, live, local, offsets, tiles_ref, ao_ref, kernel_ref, weights_ref, acc_ref
                )

        return carry

    lax.fori_loop(0, ao_ref.shape[0], step, 0)


def inner_kernel(
    geo, index_ref, centre_ref, offsets_ref, counts_ref,
    density_ref, ao_in, kernel_in, weights_ref,
    tiles_ref, acc_ref, ao_ref, kernel_ref, sems,
):
    tiles_copy = pltpu.make_async_copy(density_ref, tiles_ref.at[pl.ds(0, geo.own)], sems.at[0, 0])
    tiles_copy.start()

    def copies(b):
        return (
            pltpu.make_async_copy(ao_in.at[b], ao_ref.at[b], sems.at[1, b]),
            pltpu.make_async_copy(kernel_in.at[b], kernel_ref.at[b], sems.at[2, b]),
        )

    def start(b, carry):
        for copy in copies(b):
            copy.start()
        return carry

    def arrived(b):
        for copy in copies(b):
            copy.wait()

    lax.fori_loop(0, ao_ref.shape[0], start, 0)
    acc_ref[...] = jnp.zeros_like(acc_ref)
    tiles_copy.wait()
    scalars = (index_ref, centre_ref, offsets_ref, counts_ref)
    each_batch(geo, True, scalars, tiles_ref, ao_ref, kernel_ref, weights_ref, acc_ref, arrived)


def edge_kernel(
    geo, index_ref, centre_ref, offsets_ref, counts_ref,
    first_ref, second_ref, ao_ref, kernel_ref, weights_ref, tiles_in, acc_in,
    tiles_ref, acc_ref, first_out, second_out, sems,
):
    odd = index_ref[0] % 2
    low, high = geo.own, geo.own + geo.halo
    first_at = jnp.where(odd == 1, low, high)
    second_at = jnp.where(odd == 1, high, low)
    run_copies(
        [
            pltpu.make_async_copy(first_ref, tiles_ref.at[pl.ds(first_at, geo.halo)], sems.at[0]),
            pltpu.make_async_copy(second_ref, tiles_ref.at[pl.ds(second_at, geo.halo)], sems.at[1]),
        ]
    )
    scalars = (index_ref, centre_ref, offsets_ref, counts_ref)
    each_batch(geo, False, scalars, tiles_ref, ao_ref, kernel_ref, weights_ref, acc_ref)
    first_out[...] = acc_ref[pl.ds(first_at, geo.halo)].astype(first_out.dtype)
    second_out[...] = acc_ref[pl.ds(second_at, geo.halo)].astype(second_out.dtype)


def quiet_kernel(geo, acc_ref, out_ref, sems):
    run_copies(
        [
            pltpu.make_async_copy(
                acc_ref.at[pl.ds(start, count)], out_ref.at[pl.ds(start, count)], sems.at[i]
            )
            for i, (start, count) in enumerate(geo.quiet)
        ]
    )


def finish_kernel(geo, index_ref, first_ref, second_ref, acc_ref, out_in, out_ref, total, sems):
    odd = index_ref[0] % 2 == 1

    def add(from_up, from_down):
        copies = []
        for side, (pack, ref) in enumerate(((geo.up_pack, from_up), (geo.down_pack, from_down))):
            for start, place, count in pack:
                spot = pl.ds(side * geo.halo + place, count)
                total[spot] = acc_ref[pl.ds(start, count)] + ref[pl.ds(place, count)].astype(
                    jnp.float32
                )
                copy = pltpu.make_async_copy(
                    total.at[spot], out_ref.at[pl.ds(start, count)], sems.at[len(copies)]
                )
                copy.start()
                copies.append(copy)
        for copy in copies:
            copy.wait()

    @pl.when(jnp.logical_not(odd))
    def _():
        add(first_ref, second_ref)

    @pl.when(odd)
    def _():
        add(second_ref, first_ref)


def call(kernel, out_shape, in_specs, out_specs, scratch, cost, aliases=None):
    return pl.pallas_call(
        kernel,
        out_shape=out_shape,
        in_specs=in_specs,
        out_specs=out_specs,
        scratch_shapes=scratch,
        input_output_aliases=aliases or {},
        cost_estimate=pl.CostEstimate(flops=cost[0], bytes_accessed=cost[1], transcendentals=0),
        compiler_params=pltpu.CompilerParams(vmem_limit_bytes=cost[2] * MIB),
    )


def exchange_pairs(first, second, size):
    lower = [(i, i + 1) for i in range(0, size - 1, 2)]
    upper = [(i, i + 1) for i in range(1, size - 1, 2)]
    both = lambda pairs: pairs + [(j, i) for i, j in pairs]
    got_second = lax.ppermute(second, "blk", both(upper))
    got_first = lax.ppermute(first, "blk", both(lower))
    return tuple(pltpu.with_memory_space_constraint(got, pltpu.VMEM) for got in (got_first, got_second))


def local(density, ao_values, kernel, grid_weights, centre, sig_offsets, counts):
    rows, band, nb, _ = density.shape
    batches, slots, _, pts = ao_values.shape
    size = lax.axis_size("blk")
    geo = Geometry(rows, band)
    block = nb * nb
    index = lax.axis_index("blk").astype(jnp.int32).reshape(1)
    offsets = sig_offsets.T
    flat = pltpu.with_memory_space_constraint(density.reshape(geo.own, nb, nb), pltpu.HBM)
    pack = pltpu.VMEM((geo.halo, nb, nb), jnp.bfloat16)
    dma = pltpu.SemaphoreType.DMA

    first, second = call(
        functools.partial(pack_kernel, geo),
        (pack, pack),
        [SMEM_SPEC, ANY_SPEC],
        (VMEM_SPEC, VMEM_SPEC),
        [dma((2 * geo.reach,))],
        (0, 8 * geo.halo * block, 8),
    )(index, flat)
    first, second = exchange_pairs(first, second, size)

    scalars = (index, centre, offsets, counts)
    flops = batches * slots * nb * pts * (4 * slots * nb + 2 * pts)
    ao = pltpu.with_memory_space_constraint(ao_values, pltpu.HBM)
    potential = pltpu.with_memory_space_constraint(kernel, pltpu.HBM)
    tiles, acc, ao, potential = call(
        functools.partial(inner_kernel, geo),
        (
            pltpu.VMEM((geo.total, nb, nb), jnp.bfloat16),
            pltpu.VMEM((geo.total, nb, nb), jnp.float32),
            pltpu.VMEM(ao_values.shape, jnp.bfloat16),
            pltpu.VMEM(kernel.shape, jnp.bfloat16),
        ),
        [SMEM_SPEC] * 4 + [ANY_SPEC] * 3 + [VMEM_SPEC],
        (VMEM_SPEC,) * 4,
        [dma((3, batches))],
        (flops, 2 * geo.own * block, 16),
    )(*scalars, flat, ao, potential, grid_weights)

    tiles, acc, first, second = call(
        functools.partial(edge_kernel, geo),
        (
            pltpu.VMEM((geo.total, nb, nb), jnp.bfloat16),
            pltpu.VMEM((geo.total, nb, nb), jnp.float32),
            pack,
            pack,
        ),
        [SMEM_SPEC] * 4 + [VMEM_SPEC] * 7,
        (VMEM_SPEC,) * 4,
        [dma((2,))],
        (flops, 8 * geo.halo * block, 16),
        {9: 0, 10: 1},
    )(*scalars, first, second, ao, potential, grid_weights, tiles, acc)
    first, second = exchange_pairs(first, second, size)

    out = call(
        functools.partial(quiet_kernel, geo),
        jax.ShapeDtypeStruct((geo.own, nb, nb), jnp.float32),
        [VMEM_SPEC],
        ANY_SPEC,
        [dma((len(geo.quiet),))],
        (0, 4 * geo.own * block, 16),
    )(acc)
    out = call(
        functools.partial(finish_kernel, geo),
        jax.ShapeDtypeStruct((geo.own, nb, nb), jnp.float32),
        [SMEM_SPEC] + [VMEM_SPEC] * 3 + [ANY_SPEC],
        ANY_SPEC,
        [pltpu.VMEM((2 * geo.halo, nb, nb), jnp.float32), dma((2 * geo.reach,))],
        (0, 20 * geo.halo * block, 16),
        {4: 0},
    )(index, first, second, acc, out)
    return out.reshape(rows, band, nb, nb)


def solution(mesh):
    placed = (
        P(("groups", "blk"), None, None, None),
        P(("groups", "blk"), None, None, None),
        P(("groups", "blk"), None, None),
        P(("groups", "blk"), None),
        P(("groups", "blk")),
        P(("groups", "blk"), None),
        P(("groups", "blk")),
    )
    return jax.shard_map(
        local,
        mesh=mesh,
        in_specs=placed,
        out_specs=P(("groups", "blk"), None, None, None),
        check_vma=False,
    )
```

```python
import functools

import jax
import jax.numpy as jnp
from jax import lax
from jax.experimental import pallas as pl
from jax.experimental.pallas import tpu as pltpu
from jax.sharding import PartitionSpec as P

MIB = 1 << 20
GROUP = 2
LISTS = 6
SMEM_SPEC = pl.BlockSpec(memory_space=pltpu.SMEM)
VMEM_SPEC = pl.BlockSpec(memory_space=pltpu.VMEM)
ANY_SPEC = pl.BlockSpec(memory_space=pl.ANY)


class Geometry:
    def __init__(self, rows, band, batches, slots):
        self.rows, self.band, self.batches, self.slots = rows, band, batches, slots
        self.half = half = (band - 1) // 2
        self.reach = reach = half // 2
        self.own = rows * band
        low = [(-m, reach + m, band) for m in range(reach, 0, -1)]
        high = [(rows + m, 0, 3 * reach - m) for m in range(reach)]
        self.halo = sum(stop - start for _, start, stop in low)
        low_cut = [half - row for row, _, _ in low]
        high_cut = [rows - row + half for row, _, _ in high]
        early = (
            [(row, cut, stop) for (row, _, stop), cut in zip(low, low_cut)],
            [(row, start, cut) for (row, start, _), cut in zip(high, high_cut)],
        )
        late = (
            [(row, start, cut) for (row, start, _), cut in zip(low, low_cut)],
            [(row, cut, stop) for (row, _, stop), cut in zip(high, high_cut)],
        )
        self.early = sum(stop - start for _, start, stop in early[0])
        self.late = self.halo - self.early
        self.first_at = self.own
        self.early_at = self.own + self.halo
        self.late_at = self.early_at + self.early
        self.spare = self.late_at + self.late
        cut = (self.halo + 1) // 2
        self.pieces = ((0, cut), (cut, self.halo - cut))
        self.halo_base = self.bases((low, high))
        self.early_base = self.bases(early)
        self.late_base = self.bases(late)
        shifts = (rows, -rows)
        self.packs = [self.places(*pair) for pair in zip((low, high), shifts)]
        self.early_packs = [self.places(*pair) for pair in zip(early, shifts)]
        self.late_packs = [self.places(*pair) for pair in zip(late, shifts)]
        touched = set()
        for start, _, count in self.packs[0] + self.packs[1]:
            touched.update(range(start, start + count))
        self.quiet = []
        for index in range(self.own):
            if index in touched:
                continue
            if self.quiet and sum(self.quiet[-1]) == index:
                self.quiet[-1] = (self.quiet[-1][0], self.quiet[-1][1] + 1)
            else:
                self.quiet.append((index, 1))
        self.list_size = batches + 2
        self.lengths_at = LISTS * self.list_size
        self.local_at = self.lengths_at + LISTS
        self.count_at = self.local_at + batches
        self.offsets_at = self.count_at + batches
        self.meta_size = self.offsets_at + slots * batches

    def bases(self, sides):
        found = {}
        for segments in sides:
            place = 0
            for row, start, stop in segments:
                found[row] = place - start
                place += stop - start
        return found

    def places(self, segments, shift):
        pack, place = ([], 0)
        for row, start, stop in segments:
            pack.append(((row + shift) * self.band + start, place, stop - start))
            place += stop - start
        return pack

    def near_packs(self, piece):
        begin, count = self.pieces[piece]
        found = []
        for pack in self.packs:
            part = []
            for start, place, size in pack:
                low, high = max(place, begin), min(place + size, begin + count)
                if low < high:
                    part.append((start + low - place, low - begin, high - low))
            found.append(part)
        return found

    def pick(self, bases, shift, row, otherwise):
        value = otherwise
        for at, base in bases.items():
            value = jnp.where(row == at, base + shift, value)
        return value


def run_copies(copies):
    for copy in copies:
        copy.start()
    for copy in copies:
        copy.wait()


def by_parity(index_ref, body, first, second):
    odd = index_ref[0] % 2 == 1

    @pl.when(jnp.logical_not(odd))
    def _():
        body(first, second)

    @pl.when(odd)
    def _():
        body(second, first)


def pack_copies(geo, index_ref, density_ref, out_ref, sems, first, act):
    odd = index_ref[0] % 2 == 1
    upper = jnp.logical_not(odd) if first else odd
    for pack, chosen in zip(geo.packs, (upper, jnp.logical_not(upper))):

        @pl.when(chosen)
        def _(pack=pack):
            for i, (start, place, count) in enumerate(pack):
                act(
                    pltpu.make_async_copy(
                        density_ref.at[pl.ds(start, count)], out_ref.at[pl.ds(place, count)], sems.at[i]
                    )
                )


def pack_kernel(geo, index_ref, density_ref, first_ref, second_ref, sems):
    packing = (geo, index_ref, density_ref)
    for act in (lambda copy: copy.start(), lambda copy: copy.wait()):
        pack_copies(*packing, second_ref, sems.at[1], False, act)
        pack_copies(*packing, first_ref, sems.at[0], True, act)


CROSS_MANY, CROSS_FEW, NEAR_MANY, NEAR_FEW, INNER_MANY, INNER_FEW = range(LISTS)


def build_lists(geo, index_ref, centre_ref, offsets_ref, counts_ref, meta_ref):
    first = index_ref[0] * geo.rows
    odd = index_ref[0] % 2 == 1
    lengths = [jnp.int32(0)] * LISTS
    for b in range(geo.batches):
        local = centre_ref[b] - first
        count = counts_ref[b]
        meta_ref[geo.local_at + b] = local
        meta_ref[geo.count_at + b] = count
        low = high = jnp.bool_(False)
        for k in range(geo.slots):
            offset = offsets_ref[k, b]
            meta_ref[geo.offsets_at + k * geo.batches + b] = offset
            row = local + offset
            low = low | ((k < count) & (row < 0))
            high = high | ((k < count) & (row >= geo.rows))
        cross = (odd & high) | (jnp.logical_not(odd) & low)
        near = (odd & low) | (jnp.logical_not(odd) & high)
        inner = jnp.logical_not(low | high)
        many = count > 2
        few = (count > 0) & jnp.logical_not(many)
        kinds = [kind & size for kind in (cross, near, inner) for size in (many, few)]
        for which, member in enumerate(kinds):
            meta_ref[which * geo.list_size + lengths[which]] = b
            lengths[which] = lengths[which] + member.astype(jnp.int32)
    for which in range(LISTS):
        meta_ref[which * geo.list_size + lengths[which]] = geo.batches
        meta_ref[geo.lengths_at + which] = lengths[which]


def each_group(geo, meta_ref, which, size, body):
    length = meta_ref[geo.lengths_at + which]

    def step(i, carry):
        chosen = []
        for n in range(size):
            place = i * size + n
            there = place < length
            b = meta_ref[which * geo.list_size + jnp.minimum(place, length)]
            chosen.append((jnp.where(there, b, 0), there))
        body(chosen)
        return carry

    lax.fori_loop(0, (length + size - 1) // size, step, 0)


class Slots:
    def __init__(self, geo, meta_ref, b, there, width):
        local = meta_ref[geo.local_at + b]
        count = jnp.where(there, meta_ref[geo.count_at + b], 0)
        self.offset = [meta_ref[geo.offsets_at + k * geo.batches + b] for k in range(width)]
        self.local = local
        self.row = [local + offset for offset in self.offset]
        self.live = [k < count for k in range(width)]
        self.own = [(row >= 0) & (row < geo.rows) for row in self.row]
        self.width = width


def panels(slots, ao_ref, b):
    return jnp.concatenate(
        [
            ao_ref[b, k] * jnp.where(slots.live[k], 1.0, 0.0).astype(ao_ref.dtype)
            for k in range(slots.width)
        ],
        axis=0,
    )


def gathered(tiles_ref, places):
    return jnp.concatenate(
        [jnp.concatenate([tiles_ref[place] for place in row], axis=1) for row in places], axis=0
    )


def chain(xs, tiles, batches, kernel_ref, weights_ref):
    fs = [
        jnp.dot(t, x, preferred_element_type=jnp.float32).astype(jnp.bfloat16)
        for t, x in zip(tiles, xs)
    ]
    gs = [
        jnp.dot(f, kernel_ref[b], preferred_element_type=jnp.float32) for f, b in zip(fs, batches)
    ]
    hs = [(g * weights_ref[pl.ds(b, 1), :]).astype(jnp.bfloat16) for g, b in zip(gs, batches)]
    return [
        lax.dot_general(x, h, (((1,), (1,)), ((), ())), preferred_element_type=jnp.float32)
        for x, h in zip(xs, hs)
    ]


def scatter(part, target, nb, acc_ref):
    for k, row in enumerate(target):
        for j, place in enumerate(row):
            acc_ref[place] += part[k * nb : (k + 1) * nb, j * nb : (j + 1) * nb]


def add_whole(geo, chosen, width, meta_ref, tiles_ref, ao_ref, kernel_ref, weights_ref, acc_ref):
    xs, tiles, targets = ([], [], [])
    for b, there in chosen:
        slots = Slots(geo, meta_ref, b, there, width)
        xs.append(panels(slots, ao_ref, b))
        places, target = ([], [])
        for k in range(width):
            row = slots.row[k]
            base = jnp.where(slots.live[k] & slots.own[k], row, 0) * geo.band
            base = jnp.where(
                slots.live[k], geo.pick(geo.halo_base, geo.first_at, row, base), base
            )
            place = [base + slots.offset[j] - slots.offset[k] + geo.half for j in range(width)]
            places.append(place)
            target.append(
                [jnp.where(slots.live[k] & slots.live[j], place[j], geo.spare) for j in range(width)]
            )
        tiles.append(gathered(tiles_ref, places))
        targets.append(target)
    parts = chain(xs, tiles, [b for b, _ in chosen], kernel_ref, weights_ref)
    for part, target in zip(parts, targets):
        scatter(part, target, ao_ref.shape[2], acc_ref)


def add_own(geo, chosen, width, meta_ref, tiles_ref, ao_ref, kernel_ref, weights_ref, acc_ref):
    xs, tiles, targets = ([], [], [])
    for b, there in chosen:
        slots = Slots(geo, meta_ref, b, there, width)
        xs.append(panels(slots, ao_ref, b))
        places, target = ([], [])
        for k in range(width):
            row = slots.row[k]
            band = [slots.offset[j] - slots.offset[k] + geo.half for j in range(width)]
            base = jnp.where(slots.own[k], row, 0) * geo.band
            places.append([base + o for o in band])
            base = geo.pick(geo.early_base, geo.early_at, row, base)
            target.append(
                [
                    jnp.where(
                        slots.live[k] & slots.live[j] & slots.own[j], base + band[j], geo.spare
                    )
                    for j in range(width)
                ]
            )
        tiles.append(gathered(tiles_ref, places))
        targets.append(target)
    parts = chain(xs, tiles, [b for b, _ in chosen], kernel_ref, weights_ref)
    for part, target in zip(parts, targets):
        scatter(part, target, ao_ref.shape[2], acc_ref)


def add_halo(geo, chosen, width, meta_ref, halo_ref, ao_ref, kernel_ref, weights_ref, acc_ref):
    outer = min(geo.reach, width)
    xs, tiles, targets = ([], [], [])
    for b, there in chosen:
        slots = Slots(geo, meta_ref, b, there, width)
        xs.append(panels(slots, ao_ref, b))
        found = jnp.int32(0)
        picked = [jnp.int32(0)] * outer
        for k in range(width):
            away = slots.live[k] & jnp.logical_not(slots.own[k])
            for i in range(outer):
                picked[i] = jnp.where(away & (found <= i), slots.offset[k], picked[i])
            found = found + away.astype(jnp.int32)
        places, target = ([], [[None] * outer for _ in range(width)])
        for i in range(outer):
            base = geo.pick(geo.halo_base, 0, slots.local + picked[i], 0)
            places.append(
                [
                    jnp.where(there, base + slots.offset[j] - picked[i] + geo.half, 0)
                    for j in range(width)
                ]
            )
        for k in range(width):
            row = slots.row[k]
            base = geo.pick(geo.late_base, geo.late_at, row, row * geo.band)
            for i in range(outer):
                target[k][i] = jnp.where(
                    slots.live[k] & (i < found),
                    base + picked[i] - slots.offset[k] + geo.half,
                    geo.spare,
                )
        tiles.append(gathered(halo_ref, places))
        targets.append(target)
    parts = chain(xs, tiles, [b for b, _ in chosen], kernel_ref, weights_ref)
    for part, target in zip(parts, targets):
        scatter(part, target, ao_ref.shape[2], acc_ref)


def early_kernel(
    geo, index_ref, centre_ref, offsets_ref, counts_ref, density_ref, ao_ref, kernel_ref, weights_ref,
    meta_ref, tiles_ref, acc_ref, early_out, sem,
):
    copy = pltpu.make_async_copy(density_ref, tiles_ref.at[pl.ds(0, geo.own)], sem)
    copy.start()
    build_lists(geo, index_ref, centre_ref, offsets_ref, counts_ref, meta_ref)
    acc_ref[...] = jnp.zeros_like(acc_ref)
    copy.wait()
    refs = (meta_ref, tiles_ref, ao_ref, kernel_ref, weights_ref, acc_ref)
    for which, width in ((CROSS_MANY, geo.slots), (CROSS_FEW, 2)):
        each_group(
            geo, meta_ref, which, GROUP, lambda chosen, width=width: add_own(geo, chosen, width, *refs)
        )
    early_out[...] = acc_ref[pl.ds(geo.early_at, geo.early)].astype(early_out.dtype)


def near_kernel(
    geo, meta_ref, halo_ref, ao_ref, kernel_ref, weights_ref, tiles_in, acc_in,
    tiles_ref, acc_ref, *rest,
):
    outs, sem = rest[:-1], rest[-1]
    run_copies(
        [pltpu.make_async_copy(halo_ref, tiles_ref.at[pl.ds(geo.first_at, geo.halo)], sem)]
    )
    refs = (meta_ref, tiles_ref, ao_ref, kernel_ref, weights_ref, acc_ref)
    for which, width in ((NEAR_MANY, geo.slots), (NEAR_FEW, 2)):
        each_group(
            geo, meta_ref, which, GROUP, lambda chosen, width=width: add_whole(geo, chosen, width, *refs)
        )
    for out, (start, count) in zip(outs, geo.pieces):
        out[...] = acc_ref[pl.ds(geo.first_at + start, count)].astype(out.dtype)


def late_kernel(
    geo, meta_ref, halo_ref, ao_ref, kernel_ref, weights_ref, acc_in, acc_ref, late_out
):
    refs = (meta_ref, halo_ref, ao_ref, kernel_ref, weights_ref, acc_ref)
    for which, width in ((CROSS_MANY, geo.slots), (CROSS_FEW, 2)):
        each_group(
            geo, meta_ref, which, GROUP, lambda chosen, width=width: add_halo(geo, chosen, width, *refs)
        )
    late_out[...] = acc_ref[pl.ds(geo.late_at, geo.late)].astype(late_out.dtype)


def inner_kernel(
    geo, meta_ref, tiles_ref, ao_ref, kernel_ref, weights_ref, acc_in, acc_ref, out_ref, sems
):
    refs = (meta_ref, tiles_ref, ao_ref, kernel_ref, weights_ref, acc_ref)
    for which, width in ((INNER_MANY, geo.slots), (INNER_FEW, 2)):
        each_group(
            geo, meta_ref, which, GROUP, lambda chosen, width=width: add_whole(geo, chosen, width, *refs)
        )
    run_copies(
        [
            pltpu.make_async_copy(
                acc_ref.at[pl.ds(start, count)], out_ref.at[pl.ds(start, count)], sems.at[i]
            )
            for i, (start, count) in enumerate(geo.quiet)
        ]
    )


def finish_kernel(
    geo, index_ref, early_ref, late_ref, near_a, near_b, acc_ref, out_in, out_ref, total, sems
):
    def add(up, down):
        copies = []
        for side, parts in enumerate((up, down)):
            for packs, ref in parts:
                for start, place, count in packs[side]:
                    spot = pl.ds(len(copies) * geo.band, count)
                    total[spot] = acc_ref[pl.ds(start, count)] + ref[pl.ds(place, count)].astype(
                        jnp.float32
                    )
                    copy = pltpu.make_async_copy(
                        total.at[spot], out_ref.at[pl.ds(start, count)], sems.at[len(copies)]
                    )
                    copy.start()
                    copies.append(copy)
        for copy in copies:
            copy.wait()

    near = ((geo.near_packs(0), near_a), (geo.near_packs(1), near_b))
    by_parity(index_ref, add, near, ((geo.early_packs, early_ref), (geo.late_packs, late_ref)))


def call(kernel, out_shape, in_specs, out_specs, scratch, aliases=None, cost=None):
    return pl.pallas_call(
        kernel,
        out_shape=out_shape,
        in_specs=in_specs,
        out_specs=out_specs,
        scratch_shapes=scratch,
        input_output_aliases=aliases or {},
        cost_estimate=cost,
        compiler_params=pltpu.CompilerParams(vmem_limit_bytes=16 * MIB),
    )


def to_first(x, size):
    pairs = [(i, i + 1) for i in range(0, size - 1, 2)]
    got = lax.ppermute(x, "blk", pairs + [(j, i) for i, j in pairs])
    return pltpu.with_memory_space_constraint(got, pltpu.VMEM)


def to_second(x, size):
    pairs = [(i, i + 1) for i in range(1, size - 1, 2)]
    got = lax.ppermute(x, "blk", pairs + [(j, i) for i, j in pairs])
    return pltpu.with_memory_space_constraint(got, pltpu.VMEM)


def local(density, ao_values, kernel, grid_weights, centre, sig_offsets, counts):
    rows, band, nb, _ = density.shape
    batches, slots, _, pts = ao_values.shape
    size = lax.axis_size("blk")
    geo = Geometry(rows, band, batches, slots)
    index = lax.axis_index("blk").astype(jnp.int32).reshape(1)
    in_hbm = lambda x: pltpu.with_memory_space_constraint(x, pltpu.HBM)
    flat = in_hbm(density.reshape(geo.own, nb, nb))
    pack = lambda count: pltpu.VMEM((count, nb, nb), jnp.bfloat16)
    dma = pltpu.SemaphoreType.DMA
    tiles_type = pltpu.VMEM((geo.own + geo.halo, nb, nb), jnp.bfloat16)
    acc_type = pltpu.VMEM((geo.spare + 1, nb, nb), jnp.float32)

    near_halo, cross_halo = call(
        functools.partial(pack_kernel, geo),
        (pack(geo.halo),) * 2,
        [SMEM_SPEC, ANY_SPEC],
        (VMEM_SPEC,) * 2,
        [dma((2, geo.reach))],
        cost=pl.CostEstimate(flops=10**10, bytes_accessed=10**8, transcendentals=0),
    )(index, flat)
    cross_halo = to_second(cross_halo, size)
    near_halo = to_first(near_halo, size)

    panel = (ao_values, kernel, grid_weights)
    meta, tiles, acc, early = call(
        functools.partial(early_kernel, geo),
        (pltpu.SMEM((geo.meta_size,), jnp.int32), tiles_type, acc_type, pack(geo.early)),
        [SMEM_SPEC] * 4 + [ANY_SPEC] + [VMEM_SPEC] * 3,
        (SMEM_SPEC,) + (VMEM_SPEC,) * 3,
        [dma],
    )(index, in_hbm(centre), in_hbm(sig_offsets.T), in_hbm(counts), flat, *panel)
    early = to_second(early, size)

    tiles, acc, *near = call(
        functools.partial(near_kernel, geo),
        (tiles_type, acc_type) + tuple(pack(count) for _, count in geo.pieces),
        [SMEM_SPEC] + [VMEM_SPEC] * 6,
        (VMEM_SPEC,) * 4,
        [dma],
        {5: 0, 6: 1},
    )(meta, near_halo, *panel, tiles, acc)
    near = [to_first(piece, size) for piece in near]

    acc, late = call(
        functools.partial(late_kernel, geo),
        (acc_type, pack(geo.late)),
        [SMEM_SPEC] + [VMEM_SPEC] * 5,
        (VMEM_SPEC,) * 2,
        [],
        {5: 0},
    )(meta, cross_halo, *panel, acc)
    late = to_second(late, size)

    whole = jax.ShapeDtypeStruct((geo.own, nb, nb), jnp.float32)
    acc, out = call(
        functools.partial(inner_kernel, geo),
        (acc_type, whole),
        [SMEM_SPEC] + [VMEM_SPEC] * 5,
        (VMEM_SPEC, ANY_SPEC),
        [dma((len(geo.quiet),))],
        {5: 0},
    )(meta, tiles, *panel, acc)

    pieces = 2 * (2 * geo.reach)
    out = call(
        functools.partial(finish_kernel, geo),
        whole,
        [SMEM_SPEC] + [VMEM_SPEC] * 5 + [ANY_SPEC],
        ANY_SPEC,
        [pltpu.VMEM((pieces * band, nb, nb), jnp.float32), dma((pieces,))],
        {6: 0},
    )(index, early, late, *near, acc, out)
    return out.reshape(rows, band, nb, nb)


def solution(mesh):
    placed = (
        P(("groups", "blk"), None, None, None),
        P(("groups", "blk"), None, None, None),
        P(("groups", "blk"), None, None),
        P(("groups", "blk"), None),
        P(("groups", "blk")),
        P(("groups", "blk"), None),
        P(("groups", "blk")),
    )
    return jax.shard_map(
        local,
        mesh=mesh,
        in_specs=placed,
        out_specs=P(("groups", "blk"), None, None, None),
        check_vma=False,
    )
```

```python
import functools

import jax
import jax.numpy as jnp
from jax import lax
from jax.experimental import pallas as pl
from jax.experimental.pallas import tpu as pltpu
from jax.sharding import PartitionSpec as P

MIB = 1 << 20
GROUP = 2
LISTS = 6
SMEM_SPEC = pl.BlockSpec(memory_space=pltpu.SMEM)
VMEM_SPEC = pl.BlockSpec(memory_space=pltpu.VMEM)
ANY_SPEC = pl.BlockSpec(memory_space=pl.ANY)


class Geometry:
    def __init__(self, rows, band, batches, slots):
        self.rows, self.band, self.batches, self.slots = rows, band, batches, slots
        self.half = half = (band - 1) // 2
        self.reach = reach = half // 2
        self.own = rows * band
        low = [(-m, reach + m, band) for m in range(reach, 0, -1)]
        high = [(rows + m, 0, 3 * reach - m) for m in range(reach)]
        self.halo = sum(stop - start for _, start, stop in low)
        low_cut = [half - row for row, _, _ in low]
        high_cut = [rows - row + half for row, _, _ in high]
        early = (
            [(row, cut, stop) for (row, _, stop), cut in zip(low, low_cut)],
            [(row, start, cut) for (row, start, _), cut in zip(high, high_cut)],
        )
        late = (
            [(row, start, cut) for (row, start, _), cut in zip(low, low_cut)],
            [(row, cut, stop) for (row, _, stop), cut in zip(high, high_cut)],
        )
        self.early = sum(stop - start for _, start, stop in early[0])
        self.late = self.halo - self.early
        self.first_at = self.own
        self.early_at = self.own + self.halo
        self.late_at = self.early_at + self.early
        self.spare = self.late_at + self.late
        self.halo_base = self.bases((low, high))
        self.early_base = self.bases(early)
        self.late_base = self.bases(late)
        shifts = (rows, -rows)
        self.packs = [self.places(*pair) for pair in zip((low, high), shifts)]
        self.early_packs = [self.places(*pair) for pair in zip(early, shifts)]
        self.late_packs = [self.places(*pair) for pair in zip(late, shifts)]
        self.quiet = [self.others(self.packs[1 - near]) for near in range(2)]
        self.list_size = batches + 2
        self.lengths_at = LISTS * self.list_size
        self.local_at = self.lengths_at + LISTS
        self.count_at = self.local_at + batches
        self.offsets_at = self.count_at + batches
        self.meta_size = self.offsets_at + slots * batches

    def bases(self, sides):
        found = {}
        for segments in sides:
            place = 0
            for row, start, stop in segments:
                found[row] = place - start
                place += stop - start
        return found

    def places(self, segments, shift):
        pack, place = ([], 0)
        for row, start, stop in segments:
            pack.append(((row + shift) * self.band + start, place, stop - start))
            place += stop - start
        return pack

    def others(self, pack):
        touched = set()
        for start, _, count in pack:
            touched.update(range(start, start + count))
        runs = []
        for index in range(self.own):
            if index in touched:
                continue
            if runs and sum(runs[-1]) == index:
                runs[-1] = (runs[-1][0], runs[-1][1] + 1)
            else:
                runs.append((index, 1))
        return runs

    def pick(self, bases, shift, row, otherwise):
        value = otherwise
        for at, base in bases.items():
            value = jnp.where(row == at, base + shift, value)
        return value


def run_copies(copies):
    for copy in copies:
        copy.start()
    for copy in copies:
        copy.wait()


def by_parity(index_ref, body, first, second):
    odd = index_ref[0] % 2 == 1

    @pl.when(jnp.logical_not(odd))
    def _():
        body(first, second)

    @pl.when(odd)
    def _():
        body(second, first)


def pack_kernel(geo, index_ref, density_ref, near_ref, cross_ref, sems):
    def fill(up, down):
        copies = []
        for pack, ref in zip(geo.packs, (up, down)):
            for start, place, count in pack:
                copies.append(
                    pltpu.make_async_copy(
                        density_ref.at[pl.ds(start, count)],
                        ref.at[pl.ds(place, count)],
                        sems.at[len(copies)],
                    )
                )
        run_copies(copies)

    by_parity(index_ref, fill, near_ref, cross_ref)


CROSS_MANY, CROSS_FEW, NEAR_MANY, NEAR_FEW, INNER_MANY, INNER_FEW = range(LISTS)


def build_lists(geo, index_ref, centre_ref, offsets_ref, counts_ref, meta_ref):
    first = index_ref[0] * geo.rows
    odd = index_ref[0] % 2 == 1
    lengths = [jnp.int32(0)] * LISTS
    for b in range(geo.batches):
        local = centre_ref[b] - first
        count = counts_ref[b]
        meta_ref[geo.local_at + b] = local
        meta_ref[geo.count_at + b] = count
        low = high = jnp.bool_(False)
        for k in range(geo.slots):
            offset = offsets_ref[k, b]
            meta_ref[geo.offsets_at + k * geo.batches + b] = offset
            row = local + offset
            low = low | ((k < count) & (row < 0))
            high = high | ((k < count) & (row >= geo.rows))
        cross = (odd & high) | (jnp.logical_not(odd) & low)
        near = (odd & low) | (jnp.logical_not(odd) & high)
        inner = jnp.logical_not(low | high)
        many = count > 2
        few = (count > 0) & jnp.logical_not(many)
        kinds = [kind & size for kind in (cross, near, inner) for size in (many, few)]
        for which, member in enumerate(kinds):
            meta_ref[which * geo.list_size + lengths[which]] = b
            lengths[which] = lengths[which] + member.astype(jnp.int32)
    for which in range(LISTS):
        meta_ref[which * geo.list_size + lengths[which]] = geo.batches
        meta_ref[geo.lengths_at + which] = lengths[which]


def each_group(geo, meta_ref, which, size, body):
    length = meta_ref[geo.lengths_at + which]

    def step(i, carry):
        chosen = []
        for n in range(size):
            place = i * size + n
            there = place < length
            b = meta_ref[which * geo.list_size + jnp.minimum(place, length)]
            chosen.append((jnp.where(there, b, 0), there))
        body(chosen)
        return carry

    lax.fori_loop(0, (length + size - 1) // size, step, 0)


class Slots:
    def __init__(self, geo, meta_ref, b, there, width):
        local = meta_ref[geo.local_at + b]
        count = jnp.where(there, meta_ref[geo.count_at + b], 0)
        self.offset = [meta_ref[geo.offsets_at + k * geo.batches + b] for k in range(width)]
        self.local = local
        self.row = [local + offset for offset in self.offset]
        self.live = [k < count for k in range(width)]
        self.own = [(row >= 0) & (row < geo.rows) for row in self.row]
        self.width = width


def panels(slots, ao_ref, b):
    return jnp.concatenate(
        [
            ao_ref[b, k] * jnp.where(slots.live[k], 1.0, 0.0).astype(ao_ref.dtype)
            for k in range(slots.width)
        ],
        axis=0,
    )


def gathered(tiles_ref, places):
    return jnp.concatenate(
        [jnp.concatenate([tiles_ref[place] for place in row], axis=1) for row in places], axis=0
    )


def chain(xs, tiles, batches, kernel_ref, weights_ref):
    fs = [
        jnp.dot(t, x, preferred_element_type=jnp.float32).astype(jnp.bfloat16)
        for t, x in zip(tiles, xs)
    ]
    gs = [
        jnp.dot(f, kernel_ref[b], preferred_element_type=jnp.float32) for f, b in zip(fs, batches)
    ]
    hs = [(g * weights_ref[pl.ds(b, 1), :]).astype(jnp.bfloat16) for g, b in zip(gs, batches)]
    return [
        lax.dot_general(x, h, (((1,), (1,)), ((), ())), preferred_element_type=jnp.float32)
        for x, h in zip(xs, hs)
    ]


def scatter(part, target, nb, acc_ref):
    for k, row in enumerate(target):
        for j, place in enumerate(row):
            acc_ref[place] += part[k * nb : (k + 1) * nb, j * nb : (j + 1) * nb]


def add_whole(geo, chosen, width, meta_ref, tiles_ref, ao_ref, kernel_ref, weights_ref, acc_ref):
    xs, tiles, targets = ([], [], [])
    for b, there in chosen:
        slots = Slots(geo, meta_ref, b, there, width)
        xs.append(panels(slots, ao_ref, b))
        places, target = ([], [])
        for k in range(width):
            row = slots.row[k]
            base = jnp.where(slots.live[k] & slots.own[k], row, 0) * geo.band
            base = jnp.where(
                slots.live[k], geo.pick(geo.halo_base, geo.first_at, row, base), base
            )
            place = [base + slots.offset[j] - slots.offset[k] + geo.half for j in range(width)]
            places.append(place)
            target.append(
                [jnp.where(slots.live[k] & slots.live[j], place[j], geo.spare) for j in range(width)]
            )
        tiles.append(gathered(tiles_ref, places))
        targets.append(target)
    parts = chain(xs, tiles, [b for b, _ in chosen], kernel_ref, weights_ref)
    for part, target in zip(parts, targets):
        scatter(part, target, ao_ref.shape[2], acc_ref)


def add_own(geo, chosen, width, meta_ref, tiles_ref, ao_ref, kernel_ref, weights_ref, acc_ref):
    xs, tiles, targets = ([], [], [])
    for b, there in chosen:
        slots = Slots(geo, meta_ref, b, there, width)
        xs.append(panels(slots, ao_ref, b))
        places, target = ([], [])
        for k in range(width):
            row = slots.row[k]
            band = [slots.offset[j] - slots.offset[k] + geo.half for j in range(width)]
            base = jnp.where(slots.own[k], row, 0) * geo.band
            places.append([base + o for o in band])
            base = geo.pick(geo.early_base, geo.early_at, row, base)
            target.append(
                [
                    jnp.where(
                        slots.live[k] & slots.live[j] & slots.own[j], base + band[j], geo.spare
                    )
                    for j in range(width)
                ]
            )
        tiles.append(gathered(tiles_ref, places))
        targets.append(target)
    parts = chain(xs, tiles, [b for b, _ in chosen], kernel_ref, weights_ref)
    for part, target in zip(parts, targets):
        scatter(part, target, ao_ref.shape[2], acc_ref)


def add_halo(geo, chosen, width, meta_ref, halo_ref, ao_ref, kernel_ref, weights_ref, acc_ref):
    outer = min(geo.reach, width)
    xs, tiles, targets = ([], [], [])
    for b, there in chosen:
        slots = Slots(geo, meta_ref, b, there, width)
        xs.append(panels(slots, ao_ref, b))
        found = jnp.int32(0)
        picked = [jnp.int32(0)] * outer
        for k in range(width):
            away = slots.live[k] & jnp.logical_not(slots.own[k])
            for i in range(outer):
                picked[i] = jnp.where(away & (found <= i), slots.offset[k], picked[i])
            found = found + away.astype(jnp.int32)
        places, target = ([], [[None] * outer for _ in range(width)])
        for i in range(outer):
            base = geo.pick(geo.halo_base, 0, slots.local + picked[i], 0)
            places.append(
                [
                    jnp.where(there, base + slots.offset[j] - picked[i] + geo.half, 0)
                    for j in range(width)
                ]
            )
        for k in range(width):
            row = slots.row[k]
            base = geo.pick(geo.late_base, geo.late_at, row, row * geo.band)
            for i in range(outer):
                target[k][i] = jnp.where(
                    slots.live[k] & (i < found),
                    base + picked[i] - slots.offset[k] + geo.half,
                    geo.spare,
                )
        tiles.append(gathered(halo_ref, places))
        targets.append(target)
    parts = chain(xs, tiles, [b for b, _ in chosen], kernel_ref, weights_ref)
    for part, target in zip(parts, targets):
        scatter(part, target, ao_ref.shape[2], acc_ref)


def early_kernel(
    geo, index_ref, centre_ref, offsets_ref, counts_ref, density_ref, ao_ref, kernel_ref, weights_ref,
    meta_ref, tiles_ref, acc_ref, early_out, sem,
):
    copy = pltpu.make_async_copy(density_ref, tiles_ref.at[pl.ds(0, geo.own)], sem)
    copy.start()
    build_lists(geo, index_ref, centre_ref, offsets_ref, counts_ref, meta_ref)
    acc_ref[...] = jnp.zeros_like(acc_ref)
    copy.wait()
    refs = (meta_ref, tiles_ref, ao_ref, kernel_ref, weights_ref, acc_ref)
    for which, width in ((CROSS_MANY, geo.slots), (CROSS_FEW, 2)):
        each_group(
            geo, meta_ref, which, GROUP, lambda chosen, width=width: add_own(geo, chosen, width, *refs)
        )
    early_out[...] = acc_ref[pl.ds(geo.early_at, geo.early)].astype(early_out.dtype)


def near_kernel(
    geo, meta_ref, halo_ref, ao_ref, kernel_ref, weights_ref, tiles_in, acc_in,
    tiles_ref, acc_ref, first_out, sem,
):
    run_copies(
        [pltpu.make_async_copy(halo_ref, tiles_ref.at[pl.ds(geo.first_at, geo.halo)], sem)]
    )
    refs = (meta_ref, tiles_ref, ao_ref, kernel_ref, weights_ref, acc_ref)
    for which, width in ((NEAR_MANY, geo.slots), (NEAR_FEW, 2)):
        each_group(
            geo, meta_ref, which, GROUP, lambda chosen, width=width: add_whole(geo, chosen, width, *refs)
        )
    first_out[...] = acc_ref[pl.ds(geo.first_at, geo.halo)].astype(first_out.dtype)


def late_kernel(
    geo, meta_ref, halo_ref, ao_ref, kernel_ref, weights_ref, acc_in, acc_ref, late_out
):
    refs = (meta_ref, halo_ref, ao_ref, kernel_ref, weights_ref, acc_ref)
    for which, width in ((CROSS_MANY, geo.slots), (CROSS_FEW, 2)):
        each_group(
            geo, meta_ref, which, GROUP, lambda chosen, width=width: add_halo(geo, chosen, width, *refs)
        )
    late_out[...] = acc_ref[pl.ds(geo.late_at, geo.late)].astype(late_out.dtype)


def inner_kernel(
    geo, index_ref, meta_ref, first_ref, tiles_ref, ao_ref, kernel_ref, weights_ref, acc_in,
    acc_ref, out_ref, sems,
):
    refs = (meta_ref, tiles_ref, ao_ref, kernel_ref, weights_ref, acc_ref)
    for which, width in ((INNER_MANY, geo.slots), (INNER_FEW, 2)):
        each_group(
            geo, meta_ref, which, GROUP, lambda chosen, width=width: add_whole(geo, chosen, width, *refs)
        )

    def finish_near(up, down):
        near = 0 if up else 1
        for start, place, count in geo.packs[near]:
            acc_ref[pl.ds(start, count)] += first_ref[pl.ds(place, count)].astype(jnp.float32)
        run_copies(
            [
                pltpu.make_async_copy(
                    acc_ref.at[pl.ds(start, count)], out_ref.at[pl.ds(start, count)], sems.at[i]
                )
                for i, (start, count) in enumerate(geo.quiet[near])
            ]
        )

    by_parity(index_ref, finish_near, True, False)


def finish_kernel(geo, index_ref, early_ref, late_ref, acc_ref, out_in, out_ref, total, sems):
    def add(up, down):
        copies = []
        for packs, ref in ((geo.early_packs, early_ref), (geo.late_packs, late_ref)):
            for start, place, count in packs[0 if up else 1]:
                spot = pl.ds(len(copies) * geo.band, count)
                total[spot] = acc_ref[pl.ds(start, count)] + ref[pl.ds(place, count)].astype(
                    jnp.float32
                )
                copy = pltpu.make_async_copy(
                    total.at[spot], out_ref.at[pl.ds(start, count)], sems.at[len(copies)]
                )
                copy.start()
                copies.append(copy)
        for copy in copies:
            copy.wait()

    by_parity(index_ref, add, False, True)


def call(kernel, out_shape, in_specs, out_specs, scratch, aliases=None, cost=None):
    return pl.pallas_call(
        kernel,
        out_shape=out_shape,
        in_specs=in_specs,
        out_specs=out_specs,
        scratch_shapes=scratch,
        input_output_aliases=aliases or {},
        cost_estimate=cost,
        compiler_params=pltpu.CompilerParams(vmem_limit_bytes=16 * MIB),
    )


def to_first(x, size):
    pairs = [(i, i + 1) for i in range(0, size - 1, 2)]
    got = lax.ppermute(x, "blk", pairs + [(j, i) for i, j in pairs])
    return pltpu.with_memory_space_constraint(got, pltpu.VMEM)


def to_second(x, size):
    pairs = [(i, i + 1) for i in range(1, size - 1, 2)]
    got = lax.ppermute(x, "blk", pairs + [(j, i) for i, j in pairs])
    return pltpu.with_memory_space_constraint(got, pltpu.VMEM)


def local(density, ao_values, kernel, grid_weights, centre, sig_offsets, counts):
    rows, band, nb, _ = density.shape
    batches, slots, _, pts = ao_values.shape
    size = lax.axis_size("blk")
    geo = Geometry(rows, band, batches, slots)
    index = lax.axis_index("blk").astype(jnp.int32).reshape(1)
    in_hbm = lambda x: pltpu.with_memory_space_constraint(x, pltpu.HBM)
    flat = in_hbm(density.reshape(geo.own, nb, nb))
    pack = lambda count: pltpu.VMEM((count, nb, nb), jnp.bfloat16)
    dma = pltpu.SemaphoreType.DMA
    tiles_type = pltpu.VMEM((geo.own + geo.halo, nb, nb), jnp.bfloat16)
    acc_type = pltpu.VMEM((geo.spare + 1, nb, nb), jnp.float32)

    near_halo, cross_halo = call(
        functools.partial(pack_kernel, geo),
        (pack(geo.halo),) * 2,
        [SMEM_SPEC, ANY_SPEC],
        (VMEM_SPEC,) * 2,
        [dma((2 * geo.reach,))],
        cost=pl.CostEstimate(flops=10**10, bytes_accessed=10**8, transcendentals=0),
    )(index, flat)
    cross_halo = to_second(cross_halo, size)
    near_halo = to_first(near_halo, size)

    panel = (ao_values, kernel, grid_weights)
    meta, tiles, acc, early = call(
        functools.partial(early_kernel, geo),
        (pltpu.SMEM((geo.meta_size,), jnp.int32), tiles_type, acc_type, pack(geo.early)),
        [SMEM_SPEC] * 4 + [ANY_SPEC] + [VMEM_SPEC] * 3,
        (SMEM_SPEC,) + (VMEM_SPEC,) * 3,
        [dma],
    )(index, in_hbm(centre), in_hbm(sig_offsets.T), in_hbm(counts), flat, *panel)
    early = to_second(early, size)

    tiles, acc, first = call(
        functools.partial(near_kernel, geo),
        (tiles_type, acc_type, pack(geo.halo)),
        [SMEM_SPEC] + [VMEM_SPEC] * 6,
        (VMEM_SPEC,) * 3,
        [dma],
        {5: 0, 6: 1},
    )(meta, near_halo, *panel, tiles, acc)
    first = to_first(first, size)

    acc, late = call(
        functools.partial(late_kernel, geo),
        (acc_type, pack(geo.late)),
        [SMEM_SPEC] + [VMEM_SPEC] * 5,
        (VMEM_SPEC,) * 2,
        [],
        {5: 0},
    )(meta, cross_halo, *panel, acc)
    late = to_second(late, size)

    whole = jax.ShapeDtypeStruct((geo.own, nb, nb), jnp.float32)
    acc, out = call(
        functools.partial(inner_kernel, geo),
        (acc_type, whole),
        [SMEM_SPEC] * 2 + [VMEM_SPEC] * 6,
        (VMEM_SPEC, ANY_SPEC),
        [dma((max(len(runs) for runs in geo.quiet),))],
        {7: 0},
    )(index, meta, first, tiles, *panel, acc)

    parts = 2 * geo.reach
    out = call(
        functools.partial(finish_kernel, geo),
        whole,
        [SMEM_SPEC] + [VMEM_SPEC] * 3 + [ANY_SPEC],
        ANY_SPEC,
        [pltpu.VMEM((parts * band, nb, nb), jnp.float32), dma((parts,))],
        {4: 0},
    )(index, early, late, acc, out)
    return out.reshape(rows, band, nb, nb)


def solution(mesh):
    placed = (
        P(("groups", "blk"), None, None, None),
        P(("groups", "blk"), None, None, None),
        P(("groups", "blk"), None, None),
        P(("groups", "blk"), None),
        P(("groups", "blk")),
        P(("groups", "blk"), None),
        P(("groups", "blk")),
    )
    return jax.shard_map(
        local,
        mesh=mesh,
        in_specs=placed,
        out_specs=P(("groups", "blk"), None, None, None),
        check_vma=False,
    )
```

```python
import functools

import jax
import jax.numpy as jnp
from jax import lax
from jax.experimental import pallas as pl
from jax.experimental.pallas import tpu as pltpu
from jax.sharding import PartitionSpec as P

MIB = 1 << 20
GROUP = 2
LISTS = 6
SMEM_SPEC = pl.BlockSpec(memory_space=pltpu.SMEM)
VMEM_SPEC = pl.BlockSpec(memory_space=pltpu.VMEM)
ANY_SPEC = pl.BlockSpec(memory_space=pl.ANY)


class Geometry:
    def __init__(self, rows, band, batches, slots):
        self.rows, self.band, self.batches, self.slots = rows, band, batches, slots
        self.half = half = (band - 1) // 2
        self.reach = reach = half // 2
        self.own = rows * band
        low = [(-m, reach + m, band) for m in range(reach, 0, -1)]
        high = [(rows + m, 0, 3 * reach - m) for m in range(reach)]
        self.halo = sum(stop - start for _, start, stop in low)
        low_cut = [half - row for row, _, _ in low]
        high_cut = [rows - row + half for row, _, _ in high]
        early = (
            [(row, cut, stop) for (row, _, stop), cut in zip(low, low_cut)],
            [(row, start, cut) for (row, start, _), cut in zip(high, high_cut)],
        )
        late = (
            [(row, start, cut) for (row, start, _), cut in zip(low, low_cut)],
            [(row, cut, stop) for (row, _, stop), cut in zip(high, high_cut)],
        )
        self.early = sum(stop - start for _, start, stop in early[0])
        self.late = self.halo - self.early
        self.first_at = self.own
        self.early_at = self.own + self.halo
        self.late_at = self.early_at + self.early
        self.spare = self.late_at + self.late
        self.halo_base = self.bases((low, high))
        self.early_base = self.bases(early)
        self.late_base = self.bases(late)
        shifts = (rows, -rows)
        self.packs = [self.places(*pair) for pair in zip((low, high), shifts)]
        self.early_packs = [self.places(*pair) for pair in zip(early, shifts)]
        self.late_packs = [self.places(*pair) for pair in zip(late, shifts)]
        self.quiet = [self.others(self.packs[1 - near]) for near in range(2)]
        self.list_size = batches + 2
        self.lengths_at = LISTS * self.list_size
        self.local_at = self.lengths_at + LISTS
        self.count_at = self.local_at + batches
        self.offsets_at = self.count_at + batches
        self.meta_size = self.offsets_at + slots * batches

    def bases(self, sides):
        found = {}
        for segments in sides:
            place = 0
            for row, start, stop in segments:
                found[row] = place - start
                place += stop - start
        return found

    def places(self, segments, shift):
        pack, place = ([], 0)
        for row, start, stop in segments:
            pack.append(((row + shift) * self.band + start, place, stop - start))
            place += stop - start
        return pack

    def others(self, pack):
        touched = set()
        for start, _, count in pack:
            touched.update(range(start, start + count))
        runs = []
        for index in range(self.own):
            if index in touched:
                continue
            if runs and sum(runs[-1]) == index:
                runs[-1] = (runs[-1][0], runs[-1][1] + 1)
            else:
                runs.append((index, 1))
        return runs

    def pick(self, bases, shift, row, otherwise):
        value = otherwise
        for at, base in bases.items():
            value = jnp.where(row == at, base + shift, value)
        return value


def run_copies(copies):
    for copy in copies:
        copy.start()
    for copy in copies:
        copy.wait()


def by_parity(index_ref, body, first, second):
    odd = index_ref[0] % 2 == 1

    @pl.when(jnp.logical_not(odd))
    def _():
        body(first, second)

    @pl.when(odd)
    def _():
        body(second, first)


def pack_kernel(geo, index_ref, density_ref, near_ref, cross_ref, sems):
    def fill(up, down):
        copies = []
        for pack, ref in zip(geo.packs, (up, down)):
            for start, place, count in pack:
                copies.append(
                    pltpu.make_async_copy(
                        density_ref.at[pl.ds(start, count)],
                        ref.at[pl.ds(place, count)],
                        sems.at[len(copies)],
                    )
                )
        run_copies(copies)

    by_parity(index_ref, fill, near_ref, cross_ref)


CROSS_MANY, CROSS_FEW, NEAR_MANY, NEAR_FEW, INNER_MANY, INNER_FEW = range(LISTS)


def build_lists(geo, index_ref, centre_ref, offsets_ref, counts_ref, meta_ref):
    first = index_ref[0] * geo.rows
    odd = index_ref[0] % 2 == 1
    lengths = [jnp.int32(0)] * LISTS
    for b in range(geo.batches):
        local = centre_ref[b] - first
        count = counts_ref[b]
        meta_ref[geo.local_at + b] = local
        meta_ref[geo.count_at + b] = count
        low = high = jnp.bool_(False)
        for k in range(geo.slots):
            offset = offsets_ref[k, b]
            meta_ref[geo.offsets_at + k * geo.batches + b] = offset
            row = local + offset
            low = low | ((k < count) & (row < 0))
            high = high | ((k < count) & (row >= geo.rows))
        cross = (odd & high) | (jnp.logical_not(odd) & low)
        near = (odd & low) | (jnp.logical_not(odd) & high)
        inner = jnp.logical_not(low | high)
        many = count > 2
        few = (count > 0) & jnp.logical_not(many)
        kinds = [kind & size for kind in (cross, near, inner) for size in (many, few)]
        for which, member in enumerate(kinds):
            meta_ref[which * geo.list_size + lengths[which]] = b
            lengths[which] = lengths[which] + member.astype(jnp.int32)
    for which in range(LISTS):
        meta_ref[which * geo.list_size + lengths[which]] = geo.batches
        meta_ref[geo.lengths_at + which] = lengths[which]


def each_group(geo, meta_ref, which, size, body):
    length = meta_ref[geo.lengths_at + which]

    def step(i, carry):
        chosen = []
        for n in range(size):
            place = i * size + n
            there = place < length
            b = meta_ref[which * geo.list_size + jnp.minimum(place, length)]
            chosen.append((jnp.where(there, b, 0), there))
        body(chosen)
        return carry

    lax.fori_loop(0, (length + size - 1) // size, step, 0)


class Slots:
    def __init__(self, geo, meta_ref, b, there, width):
        local = meta_ref[geo.local_at + b]
        count = jnp.where(there, meta_ref[geo.count_at + b], 0)
        self.offset = [meta_ref[geo.offsets_at + k * geo.batches + b] for k in range(width)]
        self.local = local
        self.row = [local + offset for offset in self.offset]
        self.live = [k < count for k in range(width)]
        self.own = [(row >= 0) & (row < geo.rows) for row in self.row]
        self.width = width


def panels(slots, ao_ref, b):
    return jnp.concatenate(
        [
            ao_ref[b, k] * jnp.where(slots.live[k], 1.0, 0.0).astype(ao_ref.dtype)
            for k in range(slots.width)
        ],
        axis=0,
    )


def gathered(tiles_ref, places):
    return jnp.concatenate(
        [jnp.concatenate([tiles_ref[place] for place in row], axis=1) for row in places], axis=0
    )


def chain(xs, tiles, batches, kernel_ref, weights_ref):
    fs = [
        jnp.dot(t, x, preferred_element_type=jnp.float32).astype(jnp.bfloat16)
        for t, x in zip(tiles, xs)
    ]
    gs = [
        jnp.dot(f, kernel_ref[b], preferred_element_type=jnp.float32) for f, b in zip(fs, batches)
    ]
    hs = [(g * weights_ref[pl.ds(b, 1), :]).astype(jnp.bfloat16) for g, b in zip(gs, batches)]
    return [
        lax.dot_general(x, h, (((1,), (1,)), ((), ())), preferred_element_type=jnp.float32)
        for x, h in zip(xs, hs)
    ]


def scatter(part, target, nb, acc_ref):
    for k, row in enumerate(target):
        for j, place in enumerate(row):
            acc_ref[place] += part[k * nb : (k + 1) * nb, j * nb : (j + 1) * nb]


def add_whole(geo, chosen, width, meta_ref, tiles_ref, ao_ref, kernel_ref, weights_ref, acc_ref):
    xs, tiles, targets = ([], [], [])
    for b, there in chosen:
        slots = Slots(geo, meta_ref, b, there, width)
        xs.append(panels(slots, ao_ref, b))
        places, target = ([], [])
        for k in range(width):
            row = slots.row[k]
            base = jnp.where(slots.live[k] & slots.own[k], row, 0) * geo.band
            base = jnp.where(
                slots.live[k], geo.pick(geo.halo_base, geo.first_at, row, base), base
            )
            place = [base + slots.offset[j] - slots.offset[k] + geo.half for j in range(width)]
            places.append(place)
            target.append(
                [jnp.where(slots.live[k] & slots.live[j], place[j], geo.spare) for j in range(width)]
            )
        tiles.append(gathered(tiles_ref, places))
        targets.append(target)
    parts = chain(xs, tiles, [b for b, _ in chosen], kernel_ref, weights_ref)
    for part, target in zip(parts, targets):
        scatter(part, target, ao_ref.shape[2], acc_ref)


def add_own(geo, chosen, width, meta_ref, tiles_ref, ao_ref, kernel_ref, weights_ref, acc_ref):
    xs, tiles, targets = ([], [], [])
    for b, there in chosen:
        slots = Slots(geo, meta_ref, b, there, width)
        xs.append(panels(slots, ao_ref, b))
        places, target = ([], [])
        for k in range(width):
            row = slots.row[k]
            band = [slots.offset[j] - slots.offset[k] + geo.half for j in range(width)]
            base = jnp.where(slots.own[k], row, 0) * geo.band
            places.append([base + o for o in band])
            base = geo.pick(geo.early_base, geo.early_at, row, base)
            target.append(
                [
                    jnp.where(
                        slots.live[k] & slots.live[j] & slots.own[j], base + band[j], geo.spare
                    )
                    for j in range(width)
                ]
            )
        tiles.append(gathered(tiles_ref, places))
        targets.append(target)
    parts = chain(xs, tiles, [b for b, _ in chosen], kernel_ref, weights_ref)
    for part, target in zip(parts, targets):
        scatter(part, target, ao_ref.shape[2], acc_ref)


def add_halo(geo, chosen, width, meta_ref, halo_ref, ao_ref, kernel_ref, weights_ref, acc_ref):
    outer = min(geo.reach, width)
    xs, tiles, targets = ([], [], [])
    for b, there in chosen:
        slots = Slots(geo, meta_ref, b, there, width)
        xs.append(panels(slots, ao_ref, b))
        found = jnp.int32(0)
        picked = [jnp.int32(0)] * outer
        for k in range(width):
            away = slots.live[k] & jnp.logical_not(slots.own[k])
            for i in range(outer):
                picked[i] = jnp.where(away & (found <= i), slots.offset[k], picked[i])
            found = found + away.astype(jnp.int32)
        places, target = ([], [[None] * outer for _ in range(width)])
        for i in range(outer):
            base = geo.pick(geo.halo_base, 0, slots.local + picked[i], 0)
            places.append(
                [
                    jnp.where(there, base + slots.offset[j] - picked[i] + geo.half, 0)
                    for j in range(width)
                ]
            )
        for k in range(width):
            row = slots.row[k]
            base = geo.pick(geo.late_base, geo.late_at, row, row * geo.band)
            for i in range(outer):
                target[k][i] = jnp.where(
                    slots.live[k] & (i < found),
                    base + picked[i] - slots.offset[k] + geo.half,
                    geo.spare,
                )
        tiles.append(gathered(halo_ref, places))
        targets.append(target)
    parts = chain(xs, tiles, [b for b, _ in chosen], kernel_ref, weights_ref)
    for part, target in zip(parts, targets):
        scatter(part, target, ao_ref.shape[2], acc_ref)


def early_kernel(
    geo, index_ref, centre_ref, offsets_ref, counts_ref, density_ref, ao_ref, kernel_ref, weights_ref,
    meta_ref, tiles_ref, acc_ref, early_out, sem,
):
    copy = pltpu.make_async_copy(density_ref, tiles_ref.at[pl.ds(0, geo.own)], sem)
    copy.start()
    build_lists(geo, index_ref, centre_ref, offsets_ref, counts_ref, meta_ref)
    acc_ref[...] = jnp.zeros_like(acc_ref)
    copy.wait()
    refs = (meta_ref, tiles_ref, ao_ref, kernel_ref, weights_ref, acc_ref)
    for which, width in ((CROSS_MANY, geo.slots), (CROSS_FEW, 2)):
        each_group(
            geo, meta_ref, which, GROUP, lambda chosen, width=width: add_own(geo, chosen, width, *refs)
        )
    early_out[...] = acc_ref[pl.ds(geo.early_at, geo.early)].astype(early_out.dtype)


def near_kernel(
    geo, meta_ref, halo_ref, ao_ref, kernel_ref, weights_ref, tiles_in, acc_in,
    tiles_ref, acc_ref, first_out, sem,
):
    run_copies(
        [pltpu.make_async_copy(halo_ref, tiles_ref.at[pl.ds(geo.first_at, geo.halo)], sem)]
    )
    refs = (meta_ref, tiles_ref, ao_ref, kernel_ref, weights_ref, acc_ref)
    for which, width in ((NEAR_MANY, geo.slots), (NEAR_FEW, 2)):
        each_group(
            geo, meta_ref, which, GROUP, lambda chosen, width=width: add_whole(geo, chosen, width, *refs)
        )
    first_out[...] = acc_ref[pl.ds(geo.first_at, geo.halo)].astype(first_out.dtype)


def partner_part(index_ref, pair_ref, count):
    return pair_ref.at[pl.ds(jnp.where(index_ref[0] % 2 == 1, count, 0), count)]


def late_kernel(
    geo, index_ref, meta_ref, pair_ref, ao_ref, kernel_ref, weights_ref, acc_in, acc_ref, late_out,
    halo_ref, sem,
):
    run_copies([pltpu.make_async_copy(partner_part(index_ref, pair_ref, geo.halo), halo_ref, sem)])
    refs = (meta_ref, halo_ref, ao_ref, kernel_ref, weights_ref, acc_ref)
    for which, width in ((CROSS_MANY, geo.slots), (CROSS_FEW, 2)):
        each_group(
            geo, meta_ref, which, GROUP, lambda chosen, width=width: add_halo(geo, chosen, width, *refs)
        )
    late_out[...] = acc_ref[pl.ds(geo.late_at, geo.late)].astype(late_out.dtype)


def inner_kernel(
    geo, index_ref, meta_ref, first_ref, tiles_ref, ao_ref, kernel_ref, weights_ref, acc_in,
    acc_ref, out_ref, sems,
):
    refs = (meta_ref, tiles_ref, ao_ref, kernel_ref, weights_ref, acc_ref)
    for which, width in ((INNER_MANY, geo.slots), (INNER_FEW, 2)):
        each_group(
            geo, meta_ref, which, GROUP, lambda chosen, width=width: add_whole(geo, chosen, width, *refs)
        )

    def finish_near(up, down):
        near = 0 if up else 1
        for start, place, count in geo.packs[near]:
            acc_ref[pl.ds(start, count)] += first_ref[pl.ds(place, count)].astype(jnp.float32)
        run_copies(
            [
                pltpu.make_async_copy(
                    acc_ref.at[pl.ds(start, count)], out_ref.at[pl.ds(start, count)], sems.at[i]
                )
                for i, (start, count) in enumerate(geo.quiet[near])
            ]
        )

    by_parity(index_ref, finish_near, True, False)


def finish_kernel(geo, index_ref, early_ref, late_ref, acc_ref, out_in, out_ref, total, sems):
    def add(up, down):
        copies = []
        for packs, ref in ((geo.early_packs, early_ref), (geo.late_packs, late_ref)):
            for start, place, count in packs[0 if up else 1]:
                spot = pl.ds(len(copies) * geo.band, count)
                total[spot] = acc_ref[pl.ds(start, count)] + ref[pl.ds(place, count)].astype(
                    jnp.float32
                )
                copy = pltpu.make_async_copy(
                    total.at[spot], out_ref.at[pl.ds(start, count)], sems.at[len(copies)]
                )
                copy.start()
                copies.append(copy)
        for copy in copies:
            copy.wait()

    by_parity(index_ref, add, False, True)


def call(kernel, out_shape, in_specs, out_specs, scratch, aliases=None, cost=None):
    return pl.pallas_call(
        kernel,
        out_shape=out_shape,
        in_specs=in_specs,
        out_specs=out_specs,
        scratch_shapes=scratch,
        input_output_aliases=aliases or {},
        cost_estimate=cost,
        compiler_params=pltpu.CompilerParams(vmem_limit_bytes=16 * MIB),
    )


def to_first(x, size):
    pairs = [(i, i + 1) for i in range(0, size - 1, 2)]
    got = lax.ppermute(x, "blk", pairs + [(j, i) for i, j in pairs])
    return pltpu.with_memory_space_constraint(got, pltpu.VMEM)


def to_second(x, size):
    pairs = [(i, i + 1) for i in range(1, size - 1, 2)]
    got = lax.ppermute(x, "blk", pairs + [(j, i) for i, j in pairs])
    return pltpu.with_memory_space_constraint(got, pltpu.VMEM)


def gathered_pairs(x, size):
    groups = [[i, i + 1] for i in range(1, size - 1, 2)] + [[0, size - 1]]
    got = lax.all_gather(x, "blk", axis_index_groups=groups, tiled=True)
    return pltpu.with_memory_space_constraint(got, pltpu.HBM)


def local(density, ao_values, kernel, grid_weights, centre, sig_offsets, counts):
    rows, band, nb, _ = density.shape
    batches, slots, _, pts = ao_values.shape
    size = lax.axis_size("blk")
    geo = Geometry(rows, band, batches, slots)
    index = lax.axis_index("blk").astype(jnp.int32).reshape(1)
    in_hbm = lambda x: pltpu.with_memory_space_constraint(x, pltpu.HBM)
    flat = in_hbm(density.reshape(geo.own, nb, nb))
    pack = lambda count: pltpu.VMEM((count, nb, nb), jnp.bfloat16)
    dma = pltpu.SemaphoreType.DMA
    tiles_type = pltpu.VMEM((geo.own + geo.halo, nb, nb), jnp.bfloat16)
    acc_type = pltpu.VMEM((geo.spare + 1, nb, nb), jnp.float32)

    near_halo, cross_halo = call(
        functools.partial(pack_kernel, geo),
        (pack(geo.halo), jax.ShapeDtypeStruct((geo.halo, nb, nb), jnp.bfloat16)),
        [SMEM_SPEC, ANY_SPEC],
        (VMEM_SPEC, ANY_SPEC),
        [dma((2 * geo.reach,))],
        cost=pl.CostEstimate(flops=10**10, bytes_accessed=10**8, transcendentals=0),
    )(index, flat)
    cross_halo = gathered_pairs(cross_halo, size)
    near_halo = to_first(near_halo, size)

    panel = (ao_values, kernel, grid_weights)
    meta, tiles, acc, early = call(
        functools.partial(early_kernel, geo),
        (pltpu.SMEM((geo.meta_size,), jnp.int32), tiles_type, acc_type, pack(geo.early)),
        [SMEM_SPEC] * 4 + [ANY_SPEC] + [VMEM_SPEC] * 3,
        (SMEM_SPEC,) + (VMEM_SPEC,) * 3,
        [dma],
    )(index, in_hbm(centre), in_hbm(sig_offsets.T), in_hbm(counts), flat, *panel)
    early = to_second(early, size)

    tiles, acc, first = call(
        functools.partial(near_kernel, geo),
        (tiles_type, acc_type, pack(geo.halo)),
        [SMEM_SPEC] + [VMEM_SPEC] * 6,
        (VMEM_SPEC,) * 3,
        [dma],
        {5: 0, 6: 1},
    )(meta, near_halo, *panel, tiles, acc)
    first = to_first(first, size)

    acc, late = call(
        functools.partial(late_kernel, geo),
        (acc_type, pack(geo.late)),
        [SMEM_SPEC] * 2 + [ANY_SPEC] + [VMEM_SPEC] * 4,
        (VMEM_SPEC,) * 2,
        [pack(geo.halo), dma],
        {6: 0},
    )(index, meta, cross_halo, *panel, acc)
    late = to_second(late, size)

    whole = jax.ShapeDtypeStruct((geo.own, nb, nb), jnp.float32)
    acc, out = call(
        functools.partial(inner_kernel, geo),
        (acc_type, whole),
        [SMEM_SPEC] * 2 + [VMEM_SPEC] * 6,
        (VMEM_SPEC, ANY_SPEC),
        [dma((max(len(runs) for runs in geo.quiet),))],
        {7: 0},
    )(index, meta, first, tiles, *panel, acc)

    parts = 2 * geo.reach
    out = call(
        functools.partial(finish_kernel, geo),
        whole,
        [SMEM_SPEC] + [VMEM_SPEC] * 3 + [ANY_SPEC],
        ANY_SPEC,
        [pltpu.VMEM((parts * band, nb, nb), jnp.float32), dma((parts,))],
        {4: 0},
    )(index, early, late, acc, out)
    return out.reshape(rows, band, nb, nb)


def solution(mesh):
    placed = (
        P(("groups", "blk"), None, None, None),
        P(("groups", "blk"), None, None, None),
        P(("groups", "blk"), None, None),
        P(("groups", "blk"), None),
        P(("groups", "blk")),
        P(("groups", "blk"), None),
        P(("groups", "blk")),
    )
    return jax.shard_map(
        local,
        mesh=mesh,
        in_specs=placed,
        out_specs=P(("groups", "blk"), None, None, None),
        check_vma=False,
    )
```

```python
import functools

import jax
import jax.numpy as jnp
from jax import lax
from jax.experimental import pallas as pl
from jax.experimental.pallas import tpu as pltpu
from jax.sharding import PartitionSpec as P

MIB = 1 << 20
GROUP = 2
LISTS = 6
SMEM_SPEC = pl.BlockSpec(memory_space=pltpu.SMEM)
VMEM_SPEC = pl.BlockSpec(memory_space=pltpu.VMEM)
ANY_SPEC = pl.BlockSpec(memory_space=pl.ANY)


class Geometry:
    def __init__(self, rows, band, batches, slots):
        self.rows, self.band, self.batches, self.slots = rows, band, batches, slots
        self.half = half = (band - 1) // 2
        self.reach = reach = half // 2
        self.own = rows * band
        low = [(-m, reach + m, band) for m in range(reach, 0, -1)]
        high = [(rows + m, 0, 3 * reach - m) for m in range(reach)]
        self.halo = sum(stop - start for _, start, stop in low)
        low_cut = [half - row for row, _, _ in low]
        high_cut = [rows - row + half for row, _, _ in high]
        early = (
            [(row, cut, stop) for (row, _, stop), cut in zip(low, low_cut)],
            [(row, start, cut) for (row, start, _), cut in zip(high, high_cut)],
        )
        late = (
            [(row, start, cut) for (row, start, _), cut in zip(low, low_cut)],
            [(row, cut, stop) for (row, _, stop), cut in zip(high, high_cut)],
        )
        self.early = sum(stop - start for _, start, stop in early[0])
        self.late = self.halo - self.early
        self.first_at = self.own
        self.early_at = self.own + self.halo
        self.late_at = self.early_at + self.early
        self.spare = self.late_at + self.late
        self.halo_base = self.bases((low, high))
        self.early_base = self.bases(early)
        self.late_base = self.bases(late)
        shifts = (rows, -rows)
        self.packs = [self.places(*pair) for pair in zip((low, high), shifts)]
        self.early_packs = [self.places(*pair) for pair in zip(early, shifts)]
        self.late_packs = [self.places(*pair) for pair in zip(late, shifts)]
        self.quiet = [self.others(self.packs[1 - near]) for near in range(2)]
        self.list_size = batches + 2
        self.lengths_at = LISTS * self.list_size
        self.local_at = self.lengths_at + LISTS
        self.count_at = self.local_at + batches
        self.offsets_at = self.count_at + batches
        self.odd_at = self.offsets_at + slots * batches
        self.meta_size = self.odd_at + 1

    def bases(self, sides):
        found = {}
        for segments in sides:
            place = 0
            for row, start, stop in segments:
                found[row] = place - start
                place += stop - start
        return found

    def places(self, segments, shift):
        pack, place = ([], 0)
        for row, start, stop in segments:
            pack.append(((row + shift) * self.band + start, place, stop - start))
            place += stop - start
        return pack

    def others(self, pack):
        touched = set()
        for start, _, count in pack:
            touched.update(range(start, start + count))
        runs = []
        for index in range(self.own):
            if index in touched:
                continue
            if runs and sum(runs[-1]) == index:
                runs[-1] = (runs[-1][0], runs[-1][1] + 1)
            else:
                runs.append((index, 1))
        return runs

    def pick(self, bases, shift, row, otherwise):
        value = otherwise
        for at, base in bases.items():
            value = jnp.where(row == at, base + shift, value)
        return value


def run_copies(copies):
    for copy in copies:
        copy.start()
    for copy in copies:
        copy.wait()


def by_parity(odd, body, first, second):
    @pl.when(jnp.logical_not(odd))
    def _():
        body(first, second)

    @pl.when(odd)
    def _():
        body(second, first)


CROSS_MANY, CROSS_FEW, NEAR_MANY, NEAR_FEW, INNER_MANY, INNER_FEW = range(LISTS)


def build_lists(geo, index, centre_ref, offsets_ref, counts_ref, meta_ref):
    first = index * geo.rows
    odd = index % 2 == 1
    meta_ref[geo.odd_at] = odd.astype(jnp.int32)
    lengths = [jnp.int32(0)] * LISTS
    for b in range(geo.batches):
        local = centre_ref[b] - first
        count = counts_ref[b]
        meta_ref[geo.local_at + b] = local
        meta_ref[geo.count_at + b] = count
        low = high = jnp.bool_(False)
        for k in range(geo.slots):
            offset = offsets_ref[k, b]
            meta_ref[geo.offsets_at + k * geo.batches + b] = offset
            row = local + offset
            low = low | ((k < count) & (row < 0))
            high = high | ((k < count) & (row >= geo.rows))
        cross = (odd & high) | (jnp.logical_not(odd) & low)
        near = (odd & low) | (jnp.logical_not(odd) & high)
        inner = jnp.logical_not(low | high)
        many = count > 2
        few = (count > 0) & jnp.logical_not(many)
        kinds = [kind & size for kind in (cross, near, inner) for size in (many, few)]
        for which, member in enumerate(kinds):
            meta_ref[which * geo.list_size + lengths[which]] = b
            lengths[which] = lengths[which] + member.astype(jnp.int32)
    for which in range(LISTS):
        meta_ref[which * geo.list_size + lengths[which]] = geo.batches
        meta_ref[geo.lengths_at + which] = lengths[which]


def zone(geo, odd, cross):
    span = min(2 * geo.reach, geo.rows) * geo.band
    if not cross:
        span = geo.own - span
    return pl.ds(jnp.where(odd == cross, geo.own - span, 0), span)


def pack_kernel(
    geo, density_ref, centre_in, offsets_in, counts_in,
    near_ref, cross_ref, meta_ref, acc_ref,
    centre_ref, offsets_ref, counts_ref, sems,
):
    index = lax.axis_index("blk")
    odd = index % 2 == 1

    def copies(up, down):
        return [
            pltpu.make_async_copy(
                density_ref.at[pl.ds(start, count)], ref.at[pl.ds(place, count)], sems.at[side, i]
            )
            for side, (pack, ref) in enumerate(zip(geo.packs, (up, down)))
            for i, (start, place, count) in enumerate(pack)
        ]

    def start(up, down):
        for copy in copies(up, down):
            copy.start()

    by_parity(odd, start, near_ref, cross_ref)
    scalars = [
        pltpu.make_async_copy(*pair, sems.at[2, i])
        for i, pair in enumerate(
            ((centre_in, centre_ref), (offsets_in, offsets_ref), (counts_in, counts_ref))
        )
    ]
    for copy in scalars:
        copy.start()
    for where in (zone(geo, odd, False), pl.ds(geo.first_at, geo.halo), pl.ds(geo.late_at, geo.late)):
        acc_ref[where] = jnp.zeros_like(acc_ref[where])
    for copy in scalars:
        copy.wait()
    build_lists(geo, index, centre_ref, offsets_ref, counts_ref, meta_ref)
    for copy in copies(near_ref, cross_ref):
        copy.wait()


def each_group(geo, meta_ref, which, size, body):
    length = meta_ref[geo.lengths_at + which]

    def step(i, carry):
        chosen = []
        for n in range(size):
            place = i * size + n
            there = place < length
            b = meta_ref[which * geo.list_size + jnp.minimum(place, length)]
            chosen.append((jnp.where(there, b, 0), there))
        body(chosen)
        return carry

    lax.fori_loop(0, (length + size - 1) // size, step, 0)


class Slots:
    def __init__(self, geo, meta_ref, b, there, width):
        local = meta_ref[geo.local_at + b]
        count = jnp.where(there, meta_ref[geo.count_at + b], 0)
        self.offset = [meta_ref[geo.offsets_at + k * geo.batches + b] for k in range(width)]
        self.local = local
        self.row = [local + offset for offset in self.offset]
        self.live = [k < count for k in range(width)]
        self.own = [(row >= 0) & (row < geo.rows) for row in self.row]
        self.width = width


def panels(slots, ao_ref, b):
    return jnp.concatenate(
        [
            ao_ref[b, k] * jnp.where(slots.live[k], 1.0, 0.0).astype(ao_ref.dtype)
            for k in range(slots.width)
        ],
        axis=0,
    )


def gathered(tiles_ref, places):
    return jnp.concatenate(
        [jnp.concatenate([tiles_ref[place] for place in row], axis=1) for row in places], axis=0
    )


def chain(xs, tiles, batches, kernel_ref, weights_ref):
    fs = [
        jnp.dot(t, x, preferred_element_type=jnp.float32).astype(jnp.bfloat16)
        for t, x in zip(tiles, xs)
    ]
    gs = [
        jnp.dot(f, kernel_ref[b], preferred_element_type=jnp.float32) for f, b in zip(fs, batches)
    ]
    hs = [(g * weights_ref[pl.ds(b, 1), :]).astype(jnp.bfloat16) for g, b in zip(gs, batches)]
    return [
        lax.dot_general(x, h, (((1,), (1,)), ((), ())), preferred_element_type=jnp.float32)
        for x, h in zip(xs, hs)
    ]


def scatter(part, target, nb, acc_ref):
    for k, row in enumerate(target):
        for j, place in enumerate(row):
            acc_ref[place] += part[k * nb : (k + 1) * nb, j * nb : (j + 1) * nb]


def add_whole(
    geo, chosen, width, meta_ref, tiles_ref, ao_ref, kernel_ref, weights_ref, acc_ref, halo_ref=None
):
    xs, tiles, targets = ([], [], [])
    for b, there in chosen:
        slots = Slots(geo, meta_ref, b, there, width)
        xs.append(panels(slots, ao_ref, b))
        rows, target = ([], [])
        for k in range(width):
            band = [slots.offset[j] - slots.offset[k] + geo.half for j in range(width)]
            own = slots.own[k]
            base = jnp.where(slots.live[k] & own, slots.row[k], 0) * geo.band
            row = jnp.concatenate([tiles_ref[base + o] for o in band], axis=1)
            if halo_ref is not None:
                away = slots.live[k] & jnp.logical_not(own)
                outside = jnp.where(away, geo.pick(geo.halo_base, 0, slots.row[k], 0), 0)
                other = [halo_ref[jnp.where(away, outside + o, 0)] for o in band]
                row = jnp.where(away, jnp.concatenate(other, axis=1), row)
                base = jnp.where(away, outside + geo.first_at, base)
            rows.append(row)
            target.append(
                [
                    jnp.where(slots.live[k] & slots.live[j], base + band[j], geo.spare)
                    for j in range(width)
                ]
            )
        tiles.append(jnp.concatenate(rows, axis=0))
        targets.append(target)
    parts = chain(xs, tiles, [b for b, _ in chosen], kernel_ref, weights_ref)
    for part, target in zip(parts, targets):
        scatter(part, target, ao_ref.shape[2], acc_ref)


def add_own(geo, chosen, width, meta_ref, tiles_ref, ao_ref, kernel_ref, weights_ref, acc_ref):
    xs, tiles, targets = ([], [], [])
    for b, there in chosen:
        slots = Slots(geo, meta_ref, b, there, width)
        xs.append(panels(slots, ao_ref, b))
        places, target = ([], [])
        for k in range(width):
            row = slots.row[k]
            band = [slots.offset[j] - slots.offset[k] + geo.half for j in range(width)]
            base = jnp.where(slots.own[k], row, 0) * geo.band
            places.append([base + o for o in band])
            base = geo.pick(geo.early_base, geo.early_at, row, base)
            target.append(
                [
                    jnp.where(
                        slots.live[k] & slots.live[j] & slots.own[j], base + band[j], geo.spare
                    )
                    for j in range(width)
                ]
            )
        tiles.append(gathered(tiles_ref, places))
        targets.append(target)
    parts = chain(xs, tiles, [b for b, _ in chosen], kernel_ref, weights_ref)
    for part, target in zip(parts, targets):
        scatter(part, target, ao_ref.shape[2], acc_ref)


def add_halo(geo, chosen, width, meta_ref, halo_ref, ao_ref, kernel_ref, weights_ref, acc_ref):
    outer = min(geo.reach, width)
    xs, tiles, targets = ([], [], [])
    for b, there in chosen:
        slots = Slots(geo, meta_ref, b, there, width)
        xs.append(panels(slots, ao_ref, b))
        found = jnp.int32(0)
        picked = [jnp.int32(0)] * outer
        for k in range(width):
            away = slots.live[k] & jnp.logical_not(slots.own[k])
            for i in range(outer):
                picked[i] = jnp.where(away & (found <= i), slots.offset[k], picked[i])
            found = found + away.astype(jnp.int32)
        places, target = ([], [[None] * outer for _ in range(width)])
        for i in range(outer):
            base = geo.pick(geo.halo_base, 0, slots.local + picked[i], 0)
            places.append(
                [
                    jnp.where(there, base + slots.offset[j] - picked[i] + geo.half, 0)
                    for j in range(width)
                ]
            )
        for k in range(width):
            row = slots.row[k]
            base = geo.pick(geo.late_base, geo.late_at, row, row * geo.band)
            for i in range(outer):
                target[k][i] = jnp.where(
                    slots.live[k] & (i < found),
                    base + picked[i] - slots.offset[k] + geo.half,
                    geo.spare,
                )
        tiles.append(gathered(halo_ref, places))
        targets.append(target)
    parts = chain(xs, tiles, [b for b, _ in chosen], kernel_ref, weights_ref)
    for part, target in zip(parts, targets):
        scatter(part, target, ao_ref.shape[2], acc_ref)


def early_kernel(
    geo, meta_ref, tiles_ref, ao_ref, kernel_ref, weights_ref, acc_in, acc_ref, early_out
):
    odd = meta_ref[geo.odd_at] == 1
    for where in (zone(geo, odd, True), pl.ds(geo.early_at, geo.early), pl.ds(geo.spare, 1)):
        acc_ref[where] = jnp.zeros_like(acc_ref[where])
    refs = (meta_ref, tiles_ref, ao_ref, kernel_ref, weights_ref, acc_ref)
    for which, width in ((CROSS_MANY, geo.slots), (CROSS_FEW, 2)):
        each_group(
            geo, meta_ref, which, GROUP, lambda chosen, width=width: add_own(geo, chosen, width, *refs)
        )
    early_out[...] = acc_ref[pl.ds(geo.early_at, geo.early)].astype(early_out.dtype)


def near_kernel(
    geo, meta_ref, halo_ref, tiles_ref, ao_ref, kernel_ref, weights_ref, acc_in, acc_ref, first_out
):
    refs = (meta_ref, tiles_ref, ao_ref, kernel_ref, weights_ref, acc_ref, halo_ref)
    for which, width in ((NEAR_MANY, geo.slots), (NEAR_FEW, 2)):
        each_group(
            geo, meta_ref, which, GROUP, lambda chosen, width=width: add_whole(geo, chosen, width, *refs)
        )
    first_out[...] = acc_ref[pl.ds(geo.first_at, geo.halo)].astype(first_out.dtype)


def late_kernel(
    geo, meta_ref, halo_ref, ao_ref, kernel_ref, weights_ref, acc_in, acc_ref, late_out
):
    refs = (meta_ref, halo_ref, ao_ref, kernel_ref, weights_ref, acc_ref)
    for which, width in ((CROSS_MANY, geo.slots), (CROSS_FEW, 2)):
        each_group(
            geo, meta_ref, which, GROUP, lambda chosen, width=width: add_halo(geo, chosen, width, *refs)
        )
    late_out[...] = acc_ref[pl.ds(geo.late_at, geo.late)].astype(late_out.dtype)


def inner_kernel(
    geo, meta_ref, first_ref, tiles_ref, ao_ref, kernel_ref, weights_ref, acc_in,
    acc_ref, out_ref, sems,
):
    refs = (meta_ref, tiles_ref, ao_ref, kernel_ref, weights_ref, acc_ref)
    for which, width in ((INNER_MANY, geo.slots), (INNER_FEW, 2)):
        each_group(
            geo, meta_ref, which, GROUP, lambda chosen, width=width: add_whole(geo, chosen, width, *refs)
        )

    def finish_near(up, down):
        near = 0 if up else 1
        for start, place, count in geo.packs[near]:
            acc_ref[pl.ds(start, count)] += first_ref[pl.ds(place, count)].astype(jnp.float32)
        run_copies(
            [
                pltpu.make_async_copy(
                    acc_ref.at[pl.ds(start, count)], out_ref.at[pl.ds(start, count)], sems.at[i]
                )
                for i, (start, count) in enumerate(geo.quiet[near])
            ]
        )

    by_parity(meta_ref[geo.odd_at] == 1, finish_near, True, False)


def finish_kernel(geo, meta_ref, early_ref, late_ref, acc_ref, out_in, out_ref, total, sems):
    def add(up, down):
        copies = []
        for packs, ref in ((geo.early_packs, early_ref), (geo.late_packs, late_ref)):
            for start, place, count in packs[0 if up else 1]:
                spot = pl.ds(len(copies) * geo.band, count)
                total[spot] = acc_ref[pl.ds(start, count)] + ref[pl.ds(place, count)].astype(
                    jnp.float32
                )
                copy = pltpu.make_async_copy(
                    total.at[spot], out_ref.at[pl.ds(start, count)], sems.at[len(copies)]
                )
                copy.start()
                copies.append(copy)
        for copy in copies:
            copy.wait()

    by_parity(meta_ref[geo.odd_at] == 1, add, False, True)


def call(kernel, out_shape, in_specs, out_specs, scratch, aliases=None, cost=None):
    return pl.pallas_call(
        kernel,
        out_shape=out_shape,
        in_specs=in_specs,
        out_specs=out_specs,
        scratch_shapes=scratch,
        input_output_aliases=aliases or {},
        cost_estimate=cost,
        compiler_params=pltpu.CompilerParams(vmem_limit_bytes=16 * MIB),
    )


def to_first(x, size):
    pairs = [(i, i + 1) for i in range(0, size - 1, 2)]
    got = lax.ppermute(x, "blk", pairs + [(j, i) for i, j in pairs])
    return pltpu.with_memory_space_constraint(got, pltpu.VMEM)


def to_second(x, size):
    pairs = [(i, i + 1) for i in range(1, size - 1, 2)]
    got = lax.ppermute(x, "blk", pairs + [(j, i) for i, j in pairs])
    return pltpu.with_memory_space_constraint(got, pltpu.VMEM)


def local(density, ao_values, kernel, grid_weights, centre, sig_offsets, counts):
    rows, band, nb, _ = density.shape
    batches, slots, _, pts = ao_values.shape
    size = lax.axis_size("blk")
    geo = Geometry(rows, band, batches, slots)
    in_hbm = lambda x: pltpu.with_memory_space_constraint(x, pltpu.HBM)
    tiles = density.reshape(geo.own, nb, nb)
    pack = lambda count: pltpu.VMEM((count, nb, nb), jnp.bfloat16)
    dma = pltpu.SemaphoreType.DMA
    acc_type = pltpu.VMEM((geo.spare + 1, nb, nb), jnp.float32)

    near_halo, cross_halo, meta, acc = call(
        functools.partial(pack_kernel, geo),
        (pack(geo.halo),) * 2 + (pltpu.SMEM((geo.meta_size,), jnp.int32), acc_type),
        [ANY_SPEC] * 4,
        (VMEM_SPEC,) * 2 + (SMEM_SPEC, VMEM_SPEC),
        [
            pltpu.SMEM((batches,), jnp.int32),
            pltpu.SMEM((slots, batches), jnp.int32),
            pltpu.SMEM((batches,), jnp.int32),
            dma((3, max(geo.reach, 3))),
        ],
        cost=pl.CostEstimate(flops=10**10, bytes_accessed=10**8, transcendentals=0),
    )(in_hbm(tiles), in_hbm(centre), in_hbm(sig_offsets.T), in_hbm(counts))
    cross_halo = to_second(cross_halo, size)
    near_halo = to_first(near_halo, size)

    panel = (tiles, ao_values, kernel, grid_weights)
    acc, early = call(
        functools.partial(early_kernel, geo),
        (acc_type, pack(geo.early)),
        [SMEM_SPEC] + [VMEM_SPEC] * 5,
        (VMEM_SPEC,) * 2,
        [],
        {5: 0},
    )(meta, *panel, acc)
    early = to_second(early, size)

    acc, first = call(
        functools.partial(near_kernel, geo),
        (acc_type, pack(geo.halo)),
        [SMEM_SPEC] + [VMEM_SPEC] * 6,
        (VMEM_SPEC,) * 2,
        [],
        {6: 0},
    )(meta, near_halo, *panel, acc)
    first = to_first(first, size)

    acc, late = call(
        functools.partial(late_kernel, geo),
        (acc_type, pack(geo.late)),
        [SMEM_SPEC] + [VMEM_SPEC] * 5,
        (VMEM_SPEC,) * 2,
        [],
        {5: 0},
    )(meta, cross_halo, *panel[1:], acc)
    late = to_second(late, size)

    whole = jax.ShapeDtypeStruct((geo.own, nb, nb), jnp.float32)
    acc, out = call(
        functools.partial(inner_kernel, geo),
        (acc_type, whole),
        [SMEM_SPEC] + [VMEM_SPEC] * 6,
        (VMEM_SPEC, ANY_SPEC),
        [dma((max(len(runs) for runs in geo.quiet),))],
        {6: 0},
    )(meta, first, *panel, acc)

    parts = 2 * geo.reach
    out = call(
        functools.partial(finish_kernel, geo),
        whole,
        [SMEM_SPEC] + [VMEM_SPEC] * 3 + [ANY_SPEC],
        ANY_SPEC,
        [pltpu.VMEM((parts * band, nb, nb), jnp.float32), dma((parts,))],
        {4: 0},
    )(meta, early, late, acc, out)
    return out.reshape(rows, band, nb, nb)


def solution(mesh):
    placed = (
        P(("groups", "blk"), None, None, None),
        P(("groups", "blk"), None, None, None),
        P(("groups", "blk"), None, None),
        P(("groups", "blk"), None),
        P(("groups", "blk")),
        P(("groups", "blk"), None),
        P(("groups", "blk")),
    )
    return jax.shard_map(
        local,
        mesh=mesh,
        in_specs=placed,
        out_specs=P(("groups", "blk"), None, None, None),
        check_vma=False,
    )
```

```python
import functools

import jax
import jax.numpy as jnp
from jax import lax
from jax.experimental import pallas as pl
from jax.experimental.pallas import tpu as pltpu
from jax.sharding import PartitionSpec as P

MIB = 1 << 20
GROUP = 2
LISTS = 6
BUDGET = 43
COST = (10, 7)
SMEM_SPEC = pl.BlockSpec(memory_space=pltpu.SMEM)
VMEM_SPEC = pl.BlockSpec(memory_space=pltpu.VMEM)
ANY_SPEC = pl.BlockSpec(memory_space=pl.ANY)


class Geometry:
    def __init__(self, rows, band, batches, slots):
        self.rows, self.band, self.batches, self.slots = rows, band, batches, slots
        self.half = half = (band - 1) // 2
        self.reach = reach = half // 2
        self.own = rows * band
        low = [(-m, reach + m, band) for m in range(reach, 0, -1)]
        high = [(rows + m, 0, 3 * reach - m) for m in range(reach)]
        self.halo = sum(stop - start for _, start, stop in low)
        low_cut = [half - row for row, _, _ in low]
        high_cut = [rows - row + half for row, _, _ in high]
        early = (
            [(row, cut, stop) for (row, _, stop), cut in zip(low, low_cut)],
            [(row, start, cut) for (row, start, _), cut in zip(high, high_cut)],
        )
        late = (
            [(row, start, cut) for (row, start, _), cut in zip(low, low_cut)],
            [(row, cut, stop) for (row, _, stop), cut in zip(high, high_cut)],
        )
        self.early = sum(stop - start for _, start, stop in early[0])
        self.late = self.halo - self.early
        self.first_at = self.own
        self.early_at = self.own + self.halo
        self.late_at = self.early_at + self.early
        self.spare = self.late_at + self.late
        self.halo_base = self.bases((low, high))
        self.early_base = self.bases(early)
        self.late_base = self.bases(late)
        shifts = (rows, -rows)
        self.packs = [self.places(*pair) for pair in zip((low, high), shifts)]
        self.early_packs = [self.places(*pair) for pair in zip(early, shifts)]
        self.late_packs = [self.places(*pair) for pair in zip(late, shifts)]
        self.quiet = [self.others(self.packs[1 - near]) for near in range(2)]
        self.list_size = batches + 2
        self.lengths_at = LISTS * self.list_size
        self.local_at = self.lengths_at + LISTS
        self.count_at = self.local_at + batches
        self.offsets_at = self.count_at + batches
        self.odd_at = self.offsets_at + slots * batches
        self.meta_size = self.odd_at + 1

    def bases(self, sides):
        found = {}
        for segments in sides:
            place = 0
            for row, start, stop in segments:
                found[row] = place - start
                place += stop - start
        return found

    def places(self, segments, shift):
        pack, place = ([], 0)
        for row, start, stop in segments:
            pack.append(((row + shift) * self.band + start, place, stop - start))
            place += stop - start
        return pack

    def others(self, pack):
        touched = set()
        for start, _, count in pack:
            touched.update(range(start, start + count))
        runs = []
        for index in range(self.own):
            if index in touched:
                continue
            if runs and sum(runs[-1]) == index:
                runs[-1] = (runs[-1][0], runs[-1][1] + 1)
            else:
                runs.append((index, 1))
        return runs

    def pick(self, bases, shift, row, otherwise):
        value = otherwise
        for at, base in bases.items():
            value = jnp.where(row == at, base + shift, value)
        return value


def run_copies(copies):
    for copy in copies:
        copy.start()
    for copy in copies:
        copy.wait()


def by_parity(odd, body, first, second):
    @pl.when(jnp.logical_not(odd))
    def _():
        body(first, second)

    @pl.when(odd)
    def _():
        body(second, first)


CROSS_MANY, CROSS_FEW, NEAR_MANY, NEAR_FEW, INNER_MANY, INNER_FEW = range(LISTS)


def build_lists(geo, index, centre_ref, offsets_ref, counts_ref, meta_ref):
    first = index * geo.rows
    odd = index % 2 == 1
    meta_ref[geo.odd_at] = odd.astype(jnp.int32)
    lengths = [jnp.int32(0)] * LISTS
    for b in range(geo.batches):
        local = centre_ref[b] - first
        count = counts_ref[b]
        meta_ref[geo.local_at + b] = local
        meta_ref[geo.count_at + b] = count
        low = high = jnp.bool_(False)
        for k in range(geo.slots):
            offset = offsets_ref[k, b]
            meta_ref[geo.offsets_at + k * geo.batches + b] = offset
            row = local + offset
            low = low | ((k < count) & (row < 0))
            high = high | ((k < count) & (row >= geo.rows))
        cross = (odd & high) | (jnp.logical_not(odd) & low)
        near = (odd & low) | (jnp.logical_not(odd) & high)
        inner = jnp.logical_not(low | high)
        many = count > 2
        few = (count > 0) & jnp.logical_not(many)
        kinds = [kind & size for kind in (cross, near, inner) for size in (many, few)]
        for which, member in enumerate(kinds):
            meta_ref[which * geo.list_size + lengths[which]] = b
            lengths[which] = lengths[which] + member.astype(jnp.int32)
    for which in range(LISTS):
        meta_ref[which * geo.list_size + lengths[which]] = geo.batches
        meta_ref[geo.lengths_at + which] = lengths[which]


def zone(geo, odd, cross):
    span = min(2 * geo.reach, geo.rows) * geo.band
    if not cross:
        span = geo.own - span
    return pl.ds(jnp.where(odd == cross, geo.own - span, 0), span)


def pack_kernel(
    geo, density_ref, centre_in, offsets_in, counts_in,
    near_ref, cross_ref, meta_ref, acc_ref,
    centre_ref, offsets_ref, counts_ref, sems,
):
    index = lax.axis_index("blk")
    odd = index % 2 == 1

    def copies(up, down):
        return [
            pltpu.make_async_copy(
                density_ref.at[pl.ds(start, count)], ref.at[pl.ds(place, count)], sems.at[side, i]
            )
            for side, (pack, ref) in enumerate(zip(geo.packs, (up, down)))
            for i, (start, place, count) in enumerate(pack)
        ]

    def start(up, down):
        for copy in copies(up, down):
            copy.start()

    by_parity(odd, start, near_ref, cross_ref)
    scalars = [
        pltpu.make_async_copy(*pair, sems.at[2, i])
        for i, pair in enumerate(
            ((centre_in, centre_ref), (offsets_in, offsets_ref), (counts_in, counts_ref))
        )
    ]
    for copy in scalars:
        copy.start()
    for where in (zone(geo, odd, False), pl.ds(geo.first_at, geo.halo), pl.ds(geo.late_at, geo.late)):
        acc_ref[where] = jnp.zeros_like(acc_ref[where])
    for copy in scalars:
        copy.wait()
    build_lists(geo, index, centre_ref, offsets_ref, counts_ref, meta_ref)
    for copy in copies(near_ref, cross_ref):
        copy.wait()


def group_count(geo, meta_ref, which):
    return (meta_ref[geo.lengths_at + which] + GROUP - 1) // GROUP


def inner_share(geo, meta_ref):
    room = BUDGET
    for which in (CROSS_MANY, CROSS_FEW, NEAR_MANY, NEAR_FEW):
        room = room - COST[which % 2] * group_count(geo, meta_ref, which)
    share = []
    for which in (INNER_MANY, INNER_FEW):
        cost = COST[which % 2]
        taken = jnp.minimum(jnp.maximum(room, 0) // cost, group_count(geo, meta_ref, which))
        room = room - cost * taken
        share.append(taken)
    return share


def each_group(geo, meta_ref, which, body, begin=0, end=None):
    length = meta_ref[geo.lengths_at + which]

    def step(i, carry):
        chosen = []
        for n in range(GROUP):
            place = i * GROUP + n
            there = place < length
            b = meta_ref[which * geo.list_size + jnp.minimum(place, length)]
            chosen.append((jnp.where(there, b, 0), there))
        body(chosen)
        return carry

    lax.fori_loop(begin, group_count(geo, meta_ref, which) if end is None else end, step, 0)


class Slots:
    def __init__(self, geo, meta_ref, b, there, width):
        local = meta_ref[geo.local_at + b]
        count = jnp.where(there, meta_ref[geo.count_at + b], 0)
        self.offset = [meta_ref[geo.offsets_at + k * geo.batches + b] for k in range(width)]
        self.local = local
        self.row = [local + offset for offset in self.offset]
        self.live = [k < count for k in range(width)]
        self.own = [(row >= 0) & (row < geo.rows) for row in self.row]
        self.width = width


def panels(slots, ao_ref, b):
    return jnp.concatenate(
        [
            ao_ref[b, k] * jnp.where(slots.live[k], 1.0, 0.0).astype(ao_ref.dtype)
            for k in range(slots.width)
        ],
        axis=0,
    )


def gathered(tiles_ref, places):
    return jnp.concatenate(
        [jnp.concatenate([tiles_ref[place] for place in row], axis=1) for row in places], axis=0
    )


def chain(xs, tiles, batches, kernel_ref, weights_ref):
    fs = [
        jnp.dot(t, x, preferred_element_type=jnp.float32).astype(jnp.bfloat16)
        for t, x in zip(tiles, xs)
    ]
    gs = [
        jnp.dot(f, kernel_ref[b], preferred_element_type=jnp.float32) for f, b in zip(fs, batches)
    ]
    hs = [(g * weights_ref[pl.ds(b, 1), :]).astype(jnp.bfloat16) for g, b in zip(gs, batches)]
    return [
        lax.dot_general(x, h, (((1,), (1,)), ((), ())), preferred_element_type=jnp.float32)
        for x, h in zip(xs, hs)
    ]


def scatter(part, target, nb, acc_ref):
    for k, row in enumerate(target):
        for j, place in enumerate(row):
            acc_ref[place] += part[k * nb : (k + 1) * nb, j * nb : (j + 1) * nb]


def add_whole(
    geo, chosen, width, meta_ref, tiles_ref, ao_ref, kernel_ref, weights_ref, acc_ref, halo_ref=None
):
    xs, tiles, targets = ([], [], [])
    for b, there in chosen:
        slots = Slots(geo, meta_ref, b, there, width)
        xs.append(panels(slots, ao_ref, b))
        rows, target = ([], [])
        for k in range(width):
            band = [slots.offset[j] - slots.offset[k] + geo.half for j in range(width)]
            own = slots.own[k]
            base = jnp.where(slots.live[k] & own, slots.row[k], 0) * geo.band
            row = jnp.concatenate([tiles_ref[base + o] for o in band], axis=1)
            if halo_ref is not None:
                away = slots.live[k] & jnp.logical_not(own)
                outside = jnp.where(away, geo.pick(geo.halo_base, 0, slots.row[k], 0), 0)
                other = [halo_ref[jnp.where(away, outside + o, 0)] for o in band]
                row = jnp.where(away, jnp.concatenate(other, axis=1), row)
                base = jnp.where(away, outside + geo.first_at, base)
            rows.append(row)
            target.append(
                [
                    jnp.where(slots.live[k] & slots.live[j], base + band[j], geo.spare)
                    for j in range(width)
                ]
            )
        tiles.append(jnp.concatenate(rows, axis=0))
        targets.append(target)
    parts = chain(xs, tiles, [b for b, _ in chosen], kernel_ref, weights_ref)
    for part, target in zip(parts, targets):
        scatter(part, target, ao_ref.shape[2], acc_ref)


def add_own(geo, chosen, width, meta_ref, tiles_ref, ao_ref, kernel_ref, weights_ref, acc_ref):
    xs, tiles, targets = ([], [], [])
    for b, there in chosen:
        slots = Slots(geo, meta_ref, b, there, width)
        xs.append(panels(slots, ao_ref, b))
        places, target = ([], [])
        for k in range(width):
            row = slots.row[k]
            band = [slots.offset[j] - slots.offset[k] + geo.half for j in range(width)]
            base = jnp.where(slots.own[k], row, 0) * geo.band
            places.append([base + o for o in band])
            base = geo.pick(geo.early_base, geo.early_at, row, base)
            target.append(
                [
                    jnp.where(
                        slots.live[k] & slots.live[j] & slots.own[j], base + band[j], geo.spare
                    )
                    for j in range(width)
                ]
            )
        tiles.append(gathered(tiles_ref, places))
        targets.append(target)
    parts = chain(xs, tiles, [b for b, _ in chosen], kernel_ref, weights_ref)
    for part, target in zip(parts, targets):
        scatter(part, target, ao_ref.shape[2], acc_ref)


def add_halo(geo, chosen, width, meta_ref, halo_ref, ao_ref, kernel_ref, weights_ref, acc_ref):
    outer = min(geo.reach, width)
    xs, tiles, targets = ([], [], [])
    for b, there in chosen:
        slots = Slots(geo, meta_ref, b, there, width)
        xs.append(panels(slots, ao_ref, b))
        found = jnp.int32(0)
        picked = [jnp.int32(0)] * outer
        for k in range(width):
            away = slots.live[k] & jnp.logical_not(slots.own[k])
            for i in range(outer):
                picked[i] = jnp.where(away & (found <= i), slots.offset[k], picked[i])
            found = found + away.astype(jnp.int32)
        places, target = ([], [[None] * outer for _ in range(width)])
        for i in range(outer):
            base = geo.pick(geo.halo_base, 0, slots.local + picked[i], 0)
            places.append(
                [
                    jnp.where(there, base + slots.offset[j] - picked[i] + geo.half, 0)
                    for j in range(width)
                ]
            )
        for k in range(width):
            row = slots.row[k]
            base = geo.pick(geo.late_base, geo.late_at, row, row * geo.band)
            for i in range(outer):
                target[k][i] = jnp.where(
                    slots.live[k] & (i < found),
                    base + picked[i] - slots.offset[k] + geo.half,
                    geo.spare,
                )
        tiles.append(gathered(halo_ref, places))
        targets.append(target)
    parts = chain(xs, tiles, [b for b, _ in chosen], kernel_ref, weights_ref)
    for part, target in zip(parts, targets):
        scatter(part, target, ao_ref.shape[2], acc_ref)


def early_kernel(
    geo, meta_ref, tiles_ref, ao_ref, kernel_ref, weights_ref, acc_in, acc_ref, early_out
):
    odd = meta_ref[geo.odd_at] == 1
    for where in (zone(geo, odd, True), pl.ds(geo.early_at, geo.early), pl.ds(geo.spare, 1)):
        acc_ref[where] = jnp.zeros_like(acc_ref[where])
    refs = (meta_ref, tiles_ref, ao_ref, kernel_ref, weights_ref, acc_ref)
    for which, width in ((CROSS_MANY, geo.slots), (CROSS_FEW, 2)):
        each_group(
            geo, meta_ref, which, lambda chosen, width=width: add_own(geo, chosen, width, *refs)
        )
    early_out[...] = acc_ref[pl.ds(geo.early_at, geo.early)].astype(early_out.dtype)


def near_kernel(
    geo, meta_ref, halo_ref, tiles_ref, ao_ref, kernel_ref, weights_ref, acc_in, acc_ref, first_out
):
    refs = (meta_ref, tiles_ref, ao_ref, kernel_ref, weights_ref, acc_ref, halo_ref)
    for which, width in ((NEAR_MANY, geo.slots), (NEAR_FEW, 2)):
        each_group(
            geo, meta_ref, which, lambda chosen, width=width: add_whole(geo, chosen, width, *refs)
        )
    first_out[...] = acc_ref[pl.ds(geo.first_at, geo.halo)].astype(first_out.dtype)
    share = inner_share(geo, meta_ref)
    for which, width, end in ((INNER_MANY, geo.slots, share[0]), (INNER_FEW, 2, share[1])):
        each_group(
            geo,
            meta_ref,
            which,
            lambda chosen, width=width: add_whole(geo, chosen, width, *refs[:-1]),
            end=end,
        )


def late_kernel(
    geo, meta_ref, halo_ref, ao_ref, kernel_ref, weights_ref, acc_in, acc_ref, late_out
):
    refs = (meta_ref, halo_ref, ao_ref, kernel_ref, weights_ref, acc_ref)
    for which, width in ((CROSS_MANY, geo.slots), (CROSS_FEW, 2)):
        each_group(
            geo, meta_ref, which, lambda chosen, width=width: add_halo(geo, chosen, width, *refs)
        )
    late_out[...] = acc_ref[pl.ds(geo.late_at, geo.late)].astype(late_out.dtype)


def inner_kernel(
    geo, meta_ref, first_ref, tiles_ref, ao_ref, kernel_ref, weights_ref, acc_in,
    acc_ref, out_ref, sems,
):
    refs = (meta_ref, tiles_ref, ao_ref, kernel_ref, weights_ref, acc_ref)
    share = inner_share(geo, meta_ref)
    for which, width, begin in ((INNER_MANY, geo.slots, share[0]), (INNER_FEW, 2, share[1])):
        each_group(
            geo,
            meta_ref,
            which,
            lambda chosen, width=width: add_whole(geo, chosen, width, *refs),
            begin=begin,
        )

    def finish_near(up, down):
        near = 0 if up else 1
        for start, place, count in geo.packs[near]:
            acc_ref[pl.ds(start, count)] += first_ref[pl.ds(place, count)].astype(jnp.float32)
        run_copies(
            [
                pltpu.make_async_copy(
                    acc_ref.at[pl.ds(start, count)], out_ref.at[pl.ds(start, count)], sems.at[i]
                )
                for i, (start, count) in enumerate(geo.quiet[near])
            ]
        )

    by_parity(meta_ref[geo.odd_at] == 1, finish_near, True, False)


def finish_kernel(geo, meta_ref, early_ref, late_ref, acc_ref, out_in, out_ref, total, sems):
    def add(up, down):
        copies = []
        for packs, ref in ((geo.early_packs, early_ref), (geo.late_packs, late_ref)):
            for start, place, count in packs[0 if up else 1]:
                spot = pl.ds(len(copies) * geo.band, count)
                total[spot] = acc_ref[pl.ds(start, count)] + ref[pl.ds(place, count)].astype(
                    jnp.float32
                )
                copy = pltpu.make_async_copy(
                    total.at[spot], out_ref.at[pl.ds(start, count)], sems.at[len(copies)]
                )
                copy.start()
                copies.append(copy)
        for copy in copies:
            copy.wait()

    by_parity(meta_ref[geo.odd_at] == 1, add, False, True)


def call(kernel, out_shape, in_specs, out_specs, scratch, aliases=None, cost=None):
    return pl.pallas_call(
        kernel,
        out_shape=out_shape,
        in_specs=in_specs,
        out_specs=out_specs,
        scratch_shapes=scratch,
        input_output_aliases=aliases or {},
        cost_estimate=cost,
        compiler_params=pltpu.CompilerParams(vmem_limit_bytes=16 * MIB),
    )


def to_first(x, size):
    pairs = [(i, i + 1) for i in range(0, size - 1, 2)]
    got = lax.ppermute(x, "blk", pairs + [(j, i) for i, j in pairs])
    return pltpu.with_memory_space_constraint(got, pltpu.VMEM)


def to_second(x, size):
    pairs = [(i, i + 1) for i in range(1, size - 1, 2)]
    got = lax.ppermute(x, "blk", pairs + [(j, i) for i, j in pairs])
    return pltpu.with_memory_space_constraint(got, pltpu.VMEM)


def local(density, ao_values, kernel, grid_weights, centre, sig_offsets, counts):
    rows, band, nb, _ = density.shape
    batches, slots, _, pts = ao_values.shape
    size = lax.axis_size("blk")
    geo = Geometry(rows, band, batches, slots)
    in_hbm = lambda x: pltpu.with_memory_space_constraint(x, pltpu.HBM)
    tiles = density.reshape(geo.own, nb, nb)
    pack = lambda count: pltpu.VMEM((count, nb, nb), jnp.bfloat16)
    dma = pltpu.SemaphoreType.DMA
    acc_type = pltpu.VMEM((geo.spare + 1, nb, nb), jnp.float32)

    near_halo, cross_halo, meta, acc = call(
        functools.partial(pack_kernel, geo),
        (pack(geo.halo),) * 2 + (pltpu.SMEM((geo.meta_size,), jnp.int32), acc_type),
        [ANY_SPEC] * 4,
        (VMEM_SPEC,) * 2 + (SMEM_SPEC, VMEM_SPEC),
        [
            pltpu.SMEM((batches,), jnp.int32),
            pltpu.SMEM((slots, batches), jnp.int32),
            pltpu.SMEM((batches,), jnp.int32),
            dma((3, max(geo.reach, 3))),
        ],
        cost=pl.CostEstimate(flops=10**10, bytes_accessed=10**8, transcendentals=0),
    )(in_hbm(tiles), in_hbm(centre), in_hbm(sig_offsets.T), in_hbm(counts))
    cross_halo = to_second(cross_halo, size)
    near_halo = to_first(near_halo, size)

    panel = (tiles, ao_values, kernel, grid_weights)
    acc, early = call(
        functools.partial(early_kernel, geo),
        (acc_type, pack(geo.early)),
        [SMEM_SPEC] + [VMEM_SPEC] * 5,
        (VMEM_SPEC,) * 2,
        [],
        {5: 0},
    )(meta, *panel, acc)
    early = to_second(early, size)

    acc, first = call(
        functools.partial(near_kernel, geo),
        (acc_type, pack(geo.halo)),
        [SMEM_SPEC] + [VMEM_SPEC] * 6,
        (VMEM_SPEC,) * 2,
        [],
        {6: 0},
    )(meta, near_halo, *panel, acc)
    first = to_first(first, size)

    acc, late = call(
        functools.partial(late_kernel, geo),
        (acc_type, pack(geo.late)),
        [SMEM_SPEC] + [VMEM_SPEC] * 5,
        (VMEM_SPEC,) * 2,
        [],
        {5: 0},
    )(meta, cross_halo, *panel[1:], acc)
    late = to_second(late, size)

    whole = jax.ShapeDtypeStruct((geo.own, nb, nb), jnp.float32)
    acc, out = call(
        functools.partial(inner_kernel, geo),
        (acc_type, whole),
        [SMEM_SPEC] + [VMEM_SPEC] * 6,
        (VMEM_SPEC, ANY_SPEC),
        [dma((max(len(runs) for runs in geo.quiet),))],
        {6: 0},
    )(meta, first, *panel, acc)

    parts = 2 * geo.reach
    out = call(
        functools.partial(finish_kernel, geo),
        whole,
        [SMEM_SPEC] + [VMEM_SPEC] * 3 + [ANY_SPEC],
        ANY_SPEC,
        [pltpu.VMEM((parts * band, nb, nb), jnp.float32), dma((parts,))],
        {4: 0},
    )(meta, early, late, acc, out)
    return out.reshape(rows, band, nb, nb)


def solution(mesh):
    placed = (
        P(("groups", "blk"), None, None, None),
        P(("groups", "blk"), None, None, None),
        P(("groups", "blk"), None, None),
        P(("groups", "blk"), None),
        P(("groups", "blk")),
        P(("groups", "blk"), None),
        P(("groups", "blk")),
    )
    return jax.shard_map(
        local,
        mesh=mesh,
        in_specs=placed,
        out_specs=P(("groups", "blk"), None, None, None),
        check_vma=False,
    )
```

```python
import functools

import jax
import jax.numpy as jnp
from jax import lax
from jax.experimental import pallas as pl
from jax.experimental.pallas import tpu as pltpu
from jax.sharding import PartitionSpec as P

MIB = 1 << 20
GROUP = 2
LATE_GROUP = 4
LISTS = 7
BUDGET = 43
COST = (10, 7)
SMEM_SPEC = pl.BlockSpec(memory_space=pltpu.SMEM)
VMEM_SPEC = pl.BlockSpec(memory_space=pltpu.VMEM)
ANY_SPEC = pl.BlockSpec(memory_space=pl.ANY)


class Geometry:
    def __init__(self, rows, band, batches, slots):
        self.rows, self.band, self.batches, self.slots = rows, band, batches, slots
        self.half = half = (band - 1) // 2
        self.reach = reach = half // 2
        self.own = rows * band
        low = [(-m, reach + m, band) for m in range(reach, 0, -1)]
        high = [(rows + m, 0, 3 * reach - m) for m in range(reach)]
        self.halo = sum(stop - start for _, start, stop in low)
        low_cut = [half - row for row, _, _ in low]
        high_cut = [rows - row + half for row, _, _ in high]
        early = (
            [(row, cut, stop) for (row, _, stop), cut in zip(low, low_cut)],
            [(row, start, cut) for (row, start, _), cut in zip(high, high_cut)],
        )
        late = (
            [(row, start, cut) for (row, start, _), cut in zip(low, low_cut)],
            [(row, cut, stop) for (row, _, stop), cut in zip(high, high_cut)],
        )
        self.early = sum(stop - start for _, start, stop in early[0])
        self.late = self.halo - self.early
        self.first_at = self.own
        self.early_at = self.own + self.halo
        self.spare = self.early_at + self.early
        self.halo_base = self.bases((low, high))
        self.early_base = self.bases(early)
        shifts = (rows, -rows)
        self.packs = [self.places(*pair) for pair in zip((low, high), shifts)]
        self.early_packs = [self.places(*pair) for pair in zip(early, shifts)]
        self.late_packs = [self.places(*pair) for pair in zip(late, shifts)]
        self.span = min(2 * reach, rows) * band
        self.quiet = [
            self.others(self.packs[1], 0, self.span),
            self.others(self.packs[0], self.own - self.span, self.own),
        ]
        self.list_size = batches + 2
        self.lengths_at = LISTS * self.list_size
        self.local_at = self.lengths_at + LISTS
        self.count_at = self.local_at + batches
        self.offsets_at = self.count_at + batches
        self.odd_at = self.offsets_at + slots * batches
        self.meta_size = self.odd_at + 1

    def bases(self, sides):
        found = {}
        for segments in sides:
            place = 0
            for row, start, stop in segments:
                found[row] = place - start
                place += stop - start
        return found

    def places(self, segments, shift):
        pack, place = ([], 0)
        for row, start, stop in segments:
            pack.append(((row + shift) * self.band + start, place, stop - start))
            place += stop - start
        return pack

    def others(self, pack, begin, end):
        touched = set()
        for start, _, count in pack:
            touched.update(range(start, start + count))
        runs = []
        for index in range(begin, end):
            if index in touched:
                continue
            if runs and sum(runs[-1]) == index:
                runs[-1] = (runs[-1][0], runs[-1][1] + 1)
            else:
                runs.append((index, 1))
        return runs

    def pick(self, bases, shift, row, otherwise):
        value = otherwise
        for at, base in bases.items():
            value = jnp.where(row == at, base + shift, value)
        return value


def run_copies(copies):
    for copy in copies:
        copy.start()
    for copy in copies:
        copy.wait()


def by_parity(odd, body, first, second):
    @pl.when(jnp.logical_not(odd))
    def _():
        body(first, second)

    @pl.when(odd)
    def _():
        body(second, first)


CROSS_MANY, CROSS_FEW, NEAR_MANY, NEAR_FEW, INNER_MANY, INNER_FEW, CROSS = range(LISTS)


def build_lists(geo, index, centre_ref, offsets_ref, counts_ref, meta_ref):
    first = index * geo.rows
    odd = index % 2 == 1
    meta_ref[geo.odd_at] = odd.astype(jnp.int32)
    lengths = [jnp.int32(0)] * LISTS
    for b in range(geo.batches):
        local = centre_ref[b] - first
        count = counts_ref[b]
        meta_ref[geo.local_at + b] = local
        meta_ref[geo.count_at + b] = count
        low = high = jnp.bool_(False)
        for k in range(geo.slots):
            offset = offsets_ref[k, b]
            meta_ref[geo.offsets_at + k * geo.batches + b] = offset
            row = local + offset
            low = low | ((k < count) & (row < 0))
            high = high | ((k < count) & (row >= geo.rows))
        cross = (odd & high) | (jnp.logical_not(odd) & low)
        near = (odd & low) | (jnp.logical_not(odd) & high)
        inner = jnp.logical_not(low | high)
        many = count > 2
        few = (count > 0) & jnp.logical_not(many)
        kinds = [kind & size for kind in (cross, near, inner) for size in (many, few)]
        for which, member in enumerate(kinds + [cross]):
            meta_ref[which * geo.list_size + lengths[which]] = b
            lengths[which] = lengths[which] + member.astype(jnp.int32)
    for which in range(LISTS):
        meta_ref[which * geo.list_size + lengths[which]] = geo.batches
        meta_ref[geo.lengths_at + which] = lengths[which]


def zone(geo, odd, cross):
    span = geo.span if cross else geo.own - geo.span
    return pl.ds(jnp.where(odd == cross, geo.own - span, 0), span)


def pack_kernel(
    geo, density_ref, centre_in, offsets_in, counts_in,
    near_ref, cross_ref, meta_ref, acc_ref,
    centre_ref, offsets_ref, counts_ref, sems,
):
    index = lax.axis_index("blk")
    odd = index % 2 == 1

    def copies(up, down):
        return [
            pltpu.make_async_copy(
                density_ref.at[pl.ds(start, count)], ref.at[pl.ds(place, count)], sems.at[side, i]
            )
            for side, (pack, ref) in enumerate(zip(geo.packs, (up, down)))
            for i, (start, place, count) in enumerate(pack)
        ]

    def start(up, down):
        for copy in copies(up, down):
            copy.start()

    by_parity(odd, start, near_ref, cross_ref)
    scalars = [
        pltpu.make_async_copy(*pair, sems.at[2, i])
        for i, pair in enumerate(
            ((centre_in, centre_ref), (offsets_in, offsets_ref), (counts_in, counts_ref))
        )
    ]
    for copy in scalars:
        copy.start()
    for where in (zone(geo, odd, False), pl.ds(geo.first_at, geo.halo)):
        acc_ref[where] = jnp.zeros_like(acc_ref[where])
    for copy in scalars:
        copy.wait()
    build_lists(geo, index, centre_ref, offsets_ref, counts_ref, meta_ref)
    for copy in copies(near_ref, cross_ref):
        copy.wait()


def group_count(geo, meta_ref, which):
    return (meta_ref[geo.lengths_at + which] + GROUP - 1) // GROUP


def inner_share(geo, meta_ref):
    room = BUDGET
    for which in (CROSS_MANY, CROSS_FEW, NEAR_MANY, NEAR_FEW):
        room = room - COST[which % 2] * group_count(geo, meta_ref, which)
    share = []
    for which in (INNER_MANY, INNER_FEW):
        cost = COST[which % 2]
        taken = jnp.minimum(jnp.maximum(room, 0) // cost, group_count(geo, meta_ref, which))
        room = room - cost * taken
        share.append(taken)
    return share


def each_group(geo, meta_ref, which, body, size=GROUP, begin=0, end=None):
    length = meta_ref[geo.lengths_at + which]

    def step(i, carry):
        chosen = []
        for n in range(size):
            place = i * size + n
            there = place < length
            b = meta_ref[which * geo.list_size + jnp.minimum(place, length)]
            chosen.append((jnp.where(there, b, 0), there))
        body(chosen)
        return carry

    lax.fori_loop(begin, (length + size - 1) // size if end is None else end, step, 0)


class Slots:
    def __init__(self, geo, meta_ref, b, there, width):
        local = meta_ref[geo.local_at + b]
        count = jnp.where(there, meta_ref[geo.count_at + b], 0)
        self.offset = [meta_ref[geo.offsets_at + k * geo.batches + b] for k in range(width)]
        self.local = local
        self.row = [local + offset for offset in self.offset]
        self.live = [k < count for k in range(width)]
        self.own = [(row >= 0) & (row < geo.rows) for row in self.row]
        self.width = width


def panels(slots, ao_ref, b):
    return jnp.concatenate(
        [
            ao_ref[b, k] * jnp.where(slots.live[k], 1.0, 0.0).astype(ao_ref.dtype)
            for k in range(slots.width)
        ],
        axis=0,
    )


def gathered(tiles_ref, places):
    return jnp.concatenate(
        [jnp.concatenate([tiles_ref[place] for place in row], axis=1) for row in places], axis=0
    )


def potentials(xs, tiles, batches, kernel_ref):
    fs = [
        jnp.dot(t, x, preferred_element_type=jnp.float32).astype(jnp.bfloat16)
        for t, x in zip(tiles, xs)
    ]
    return [
        jnp.dot(f, kernel_ref[b], preferred_element_type=jnp.float32) for f, b in zip(fs, batches)
    ]


def outer_product(x, h):
    return lax.dot_general(x, h, (((1,), (1,)), ((), ())), preferred_element_type=jnp.float32)


def chain(xs, tiles, batches, kernel_ref, weights_ref):
    gs = potentials(xs, tiles, batches, kernel_ref)
    hs = [(g * weights_ref[pl.ds(b, 1), :]).astype(jnp.bfloat16) for g, b in zip(gs, batches)]
    return [outer_product(x, h) for x, h in zip(xs, hs)]


def scatter(part, target, nb, acc_ref):
    for k, row in enumerate(target):
        for j, place in enumerate(row):
            acc_ref[place] += part[k * nb : (k + 1) * nb, j * nb : (j + 1) * nb]


def add_whole(
    geo, chosen, width, meta_ref, tiles_ref, ao_ref, kernel_ref, weights_ref, acc_ref, halo_ref=None
):
    xs, tiles, targets = ([], [], [])
    for b, there in chosen:
        slots = Slots(geo, meta_ref, b, there, width)
        xs.append(panels(slots, ao_ref, b))
        rows, target = ([], [])
        for k in range(width):
            band = [slots.offset[j] - slots.offset[k] + geo.half for j in range(width)]
            own = slots.own[k]
            base = jnp.where(slots.live[k] & own, slots.row[k], 0) * geo.band
            row = jnp.concatenate([tiles_ref[base + o] for o in band], axis=1)
            if halo_ref is not None:
                away = slots.live[k] & jnp.logical_not(own)
                outside = jnp.where(away, geo.pick(geo.halo_base, 0, slots.row[k], 0), 0)
                other = [halo_ref[jnp.where(away, outside + o, 0)] for o in band]
                row = jnp.where(away, jnp.concatenate(other, axis=1), row)
                base = jnp.where(away, outside + geo.first_at, base)
            rows.append(row)
            target.append(
                [
                    jnp.where(slots.live[k] & slots.live[j], base + band[j], geo.spare)
                    for j in range(width)
                ]
            )
        tiles.append(jnp.concatenate(rows, axis=0))
        targets.append(target)
    parts = chain(xs, tiles, [b for b, _ in chosen], kernel_ref, weights_ref)
    for part, target in zip(parts, targets):
        scatter(part, target, ao_ref.shape[2], acc_ref)


def add_own(geo, chosen, width, meta_ref, tiles_ref, ao_ref, kernel_ref, weights_ref, acc_ref):
    xs, tiles, targets = ([], [], [])
    for b, there in chosen:
        slots = Slots(geo, meta_ref, b, there, width)
        xs.append(panels(slots, ao_ref, b))
        places, target = ([], [])
        for k in range(width):
            row = slots.row[k]
            band = [slots.offset[j] - slots.offset[k] + geo.half for j in range(width)]
            base = jnp.where(slots.own[k], row, 0) * geo.band
            places.append([base + o for o in band])
            base = geo.pick(geo.early_base, geo.early_at, row, base)
            target.append(
                [
                    jnp.where(
                        slots.live[k] & slots.live[j] & slots.own[j], base + band[j], geo.spare
                    )
                    for j in range(width)
                ]
            )
        tiles.append(gathered(tiles_ref, places))
        targets.append(target)
    parts = chain(xs, tiles, [b for b, _ in chosen], kernel_ref, weights_ref)
    for part, target in zip(parts, targets):
        scatter(part, target, ao_ref.shape[2], acc_ref)


def halo_rows(geo, meta_ref, slots):
    odd = meta_ref[geo.odd_at] == 1
    rows, places, present = ([], [], [])
    for i in range(geo.reach):
        row = jnp.where(odd, geo.rows + i, i - geo.reach)
        place, found = (jnp.int32(0), jnp.bool_(False))
        for k in range(slots.width):
            hit = slots.live[k] & (slots.row[k] == row)
            place = jnp.where(hit, k, place)
            found = found | hit
        rows.append(row)
        places.append(place)
        present.append(found)
    return rows, places, present


def add_corner(geo, chosen, meta_ref, halo_ref, ao_ref, kernel_ref, weights_ref, h_ref, total_ref):
    nb = ao_ref.shape[2]
    factor = lambda flag: jnp.where(flag, 1.0, 0.0)
    xs, sides, tiles, masks = ([], [], [], [])
    for b, there in chosen:
        slots = Slots(geo, meta_ref, b, there, geo.slots)
        rows, places, present = halo_rows(geo, meta_ref, slots)
        xs.append(panels(slots, ao_ref, b))
        sides.append(
            jnp.concatenate(
                [
                    ao_ref[b, place] * factor(found).astype(ao_ref.dtype)
                    for place, found in zip(places, present)
                ],
                axis=0,
            )
        )
        picked = []
        for row, found in zip(rows, present):
            base = geo.pick(geo.halo_base, 0, row, 0) - row + geo.half
            picked.append([jnp.where(found, base + column, 0) for column in slots.row])
        tiles.append(gathered(halo_ref, picked))
        masks.append([factor(found) for found in present])
    gs = potentials(xs, tiles, [b for b, _ in chosen], kernel_ref)
    hs = []
    for g, mask, (b, there) in zip(gs, masks, chosen):
        weights = weights_ref[pl.ds(b, 1), :]
        h = jnp.concatenate(
            [g[i * nb : (i + 1) * nb] * (weights * mask[i]) for i in range(geo.reach)], axis=0
        ).astype(jnp.bfloat16)
        h_ref[jnp.where(there, b, geo.batches)] = h
        hs.append(h)
    total_ref[...] += outer_product(
        jnp.concatenate(sides, axis=1), jnp.concatenate(hs, axis=1)
    )


def add_columns(geo, chosen, width, meta_ref, ao_ref, h_ref, acc_ref):
    parts, targets = ([], [])
    for b, there in chosen:
        slots = Slots(geo, meta_ref, b, there, width)
        rows, _, present = halo_rows(geo, meta_ref, slots)
        parts.append(outer_product(ao_ref[b, pl.ds(0, width)].reshape(-1, ao_ref.shape[3]), h_ref[b]))
        targets.append(
            [
                [
                    jnp.where(
                        slots.live[k] & slots.own[k] & found,
                        slots.row[k] * geo.band + row - slots.row[k] + geo.half,
                        geo.spare,
                    )
                    for row, found in zip(rows, present)
                ]
                for k in range(width)
            ]
        )
    for part, target in zip(parts, targets):
        scatter(part, target, ao_ref.shape[2], acc_ref)


def early_kernel(
    geo, meta_ref, tiles_ref, ao_ref, kernel_ref, weights_ref, acc_in, acc_ref, early_out
):
    odd = meta_ref[geo.odd_at] == 1
    for where in (zone(geo, odd, True), pl.ds(geo.early_at, geo.early), pl.ds(geo.spare, 1)):
        acc_ref[where] = jnp.zeros_like(acc_ref[where])
    refs = (meta_ref, tiles_ref, ao_ref, kernel_ref, weights_ref, acc_ref)
    for which, width in ((CROSS_MANY, geo.slots), (CROSS_FEW, 2)):
        each_group(
            geo, meta_ref, which, lambda chosen, width=width: add_own(geo, chosen, width, *refs)
        )
    early_out[...] = acc_ref[pl.ds(geo.early_at, geo.early)].astype(early_out.dtype)


def near_kernel(
    geo, meta_ref, halo_ref, tiles_ref, ao_ref, kernel_ref, weights_ref, acc_in, acc_ref, first_out
):
    refs = (meta_ref, tiles_ref, ao_ref, kernel_ref, weights_ref, acc_ref, halo_ref)
    for which, width in ((NEAR_MANY, geo.slots), (NEAR_FEW, 2)):
        each_group(
            geo, meta_ref, which, lambda chosen, width=width: add_whole(geo, chosen, width, *refs)
        )
    first_out[...] = acc_ref[pl.ds(geo.first_at, geo.halo)].astype(first_out.dtype)
    share = inner_share(geo, meta_ref)
    for which, width, end in ((INNER_MANY, geo.slots, share[0]), (INNER_FEW, 2, share[1])):
        each_group(
            geo,
            meta_ref,
            which,
            lambda chosen, width=width: add_whole(geo, chosen, width, *refs[:-1]),
            end=end,
        )


def late_kernel(
    geo, meta_ref, halo_ref, ao_ref, kernel_ref, weights_ref, h_ref, late_out, total_ref
):
    nb = ao_ref.shape[2]
    total_ref[...] = jnp.zeros_like(total_ref)

    def work(chosen):
        add_corner(
            geo, chosen, meta_ref, halo_ref, ao_ref, kernel_ref, weights_ref, h_ref, total_ref
        )

    groups = (meta_ref[geo.lengths_at + CROSS] + 1) // LATE_GROUP
    each_group(geo, meta_ref, CROSS, work, size=LATE_GROUP, end=groups)
    each_group(geo, meta_ref, CROSS, work, size=LATE_GROUP // 2, begin=2 * groups)
    for i in range(geo.reach):
        for j in range(geo.reach):
            late_out[i * geo.reach + j] = total_ref[
                i * nb : (i + 1) * nb, j * nb : (j + 1) * nb
            ].astype(late_out.dtype)


def inner_kernel(
    geo, meta_ref, first_ref, tiles_ref, ao_ref, kernel_ref, weights_ref, h_ref, acc_in,
    acc_ref, out_ref, sems,
):
    odd = meta_ref[geo.odd_at] == 1
    refs = (meta_ref, tiles_ref, ao_ref, kernel_ref, weights_ref, acc_ref)
    share = inner_share(geo, meta_ref)
    for which, width, begin in ((INNER_MANY, geo.slots, share[0]), (INNER_FEW, 2, share[1])):
        each_group(
            geo,
            meta_ref,
            which,
            lambda chosen, width=width: add_whole(geo, chosen, width, *refs),
            begin=begin,
        )

    def add_near(up, down):
        for start, place, count in geo.packs[0 if up else 1]:
            acc_ref[pl.ds(start, count)] += first_ref[pl.ds(place, count)].astype(jnp.float32)

    by_parity(odd, add_near, True, False)
    done = zone(geo, odd, False)
    copy = pltpu.make_async_copy(acc_ref.at[done], out_ref.at[done], sems.at[0])
    copy.start()
    for which, width in ((CROSS_MANY, geo.slots), (CROSS_FEW, 2)):
        each_group(
            geo,
            meta_ref,
            which,
            lambda chosen, width=width: add_columns(
                geo, chosen, width, meta_ref, ao_ref, h_ref, acc_ref
            ),
        )

    def write_quiet(up, down):
        run_copies(
            [
                pltpu.make_async_copy(
                    acc_ref.at[pl.ds(start, count)], out_ref.at[pl.ds(start, count)], sems.at[1 + i]
                )
                for i, (start, count) in enumerate(geo.quiet[0 if up else 1])
            ]
        )

    by_parity(odd, write_quiet, True, False)
    copy.wait()


def finish_kernel(geo, meta_ref, early_ref, late_ref, acc_ref, out_in, out_ref, total, sems):
    def add(up, down):
        copies = []
        for packs, ref in ((geo.early_packs, early_ref), (geo.late_packs, late_ref)):
            for start, place, count in packs[0 if up else 1]:
                spot = pl.ds(len(copies) * geo.band, count)
                total[spot] = acc_ref[pl.ds(start, count)] + ref[pl.ds(place, count)].astype(
                    jnp.float32
                )
                copy = pltpu.make_async_copy(
                    total.at[spot], out_ref.at[pl.ds(start, count)], sems.at[len(copies)]
                )
                copy.start()
                copies.append(copy)
        for copy in copies:
            copy.wait()

    by_parity(meta_ref[geo.odd_at] == 1, add, False, True)


def call(kernel, out_shape, in_specs, out_specs, scratch, aliases=None, cost=None):
    return pl.pallas_call(
        kernel,
        out_shape=out_shape,
        in_specs=in_specs,
        out_specs=out_specs,
        scratch_shapes=scratch,
        input_output_aliases=aliases or {},
        cost_estimate=cost,
        compiler_params=pltpu.CompilerParams(vmem_limit_bytes=16 * MIB),
    )


def to_first(x, size):
    pairs = [(i, i + 1) for i in range(0, size - 1, 2)]
    got = lax.ppermute(x, "blk", pairs + [(j, i) for i, j in pairs])
    return pltpu.with_memory_space_constraint(got, pltpu.VMEM)


def to_second(x, size):
    pairs = [(i, i + 1) for i in range(1, size - 1, 2)]
    got = lax.ppermute(x, "blk", pairs + [(j, i) for i, j in pairs])
    return pltpu.with_memory_space_constraint(got, pltpu.VMEM)


def local(density, ao_values, kernel, grid_weights, centre, sig_offsets, counts):
    rows, band, nb, _ = density.shape
    batches, slots, _, pts = ao_values.shape
    size = lax.axis_size("blk")
    geo = Geometry(rows, band, batches, slots)
    in_hbm = lambda x: pltpu.with_memory_space_constraint(x, pltpu.HBM)
    tiles = density.reshape(geo.own, nb, nb)
    pack = lambda count: pltpu.VMEM((count, nb, nb), jnp.bfloat16)
    dma = pltpu.SemaphoreType.DMA
    acc_type = pltpu.VMEM((geo.spare + 1, nb, nb), jnp.float32)

    near_halo, cross_halo, meta, acc = call(
        functools.partial(pack_kernel, geo),
        (pack(geo.halo),) * 2 + (pltpu.SMEM((geo.meta_size,), jnp.int32), acc_type),
        [ANY_SPEC] * 4,
        (VMEM_SPEC,) * 2 + (SMEM_SPEC, VMEM_SPEC),
        [
            pltpu.SMEM((batches,), jnp.int32),
            pltpu.SMEM((slots, batches), jnp.int32),
            pltpu.SMEM((batches,), jnp.int32),
            dma((3, max(geo.reach, 3))),
        ],
        cost=pl.CostEstimate(flops=10**10, bytes_accessed=10**8, transcendentals=0),
    )(in_hbm(tiles), in_hbm(centre), in_hbm(sig_offsets.T), in_hbm(counts))
    cross_halo = to_second(cross_halo, size)
    near_halo = to_first(near_halo, size)

    panel = (tiles, ao_values, kernel, grid_weights)
    acc, early = call(
        functools.partial(early_kernel, geo),
        (acc_type, pack(geo.early)),
        [SMEM_SPEC] + [VMEM_SPEC] * 5,
        (VMEM_SPEC,) * 2,
        [],
        {5: 0},
    )(meta, *panel, acc)
    early = to_second(early, size)

    acc, first = call(
        functools.partial(near_kernel, geo),
        (acc_type, pack(geo.halo)),
        [SMEM_SPEC] + [VMEM_SPEC] * 6,
        (VMEM_SPEC,) * 2,
        [],
        {6: 0},
    )(meta, near_halo, *panel, acc)
    first = to_first(first, size)

    h_type = pltpu.VMEM((batches + 1, geo.reach * nb, pts), jnp.bfloat16)
    h, late = call(
        functools.partial(late_kernel, geo),
        (h_type, pack(geo.late)),
        [SMEM_SPEC] + [VMEM_SPEC] * 4,
        (VMEM_SPEC,) * 2,
        [pltpu.VMEM((geo.reach * nb, geo.reach * nb), jnp.float32)],
    )(meta, cross_halo, *panel[1:])
    late = to_second(late, size)

    whole = jax.ShapeDtypeStruct((geo.own, nb, nb), jnp.float32)
    acc, out = call(
        functools.partial(inner_kernel, geo),
        (acc_type, whole),
        [SMEM_SPEC] + [VMEM_SPEC] * 7,
        (VMEM_SPEC, ANY_SPEC),
        [dma((1 + max(len(runs) for runs in geo.quiet),))],
        {7: 0},
    )(meta, first, *panel, h, acc)

    parts = 2 * geo.reach
    out = call(
        functools.partial(finish_kernel, geo),
        whole,
        [SMEM_SPEC] + [VMEM_SPEC] * 3 + [ANY_SPEC],
        ANY_SPEC,
        [pltpu.VMEM((parts * band, nb, nb), jnp.float32), dma((parts,))],
        {4: 0},
    )(meta, early, late, acc, out)
    return out.reshape(rows, band, nb, nb)


def solution(mesh):
    placed = (
        P(("groups", "blk"), None, None, None),
        P(("groups", "blk"), None, None, None),
        P(("groups", "blk"), None, None),
        P(("groups", "blk"), None),
        P(("groups", "blk")),
        P(("groups", "blk"), None),
        P(("groups", "blk")),
    )
    return jax.shard_map(
        local,
        mesh=mesh,
        in_specs=placed,
        out_specs=P(("groups", "blk"), None, None, None),
        check_vma=False,
    )
```

```python
import functools

import jax
import jax.numpy as jnp
from jax import lax
from jax.experimental import pallas as pl
from jax.experimental.pallas import tpu as pltpu
from jax.sharding import PartitionSpec as P

MIB = 1 << 20
GROUP = 2
LATE_GROUP = 4
LISTS = 7
BUDGET = 43
EXTRA = 8
COST = (10, 7)
SMEM_SPEC = pl.BlockSpec(memory_space=pltpu.SMEM)
VMEM_SPEC = pl.BlockSpec(memory_space=pltpu.VMEM)
ANY_SPEC = pl.BlockSpec(memory_space=pl.ANY)


class Geometry:
    def __init__(self, rows, band, batches, slots):
        self.rows, self.band, self.batches, self.slots = rows, band, batches, slots
        self.half = half = (band - 1) // 2
        self.reach = reach = half // 2
        self.own = rows * band
        low = [(-m, reach + m, band) for m in range(reach, 0, -1)]
        high = [(rows + m, 0, 3 * reach - m) for m in range(reach)]
        self.halo = sum(stop - start for _, start, stop in low)
        low_cut = [half - row for row, _, _ in low]
        high_cut = [rows - row + half for row, _, _ in high]
        early = (
            [(row, cut, stop) for (row, _, stop), cut in zip(low, low_cut)],
            [(row, start, cut) for (row, start, _), cut in zip(high, high_cut)],
        )
        late = (
            [(row, start, cut) for (row, start, _), cut in zip(low, low_cut)],
            [(row, cut, stop) for (row, _, stop), cut in zip(high, high_cut)],
        )
        self.early = sum(stop - start for _, start, stop in early[0])
        self.late = self.halo - self.early
        self.first_at = self.own
        self.early_at = self.own + self.halo
        self.spare = self.early_at + self.early
        self.halo_base = self.bases((low, high))
        self.early_base = self.bases(early)
        shifts = (rows, -rows)
        self.packs = [self.places(*pair) for pair in zip((low, high), shifts)]
        self.early_packs = [self.places(*pair) for pair in zip(early, shifts)]
        self.late_packs = [self.places(*pair) for pair in zip(late, shifts)]
        self.span = min(2 * reach, rows) * band
        self.quiet = [
            self.others(self.packs[1], 0, self.span),
            self.others(self.packs[0], self.own - self.span, self.own),
        ]
        self.list_size = batches + 2
        self.lengths_at = (LISTS + 1) * self.list_size
        self.odd_at = self.lengths_at + LISTS + 1
        self.origin_at = self.odd_at + 1
        self.meta_size = self.origin_at + 1

    def bases(self, sides):
        found = {}
        for segments in sides:
            place = 0
            for row, start, stop in segments:
                found[row] = place - start
                place += stop - start
        return found

    def places(self, segments, shift):
        pack, place = ([], 0)
        for row, start, stop in segments:
            pack.append(((row + shift) * self.band + start, place, stop - start))
            place += stop - start
        return pack

    def others(self, pack, begin, end):
        touched = set()
        for start, _, count in pack:
            touched.update(range(start, start + count))
        runs = []
        for index in range(begin, end):
            if index in touched:
                continue
            if runs and sum(runs[-1]) == index:
                runs[-1] = (runs[-1][0], runs[-1][1] + 1)
            else:
                runs.append((index, 1))
        return runs

    def pick(self, bases, shift, row, otherwise):
        value = otherwise
        for at, base in bases.items():
            value = jnp.where(row == at, base + shift, value)
        return value


def run_copies(copies):
    for copy in copies:
        copy.start()
    for copy in copies:
        copy.wait()


def by_parity(odd, body, first, second):
    @pl.when(jnp.logical_not(odd))
    def _():
        body(first, second)

    @pl.when(odd)
    def _():
        body(second, first)


CROSS_MANY, CROSS_FEW, NEAR_MANY, NEAR_FEW, INNER_MANY, INNER_FEW, CROSS = range(LISTS)


class Info:
    def __init__(self, meta_ref, centre_ref, offsets_ref, counts_ref):
        self.meta, self.centre, self.offsets, self.counts = meta_ref, centre_ref, offsets_ref, counts_ref


def build_lists(geo, index, info):
    meta = info.meta
    first = index * geo.rows
    odd = index % 2
    meta[geo.odd_at] = odd
    meta[geo.origin_at] = first
    for which in range(LISTS + 1):
        meta[geo.lengths_at + which] = 0
    crossing = jnp.int32(0)
    for b in range(geo.batches):
        local = info.centre[b] - first
        count = info.counts[b]
        lowest = highest = local
        for k in range(geo.slots):
            row = jnp.where(k < count, local + info.offsets[k, b], local)
            lowest = jnp.minimum(lowest, row)
            highest = jnp.maximum(highest, row)
        low, high = lowest < 0, highest >= geo.rows
        edge = low | high
        cross = edge & (high == (odd == 1))
        kind = jnp.where(edge, jnp.where(cross, CROSS_MANY, NEAR_MANY), INNER_MANY)
        which = jnp.where(count > 0, kind + (count <= 2).astype(jnp.int32), LISTS)
        length = meta[geo.lengths_at + which]
        meta[which * geo.list_size + length] = b
        meta[geo.lengths_at + which] = length + 1
        meta[CROSS * geo.list_size + crossing] = b
        crossing = crossing + cross.astype(jnp.int32)
    meta[geo.lengths_at + CROSS] = crossing


def zone(geo, odd, cross):
    span = geo.span if cross else geo.own - geo.span
    return pl.ds(jnp.where(odd == cross, geo.own - span, 0), span)


def pack_kernel(
    geo, density_ref, centre_in, offsets_in, counts_in,
    near_ref, cross_ref, meta_ref, centre_ref, offsets_ref, counts_ref, acc_ref, sems,
):
    index = lax.axis_index("blk")
    odd = index % 2 == 1

    def copies(up, down):
        return [
            pltpu.make_async_copy(
                density_ref.at[pl.ds(start, count)], ref.at[pl.ds(place, count)], sems.at[side, i]
            )
            for side, (pack, ref) in enumerate(zip(geo.packs, (up, down)))
            for i, (start, place, count) in enumerate(pack)
        ]

    def start(up, down):
        for copy in copies(up, down):
            copy.start(priority=1)

    scalars = [
        pltpu.make_async_copy(*pair, sems.at[2, i])
        for i, pair in enumerate(
            ((centre_in, centre_ref), (offsets_in, offsets_ref), (counts_in, counts_ref))
        )
    ]
    for copy in scalars:
        copy.start()
    by_parity(odd, start, near_ref, cross_ref)
    for copy in scalars:
        copy.wait()
    build_lists(geo, index, Info(meta_ref, centre_ref, offsets_ref, counts_ref))
    for where in (zone(geo, odd, False), pl.ds(geo.first_at, geo.halo)):
        acc_ref[where] = jnp.zeros_like(acc_ref[where])
    for copy in copies(near_ref, cross_ref):
        copy.wait()


def group_count(geo, info, which):
    return (info.meta[geo.lengths_at + which] + GROUP - 1) // GROUP


def inner_share(geo, info):
    index = info.meta[geo.origin_at] // geo.rows
    room = BUDGET + jnp.where((index + 1) // 2 % 2 == 0, EXTRA, 0)
    for which in (CROSS_MANY, CROSS_FEW, NEAR_MANY, NEAR_FEW):
        room = room - COST[which % 2] * group_count(geo, info, which)
    share = []
    for which in (INNER_MANY, INNER_FEW):
        cost = COST[which % 2]
        taken = jnp.minimum(jnp.maximum(room, 0) // cost, group_count(geo, info, which))
        room = room - cost * taken
        share.append(taken)
    return share


def each_group(geo, info, which, body, size=GROUP, begin=0, end=None):
    length = info.meta[geo.lengths_at + which]

    def step(i, carry):
        chosen = []
        for n in range(size):
            place = i * size + n
            there = place < length
            b = info.meta[which * geo.list_size + jnp.where(there, place, 0)]
            chosen.append((jnp.where(there, b, 0), there))
        body(chosen)
        return carry

    lax.fori_loop(begin, (length + size - 1) // size if end is None else end, step, 0)


class Slots:
    def __init__(self, geo, info, b, there, width):
        local = info.centre[b] - info.meta[geo.origin_at]
        count = jnp.where(there, info.counts[b], 0)
        self.offset = [info.offsets[k, b] for k in range(width)]
        self.local = local
        self.row = [local + offset for offset in self.offset]
        self.live = [k < count for k in range(width)]
        self.own = [(row >= 0) & (row < geo.rows) for row in self.row]
        self.width = width


def panels(slots, ao_ref, b):
    return jnp.concatenate(
        [
            ao_ref[b, k] * jnp.where(slots.live[k], 1.0, 0.0).astype(ao_ref.dtype)
            for k in range(slots.width)
        ],
        axis=0,
    )


def gathered(tiles_ref, places):
    return jnp.concatenate(
        [jnp.concatenate([tiles_ref[place] for place in row], axis=1) for row in places], axis=0
    )


def potentials(xs, tiles, batches, kernel_ref):
    fs = [
        jnp.dot(t, x, preferred_element_type=jnp.float32).astype(jnp.bfloat16)
        for t, x in zip(tiles, xs)
    ]
    return [
        jnp.dot(f, kernel_ref[b], preferred_element_type=jnp.float32) for f, b in zip(fs, batches)
    ]


def outer_product(x, h):
    return lax.dot_general(x, h, (((1,), (1,)), ((), ())), preferred_element_type=jnp.float32)


def chain(xs, tiles, batches, kernel_ref, weights_ref):
    gs = potentials(xs, tiles, batches, kernel_ref)
    hs = [(g * weights_ref[pl.ds(b, 1), :]).astype(jnp.bfloat16) for g, b in zip(gs, batches)]
    return [outer_product(x, h) for x, h in zip(xs, hs)]


def scatter(part, target, nb, acc_ref):
    for k, row in enumerate(target):
        for j, place in enumerate(row):
            acc_ref[place] += part[k * nb : (k + 1) * nb, j * nb : (j + 1) * nb]


def add_whole(
    geo, chosen, width, info, tiles_ref, ao_ref, kernel_ref, weights_ref, acc_ref, halo_ref=None
):
    xs, tiles, targets = ([], [], [])
    for b, there in chosen:
        slots = Slots(geo, info, b, there, width)
        xs.append(panels(slots, ao_ref, b))
        rows, target = ([], [])
        for k in range(width):
            band = [slots.offset[j] - slots.offset[k] + geo.half for j in range(width)]
            own = slots.own[k]
            base = jnp.where(slots.live[k] & own, slots.row[k], 0) * geo.band
            row = jnp.concatenate([tiles_ref[base + o] for o in band], axis=1)
            if halo_ref is not None:
                away = slots.live[k] & jnp.logical_not(own)
                outside = jnp.where(away, geo.pick(geo.halo_base, 0, slots.row[k], 0), 0)
                other = [halo_ref[jnp.where(away, outside + o, 0)] for o in band]
                row = jnp.where(away, jnp.concatenate(other, axis=1), row)
                base = jnp.where(away, outside + geo.first_at, base)
            rows.append(row)
            target.append(
                [
                    jnp.where(slots.live[k] & slots.live[j], base + band[j], geo.spare)
                    for j in range(width)
                ]
            )
        tiles.append(jnp.concatenate(rows, axis=0))
        targets.append(target)
    parts = chain(xs, tiles, [b for b, _ in chosen], kernel_ref, weights_ref)
    for part, target in zip(parts, targets):
        scatter(part, target, ao_ref.shape[2], acc_ref)


def add_own(geo, chosen, width, info, tiles_ref, ao_ref, kernel_ref, weights_ref, acc_ref):
    xs, tiles, targets = ([], [], [])
    for b, there in chosen:
        slots = Slots(geo, info, b, there, width)
        xs.append(panels(slots, ao_ref, b))
        places, target = ([], [])
        for k in range(width):
            row = slots.row[k]
            band = [slots.offset[j] - slots.offset[k] + geo.half for j in range(width)]
            base = jnp.where(slots.own[k], row, 0) * geo.band
            places.append([base + o for o in band])
            base = geo.pick(geo.early_base, geo.early_at, row, base)
            target.append(
                [
                    jnp.where(
                        slots.live[k] & slots.live[j] & slots.own[j], base + band[j], geo.spare
                    )
                    for j in range(width)
                ]
            )
        tiles.append(gathered(tiles_ref, places))
        targets.append(target)
    parts = chain(xs, tiles, [b for b, _ in chosen], kernel_ref, weights_ref)
    for part, target in zip(parts, targets):
        scatter(part, target, ao_ref.shape[2], acc_ref)


def halo_rows(geo, info, slots):
    odd = info.meta[geo.odd_at] == 1
    rows, places, present = ([], [], [])
    for i in range(geo.reach):
        row = jnp.where(odd, geo.rows + i, i - geo.reach)
        place, found = (jnp.int32(0), jnp.bool_(False))
        for k in range(slots.width):
            hit = slots.live[k] & (slots.row[k] == row)
            place = jnp.where(hit, k, place)
            found = found | hit
        rows.append(row)
        places.append(place)
        present.append(found)
    return rows, places, present


def add_corner(geo, chosen, info, halo_ref, ao_ref, kernel_ref, weights_ref, h_ref, total_ref):
    nb = ao_ref.shape[2]
    factor = lambda flag: jnp.where(flag, 1.0, 0.0)
    xs, sides, tiles, masks = ([], [], [], [])
    for b, there in chosen:
        slots = Slots(geo, info, b, there, geo.slots)
        rows, places, present = halo_rows(geo, info, slots)
        xs.append(panels(slots, ao_ref, b))
        sides.append(
            jnp.concatenate(
                [
                    ao_ref[b, place] * factor(found).astype(ao_ref.dtype)
                    for place, found in zip(places, present)
                ],
                axis=0,
            )
        )
        picked = []
        for row, found in zip(rows, present):
            base = geo.pick(geo.halo_base, 0, row, 0) - row + geo.half
            picked.append([jnp.where(found, base + column, 0) for column in slots.row])
        tiles.append(gathered(halo_ref, picked))
        masks.append([factor(found) for found in present])
    gs = potentials(xs, tiles, [b for b, _ in chosen], kernel_ref)
    hs = []
    for g, mask, (b, there) in zip(gs, masks, chosen):
        weights = weights_ref[pl.ds(b, 1), :]
        h = jnp.concatenate(
            [g[i * nb : (i + 1) * nb] * (weights * mask[i]) for i in range(geo.reach)], axis=0
        ).astype(jnp.bfloat16)
        h_ref[jnp.where(there, b, geo.batches)] = h
        hs.append(h)
    total_ref[...] += outer_product(
        jnp.concatenate(sides, axis=1), jnp.concatenate(hs, axis=1)
    )


def add_columns(geo, chosen, width, info, ao_ref, h_ref, acc_ref):
    parts, targets = ([], [])
    for b, there in chosen:
        slots = Slots(geo, info, b, there, width)
        rows, _, present = halo_rows(geo, info, slots)
        parts.append(outer_product(ao_ref[b, pl.ds(0, width)].reshape(-1, ao_ref.shape[3]), h_ref[b]))
        targets.append(
            [
                [
                    jnp.where(
                        slots.live[k] & slots.own[k] & found,
                        slots.row[k] * geo.band + row - slots.row[k] + geo.half,
                        geo.spare,
                    )
                    for row, found in zip(rows, present)
                ]
                for k in range(width)
            ]
        )
    for part, target in zip(parts, targets):
        scatter(part, target, ao_ref.shape[2], acc_ref)


def early_kernel(
    geo, meta_ref, centre_ref, offsets_ref, counts_ref, tiles_ref, ao_ref, kernel_ref, weights_ref,
    acc_in, acc_ref, early_out,
):
    info = Info(meta_ref, centre_ref, offsets_ref, counts_ref)
    odd = info.meta[geo.odd_at] == 1
    for where in (zone(geo, odd, True), pl.ds(geo.early_at, geo.early), pl.ds(geo.spare, 1)):
        acc_ref[where] = jnp.zeros_like(acc_ref[where])
    refs = (info, tiles_ref, ao_ref, kernel_ref, weights_ref, acc_ref)
    for which, width in ((CROSS_MANY, geo.slots), (CROSS_FEW, 2)):
        each_group(
            geo, info, which, lambda chosen, width=width: add_own(geo, chosen, width, *refs)
        )
    early_out[...] = acc_ref[pl.ds(geo.early_at, geo.early)].astype(early_out.dtype)


def near_kernel(
    geo, meta_ref, centre_ref, offsets_ref, counts_ref, halo_ref, tiles_ref, ao_ref, kernel_ref,
    weights_ref, acc_in, acc_ref, first_out,
):
    info = Info(meta_ref, centre_ref, offsets_ref, counts_ref)
    refs = (info, tiles_ref, ao_ref, kernel_ref, weights_ref, acc_ref, halo_ref)
    for which, width in ((NEAR_MANY, geo.slots), (NEAR_FEW, 2)):
        each_group(
            geo, info, which, lambda chosen, width=width: add_whole(geo, chosen, width, *refs)
        )
    first_out[...] = acc_ref[pl.ds(geo.first_at, geo.halo)].astype(first_out.dtype)
    share = inner_share(geo, info)
    for which, width, end in ((INNER_MANY, geo.slots, share[0]), (INNER_FEW, 2, share[1])):
        each_group(
            geo,
            info,
            which,
            lambda chosen, width=width: add_whole(geo, chosen, width, *refs[:-1]),
            end=end,
        )


def late_kernel(
    geo, meta_ref, centre_ref, offsets_ref, counts_ref, halo_ref, ao_ref, kernel_ref, weights_ref,
    h_ref, late_out, total_ref,
):
    info = Info(meta_ref, centre_ref, offsets_ref, counts_ref)
    nb = ao_ref.shape[2]
    total_ref[...] = jnp.zeros_like(total_ref)

    def work(chosen):
        add_corner(
            geo, chosen, info, halo_ref, ao_ref, kernel_ref, weights_ref, h_ref, total_ref
        )

    groups = (info.meta[geo.lengths_at + CROSS] + 1) // LATE_GROUP
    each_group(geo, info, CROSS, work, size=LATE_GROUP, end=groups)
    each_group(geo, info, CROSS, work, size=LATE_GROUP // 2, begin=2 * groups)
    for i in range(geo.reach):
        for j in range(geo.reach):
            late_out[i * geo.reach + j] = total_ref[
                i * nb : (i + 1) * nb, j * nb : (j + 1) * nb
            ].astype(late_out.dtype)


def inner_kernel(
    geo, meta_ref, centre_ref, offsets_ref, counts_ref, first_ref, tiles_ref, ao_ref, kernel_ref,
    weights_ref, h_ref, acc_in, acc_ref, out_ref, sems,
):
    info = Info(meta_ref, centre_ref, offsets_ref, counts_ref)
    odd = info.meta[geo.odd_at] == 1
    refs = (info, tiles_ref, ao_ref, kernel_ref, weights_ref, acc_ref)
    share = inner_share(geo, info)
    for which, width, begin in ((INNER_MANY, geo.slots, share[0]), (INNER_FEW, 2, share[1])):
        each_group(
            geo,
            info,
            which,
            lambda chosen, width=width: add_whole(geo, chosen, width, *refs),
            begin=begin,
        )

    def add_near(up, down):
        for start, place, count in geo.packs[0 if up else 1]:
            acc_ref[pl.ds(start, count)] += first_ref[pl.ds(place, count)].astype(jnp.float32)

    by_parity(odd, add_near, True, False)
    done = zone(geo, odd, False)
    copy = pltpu.make_async_copy(acc_ref.at[done], out_ref.at[done], sems.at[0])
    copy.start()
    for which, width in ((CROSS_MANY, geo.slots), (CROSS_FEW, 2)):
        each_group(
            geo,
            info,
            which,
            lambda chosen, width=width: add_columns(
                geo, chosen, width, info, ao_ref, h_ref, acc_ref
            ),
        )

    def write_quiet(up, down):
        run_copies(
            [
                pltpu.make_async_copy(
                    acc_ref.at[pl.ds(start, count)], out_ref.at[pl.ds(start, count)], sems.at[1 + i]
                )
                for i, (start, count) in enumerate(geo.quiet[0 if up else 1])
            ]
        )

    by_parity(odd, write_quiet, True, False)
    copy.wait()


def finish_kernel(geo, meta_ref, early_ref, late_ref, acc_ref, out_in, out_ref, total, sems):
    def add(up, down):
        copies = []
        for packs, ref in ((geo.early_packs, early_ref), (geo.late_packs, late_ref)):
            for start, place, count in packs[0 if up else 1]:
                spot = pl.ds(len(copies) * geo.band, count)
                total[spot] = acc_ref[pl.ds(start, count)] + ref[pl.ds(place, count)].astype(
                    jnp.float32
                )
                copy = pltpu.make_async_copy(
                    total.at[spot], out_ref.at[pl.ds(start, count)], sems.at[len(copies)]
                )
                copy.start()
                copies.append(copy)
        for copy in copies:
            copy.wait()

    by_parity(meta_ref[geo.odd_at] == 1, add, False, True)


def call(kernel, out_shape, in_specs, out_specs, scratch, aliases=None, cost=None):
    return pl.pallas_call(
        kernel,
        out_shape=out_shape,
        in_specs=in_specs,
        out_specs=out_specs,
        scratch_shapes=scratch,
        input_output_aliases=aliases or {},
        cost_estimate=cost,
        compiler_params=pltpu.CompilerParams(vmem_limit_bytes=16 * MIB),
    )


def to_first(x, size):
    pairs = [(i, i + 1) for i in range(0, size - 1, 2)]
    got = lax.ppermute(x, "blk", pairs + [(j, i) for i, j in pairs])
    return pltpu.with_memory_space_constraint(got, pltpu.VMEM)


def to_second(x, size):
    pairs = [(i, i + 1) for i in range(1, size - 1, 2)]
    got = lax.ppermute(x, "blk", pairs + [(j, i) for i, j in pairs])
    return pltpu.with_memory_space_constraint(got, pltpu.VMEM)


def local(density, ao_values, kernel, grid_weights, centre, sig_offsets, counts):
    rows, band, nb, _ = density.shape
    batches, slots, _, pts = ao_values.shape
    size = lax.axis_size("blk")
    geo = Geometry(rows, band, batches, slots)
    in_hbm = lambda x: pltpu.with_memory_space_constraint(x, pltpu.HBM)
    tiles = density.reshape(geo.own, nb, nb)
    pack = lambda count: pltpu.VMEM((count, nb, nb), jnp.bfloat16)
    dma = pltpu.SemaphoreType.DMA
    acc_type = pltpu.VMEM((geo.spare + 1, nb, nb), jnp.float32)

    smem = lambda *shape: pltpu.SMEM(shape, jnp.int32)
    near_halo, cross_halo, *info, acc = call(
        functools.partial(pack_kernel, geo),
        (pack(geo.halo),) * 2
        + (smem(geo.meta_size), smem(batches), smem(slots, batches), smem(batches), acc_type),
        [ANY_SPEC] * 4,
        (VMEM_SPEC,) * 2 + (SMEM_SPEC,) * 4 + (VMEM_SPEC,),
        [dma((3, max(geo.reach, 3)))],
        cost=pl.CostEstimate(flops=10**10, bytes_accessed=10**8, transcendentals=0),
    )(in_hbm(tiles), in_hbm(centre), in_hbm(sig_offsets.T), in_hbm(counts))
    cross_halo = to_second(cross_halo, size)
    near_halo = to_first(near_halo, size)

    panel = (tiles, ao_values, kernel, grid_weights)
    acc, early = call(
        functools.partial(early_kernel, geo),
        (acc_type, pack(geo.early)),
        [SMEM_SPEC] * 4 + [VMEM_SPEC] * 5,
        (VMEM_SPEC,) * 2,
        [],
        {8: 0},
    )(*info, *panel, acc)
    early = to_second(early, size)

    acc, first = call(
        functools.partial(near_kernel, geo),
        (acc_type, pack(geo.halo)),
        [SMEM_SPEC] * 4 + [VMEM_SPEC] * 6,
        (VMEM_SPEC,) * 2,
        [],
        {9: 0},
    )(*info, near_halo, *panel, acc)
    first = to_first(first, size)

    h_type = pltpu.VMEM((batches + 1, geo.reach * nb, pts), jnp.bfloat16)
    h, late = call(
        functools.partial(late_kernel, geo),
        (h_type, pack(geo.late)),
        [SMEM_SPEC] * 4 + [VMEM_SPEC] * 4,
        (VMEM_SPEC,) * 2,
        [pltpu.VMEM((geo.reach * nb, geo.reach * nb), jnp.float32)],
    )(*info, cross_halo, *panel[1:])
    late = to_second(late, size)

    whole = jax.ShapeDtypeStruct((geo.own, nb, nb), jnp.float32)
    acc, out = call(
        functools.partial(inner_kernel, geo),
        (acc_type, whole),
        [SMEM_SPEC] * 4 + [VMEM_SPEC] * 7,
        (VMEM_SPEC, ANY_SPEC),
        [dma((1 + max(len(runs) for runs in geo.quiet),))],
        {10: 0},
    )(*info, first, *panel, h, acc)

    parts = 2 * geo.reach
    out = call(
        functools.partial(finish_kernel, geo),
        whole,
        [SMEM_SPEC] + [VMEM_SPEC] * 3 + [ANY_SPEC],
        ANY_SPEC,
        [pltpu.VMEM((parts * band, nb, nb), jnp.float32), dma((parts,))],
        {4: 0},
    )(info[0], early, late, acc, out)
    return out.reshape(rows, band, nb, nb)


def solution(mesh):
    placed = (
        P(("groups", "blk"), None, None, None),
        P(("groups", "blk"), None, None, None),
        P(("groups", "blk"), None, None),
        P(("groups", "blk"), None),
        P(("groups", "blk")),
        P(("groups", "blk"), None),
        P(("groups", "blk")),
    )
    return jax.shard_map(
        local,
        mesh=mesh,
        in_specs=placed,
        out_specs=P(("groups", "blk"), None, None, None),
        check_vma=False,
    )
```

```python
import functools

import jax
import jax.numpy as jnp
from jax import lax
from jax.experimental import pallas as pl
from jax.experimental.pallas import tpu as pltpu
from jax.sharding import PartitionSpec as P

MIB = 1 << 20
GROUP = 2
LATE_GROUP = 4
LISTS = 7
BUDGET = 37
COST = (10, 7)
SMEM_SPEC = pl.BlockSpec(memory_space=pltpu.SMEM)
VMEM_SPEC = pl.BlockSpec(memory_space=pltpu.VMEM)
ANY_SPEC = pl.BlockSpec(memory_space=pl.ANY)


class Geometry:
    def __init__(self, rows, band, batches, slots):
        self.rows, self.band, self.batches, self.slots = rows, band, batches, slots
        self.half = half = (band - 1) // 2
        self.reach = reach = half // 2
        self.own = rows * band
        low = [(-m, reach + m, band) for m in range(reach, 0, -1)]
        high = [(rows + m, 0, 3 * reach - m) for m in range(reach)]
        self.halo = sum(stop - start for _, start, stop in low)
        low_cut = [half - row for row, _, _ in low]
        high_cut = [rows - row + half for row, _, _ in high]
        early = (
            [(row, cut, stop) for (row, _, stop), cut in zip(low, low_cut)],
            [(row, start, cut) for (row, start, _), cut in zip(high, high_cut)],
        )
        late = (
            [(row, start, cut) for (row, start, _), cut in zip(low, low_cut)],
            [(row, cut, stop) for (row, _, stop), cut in zip(high, high_cut)],
        )
        self.early = sum(stop - start for _, start, stop in early[0])
        self.late = self.halo - self.early
        self.first_at = self.own
        self.early_at = self.own + self.halo
        self.spare = self.early_at + self.early
        cut = (self.halo + 1) // 2
        self.pieces = ((0, cut), (cut, self.halo - cut))
        self.halo_base = self.bases((low, high))
        self.early_base = self.bases(early)
        shifts = (rows, -rows)
        self.packs = [self.places(*pair) for pair in zip((low, high), shifts)]
        self.early_packs = [self.places(*pair) for pair in zip(early, shifts)]
        self.late_packs = [self.places(*pair) for pair in zip(late, shifts)]
        self.span = min(2 * reach, rows) * band
        self.quiet = [
            self.others(self.packs[1], 0, self.span),
            self.others(self.packs[0], self.own - self.span, self.own),
        ]
        self.list_size = batches + 2
        self.lengths_at = LISTS * self.list_size
        self.local_at = self.lengths_at + LISTS
        self.count_at = self.local_at + batches
        self.offsets_at = self.count_at + batches
        self.odd_at = self.offsets_at + slots * batches
        self.meta_size = self.odd_at + 1

    def bases(self, sides):
        found = {}
        for segments in sides:
            place = 0
            for row, start, stop in segments:
                found[row] = place - start
                place += stop - start
        return found

    def places(self, segments, shift):
        pack, place = ([], 0)
        for row, start, stop in segments:
            pack.append(((row + shift) * self.band + start, place, stop - start))
            place += stop - start
        return pack

    def others(self, pack, begin, end):
        touched = set()
        for start, _, count in pack:
            touched.update(range(start, start + count))
        runs = []
        for index in range(begin, end):
            if index in touched:
                continue
            if runs and sum(runs[-1]) == index:
                runs[-1] = (runs[-1][0], runs[-1][1] + 1)
            else:
                runs.append((index, 1))
        return runs

    def near_packs(self, piece):
        begin, count = self.pieces[piece]
        found = []
        for pack in self.packs:
            part = []
            for start, place, size in pack:
                low, high = max(place, begin), min(place + size, begin + count)
                if low < high:
                    part.append((start + low - place, low - begin, high - low))
            found.append(part)
        return found

    def pick(self, bases, shift, row, otherwise):
        value = otherwise
        for at, base in bases.items():
            value = jnp.where(row == at, base + shift, value)
        return value


def run_copies(copies):
    for copy in copies:
        copy.start()
    for copy in copies:
        copy.wait()


def by_parity(odd, body, first, second):
    @pl.when(jnp.logical_not(odd))
    def _():
        body(first, second)

    @pl.when(odd)
    def _():
        body(second, first)


CROSS_MANY, CROSS_FEW, NEAR_MANY, NEAR_FEW, INNER_MANY, INNER_FEW, CROSS = range(LISTS)


def build_lists(geo, index, centre_ref, offsets_ref, counts_ref, meta_ref):
    first = index * geo.rows
    odd = index % 2 == 1
    meta_ref[geo.odd_at] = odd.astype(jnp.int32)
    lengths = [jnp.int32(0)] * LISTS
    for b in range(geo.batches):
        local = centre_ref[b] - first
        count = counts_ref[b]
        meta_ref[geo.local_at + b] = local
        meta_ref[geo.count_at + b] = count
        low = high = jnp.bool_(False)
        for k in range(geo.slots):
            offset = offsets_ref[k, b]
            meta_ref[geo.offsets_at + k * geo.batches + b] = offset
            row = local + offset
            low = low | ((k < count) & (row < 0))
            high = high | ((k < count) & (row >= geo.rows))
        cross = (odd & high) | (jnp.logical_not(odd) & low)
        near = (odd & low) | (jnp.logical_not(odd) & high)
        inner = jnp.logical_not(low | high)
        many = count > 2
        few = (count > 0) & jnp.logical_not(many)
        kinds = [kind & size for kind in (cross, near, inner) for size in (many, few)]
        for which, member in enumerate(kinds + [cross]):
            meta_ref[which * geo.list_size + lengths[which]] = b
            lengths[which] = lengths[which] + member.astype(jnp.int32)
    for which in range(LISTS):
        meta_ref[which * geo.list_size + lengths[which]] = geo.batches
        meta_ref[geo.lengths_at + which] = lengths[which]


def zone(geo, odd, cross):
    span = geo.span if cross else geo.own - geo.span
    return pl.ds(jnp.where(odd == cross, geo.own - span, 0), span)


def pack_kernel(geo, density_ref, cross_ref, sems):
    odd = lax.axis_index("blk") % 2 == 1

    def fill(up, down):
        pack = geo.packs[0 if up else 1]
        run_copies(
            [
                pltpu.make_async_copy(
                    density_ref.at[pl.ds(start, count)], cross_ref.at[pl.ds(place, count)], sems.at[i]
                )
                for i, (start, place, count) in enumerate(pack)
            ]
        )

    by_parity(odd, fill, False, True)


def setup_kernel(
    geo, cross_ref, density_ref, centre_in, offsets_in, counts_in,
    near_a, near_b, meta_ref, acc_ref,
    centre_ref, offsets_ref, counts_ref, sems,
):
    index = lax.axis_index("blk")
    odd = index % 2 == 1
    scalars = [
        pltpu.make_async_copy(*pair, sems.at[0, i])
        for i, pair in enumerate(
            ((centre_in, centre_ref), (offsets_in, offsets_ref), (counts_in, counts_ref))
        )
    ]
    for copy in scalars:
        copy.start()

    def each_copy(act):
        def go(up, down):
            near, number = (0 if up else 1), 0
            for piece, ref in enumerate((near_a, near_b)):
                for start, place, count in geo.near_packs(piece)[near]:
                    act(
                        pltpu.make_async_copy(
                            density_ref.at[pl.ds(start, count)],
                            ref.at[pl.ds(place, count)],
                            sems.at[1, number],
                        )
                    )
                    number += 1

        by_parity(odd, go, True, False)

    each_copy(lambda copy: copy.start())
    for where in (zone(geo, odd, False), pl.ds(geo.first_at, geo.halo)):
        acc_ref[where] = jnp.zeros_like(acc_ref[where])
    for copy in scalars:
        copy.wait()
    build_lists(geo, index, centre_ref, offsets_ref, counts_ref, meta_ref)
    each_copy(lambda copy: copy.wait())


def group_count(geo, meta_ref, which):
    return (meta_ref[geo.lengths_at + which] + GROUP - 1) // GROUP


def inner_share(geo, meta_ref):
    room = BUDGET
    for which in (CROSS_MANY, CROSS_FEW):
        room = room - COST[which % 2] * group_count(geo, meta_ref, which)
    share = []
    for which in (INNER_MANY, INNER_FEW):
        cost = COST[which % 2]
        taken = jnp.minimum(jnp.maximum(room, 0) // cost, group_count(geo, meta_ref, which))
        room = room - cost * taken
        share.append(taken)
    return share


def each_group(geo, meta_ref, which, body, size=GROUP, begin=0, end=None):
    length = meta_ref[geo.lengths_at + which]

    def step(i, carry):
        chosen = []
        for n in range(size):
            place = i * size + n
            there = place < length
            b = meta_ref[which * geo.list_size + jnp.minimum(place, length)]
            chosen.append((jnp.where(there, b, 0), there))
        body(chosen)
        return carry

    lax.fori_loop(begin, (length + size - 1) // size if end is None else end, step, 0)


class Slots:
    def __init__(self, geo, meta_ref, b, there, width):
        local = meta_ref[geo.local_at + b]
        count = jnp.where(there, meta_ref[geo.count_at + b], 0)
        self.offset = [meta_ref[geo.offsets_at + k * geo.batches + b] for k in range(width)]
        self.local = local
        self.row = [local + offset for offset in self.offset]
        self.live = [k < count for k in range(width)]
        self.own = [(row >= 0) & (row < geo.rows) for row in self.row]
        self.width = width


def panels(slots, ao_ref, b):
    return jnp.concatenate(
        [
            ao_ref[b, k] * jnp.where(slots.live[k], 1.0, 0.0).astype(ao_ref.dtype)
            for k in range(slots.width)
        ],
        axis=0,
    )


def gathered(tiles_ref, places):
    return jnp.concatenate(
        [jnp.concatenate([tiles_ref[place] for place in row], axis=1) for row in places], axis=0
    )


def potentials(xs, tiles, batches, kernel_ref):
    fs = [
        jnp.dot(t, x, preferred_element_type=jnp.float32).astype(jnp.bfloat16)
        for t, x in zip(tiles, xs)
    ]
    return [
        jnp.dot(f, kernel_ref[b], preferred_element_type=jnp.float32) for f, b in zip(fs, batches)
    ]


def outer_product(x, h):
    return lax.dot_general(x, h, (((1,), (1,)), ((), ())), preferred_element_type=jnp.float32)


def chain(xs, tiles, batches, kernel_ref, weights_ref):
    gs = potentials(xs, tiles, batches, kernel_ref)
    hs = [(g * weights_ref[pl.ds(b, 1), :]).astype(jnp.bfloat16) for g, b in zip(gs, batches)]
    return [outer_product(x, h) for x, h in zip(xs, hs)]


def scatter(part, target, nb, acc_ref):
    for k, row in enumerate(target):
        for j, place in enumerate(row):
            acc_ref[place] += part[k * nb : (k + 1) * nb, j * nb : (j + 1) * nb]


def add_whole(
    geo, chosen, width, meta_ref, tiles_ref, ao_ref, kernel_ref, weights_ref, acc_ref, halo_ref=None
):
    xs, tiles, targets = ([], [], [])
    for b, there in chosen:
        slots = Slots(geo, meta_ref, b, there, width)
        xs.append(panels(slots, ao_ref, b))
        rows, target = ([], [])
        for k in range(width):
            band = [slots.offset[j] - slots.offset[k] + geo.half for j in range(width)]
            own = slots.own[k]
            base = jnp.where(slots.live[k] & own, slots.row[k], 0) * geo.band
            row = jnp.concatenate([tiles_ref[base + o] for o in band], axis=1)
            if halo_ref is not None:
                away = slots.live[k] & jnp.logical_not(own)
                outside = jnp.where(away, geo.pick(geo.halo_base, 0, slots.row[k], 0), 0)
                other = [halo_ref[jnp.where(away, outside + o, 0)] for o in band]
                row = jnp.where(away, jnp.concatenate(other, axis=1), row)
                base = jnp.where(away, outside + geo.first_at, base)
            rows.append(row)
            target.append(
                [
                    jnp.where(slots.live[k] & slots.live[j], base + band[j], geo.spare)
                    for j in range(width)
                ]
            )
        tiles.append(jnp.concatenate(rows, axis=0))
        targets.append(target)
    parts = chain(xs, tiles, [b for b, _ in chosen], kernel_ref, weights_ref)
    for part, target in zip(parts, targets):
        scatter(part, target, ao_ref.shape[2], acc_ref)


def add_own(geo, chosen, width, meta_ref, tiles_ref, ao_ref, kernel_ref, weights_ref, acc_ref):
    xs, tiles, targets = ([], [], [])
    for b, there in chosen:
        slots = Slots(geo, meta_ref, b, there, width)
        xs.append(panels(slots, ao_ref, b))
        places, target = ([], [])
        for k in range(width):
            row = slots.row[k]
            band = [slots.offset[j] - slots.offset[k] + geo.half for j in range(width)]
            base = jnp.where(slots.own[k], row, 0) * geo.band
            places.append([base + o for o in band])
            base = geo.pick(geo.early_base, geo.early_at, row, base)
            target.append(
                [
                    jnp.where(
                        slots.live[k] & slots.live[j] & slots.own[j], base + band[j], geo.spare
                    )
                    for j in range(width)
                ]
            )
        tiles.append(gathered(tiles_ref, places))
        targets.append(target)
    parts = chain(xs, tiles, [b for b, _ in chosen], kernel_ref, weights_ref)
    for part, target in zip(parts, targets):
        scatter(part, target, ao_ref.shape[2], acc_ref)


def halo_rows(geo, meta_ref, slots):
    odd = meta_ref[geo.odd_at] == 1
    rows, places, present = ([], [], [])
    for i in range(geo.reach):
        row = jnp.where(odd, geo.rows + i, i - geo.reach)
        place, found = (jnp.int32(0), jnp.bool_(False))
        for k in range(slots.width):
            hit = slots.live[k] & (slots.row[k] == row)
            place = jnp.where(hit, k, place)
            found = found | hit
        rows.append(row)
        places.append(place)
        present.append(found)
    return rows, places, present


def add_corner(geo, chosen, meta_ref, halo_ref, ao_ref, kernel_ref, weights_ref, h_ref, total_ref):
    nb = ao_ref.shape[2]
    factor = lambda flag: jnp.where(flag, 1.0, 0.0)
    xs, sides, tiles, masks = ([], [], [], [])
    for b, there in chosen:
        slots = Slots(geo, meta_ref, b, there, geo.slots)
        rows, places, present = halo_rows(geo, meta_ref, slots)
        xs.append(panels(slots, ao_ref, b))
        sides.append(
            jnp.concatenate(
                [
                    ao_ref[b, place] * factor(found).astype(ao_ref.dtype)
                    for place, found in zip(places, present)
                ],
                axis=0,
            )
        )
        picked = []
        for row, found in zip(rows, present):
            base = geo.pick(geo.halo_base, 0, row, 0) - row + geo.half
            picked.append([jnp.where(found, base + column, 0) for column in slots.row])
        tiles.append(gathered(halo_ref, picked))
        masks.append([factor(found) for found in present])
    gs = potentials(xs, tiles, [b for b, _ in chosen], kernel_ref)
    hs = []
    for g, mask, (b, there) in zip(gs, masks, chosen):
        weights = weights_ref[pl.ds(b, 1), :]
        h = jnp.concatenate(
            [g[i * nb : (i + 1) * nb] * (weights * mask[i]) for i in range(geo.reach)], axis=0
        ).astype(jnp.bfloat16)
        h_ref[jnp.where(there, b, geo.batches)] = h
        hs.append(h)
    total_ref[...] += outer_product(
        jnp.concatenate(sides, axis=1), jnp.concatenate(hs, axis=1)
    )


def add_columns(geo, chosen, width, meta_ref, ao_ref, h_ref, acc_ref):
    parts, targets = ([], [])
    for b, there in chosen:
        slots = Slots(geo, meta_ref, b, there, width)
        rows, _, present = halo_rows(geo, meta_ref, slots)
        parts.append(outer_product(ao_ref[b, pl.ds(0, width)].reshape(-1, ao_ref.shape[3]), h_ref[b]))
        targets.append(
            [
                [
                    jnp.where(
                        slots.live[k] & slots.own[k] & found,
                        slots.row[k] * geo.band + row - slots.row[k] + geo.half,
                        geo.spare,
                    )
                    for row, found in zip(rows, present)
                ]
                for k in range(width)
            ]
        )
    for part, target in zip(parts, targets):
        scatter(part, target, ao_ref.shape[2], acc_ref)


def early_kernel(
    geo, meta_ref, tiles_ref, ao_ref, kernel_ref, weights_ref, acc_in, acc_ref, early_out
):
    odd = meta_ref[geo.odd_at] == 1
    for where in (zone(geo, odd, True), pl.ds(geo.early_at, geo.early), pl.ds(geo.spare, 1)):
        acc_ref[where] = jnp.zeros_like(acc_ref[where])
    refs = (meta_ref, tiles_ref, ao_ref, kernel_ref, weights_ref, acc_ref)
    for which, width in ((CROSS_MANY, geo.slots), (CROSS_FEW, 2)):
        each_group(
            geo, meta_ref, which, lambda chosen, width=width: add_own(geo, chosen, width, *refs)
        )
    early_out[...] = acc_ref[pl.ds(geo.early_at, geo.early)].astype(early_out.dtype)
    share = inner_share(geo, meta_ref)
    for which, width, end in ((INNER_MANY, geo.slots, share[0]), (INNER_FEW, 2, share[1])):
        each_group(
            geo,
            meta_ref,
            which,
            lambda chosen, width=width: add_whole(geo, chosen, width, *refs),
            end=end,
        )


def near_kernel(
    geo, meta_ref, halo_a, halo_b, tiles_ref, ao_ref, kernel_ref, weights_ref, acc_in,
    acc_ref, out_a, out_b, halo_ref,
):
    for ref, (start, count) in zip((halo_a, halo_b), geo.pieces):
        halo_ref[pl.ds(start, count)] = ref[...]
    refs = (meta_ref, tiles_ref, ao_ref, kernel_ref, weights_ref, acc_ref, halo_ref)
    for which, width in ((NEAR_MANY, geo.slots), (NEAR_FEW, 2)):
        each_group(
            geo, meta_ref, which, lambda chosen, width=width: add_whole(geo, chosen, width, *refs)
        )
    for out, (start, count) in zip((out_a, out_b), geo.pieces):
        out[...] = acc_ref[pl.ds(geo.first_at + start, count)].astype(out.dtype)


def late_kernel(
    geo, meta_ref, halo_ref, ao_ref, kernel_ref, weights_ref, h_ref, late_out, total_ref
):
    nb = ao_ref.shape[2]
    total_ref[...] = jnp.zeros_like(total_ref)

    def work(chosen):
        add_corner(
            geo, chosen, meta_ref, halo_ref, ao_ref, kernel_ref, weights_ref, h_ref, total_ref
        )

    groups = (meta_ref[geo.lengths_at + CROSS] + 1) // LATE_GROUP
    each_group(geo, meta_ref, CROSS, work, size=LATE_GROUP, end=groups)
    each_group(geo, meta_ref, CROSS, work, size=LATE_GROUP // 2, begin=2 * groups)
    for i in range(geo.reach):
        for j in range(geo.reach):
            late_out[i * geo.reach + j] = total_ref[
                i * nb : (i + 1) * nb, j * nb : (j + 1) * nb
            ].astype(late_out.dtype)


def inner_kernel(
    geo, meta_ref, first_a, first_b, tiles_ref, ao_ref, kernel_ref, weights_ref, h_ref, acc_in,
    acc_ref, out_ref, sems,
):
    odd = meta_ref[geo.odd_at] == 1
    refs = (meta_ref, tiles_ref, ao_ref, kernel_ref, weights_ref, acc_ref)
    share = inner_share(geo, meta_ref)
    for which, width, begin in ((INNER_MANY, geo.slots, share[0]), (INNER_FEW, 2, share[1])):
        each_group(
            geo,
            meta_ref,
            which,
            lambda chosen, width=width: add_whole(geo, chosen, width, *refs),
            begin=begin,
        )

    def add_near(up, down):
        for piece, ref in enumerate((first_a, first_b)):
            for start, place, count in geo.near_packs(piece)[0 if up else 1]:
                acc_ref[pl.ds(start, count)] += ref[pl.ds(place, count)].astype(jnp.float32)

    by_parity(odd, add_near, True, False)
    done = zone(geo, odd, False)
    copy = pltpu.make_async_copy(acc_ref.at[done], out_ref.at[done], sems.at[0])
    copy.start()
    for which, width in ((CROSS_MANY, geo.slots), (CROSS_FEW, 2)):
        each_group(
            geo,
            meta_ref,
            which,
            lambda chosen, width=width: add_columns(
                geo, chosen, width, meta_ref, ao_ref, h_ref, acc_ref
            ),
        )

    def write_quiet(up, down):
        run_copies(
            [
                pltpu.make_async_copy(
                    acc_ref.at[pl.ds(start, count)], out_ref.at[pl.ds(start, count)], sems.at[1 + i]
                )
                for i, (start, count) in enumerate(geo.quiet[0 if up else 1])
            ]
        )

    by_parity(odd, write_quiet, True, False)
    copy.wait()


def finish_kernel(geo, meta_ref, early_ref, late_ref, acc_ref, out_in, out_ref, total, sems):
    def add(up, down):
        copies = []
        for packs, ref in ((geo.early_packs, early_ref), (geo.late_packs, late_ref)):
            for start, place, count in packs[0 if up else 1]:
                spot = pl.ds(len(copies) * geo.band, count)
                total[spot] = acc_ref[pl.ds(start, count)] + ref[pl.ds(place, count)].astype(
                    jnp.float32
                )
                copy = pltpu.make_async_copy(
                    total.at[spot], out_ref.at[pl.ds(start, count)], sems.at[len(copies)]
                )
                copy.start()
                copies.append(copy)
        for copy in copies:
            copy.wait()

    by_parity(meta_ref[geo.odd_at] == 1, add, False, True)


def call(kernel, out_shape, in_specs, out_specs, scratch, aliases=None, cost=None):
    return pl.pallas_call(
        kernel,
        out_shape=out_shape,
        in_specs=in_specs,
        out_specs=out_specs,
        scratch_shapes=scratch,
        input_output_aliases=aliases or {},
        cost_estimate=cost,
        compiler_params=pltpu.CompilerParams(vmem_limit_bytes=16 * MIB),
    )


def to_first(x, size):
    pairs = [(i, i + 1) for i in range(0, size - 1, 2)]
    got = lax.ppermute(x, "blk", pairs + [(j, i) for i, j in pairs])
    return pltpu.with_memory_space_constraint(got, pltpu.VMEM)


def to_second(x, size):
    pairs = [(i, i + 1) for i in range(1, size - 1, 2)]
    got = lax.ppermute(x, "blk", pairs + [(j, i) for i, j in pairs])
    return pltpu.with_memory_space_constraint(got, pltpu.VMEM)


def local(density, ao_values, kernel, grid_weights, centre, sig_offsets, counts):
    rows, band, nb, _ = density.shape
    batches, slots, _, pts = ao_values.shape
    size = lax.axis_size("blk")
    geo = Geometry(rows, band, batches, slots)
    in_hbm = lambda x: pltpu.with_memory_space_constraint(x, pltpu.HBM)
    tiles = density.reshape(geo.own, nb, nb)
    pack = lambda count: pltpu.VMEM((count, nb, nb), jnp.bfloat16)
    dma = pltpu.SemaphoreType.DMA
    acc_type = pltpu.VMEM((geo.spare + 1, nb, nb), jnp.float32)

    hbm_tiles = in_hbm(tiles)
    cross = call(
        functools.partial(pack_kernel, geo),
        pack(geo.halo),
        [ANY_SPEC],
        VMEM_SPEC,
        [dma((geo.reach,))],
        cost=pl.CostEstimate(flops=10**10, bytes_accessed=10**8, transcendentals=0),
    )(hbm_tiles)
    cross_halo = to_second(cross, size)
    pieces = tuple(pack(count) for _, count in geo.pieces)
    *near_halo, meta, acc = call(
        functools.partial(setup_kernel, geo),
        pieces + (pltpu.SMEM((geo.meta_size,), jnp.int32), acc_type),
        [VMEM_SPEC] + [ANY_SPEC] * 4,
        (VMEM_SPEC,) * 2 + (SMEM_SPEC, VMEM_SPEC),
        [
            pltpu.SMEM((batches,), jnp.int32),
            pltpu.SMEM((slots, batches), jnp.int32),
            pltpu.SMEM((batches,), jnp.int32),
            dma((2, 2 * geo.reach + 1)),
        ],
    )(cross, hbm_tiles, in_hbm(centre), in_hbm(sig_offsets.T), in_hbm(counts))
    near_halo = [to_first(piece, size) for piece in near_halo]
    panel = (tiles, ao_values, kernel, grid_weights)
    acc, early = call(
        functools.partial(early_kernel, geo),
        (acc_type, pack(geo.early)),
        [SMEM_SPEC] + [VMEM_SPEC] * 5,
        (VMEM_SPEC,) * 2,
        [],
        {5: 0},
    )(meta, *panel, acc)
    early = to_second(early, size)

    acc, *first = call(
        functools.partial(near_kernel, geo),
        (acc_type,) + pieces,
        [SMEM_SPEC] + [VMEM_SPEC] * 7,
        (VMEM_SPEC,) * 3,
        [pack(geo.halo)],
        {7: 0},
    )(meta, *near_halo, *panel, acc)
    first = [to_first(piece, size) for piece in first]

    h_type = pltpu.VMEM((batches + 1, geo.reach * nb, pts), jnp.bfloat16)
    h, late = call(
        functools.partial(late_kernel, geo),
        (h_type, pack(geo.late)),
        [SMEM_SPEC] + [VMEM_SPEC] * 4,
        (VMEM_SPEC,) * 2,
        [pltpu.VMEM((geo.reach * nb, geo.reach * nb), jnp.float32)],
    )(meta, cross_halo, *panel[1:])
    late = to_second(late, size)

    whole = jax.ShapeDtypeStruct((geo.own, nb, nb), jnp.float32)
    acc, out = call(
        functools.partial(inner_kernel, geo),
        (acc_type, whole),
        [SMEM_SPEC] + [VMEM_SPEC] * 8,
        (VMEM_SPEC, ANY_SPEC),
        [dma((1 + max(len(runs) for runs in geo.quiet),))],
        {8: 0},
    )(meta, *first, *panel, h, acc)

    parts = 2 * geo.reach
    out = call(
        functools.partial(finish_kernel, geo),
        whole,
        [SMEM_SPEC] + [VMEM_SPEC] * 3 + [ANY_SPEC],
        ANY_SPEC,
        [pltpu.VMEM((parts * band, nb, nb), jnp.float32), dma((parts,))],
        {4: 0},
    )(meta, early, late, acc, out)
    return out.reshape(rows, band, nb, nb)


def solution(mesh):
    placed = (
        P(("groups", "blk"), None, None, None),
        P(("groups", "blk"), None, None, None),
        P(("groups", "blk"), None, None),
        P(("groups", "blk"), None),
        P(("groups", "blk")),
        P(("groups", "blk"), None),
        P(("groups", "blk")),
    )
    return jax.shard_map(
        local,
        mesh=mesh,
        in_specs=placed,
        out_specs=P(("groups", "blk"), None, None, None),
        check_vma=False,
    )
```

```python
import functools

import jax
import jax.numpy as jnp
from jax import lax
from jax.experimental import pallas as pl
from jax.experimental.pallas import tpu as pltpu
from jax.sharding import PartitionSpec as P

MIB = 1 << 20
GROUP = 2
LATE_GROUP = 4
PIECE = 2
LISTS = 7
BUDGET = 43
COST = (10, 7)
SMEM_SPEC = pl.BlockSpec(memory_space=pltpu.SMEM)
VMEM_SPEC = pl.BlockSpec(memory_space=pltpu.VMEM)
ANY_SPEC = pl.BlockSpec(memory_space=pl.ANY)


class Geometry:
    def __init__(self, rows, band, batches, slots):
        self.rows, self.band, self.batches, self.slots = rows, band, batches, slots
        self.half = half = (band - 1) // 2
        self.reach = reach = half // 2
        self.own = rows * band
        low = [(-m, reach + m, band) for m in range(reach, 0, -1)]
        high = [(rows + m, 0, 3 * reach - m) for m in range(reach)]
        self.halo = sum(stop - start for _, start, stop in low)
        low_cut = [half - row for row, _, _ in low]
        high_cut = [rows - row + half for row, _, _ in high]
        early = (
            [(row, cut, stop) for (row, _, stop), cut in zip(low, low_cut)],
            [(row, start, cut) for (row, start, _), cut in zip(high, high_cut)],
        )
        late = (
            [(row, start, cut) for (row, start, _), cut in zip(low, low_cut)],
            [(row, cut, stop) for (row, _, stop), cut in zip(high, high_cut)],
        )
        self.early = sum(stop - start for _, start, stop in early[0])
        self.late = self.halo - self.early
        self.first_at = self.own
        self.early_at = self.own + self.halo
        self.spare = self.early_at + self.early
        self.halo_base = self.bases((low, high))
        self.early_base = self.bases(early)
        shifts = (rows, -rows)
        self.packs = [self.places(*pair) for pair in zip((low, high), shifts)]
        self.early_packs = [self.places(*pair) for pair in zip(early, shifts)]
        self.late_packs = [self.places(*pair) for pair in zip(late, shifts)]
        self.span = min(2 * reach, rows) * band
        self.quiet = [
            self.others(self.packs[1], 0, self.span),
            self.others(self.packs[0], self.own - self.span, self.own),
        ]
        self.list_size = batches + 2
        self.lengths_at = (LISTS + 1) * self.list_size
        self.odd_at = self.lengths_at + LISTS + 1
        self.origin_at = self.odd_at + 1
        self.meta_size = self.origin_at + 1

    def bases(self, sides):
        found = {}
        for segments in sides:
            place = 0
            for row, start, stop in segments:
                found[row] = place - start
                place += stop - start
        return found

    def places(self, segments, shift):
        pack, place = ([], 0)
        for row, start, stop in segments:
            pack.append(((row + shift) * self.band + start, place, stop - start))
            place += stop - start
        return pack

    def others(self, pack, begin, end):
        touched = set()
        for start, _, count in pack:
            touched.update(range(start, start + count))
        runs = []
        for index in range(begin, end):
            if index in touched:
                continue
            if runs and sum(runs[-1]) == index:
                runs[-1] = (runs[-1][0], runs[-1][1] + 1)
            else:
                runs.append((index, 1))
        return runs

    def pick(self, bases, shift, row, otherwise):
        value = otherwise
        for at, base in bases.items():
            value = jnp.where(row == at, base + shift, value)
        return value


def run_copies(copies):
    for copy in copies:
        copy.start()
    for copy in copies:
        copy.wait()


def by_parity(odd, body, first, second):
    @pl.when(jnp.logical_not(odd))
    def _():
        body(first, second)

    @pl.when(odd)
    def _():
        body(second, first)


CROSS_MANY, CROSS_FEW, NEAR_MANY, NEAR_FEW, INNER_MANY, INNER_FEW, CROSS = range(LISTS)


class Info:
    def __init__(self, meta_ref, centre_ref, offsets_ref, counts_ref):
        self.meta, self.centre, self.offsets, self.counts = meta_ref, centre_ref, offsets_ref, counts_ref


def build_lists(geo, index, info):
    meta = info.meta
    first = index * geo.rows
    odd = index % 2
    meta[geo.odd_at] = odd
    meta[geo.origin_at] = first
    for which in range(LISTS + 1):
        meta[geo.lengths_at + which] = 0
    crossing = jnp.int32(0)
    for b in range(geo.batches):
        local = info.centre[b] - first
        count = info.counts[b]
        lowest = highest = local
        for k in range(geo.slots):
            row = jnp.where(k < count, local + info.offsets[k, b], local)
            lowest = jnp.minimum(lowest, row)
            highest = jnp.maximum(highest, row)
        low, high = lowest < 0, highest >= geo.rows
        edge = low | high
        cross = edge & (high == (odd == 1))
        kind = jnp.where(edge, jnp.where(cross, CROSS_MANY, NEAR_MANY), INNER_MANY)
        which = jnp.where(count > 0, kind + (count <= 2).astype(jnp.int32), LISTS)
        length = meta[geo.lengths_at + which]
        meta[which * geo.list_size + length] = b
        meta[geo.lengths_at + which] = length + 1
        meta[CROSS * geo.list_size + crossing] = b
        crossing = crossing + cross.astype(jnp.int32)
    meta[geo.lengths_at + CROSS] = crossing


def zone(geo, odd, cross):
    span = geo.span if cross else geo.own - geo.span
    return pl.ds(jnp.where(odd == cross, geo.own - span, 0), span)


def pack_kernel(
    geo, density_ref, centre_in, offsets_in, counts_in,
    near_ref, cross_ref, meta_ref, centre_ref, offsets_ref, counts_ref, acc_ref, sems,
):
    index = lax.axis_index("blk")
    odd = index % 2 == 1

    def copies(up, down, near_first):
        found = []
        for side, (pack, ref) in enumerate(zip(geo.packs, (up, down))):
            number = 0
            for start, place, count in pack:
                for at in range(0, count, PIECE):
                    size = min(PIECE, count - at)
                    found.append(
                        pltpu.make_async_copy(
                            density_ref.at[pl.ds(start + at, size)],
                            ref.at[pl.ds(place + at, size)],
                            sems.at[side, number],
                        )
                    )
                    number += 1
        half = len(found) // 2
        return found[half:] + found[:half] if near_first else found

    def start(up, down):
        for copy in copies(up, down, up is near_ref):
            copy.start()

    scalars = [
        pltpu.make_async_copy(*pair, sems.at[2, i])
        for i, pair in enumerate(
            ((centre_in, centre_ref), (offsets_in, offsets_ref), (counts_in, counts_ref))
        )
    ]
    for copy in scalars:
        copy.start()
    by_parity(odd, start, near_ref, cross_ref)
    for copy in scalars:
        copy.wait()
    build_lists(geo, index, Info(meta_ref, centre_ref, offsets_ref, counts_ref))
    for where in (zone(geo, odd, False), pl.ds(geo.first_at, geo.halo)):
        acc_ref[where] = jnp.zeros_like(acc_ref[where])
    for copy in copies(near_ref, cross_ref, False):
        copy.wait()


def group_count(geo, info, which):
    return (info.meta[geo.lengths_at + which] + GROUP - 1) // GROUP


def inner_share(geo, info):
    room = BUDGET
    for which in (CROSS_MANY, CROSS_FEW, NEAR_MANY, NEAR_FEW):
        room = room - COST[which % 2] * group_count(geo, info, which)
    share = []
    for which in (INNER_MANY, INNER_FEW):
        cost = COST[which % 2]
        taken = jnp.minimum(jnp.maximum(room, 0) // cost, group_count(geo, info, which))
        room = room - cost * taken
        share.append(taken)
    return share


def each_group(geo, info, which, body, size=GROUP, begin=0, end=None):
    length = info.meta[geo.lengths_at + which]

    def step(i, carry):
        chosen = []
        for n in range(size):
            place = i * size + n
            there = place < length
            b = info.meta[which * geo.list_size + jnp.where(there, place, 0)]
            chosen.append((jnp.where(there, b, 0), there))
        body(chosen)
        return carry

    lax.fori_loop(begin, (length + size - 1) // size if end is None else end, step, 0)


class Slots:
    def __init__(self, geo, info, b, there, width):
        local = info.centre[b] - info.meta[geo.origin_at]
        count = jnp.where(there, info.counts[b], 0)
        self.offset = [info.offsets[k, b] for k in range(width)]
        self.local = local
        self.row = [local + offset for offset in self.offset]
        self.live = [k < count for k in range(width)]
        self.own = [(row >= 0) & (row < geo.rows) for row in self.row]
        self.width = width


def panels(slots, ao_ref, b):
    return jnp.concatenate(
        [
            ao_ref[b, k] * jnp.where(slots.live[k], 1.0, 0.0).astype(ao_ref.dtype)
            for k in range(slots.width)
        ],
        axis=0,
    )


def gathered(tiles_ref, places):
    return jnp.concatenate(
        [jnp.concatenate([tiles_ref[place] for place in row], axis=1) for row in places], axis=0
    )


def potentials(xs, tiles, batches, kernel_ref):
    fs = [
        jnp.dot(t, x, preferred_element_type=jnp.float32).astype(jnp.bfloat16)
        for t, x in zip(tiles, xs)
    ]
    return [
        jnp.dot(f, kernel_ref[b], preferred_element_type=jnp.float32) for f, b in zip(fs, batches)
    ]


def outer_product(x, h):
    return lax.dot_general(x, h, (((1,), (1,)), ((), ())), preferred_element_type=jnp.float32)


def chain(xs, tiles, batches, kernel_ref, weights_ref):
    gs = potentials(xs, tiles, batches, kernel_ref)
    hs = [(g * weights_ref[pl.ds(b, 1), :]).astype(jnp.bfloat16) for g, b in zip(gs, batches)]
    return [outer_product(x, h) for x, h in zip(xs, hs)]


def scatter(part, target, nb, acc_ref):
    for k, row in enumerate(target):
        for j, place in enumerate(row):
            acc_ref[place] += part[k * nb : (k + 1) * nb, j * nb : (j + 1) * nb]


def add_whole(
    geo, chosen, width, info, tiles_ref, ao_ref, kernel_ref, weights_ref, acc_ref, halo_ref=None
):
    xs, tiles, targets = ([], [], [])
    for b, there in chosen:
        slots = Slots(geo, info, b, there, width)
        xs.append(panels(slots, ao_ref, b))
        rows, target = ([], [])
        for k in range(width):
            band = [slots.offset[j] - slots.offset[k] + geo.half for j in range(width)]
            own = slots.own[k]
            base = jnp.where(slots.live[k] & own, slots.row[k], 0) * geo.band
            row = jnp.concatenate([tiles_ref[base + o] for o in band], axis=1)
            if halo_ref is not None:
                away = slots.live[k] & jnp.logical_not(own)
                outside = jnp.where(away, geo.pick(geo.halo_base, 0, slots.row[k], 0), 0)
                other = [halo_ref[jnp.where(away, outside + o, 0)] for o in band]
                row = jnp.where(away, jnp.concatenate(other, axis=1), row)
                base = jnp.where(away, outside + geo.first_at, base)
            rows.append(row)
            target.append(
                [
                    jnp.where(slots.live[k] & slots.live[j], base + band[j], geo.spare)
                    for j in range(width)
                ]
            )
        tiles.append(jnp.concatenate(rows, axis=0))
        targets.append(target)
    parts = chain(xs, tiles, [b for b, _ in chosen], kernel_ref, weights_ref)
    for part, target in zip(parts, targets):
        scatter(part, target, ao_ref.shape[2], acc_ref)


def add_own(geo, chosen, width, info, tiles_ref, ao_ref, kernel_ref, weights_ref, acc_ref):
    xs, tiles, targets = ([], [], [])
    for b, there in chosen:
        slots = Slots(geo, info, b, there, width)
        xs.append(panels(slots, ao_ref, b))
        places, target = ([], [])
        for k in range(width):
            row = slots.row[k]
            band = [slots.offset[j] - slots.offset[k] + geo.half for j in range(width)]
            base = jnp.where(slots.own[k], row, 0) * geo.band
            places.append([base + o for o in band])
            base = geo.pick(geo.early_base, geo.early_at, row, base)
            target.append(
                [
                    jnp.where(
                        slots.live[k] & slots.live[j] & slots.own[j], base + band[j], geo.spare
                    )
                    for j in range(width)
                ]
            )
        tiles.append(gathered(tiles_ref, places))
        targets.append(target)
    parts = chain(xs, tiles, [b for b, _ in chosen], kernel_ref, weights_ref)
    for part, target in zip(parts, targets):
        scatter(part, target, ao_ref.shape[2], acc_ref)


def halo_rows(geo, info, slots):
    odd = info.meta[geo.odd_at] == 1
    rows, places, present = ([], [], [])
    for i in range(geo.reach):
        row = jnp.where(odd, geo.rows + i, i - geo.reach)
        place, found = (jnp.int32(0), jnp.bool_(False))
        for k in range(slots.width):
            hit = slots.live[k] & (slots.row[k] == row)
            place = jnp.where(hit, k, place)
            found = found | hit
        rows.append(row)
        places.append(place)
        present.append(found)
    return rows, places, present


def add_corner(geo, chosen, info, halo_ref, ao_ref, kernel_ref, weights_ref, h_ref, total_ref):
    nb = ao_ref.shape[2]
    factor = lambda flag: jnp.where(flag, 1.0, 0.0)
    xs, sides, tiles, masks = ([], [], [], [])
    for b, there in chosen:
        slots = Slots(geo, info, b, there, geo.slots)
        rows, places, present = halo_rows(geo, info, slots)
        xs.append(panels(slots, ao_ref, b))
        sides.append(
            jnp.concatenate(
                [
                    ao_ref[b, place] * factor(found).astype(ao_ref.dtype)
                    for place, found in zip(places, present)
                ],
                axis=0,
            )
        )
        picked = []
        for row, found in zip(rows, present):
            base = geo.pick(geo.halo_base, 0, row, 0) - row + geo.half
            picked.append([jnp.where(found, base + column, 0) for column in slots.row])
        tiles.append(gathered(halo_ref, picked))
        masks.append([factor(found) for found in present])
    gs = potentials(xs, tiles, [b for b, _ in chosen], kernel_ref)
    hs = []
    for g, mask, (b, there) in zip(gs, masks, chosen):
        weights = weights_ref[pl.ds(b, 1), :]
        h = jnp.concatenate(
            [g[i * nb : (i + 1) * nb] * (weights * mask[i]) for i in range(geo.reach)], axis=0
        ).astype(jnp.bfloat16)
        h_ref[jnp.where(there, b, geo.batches)] = h
        hs.append(h)
    total_ref[...] += outer_product(
        jnp.concatenate(sides, axis=1), jnp.concatenate(hs, axis=1)
    )


def add_columns(geo, chosen, width, info, ao_ref, h_ref, acc_ref):
    parts, targets = ([], [])
    for b, there in chosen:
        slots = Slots(geo, info, b, there, width)
        rows, _, present = halo_rows(geo, info, slots)
        parts.append(outer_product(ao_ref[b, pl.ds(0, width)].reshape(-1, ao_ref.shape[3]), h_ref[b]))
        targets.append(
            [
                [
                    jnp.where(
                        slots.live[k] & slots.own[k] & found,
                        slots.row[k] * geo.band + row - slots.row[k] + geo.half,
                        geo.spare,
                    )
                    for row, found in zip(rows, present)
                ]
                for k in range(width)
            ]
        )
    for part, target in zip(parts, targets):
        scatter(part, target, ao_ref.shape[2], acc_ref)


def early_kernel(
    geo, meta_ref, centre_ref, offsets_ref, counts_ref, tiles_ref, ao_ref, kernel_ref, weights_ref,
    acc_in, acc_ref, early_out,
):
    info = Info(meta_ref, centre_ref, offsets_ref, counts_ref)
    odd = info.meta[geo.odd_at] == 1
    for where in (zone(geo, odd, True), pl.ds(geo.early_at, geo.early), pl.ds(geo.spare, 1)):
        acc_ref[where] = jnp.zeros_like(acc_ref[where])
    refs = (info, tiles_ref, ao_ref, kernel_ref, weights_ref, acc_ref)
    for which, width in ((CROSS_MANY, geo.slots), (CROSS_FEW, 2)):
        each_group(
            geo, info, which, lambda chosen, width=width: add_own(geo, chosen, width, *refs)
        )
    early_out[...] = acc_ref[pl.ds(geo.early_at, geo.early)].astype(early_out.dtype)


def near_kernel(
    geo, meta_ref, centre_ref, offsets_ref, counts_ref, halo_ref, tiles_ref, ao_ref, kernel_ref,
    weights_ref, acc_in, acc_ref, first_out,
):
    info = Info(meta_ref, centre_ref, offsets_ref, counts_ref)
    refs = (info, tiles_ref, ao_ref, kernel_ref, weights_ref, acc_ref, halo_ref)
    for which, width in ((NEAR_MANY, geo.slots), (NEAR_FEW, 2)):
        each_group(
            geo, info, which, lambda chosen, width=width: add_whole(geo, chosen, width, *refs)
        )
    first_out[...] = acc_ref[pl.ds(geo.first_at, geo.halo)].astype(first_out.dtype)
    share = inner_share(geo, info)
    for which, width, end in ((INNER_MANY, geo.slots, share[0]), (INNER_FEW, 2, share[1])):
        each_group(
            geo,
            info,
            which,
            lambda chosen, width=width: add_whole(geo, chosen, width, *refs[:-1]),
            end=end,
        )


def late_kernel(
    geo, meta_ref, centre_ref, offsets_ref, counts_ref, halo_ref, ao_ref, kernel_ref, weights_ref,
    h_ref, late_out, total_ref,
):
    info = Info(meta_ref, centre_ref, offsets_ref, counts_ref)
    nb = ao_ref.shape[2]
    total_ref[...] = jnp.zeros_like(total_ref)

    def work(chosen):
        add_corner(
            geo, chosen, info, halo_ref, ao_ref, kernel_ref, weights_ref, h_ref, total_ref
        )

    groups = (info.meta[geo.lengths_at + CROSS] + 1) // LATE_GROUP
    each_group(geo, info, CROSS, work, size=LATE_GROUP, end=groups)
    each_group(geo, info, CROSS, work, size=LATE_GROUP // 2, begin=2 * groups)
    for i in range(geo.reach):
        for j in range(geo.reach):
            late_out[i * geo.reach + j] = total_ref[
                i * nb : (i + 1) * nb, j * nb : (j + 1) * nb
            ].astype(late_out.dtype)


def inner_kernel(
    geo, meta_ref, centre_ref, offsets_ref, counts_ref, first_ref, tiles_ref, ao_ref, kernel_ref,
    weights_ref, h_ref, acc_in, acc_ref, out_ref, sems,
):
    info = Info(meta_ref, centre_ref, offsets_ref, counts_ref)
    odd = info.meta[geo.odd_at] == 1
    refs = (info, tiles_ref, ao_ref, kernel_ref, weights_ref, acc_ref)
    share = inner_share(geo, info)
    for which, width, begin in ((INNER_MANY, geo.slots, share[0]), (INNER_FEW, 2, share[1])):
        each_group(
            geo,
            info,
            which,
            lambda chosen, width=width: add_whole(geo, chosen, width, *refs),
            begin=begin,
        )

    def add_near(up, down):
        for start, place, count in geo.packs[0 if up else 1]:
            acc_ref[pl.ds(start, count)] += first_ref[pl.ds(place, count)].astype(jnp.float32)

    by_parity(odd, add_near, True, False)
    done = zone(geo, odd, False)
    copy = pltpu.make_async_copy(acc_ref.at[done], out_ref.at[done], sems.at[0])
    copy.start()
    for which, width in ((CROSS_MANY, geo.slots), (CROSS_FEW, 2)):
        each_group(
            geo,
            info,
            which,
            lambda chosen, width=width: add_columns(
                geo, chosen, width, info, ao_ref, h_ref, acc_ref
            ),
        )

    def write_quiet(up, down):
        run_copies(
            [
                pltpu.make_async_copy(
                    acc_ref.at[pl.ds(start, count)], out_ref.at[pl.ds(start, count)], sems.at[1 + i]
                )
                for i, (start, count) in enumerate(geo.quiet[0 if up else 1])
            ]
        )

    by_parity(odd, write_quiet, True, False)
    copy.wait()


def finish_kernel(geo, meta_ref, early_ref, late_ref, acc_ref, out_in, out_ref, total, sems):
    def add(up, down):
        copies = []
        for packs, ref in ((geo.early_packs, early_ref), (geo.late_packs, late_ref)):
            for start, place, count in packs[0 if up else 1]:
                spot = pl.ds(len(copies) * geo.band, count)
                total[spot] = acc_ref[pl.ds(start, count)] + ref[pl.ds(place, count)].astype(
                    jnp.float32
                )
                copy = pltpu.make_async_copy(
                    total.at[spot], out_ref.at[pl.ds(start, count)], sems.at[len(copies)]
                )
                copy.start()
                copies.append(copy)
        for copy in copies:
            copy.wait()

    by_parity(meta_ref[geo.odd_at] == 1, add, False, True)


def call(kernel, out_shape, in_specs, out_specs, scratch, aliases=None, cost=None):
    return pl.pallas_call(
        kernel,
        out_shape=out_shape,
        in_specs=in_specs,
        out_specs=out_specs,
        scratch_shapes=scratch,
        input_output_aliases=aliases or {},
        cost_estimate=cost,
        compiler_params=pltpu.CompilerParams(vmem_limit_bytes=16 * MIB),
    )


def to_first(x, size):
    pairs = [(i, i + 1) for i in range(0, size - 1, 2)]
    got = lax.ppermute(x, "blk", pairs + [(j, i) for i, j in pairs])
    return pltpu.with_memory_space_constraint(got, pltpu.VMEM)


def to_second(x, size):
    pairs = [(i, i + 1) for i in range(1, size - 1, 2)]
    got = lax.ppermute(x, "blk", pairs + [(j, i) for i, j in pairs])
    return pltpu.with_memory_space_constraint(got, pltpu.VMEM)


def local(density, ao_values, kernel, grid_weights, centre, sig_offsets, counts):
    rows, band, nb, _ = density.shape
    batches, slots, _, pts = ao_values.shape
    size = lax.axis_size("blk")
    geo = Geometry(rows, band, batches, slots)
    in_hbm = lambda x: pltpu.with_memory_space_constraint(x, pltpu.HBM)
    tiles = density.reshape(geo.own, nb, nb)
    pack = lambda count: pltpu.VMEM((count, nb, nb), jnp.bfloat16)
    dma = pltpu.SemaphoreType.DMA
    acc_type = pltpu.VMEM((geo.spare + 1, nb, nb), jnp.float32)

    smem = lambda *shape: pltpu.SMEM(shape, jnp.int32)
    near_halo, cross_halo, *info, acc = call(
        functools.partial(pack_kernel, geo),
        (pack(geo.halo),) * 2
        + (smem(geo.meta_size), smem(batches), smem(slots, batches), smem(batches), acc_type),
        [ANY_SPEC] * 4,
        (VMEM_SPEC,) * 2 + (SMEM_SPEC,) * 4 + (VMEM_SPEC,),
        [dma((3, max(geo.halo, 3)))],
        cost=pl.CostEstimate(flops=10**10, bytes_accessed=10**8, transcendentals=0),
    )(in_hbm(tiles), in_hbm(centre), in_hbm(sig_offsets.T), in_hbm(counts))
    cross_halo = to_second(cross_halo, size)
    near_halo = to_first(near_halo, size)

    panel = (tiles, ao_values, kernel, grid_weights)
    acc, early = call(
        functools.partial(early_kernel, geo),
        (acc_type, pack(geo.early)),
        [SMEM_SPEC] * 4 + [VMEM_SPEC] * 5,
        (VMEM_SPEC,) * 2,
        [],
        {8: 0},
    )(*info, *panel, acc)
    early = to_second(early, size)

    acc, first = call(
        functools.partial(near_kernel, geo),
        (acc_type, pack(geo.halo)),
        [SMEM_SPEC] * 4 + [VMEM_SPEC] * 6,
        (VMEM_SPEC,) * 2,
        [],
        {9: 0},
    )(*info, near_halo, *panel, acc)
    first = to_first(first, size)

    h_type = pltpu.VMEM((batches + 1, geo.reach * nb, pts), jnp.bfloat16)
    h, late = call(
        functools.partial(late_kernel, geo),
        (h_type, pack(geo.late)),
        [SMEM_SPEC] * 4 + [VMEM_SPEC] * 4,
        (VMEM_SPEC,) * 2,
        [pltpu.VMEM((geo.reach * nb, geo.reach * nb), jnp.float32)],
    )(*info, cross_halo, *panel[1:])
    late = to_second(late, size)

    whole = jax.ShapeDtypeStruct((geo.own, nb, nb), jnp.float32)
    acc, out = call(
        functools.partial(inner_kernel, geo),
        (acc_type, whole),
        [SMEM_SPEC] * 4 + [VMEM_SPEC] * 7,
        (VMEM_SPEC, ANY_SPEC),
        [dma((1 + max(len(runs) for runs in geo.quiet),))],
        {10: 0},
    )(*info, first, *panel, h, acc)

    parts = 2 * geo.reach
    out = call(
        functools.partial(finish_kernel, geo),
        whole,
        [SMEM_SPEC] + [VMEM_SPEC] * 3 + [ANY_SPEC],
        ANY_SPEC,
        [pltpu.VMEM((parts * band, nb, nb), jnp.float32), dma((parts,))],
        {4: 0},
    )(info[0], early, late, acc, out)
    return out.reshape(rows, band, nb, nb)


def solution(mesh):
    placed = (
        P(("groups", "blk"), None, None, None),
        P(("groups", "blk"), None, None, None),
        P(("groups", "blk"), None, None),
        P(("groups", "blk"), None),
        P(("groups", "blk")),
        P(("groups", "blk"), None),
        P(("groups", "blk")),
    )
    return jax.shard_map(
        local,
        mesh=mesh,
        in_specs=placed,
        out_specs=P(("groups", "blk"), None, None, None),
        check_vma=False,
    )
```

```python
import functools

import jax
import jax.numpy as jnp
from jax import lax
from jax.experimental import pallas as pl
from jax.experimental.pallas import tpu as pltpu
from jax.sharding import PartitionSpec as P

MIB = 1 << 20
GROUP = 2
LATE_GROUP = 4
LISTS = 7
BUDGET = 43
WAIT = 18
COST = (10, 7)
SMEM_SPEC = pl.BlockSpec(memory_space=pltpu.SMEM)
VMEM_SPEC = pl.BlockSpec(memory_space=pltpu.VMEM)
ANY_SPEC = pl.BlockSpec(memory_space=pl.ANY)


class Geometry:
    def __init__(self, rows, band, batches, slots):
        self.rows, self.band, self.batches, self.slots = rows, band, batches, slots
        self.half = half = (band - 1) // 2
        self.reach = reach = half // 2
        self.own = rows * band
        low = [(-m, reach + m, band) for m in range(reach, 0, -1)]
        high = [(rows + m, 0, 3 * reach - m) for m in range(reach)]
        self.halo = sum(stop - start for _, start, stop in low)
        low_cut = [half - row for row, _, _ in low]
        high_cut = [rows - row + half for row, _, _ in high]
        early = (
            [(row, cut, stop) for (row, _, stop), cut in zip(low, low_cut)],
            [(row, start, cut) for (row, start, _), cut in zip(high, high_cut)],
        )
        late = (
            [(row, start, cut) for (row, start, _), cut in zip(low, low_cut)],
            [(row, cut, stop) for (row, _, stop), cut in zip(high, high_cut)],
        )
        self.early = sum(stop - start for _, start, stop in early[0])
        self.late = self.halo - self.early
        self.first_at = self.own
        self.early_at = self.own + self.halo
        self.spare = self.early_at + self.early
        self.halo_base = self.bases((low, high))
        self.early_base = self.bases(early)
        shifts = (rows, -rows)
        self.packs = [self.places(*pair) for pair in zip((low, high), shifts)]
        self.early_packs = [self.places(*pair) for pair in zip(early, shifts)]
        self.late_packs = [self.places(*pair) for pair in zip(late, shifts)]
        self.span = min(2 * reach, rows) * band
        self.quiet = [
            self.others(self.packs[1], 0, self.span),
            self.others(self.packs[0], self.own - self.span, self.own),
        ]
        self.list_size = batches + 2
        self.lengths_at = LISTS * self.list_size
        self.local_at = self.lengths_at + LISTS
        self.count_at = self.local_at + batches
        self.offsets_at = self.count_at + batches
        self.odd_at = self.offsets_at + slots * batches
        self.meta_size = self.odd_at + 1

    def bases(self, sides):
        found = {}
        for segments in sides:
            place = 0
            for row, start, stop in segments:
                found[row] = place - start
                place += stop - start
        return found

    def places(self, segments, shift):
        pack, place = ([], 0)
        for row, start, stop in segments:
            pack.append(((row + shift) * self.band + start, place, stop - start))
            place += stop - start
        return pack

    def others(self, pack, begin, end):
        touched = set()
        for start, _, count in pack:
            touched.update(range(start, start + count))
        runs = []
        for index in range(begin, end):
            if index in touched:
                continue
            if runs and sum(runs[-1]) == index:
                runs[-1] = (runs[-1][0], runs[-1][1] + 1)
            else:
                runs.append((index, 1))
        return runs

    def pick(self, bases, shift, row, otherwise):
        value = otherwise
        for at, base in bases.items():
            value = jnp.where(row == at, base + shift, value)
        return value


def run_copies(copies):
    for copy in copies:
        copy.start()
    for copy in copies:
        copy.wait()


def by_parity(odd, body, first, second):
    @pl.when(jnp.logical_not(odd))
    def _():
        body(first, second)

    @pl.when(odd)
    def _():
        body(second, first)


CROSS_MANY, CROSS_FEW, NEAR_MANY, NEAR_FEW, INNER_MANY, INNER_FEW, CROSS = range(LISTS)


def build_lists(geo, index, centre_ref, offsets_ref, counts_ref, meta_ref):
    first = index * geo.rows
    odd = index % 2 == 1
    meta_ref[geo.odd_at] = odd.astype(jnp.int32)
    lengths = [jnp.int32(0)] * LISTS
    for b in range(geo.batches):
        local = centre_ref[b] - first
        count = counts_ref[b]
        meta_ref[geo.local_at + b] = local
        meta_ref[geo.count_at + b] = count
        low = high = jnp.bool_(False)
        for k in range(geo.slots):
            offset = offsets_ref[k, b]
            meta_ref[geo.offsets_at + k * geo.batches + b] = offset
            row = local + offset
            low = low | ((k < count) & (row < 0))
            high = high | ((k < count) & (row >= geo.rows))
        cross = (odd & high) | (jnp.logical_not(odd) & low)
        near = (odd & low) | (jnp.logical_not(odd) & high)
        inner = jnp.logical_not(low | high)
        many = count > 2
        few = (count > 0) & jnp.logical_not(many)
        kinds = [kind & size for kind in (cross, near, inner) for size in (many, few)]
        for which, member in enumerate(kinds + [cross]):
            meta_ref[which * geo.list_size + lengths[which]] = b
            lengths[which] = lengths[which] + member.astype(jnp.int32)
    for which in range(LISTS):
        meta_ref[which * geo.list_size + lengths[which]] = geo.batches
        meta_ref[geo.lengths_at + which] = lengths[which]


def zone(geo, odd, cross):
    span = geo.span if cross else geo.own - geo.span
    return pl.ds(jnp.where(odd == cross, geo.own - span, 0), span)


def pack_kernel(
    geo, density_ref, centre_in, offsets_in, counts_in,
    near_ref, cross_ref, meta_ref, acc_ref,
    centre_ref, offsets_ref, counts_ref, sems,
):
    index = lax.axis_index("blk")
    odd = index % 2 == 1

    def copies(up, down):
        return [
            pltpu.make_async_copy(
                density_ref.at[pl.ds(start, count)], ref.at[pl.ds(place, count)], sems.at[side, i]
            )
            for side, (pack, ref) in enumerate(zip(geo.packs, (up, down)))
            for i, (start, place, count) in enumerate(pack)
        ]

    def start(up, down):
        for copy in copies(up, down):
            copy.start()

    by_parity(odd, start, near_ref, cross_ref)
    scalars = [
        pltpu.make_async_copy(*pair, sems.at[2, i])
        for i, pair in enumerate(
            ((centre_in, centre_ref), (offsets_in, offsets_ref), (counts_in, counts_ref))
        )
    ]
    for copy in scalars:
        copy.start()
    for where in (zone(geo, odd, False), pl.ds(geo.first_at, geo.halo)):
        acc_ref[where] = jnp.zeros_like(acc_ref[where])
    for copy in scalars:
        copy.wait()
    build_lists(geo, index, centre_ref, offsets_ref, counts_ref, meta_ref)
    for copy in copies(near_ref, cross_ref):
        copy.wait()


def group_count(geo, meta_ref, which):
    return (meta_ref[geo.lengths_at + which] + GROUP - 1) // GROUP


def inner_share(geo, meta_ref):
    before = BUDGET
    for which in (CROSS_MANY, CROSS_FEW, NEAR_MANY, NEAR_FEW):
        before = before - COST[which % 2] * group_count(geo, meta_ref, which)
    waiting = jnp.where((lax.axis_index("blk") + 1) // 2 % 2 == 1, WAIT, 0)
    share = []
    for which in (INNER_MANY, INNER_FEW):
        cost, count = COST[which % 2], group_count(geo, meta_ref, which)
        first = jnp.minimum(jnp.maximum(before, 0) // cost, count)
        second = jnp.minimum(jnp.maximum(waiting, 0) // cost, count - first)
        before = before - cost * first
        waiting = waiting - cost * second
        share.append((0, first, first + second, count))
    return share


def inner_part(geo, meta_ref, stage, refs):
    for which, width, bounds in zip(
        (INNER_MANY, INNER_FEW), (geo.slots, 2), inner_share(geo, meta_ref)
    ):
        each_group(
            geo,
            meta_ref,
            which,
            lambda chosen, width=width: add_whole(geo, chosen, width, *refs),
            begin=bounds[stage],
            end=bounds[stage + 1],
        )


def each_group(geo, meta_ref, which, body, size=GROUP, begin=0, end=None):
    length = meta_ref[geo.lengths_at + which]

    def step(i, carry):
        chosen = []
        for n in range(size):
            place = i * size + n
            there = place < length
            b = meta_ref[which * geo.list_size + jnp.minimum(place, length)]
            chosen.append((jnp.where(there, b, 0), there))
        body(chosen)
        return carry

    lax.fori_loop(begin, (length + size - 1) // size if end is None else end, step, 0)


class Slots:
    def __init__(self, geo, meta_ref, b, there, width):
        local = meta_ref[geo.local_at + b]
        count = jnp.where(there, meta_ref[geo.count_at + b], 0)
        self.offset = [meta_ref[geo.offsets_at + k * geo.batches + b] for k in range(width)]
        self.local = local
        self.row = [local + offset for offset in self.offset]
        self.live = [k < count for k in range(width)]
        self.own = [(row >= 0) & (row < geo.rows) for row in self.row]
        self.width = width


def panels(slots, ao_ref, b):
    return jnp.concatenate(
        [
            ao_ref[b, k] * jnp.where(slots.live[k], 1.0, 0.0).astype(ao_ref.dtype)
            for k in range(slots.width)
        ],
        axis=0,
    )


def gathered(tiles_ref, places):
    return jnp.concatenate(
        [jnp.concatenate([tiles_ref[place] for place in row], axis=1) for row in places], axis=0
    )


def potentials(xs, tiles, batches, kernel_ref):
    fs = [
        jnp.dot(t, x, preferred_element_type=jnp.float32).astype(jnp.bfloat16)
        for t, x in zip(tiles, xs)
    ]
    return [
        jnp.dot(f, kernel_ref[b], preferred_element_type=jnp.float32) for f, b in zip(fs, batches)
    ]


def outer_product(x, h):
    return lax.dot_general(x, h, (((1,), (1,)), ((), ())), preferred_element_type=jnp.float32)


def chain(xs, tiles, batches, kernel_ref, weights_ref):
    gs = potentials(xs, tiles, batches, kernel_ref)
    hs = [(g * weights_ref[pl.ds(b, 1), :]).astype(jnp.bfloat16) for g, b in zip(gs, batches)]
    return [outer_product(x, h) for x, h in zip(xs, hs)]


def scatter(part, target, nb, acc_ref):
    for k, row in enumerate(target):
        for j, place in enumerate(row):
            acc_ref[place] += part[k * nb : (k + 1) * nb, j * nb : (j + 1) * nb]


def add_whole(
    geo, chosen, width, meta_ref, tiles_ref, ao_ref, kernel_ref, weights_ref, acc_ref, halo_ref=None
):
    xs, tiles, targets = ([], [], [])
    for b, there in chosen:
        slots = Slots(geo, meta_ref, b, there, width)
        xs.append(panels(slots, ao_ref, b))
        rows, target = ([], [])
        for k in range(width):
            band = [slots.offset[j] - slots.offset[k] + geo.half for j in range(width)]
            own = slots.own[k]
            base = jnp.where(slots.live[k] & own, slots.row[k], 0) * geo.band
            row = jnp.concatenate([tiles_ref[base + o] for o in band], axis=1)
            if halo_ref is not None:
                away = slots.live[k] & jnp.logical_not(own)
                outside = jnp.where(away, geo.pick(geo.halo_base, 0, slots.row[k], 0), 0)
                other = [halo_ref[jnp.where(away, outside + o, 0)] for o in band]
                row = jnp.where(away, jnp.concatenate(other, axis=1), row)
                base = jnp.where(away, outside + geo.first_at, base)
            rows.append(row)
            target.append(
                [
                    jnp.where(slots.live[k] & slots.live[j], base + band[j], geo.spare)
                    for j in range(width)
                ]
            )
        tiles.append(jnp.concatenate(rows, axis=0))
        targets.append(target)
    parts = chain(xs, tiles, [b for b, _ in chosen], kernel_ref, weights_ref)
    for part, target in zip(parts, targets):
        scatter(part, target, ao_ref.shape[2], acc_ref)


def add_own(geo, chosen, width, meta_ref, tiles_ref, ao_ref, kernel_ref, weights_ref, acc_ref):
    xs, tiles, targets = ([], [], [])
    for b, there in chosen:
        slots = Slots(geo, meta_ref, b, there, width)
        xs.append(panels(slots, ao_ref, b))
        places, target = ([], [])
        for k in range(width):
            row = slots.row[k]
            band = [slots.offset[j] - slots.offset[k] + geo.half for j in range(width)]
            base = jnp.where(slots.own[k], row, 0) * geo.band
            places.append([base + o for o in band])
            base = geo.pick(geo.early_base, geo.early_at, row, base)
            target.append(
                [
                    jnp.where(
                        slots.live[k] & slots.live[j] & slots.own[j], base + band[j], geo.spare
                    )
                    for j in range(width)
                ]
            )
        tiles.append(gathered(tiles_ref, places))
        targets.append(target)
    parts = chain(xs, tiles, [b for b, _ in chosen], kernel_ref, weights_ref)
    for part, target in zip(parts, targets):
        scatter(part, target, ao_ref.shape[2], acc_ref)


def halo_rows(geo, meta_ref, slots):
    odd = meta_ref[geo.odd_at] == 1
    rows, places, present = ([], [], [])
    for i in range(geo.reach):
        row = jnp.where(odd, geo.rows + i, i - geo.reach)
        place, found = (jnp.int32(0), jnp.bool_(False))
        for k in range(slots.width):
            hit = slots.live[k] & (slots.row[k] == row)
            place = jnp.where(hit, k, place)
            found = found | hit
        rows.append(row)
        places.append(place)
        present.append(found)
    return rows, places, present


def add_corner(geo, chosen, meta_ref, halo_ref, ao_ref, kernel_ref, weights_ref, h_ref, total_ref):
    nb = ao_ref.shape[2]
    factor = lambda flag: jnp.where(flag, 1.0, 0.0)
    xs, sides, tiles, masks = ([], [], [], [])
    for b, there in chosen:
        slots = Slots(geo, meta_ref, b, there, geo.slots)
        rows, places, present = halo_rows(geo, meta_ref, slots)
        xs.append(panels(slots, ao_ref, b))
        sides.append(
            jnp.concatenate(
                [
                    ao_ref[b, place] * factor(found).astype(ao_ref.dtype)
                    for place, found in zip(places, present)
                ],
                axis=0,
            )
        )
        picked = []
        for row, found in zip(rows, present):
            base = geo.pick(geo.halo_base, 0, row, 0) - row + geo.half
            picked.append([jnp.where(found, base + column, 0) for column in slots.row])
        tiles.append(gathered(halo_ref, picked))
        masks.append([factor(found) for found in present])
    gs = potentials(xs, tiles, [b for b, _ in chosen], kernel_ref)
    hs = []
    for g, mask, (b, there) in zip(gs, masks, chosen):
        weights = weights_ref[pl.ds(b, 1), :]
        h = jnp.concatenate(
            [g[i * nb : (i + 1) * nb] * (weights * mask[i]) for i in range(geo.reach)], axis=0
        ).astype(jnp.bfloat16)
        h_ref[jnp.where(there, b, geo.batches)] = h
        hs.append(h)
    total_ref[...] += outer_product(
        jnp.concatenate(sides, axis=1), jnp.concatenate(hs, axis=1)
    )


def add_columns(geo, chosen, width, meta_ref, ao_ref, h_ref, acc_ref):
    parts, targets = ([], [])
    for b, there in chosen:
        slots = Slots(geo, meta_ref, b, there, width)
        rows, _, present = halo_rows(geo, meta_ref, slots)
        parts.append(outer_product(ao_ref[b, pl.ds(0, width)].reshape(-1, ao_ref.shape[3]), h_ref[b]))
        targets.append(
            [
                [
                    jnp.where(
                        slots.live[k] & slots.own[k] & found,
                        slots.row[k] * geo.band + row - slots.row[k] + geo.half,
                        geo.spare,
                    )
                    for row, found in zip(rows, present)
                ]
                for k in range(width)
            ]
        )
    for part, target in zip(parts, targets):
        scatter(part, target, ao_ref.shape[2], acc_ref)


def early_kernel(
    geo, meta_ref, tiles_ref, ao_ref, kernel_ref, weights_ref, acc_in, acc_ref, early_out
):
    odd = meta_ref[geo.odd_at] == 1
    for where in (zone(geo, odd, True), pl.ds(geo.early_at, geo.early), pl.ds(geo.spare, 1)):
        acc_ref[where] = jnp.zeros_like(acc_ref[where])
    refs = (meta_ref, tiles_ref, ao_ref, kernel_ref, weights_ref, acc_ref)
    for which, width in ((CROSS_MANY, geo.slots), (CROSS_FEW, 2)):
        each_group(
            geo, meta_ref, which, lambda chosen, width=width: add_own(geo, chosen, width, *refs)
        )
    early_out[...] = acc_ref[pl.ds(geo.early_at, geo.early)].astype(early_out.dtype)


def near_kernel(
    geo, meta_ref, halo_ref, tiles_ref, ao_ref, kernel_ref, weights_ref, acc_in, acc_ref, first_out
):
    refs = (meta_ref, tiles_ref, ao_ref, kernel_ref, weights_ref, acc_ref, halo_ref)
    for which, width in ((NEAR_MANY, geo.slots), (NEAR_FEW, 2)):
        each_group(
            geo, meta_ref, which, lambda chosen, width=width: add_whole(geo, chosen, width, *refs)
        )
    first_out[...] = acc_ref[pl.ds(geo.first_at, geo.halo)].astype(first_out.dtype)
    inner_part(geo, meta_ref, 0, refs[:-1])


def waiting_kernel(
    geo, meta_ref, tiles_ref, ao_ref, kernel_ref, weights_ref, acc_in, acc_ref, done_ref
):
    inner_part(geo, meta_ref, 1, (meta_ref, tiles_ref, ao_ref, kernel_ref, weights_ref, acc_ref))
    done_ref[0] = 1


def late_kernel(
    geo, meta_ref, done_ref, halo_ref, ao_ref, kernel_ref, weights_ref, h_ref, late_out, total_ref
):
    nb = ao_ref.shape[2]
    total_ref[...] = jnp.zeros_like(total_ref)

    def work(chosen):
        add_corner(
            geo, chosen, meta_ref, halo_ref, ao_ref, kernel_ref, weights_ref, h_ref, total_ref
        )

    groups = (meta_ref[geo.lengths_at + CROSS] + 1) // LATE_GROUP
    each_group(geo, meta_ref, CROSS, work, size=LATE_GROUP, end=groups)
    each_group(geo, meta_ref, CROSS, work, size=LATE_GROUP // 2, begin=2 * groups)
    for i in range(geo.reach):
        for j in range(geo.reach):
            late_out[i * geo.reach + j] = total_ref[
                i * nb : (i + 1) * nb, j * nb : (j + 1) * nb
            ].astype(late_out.dtype)


def inner_kernel(
    geo, meta_ref, first_ref, tiles_ref, ao_ref, kernel_ref, weights_ref, h_ref, acc_in,
    acc_ref, out_ref, sems,
):
    odd = meta_ref[geo.odd_at] == 1
    refs = (meta_ref, tiles_ref, ao_ref, kernel_ref, weights_ref, acc_ref)
    inner_part(geo, meta_ref, 2, refs)

    def add_near(up, down):
        for start, place, count in geo.packs[0 if up else 1]:
            acc_ref[pl.ds(start, count)] += first_ref[pl.ds(place, count)].astype(jnp.float32)

    by_parity(odd, add_near, True, False)
    done = zone(geo, odd, False)
    copy = pltpu.make_async_copy(acc_ref.at[done], out_ref.at[done], sems.at[0])
    copy.start()
    for which, width in ((CROSS_MANY, geo.slots), (CROSS_FEW, 2)):
        each_group(
            geo,
            meta_ref,
            which,
            lambda chosen, width=width: add_columns(
                geo, chosen, width, meta_ref, ao_ref, h_ref, acc_ref
            ),
        )

    def write_quiet(up, down):
        run_copies(
            [
                pltpu.make_async_copy(
                    acc_ref.at[pl.ds(start, count)], out_ref.at[pl.ds(start, count)], sems.at[1 + i]
                )
                for i, (start, count) in enumerate(geo.quiet[0 if up else 1])
            ]
        )

    by_parity(odd, write_quiet, True, False)
    copy.wait()


def finish_kernel(geo, meta_ref, early_ref, late_ref, acc_ref, out_in, out_ref, total, sems):
    def add(up, down):
        copies = []
        for packs, ref in ((geo.early_packs, early_ref), (geo.late_packs, late_ref)):
            for start, place, count in packs[0 if up else 1]:
                spot = pl.ds(len(copies) * geo.band, count)
                total[spot] = acc_ref[pl.ds(start, count)] + ref[pl.ds(place, count)].astype(
                    jnp.float32
                )
                copy = pltpu.make_async_copy(
                    total.at[spot], out_ref.at[pl.ds(start, count)], sems.at[len(copies)]
                )
                copy.start()
                copies.append(copy)
        for copy in copies:
            copy.wait()

    by_parity(meta_ref[geo.odd_at] == 1, add, False, True)


def call(kernel, out_shape, in_specs, out_specs, scratch, aliases=None, cost=None):
    return pl.pallas_call(
        kernel,
        out_shape=out_shape,
        in_specs=in_specs,
        out_specs=out_specs,
        scratch_shapes=scratch,
        input_output_aliases=aliases or {},
        cost_estimate=cost,
        compiler_params=pltpu.CompilerParams(vmem_limit_bytes=16 * MIB),
    )


def to_first(x, size):
    pairs = [(i, i + 1) for i in range(0, size - 1, 2)]
    got = lax.ppermute(x, "blk", pairs + [(j, i) for i, j in pairs])
    return pltpu.with_memory_space_constraint(got, pltpu.VMEM)


def to_second(x, size):
    pairs = [(i, i + 1) for i in range(1, size - 1, 2)]
    got = lax.ppermute(x, "blk", pairs + [(j, i) for i, j in pairs])
    return pltpu.with_memory_space_constraint(got, pltpu.VMEM)


def local(density, ao_values, kernel, grid_weights, centre, sig_offsets, counts):
    rows, band, nb, _ = density.shape
    batches, slots, _, pts = ao_values.shape
    size = lax.axis_size("blk")
    geo = Geometry(rows, band, batches, slots)
    in_hbm = lambda x: pltpu.with_memory_space_constraint(x, pltpu.HBM)
    tiles = density.reshape(geo.own, nb, nb)
    pack = lambda count: pltpu.VMEM((count, nb, nb), jnp.bfloat16)
    dma = pltpu.SemaphoreType.DMA
    acc_type = pltpu.VMEM((geo.spare + 1, nb, nb), jnp.float32)

    near_halo, cross_halo, meta, acc = call(
        functools.partial(pack_kernel, geo),
        (pack(geo.halo),) * 2 + (pltpu.SMEM((geo.meta_size,), jnp.int32), acc_type),
        [ANY_SPEC] * 4,
        (VMEM_SPEC,) * 2 + (SMEM_SPEC, VMEM_SPEC),
        [
            pltpu.SMEM((batches,), jnp.int32),
            pltpu.SMEM((slots, batches), jnp.int32),
            pltpu.SMEM((batches,), jnp.int32),
            dma((3, max(geo.reach, 3))),
        ],
        cost=pl.CostEstimate(flops=10**10, bytes_accessed=10**8, transcendentals=0),
    )(in_hbm(tiles), in_hbm(centre), in_hbm(sig_offsets.T), in_hbm(counts))
    cross_halo = to_second(cross_halo, size)
    near_halo = to_first(near_halo, size)

    panel = (tiles, ao_values, kernel, grid_weights)
    acc, early = call(
        functools.partial(early_kernel, geo),
        (acc_type, pack(geo.early)),
        [SMEM_SPEC] + [VMEM_SPEC] * 5,
        (VMEM_SPEC,) * 2,
        [],
        {5: 0},
    )(meta, *panel, acc)
    early = to_second(early, size)

    acc, first = call(
        functools.partial(near_kernel, geo),
        (acc_type, pack(geo.halo)),
        [SMEM_SPEC] + [VMEM_SPEC] * 6,
        (VMEM_SPEC,) * 2,
        [],
        {6: 0},
    )(meta, near_halo, *panel, acc)
    first = to_first(first, size)

    acc, done = call(
        functools.partial(waiting_kernel, geo),
        (acc_type, pltpu.SMEM((1,), jnp.int32)),
        [SMEM_SPEC] + [VMEM_SPEC] * 5,
        (VMEM_SPEC, SMEM_SPEC),
        [],
        {5: 0},
    )(meta, *panel, acc)

    h_type = pltpu.VMEM((batches + 1, geo.reach * nb, pts), jnp.bfloat16)
    h, late = call(
        functools.partial(late_kernel, geo),
        (h_type, pack(geo.late)),
        [SMEM_SPEC] * 2 + [VMEM_SPEC] * 4,
        (VMEM_SPEC,) * 2,
        [pltpu.VMEM((geo.reach * nb, geo.reach * nb), jnp.float32)],
    )(meta, done, cross_halo, *panel[1:])
    late = to_second(late, size)

    whole = jax.ShapeDtypeStruct((geo.own, nb, nb), jnp.float32)
    acc, out = call(
        functools.partial(inner_kernel, geo),
        (acc_type, whole),
        [SMEM_SPEC] + [VMEM_SPEC] * 7,
        (VMEM_SPEC, ANY_SPEC),
        [dma((1 + max(len(runs) for runs in geo.quiet),))],
        {7: 0},
    )(meta, first, *panel, h, acc)

    parts = 2 * geo.reach
    out = call(
        functools.partial(finish_kernel, geo),
        whole,
        [SMEM_SPEC] + [VMEM_SPEC] * 3 + [ANY_SPEC],
        ANY_SPEC,
        [pltpu.VMEM((parts * band, nb, nb), jnp.float32), dma((parts,))],
        {4: 0},
    )(meta, early, late, acc, out)
    return out.reshape(rows, band, nb, nb)


def solution(mesh):
    placed = (
        P(("groups", "blk"), None, None, None),
        P(("groups", "blk"), None, None, None),
        P(("groups", "blk"), None, None),
        P(("groups", "blk"), None),
        P(("groups", "blk")),
        P(("groups", "blk"), None),
        P(("groups", "blk")),
    )
    return jax.shard_map(
        local,
        mesh=mesh,
        in_specs=placed,
        out_specs=P(("groups", "blk"), None, None, None),
        check_vma=False,
    )
```

```python
import functools

import jax
import jax.numpy as jnp
from jax import lax
from jax.experimental import pallas as pl
from jax.experimental.pallas import tpu as pltpu
from jax.sharding import PartitionSpec as P

MIB = 1 << 20
GROUP = 2
LATE_GROUP = 4
LISTS = 7
BUDGET = 43
WAIT = 18
COST = (10, 7)
SMEM_SPEC = pl.BlockSpec(memory_space=pltpu.SMEM)
VMEM_SPEC = pl.BlockSpec(memory_space=pltpu.VMEM)
ANY_SPEC = pl.BlockSpec(memory_space=pl.ANY)


class Geometry:
    def __init__(self, rows, band, batches, slots):
        self.rows, self.band, self.batches, self.slots = rows, band, batches, slots
        self.half = half = (band - 1) // 2
        self.reach = reach = half // 2
        self.own = rows * band
        low = [(-m, reach + m, band) for m in range(reach, 0, -1)]
        high = [(rows + m, 0, 3 * reach - m) for m in range(reach)]
        self.halo = sum(stop - start for _, start, stop in low)
        low_cut = [half - row for row, _, _ in low]
        high_cut = [rows - row + half for row, _, _ in high]
        early = (
            [(row, cut, stop) for (row, _, stop), cut in zip(low, low_cut)],
            [(row, start, cut) for (row, start, _), cut in zip(high, high_cut)],
        )
        late = (
            [(row, start, cut) for (row, start, _), cut in zip(low, low_cut)],
            [(row, cut, stop) for (row, _, stop), cut in zip(high, high_cut)],
        )
        self.early = sum(stop - start for _, start, stop in early[0])
        self.late = self.halo - self.early
        self.first_at = self.own
        self.early_at = self.own + self.halo
        self.spare = self.early_at + self.early
        self.halo_base = self.bases((low, high))
        self.early_base = self.bases(early)
        shifts = (rows, -rows)
        self.packs = [self.places(*pair) for pair in zip((low, high), shifts)]
        self.early_packs = [self.places(*pair) for pair in zip(early, shifts)]
        self.late_packs = [self.places(*pair) for pair in zip(late, shifts)]
        self.span = min(2 * reach, rows) * band
        self.quiet = [
            self.others(self.packs[1], 0, self.span),
            self.others(self.packs[0], self.own - self.span, self.own),
        ]
        self.list_size = batches + 2
        self.lengths_at = LISTS * self.list_size
        self.local_at = self.lengths_at + LISTS
        self.count_at = self.local_at + batches
        self.offsets_at = self.count_at + batches
        self.odd_at = self.offsets_at + slots * batches
        self.meta_size = self.odd_at + 1

    def bases(self, sides):
        found = {}
        for segments in sides:
            place = 0
            for row, start, stop in segments:
                found[row] = place - start
                place += stop - start
        return found

    def places(self, segments, shift):
        pack, place = ([], 0)
        for row, start, stop in segments:
            pack.append(((row + shift) * self.band + start, place, stop - start))
            place += stop - start
        return pack

    def others(self, pack, begin, end):
        touched = set()
        for start, _, count in pack:
            touched.update(range(start, start + count))
        runs = []
        for index in range(begin, end):
            if index in touched:
                continue
            if runs and sum(runs[-1]) == index:
                runs[-1] = (runs[-1][0], runs[-1][1] + 1)
            else:
                runs.append((index, 1))
        return runs

    def pick(self, bases, shift, row, otherwise):
        value = otherwise
        for at, base in bases.items():
            value = jnp.where(row == at, base + shift, value)
        return value


def run_copies(copies):
    for copy in copies:
        copy.start()
    for copy in copies:
        copy.wait()


def by_parity(odd, body, first, second):
    @pl.when(jnp.logical_not(odd))
    def _():
        body(first, second)

    @pl.when(odd)
    def _():
        body(second, first)


CROSS_MANY, CROSS_FEW, NEAR_MANY, NEAR_FEW, INNER_MANY, INNER_FEW, CROSS = range(LISTS)


def build_lists(geo, index, centre_ref, offsets_ref, counts_ref, meta_ref):
    first = index * geo.rows
    odd = index % 2 == 1
    meta_ref[geo.odd_at] = odd.astype(jnp.int32)
    lengths = [jnp.int32(0)] * LISTS
    for b in range(geo.batches):
        local = centre_ref[b] - first
        count = counts_ref[b]
        meta_ref[geo.local_at + b] = local
        meta_ref[geo.count_at + b] = count
        low = high = jnp.bool_(False)
        for k in range(geo.slots):
            offset = offsets_ref[k, b]
            meta_ref[geo.offsets_at + k * geo.batches + b] = offset
            row = local + offset
            low = low | ((k < count) & (row < 0))
            high = high | ((k < count) & (row >= geo.rows))
        cross = (odd & high) | (jnp.logical_not(odd) & low)
        near = (odd & low) | (jnp.logical_not(odd) & high)
        inner = jnp.logical_not(low | high)
        many = count > 2
        few = (count > 0) & jnp.logical_not(many)
        kinds = [kind & size for kind in (cross, near, inner) for size in (many, few)]
        for which, member in enumerate(kinds + [cross]):
            meta_ref[which * geo.list_size + lengths[which]] = b
            lengths[which] = lengths[which] + member.astype(jnp.int32)
    for which in range(LISTS):
        meta_ref[which * geo.list_size + lengths[which]] = geo.batches
        meta_ref[geo.lengths_at + which] = lengths[which]


def zone(geo, odd, cross):
    span = geo.span if cross else geo.own - geo.span
    return pl.ds(jnp.where(odd == cross, geo.own - span, 0), span)


def pack_kernel(
    geo, density_ref, centre_in, offsets_in, counts_in,
    near_ref, cross_ref, meta_ref, acc_ref,
    centre_ref, offsets_ref, counts_ref, sems,
):
    index = lax.axis_index("blk")
    odd = index % 2 == 1

    def copies(up, down):
        return [
            pltpu.make_async_copy(
                density_ref.at[pl.ds(start, count)], ref.at[pl.ds(place, count)], sems.at[side, i]
            )
            for side, (pack, ref) in enumerate(zip(geo.packs, (up, down)))
            for i, (start, place, count) in enumerate(pack)
        ]

    def start(up, down):
        for copy in copies(up, down):
            copy.start()

    by_parity(odd, start, near_ref, cross_ref)
    scalars = [
        pltpu.make_async_copy(*pair, sems.at[2, i])
        for i, pair in enumerate(
            ((centre_in, centre_ref), (offsets_in, offsets_ref), (counts_in, counts_ref))
        )
    ]
    for copy in scalars:
        copy.start()
    for where in (zone(geo, odd, False), pl.ds(geo.first_at, geo.halo)):
        acc_ref[where] = jnp.zeros_like(acc_ref[where])
    for copy in scalars:
        copy.wait()
    build_lists(geo, index, centre_ref, offsets_ref, counts_ref, meta_ref)
    for copy in copies(near_ref, cross_ref):
        copy.wait()


def group_count(geo, meta_ref, which):
    return (meta_ref[geo.lengths_at + which] + GROUP - 1) // GROUP


def inner_share(geo, meta_ref):
    before = BUDGET
    for which in (CROSS_MANY, CROSS_FEW, NEAR_MANY, NEAR_FEW):
        before = before - COST[which % 2] * group_count(geo, meta_ref, which)
    waiting = jnp.where((lax.axis_index("blk") + 1) // 2 % 2 == 1, WAIT, 0)
    share = []
    for which in (INNER_MANY, INNER_FEW):
        cost, count = COST[which % 2], group_count(geo, meta_ref, which)
        first = jnp.minimum(jnp.maximum(before, 0) // cost, count)
        second = jnp.minimum(jnp.maximum(waiting, 0) // cost, count - first)
        before = before - cost * first
        waiting = waiting - cost * second
        share.append((0, first, first + second, count))
    return share


def inner_part(geo, meta_ref, stage, refs):
    for which, width, bounds in zip(
        (INNER_MANY, INNER_FEW), (geo.slots, 2), inner_share(geo, meta_ref)
    ):
        each_group(
            geo,
            meta_ref,
            which,
            lambda chosen, width=width: add_whole(geo, chosen, width, *refs),
            begin=bounds[stage],
            end=bounds[stage + 1],
        )


def each_group(geo, meta_ref, which, body, size=GROUP, begin=0, end=None):
    length = meta_ref[geo.lengths_at + which]

    def step(i, carry):
        chosen = []
        for n in range(size):
            place = i * size + n
            there = place < length
            b = meta_ref[which * geo.list_size + jnp.minimum(place, length)]
            chosen.append((jnp.where(there, b, 0), there))
        body(chosen)
        return carry

    lax.fori_loop(begin, (length + size - 1) // size if end is None else end, step, 0)


class Slots:
    def __init__(self, geo, meta_ref, b, there, width):
        local = meta_ref[geo.local_at + b]
        count = jnp.where(there, meta_ref[geo.count_at + b], 0)
        self.offset = [meta_ref[geo.offsets_at + k * geo.batches + b] for k in range(width)]
        self.local = local
        self.row = [local + offset for offset in self.offset]
        self.live = [k < count for k in range(width)]
        self.own = [(row >= 0) & (row < geo.rows) for row in self.row]
        self.width = width


def panels(slots, ao_ref, b):
    return jnp.concatenate(
        [
            ao_ref[b, k] * jnp.where(slots.live[k], 1.0, 0.0).astype(ao_ref.dtype)
            for k in range(slots.width)
        ],
        axis=0,
    )


def gathered(tiles_ref, places):
    return jnp.concatenate(
        [jnp.concatenate([tiles_ref[place] for place in row], axis=1) for row in places], axis=0
    )


def potentials(xs, tiles, batches, kernel_ref):
    fs = [
        jnp.dot(t, x, preferred_element_type=jnp.float32).astype(jnp.bfloat16)
        for t, x in zip(tiles, xs)
    ]
    return [
        jnp.dot(f, kernel_ref[b], preferred_element_type=jnp.float32) for f, b in zip(fs, batches)
    ]


def outer_product(x, h):
    return lax.dot_general(x, h, (((1,), (1,)), ((), ())), preferred_element_type=jnp.float32)


def chain(xs, tiles, batches, kernel_ref, weights_ref):
    gs = potentials(xs, tiles, batches, kernel_ref)
    hs = [(g * weights_ref[pl.ds(b, 1), :]).astype(jnp.bfloat16) for g, b in zip(gs, batches)]
    return [outer_product(x, h) for x, h in zip(xs, hs)]


def scatter(part, target, nb, acc_ref):
    for k, row in enumerate(target):
        for j, place in enumerate(row):
            acc_ref[place] += part[k * nb : (k + 1) * nb, j * nb : (j + 1) * nb]


def add_whole(
    geo, chosen, width, meta_ref, tiles_ref, ao_ref, kernel_ref, weights_ref, acc_ref, halo_ref=None
):
    xs, tiles, targets = ([], [], [])
    for b, there in chosen:
        slots = Slots(geo, meta_ref, b, there, width)
        xs.append(panels(slots, ao_ref, b))
        rows, target = ([], [])
        for k in range(width):
            band = [slots.offset[j] - slots.offset[k] + geo.half for j in range(width)]
            own = slots.own[k]
            base = jnp.where(slots.live[k] & own, slots.row[k], 0) * geo.band
            row = jnp.concatenate([tiles_ref[base + o] for o in band], axis=1)
            if halo_ref is not None:
                away = slots.live[k] & jnp.logical_not(own)
                outside = jnp.where(away, geo.pick(geo.halo_base, 0, slots.row[k], 0), 0)
                other = [halo_ref[jnp.where(away, outside + o, 0)] for o in band]
                row = jnp.where(away, jnp.concatenate(other, axis=1), row)
                base = jnp.where(away, outside + geo.first_at, base)
            rows.append(row)
            target.append(
                [
                    jnp.where(slots.live[k] & slots.live[j], base + band[j], geo.spare)
                    for j in range(width)
                ]
            )
        tiles.append(jnp.concatenate(rows, axis=0))
        targets.append(target)
    parts = chain(xs, tiles, [b for b, _ in chosen], kernel_ref, weights_ref)
    for part, target in zip(parts, targets):
        scatter(part, target, ao_ref.shape[2], acc_ref)


def add_own(geo, chosen, width, meta_ref, tiles_ref, ao_ref, kernel_ref, weights_ref, acc_ref):
    xs, tiles, targets = ([], [], [])
    for b, there in chosen:
        slots = Slots(geo, meta_ref, b, there, width)
        xs.append(panels(slots, ao_ref, b))
        places, target = ([], [])
        for k in range(width):
            row = slots.row[k]
            band = [slots.offset[j] - slots.offset[k] + geo.half for j in range(width)]
            base = jnp.where(slots.own[k], row, 0) * geo.band
            places.append([base + o for o in band])
            base = geo.pick(geo.early_base, geo.early_at, row, base)
            target.append(
                [
                    jnp.where(
                        slots.live[k] & slots.live[j] & slots.own[j], base + band[j], geo.spare
                    )
                    for j in range(width)
                ]
            )
        tiles.append(gathered(tiles_ref, places))
        targets.append(target)
    parts = chain(xs, tiles, [b for b, _ in chosen], kernel_ref, weights_ref)
    for part, target in zip(parts, targets):
        scatter(part, target, ao_ref.shape[2], acc_ref)


def halo_rows(geo, meta_ref, slots):
    odd = meta_ref[geo.odd_at] == 1
    rows, places, present = ([], [], [])
    for i in range(geo.reach):
        row = jnp.where(odd, geo.rows + i, i - geo.reach)
        place, found = (jnp.int32(0), jnp.bool_(False))
        for k in range(slots.width):
            hit = slots.live[k] & (slots.row[k] == row)
            place = jnp.where(hit, k, place)
            found = found | hit
        rows.append(row)
        places.append(place)
        present.append(found)
    return rows, places, present


def add_corner(geo, chosen, meta_ref, halo_ref, ao_ref, kernel_ref, weights_ref, h_ref, total_ref):
    nb = ao_ref.shape[2]
    factor = lambda flag: jnp.where(flag, 1.0, 0.0)
    xs, sides, tiles, masks = ([], [], [], [])
    for b, there in chosen:
        slots = Slots(geo, meta_ref, b, there, geo.slots)
        rows, places, present = halo_rows(geo, meta_ref, slots)
        xs.append(panels(slots, ao_ref, b))
        sides.append(
            jnp.concatenate(
                [
                    ao_ref[b, place] * factor(found).astype(ao_ref.dtype)
                    for place, found in zip(places, present)
                ],
                axis=0,
            )
        )
        picked = []
        for row, found in zip(rows, present):
            base = geo.pick(geo.halo_base, 0, row, 0) - row + geo.half
            picked.append([jnp.where(found, base + column, 0) for column in slots.row])
        tiles.append(gathered(halo_ref, picked))
        masks.append([factor(found) for found in present])
    gs = potentials(xs, tiles, [b for b, _ in chosen], kernel_ref)
    hs = []
    for g, mask, (b, there) in zip(gs, masks, chosen):
        weights = weights_ref[pl.ds(b, 1), :]
        h = jnp.concatenate(
            [g[i * nb : (i + 1) * nb] * (weights * mask[i]) for i in range(geo.reach)], axis=0
        ).astype(jnp.bfloat16)
        h_ref[jnp.where(there, b, geo.batches)] = h
        hs.append(h)
    total_ref[...] += outer_product(
        jnp.concatenate(sides, axis=1), jnp.concatenate(hs, axis=1)
    )


def add_columns(geo, chosen, width, meta_ref, ao_ref, h_ref, acc_ref):
    parts, targets = ([], [])
    for b, there in chosen:
        slots = Slots(geo, meta_ref, b, there, width)
        rows, _, present = halo_rows(geo, meta_ref, slots)
        parts.append(outer_product(ao_ref[b, pl.ds(0, width)].reshape(-1, ao_ref.shape[3]), h_ref[b]))
        targets.append(
            [
                [
                    jnp.where(
                        slots.live[k] & slots.own[k] & found,
                        slots.row[k] * geo.band + row - slots.row[k] + geo.half,
                        geo.spare,
                    )
                    for row, found in zip(rows, present)
                ]
                for k in range(width)
            ]
        )
    for part, target in zip(parts, targets):
        scatter(part, target, ao_ref.shape[2], acc_ref)


def early_kernel(
    geo, meta_ref, tiles_ref, ao_ref, kernel_ref, weights_ref, acc_in, acc_ref, early_out
):
    odd = meta_ref[geo.odd_at] == 1
    for where in (zone(geo, odd, True), pl.ds(geo.early_at, geo.early), pl.ds(geo.spare, 1)):
        acc_ref[where] = jnp.zeros_like(acc_ref[where])
    refs = (meta_ref, tiles_ref, ao_ref, kernel_ref, weights_ref, acc_ref)
    for which, width in ((CROSS_MANY, geo.slots), (CROSS_FEW, 2)):
        each_group(
            geo, meta_ref, which, lambda chosen, width=width: add_own(geo, chosen, width, *refs)
        )
    early_out[...] = acc_ref[pl.ds(geo.early_at, geo.early)].astype(early_out.dtype)


def near_kernel(
    geo, meta_ref, halo_ref, tiles_ref, ao_ref, kernel_ref, weights_ref, acc_in, acc_ref, first_out
):
    refs = (meta_ref, tiles_ref, ao_ref, kernel_ref, weights_ref, acc_ref, halo_ref)
    for which, width in ((NEAR_MANY, geo.slots), (NEAR_FEW, 2)):
        each_group(
            geo, meta_ref, which, lambda chosen, width=width: add_whole(geo, chosen, width, *refs)
        )
    first_out[...] = acc_ref[pl.ds(geo.first_at, geo.halo)].astype(first_out.dtype)
    inner_part(geo, meta_ref, 0, refs[:-1])


def waiting_kernel(
    geo, meta_ref, tiles_ref, ao_ref, kernel_ref, weights_ref, acc_in, acc_ref, done_ref
):
    inner_part(geo, meta_ref, 1, (meta_ref, tiles_ref, ao_ref, kernel_ref, weights_ref, acc_ref))
    done_ref[0] = 1


def late_kernel(
    geo, meta_ref, done_ref, halo_ref, ao_ref, kernel_ref, weights_ref, h_ref, late_out, total_ref
):
    nb = ao_ref.shape[2]
    total_ref[...] = jnp.zeros_like(total_ref)

    def work(chosen):
        add_corner(
            geo, chosen, meta_ref, halo_ref, ao_ref, kernel_ref, weights_ref, h_ref, total_ref
        )

    groups = (meta_ref[geo.lengths_at + CROSS] + 1) // LATE_GROUP
    each_group(geo, meta_ref, CROSS, work, size=LATE_GROUP, end=groups)
    each_group(geo, meta_ref, CROSS, work, size=LATE_GROUP // 2, begin=2 * groups)
    for i in range(geo.reach):
        for j in range(geo.reach):
            late_out[i * geo.reach + j] = total_ref[
                i * nb : (i + 1) * nb, j * nb : (j + 1) * nb
            ].astype(late_out.dtype)


def inner_kernel(
    geo, meta_ref, first_ref, tiles_ref, ao_ref, kernel_ref, weights_ref, h_ref, acc_in,
    acc_ref, out_ref, sems,
):
    odd = meta_ref[geo.odd_at] == 1
    refs = (meta_ref, tiles_ref, ao_ref, kernel_ref, weights_ref, acc_ref)
    inner_part(geo, meta_ref, 2, refs)

    def add_near(up, down):
        for start, place, count in geo.packs[0 if up else 1]:
            acc_ref[pl.ds(start, count)] += first_ref[pl.ds(place, count)].astype(jnp.float32)

    by_parity(odd, add_near, True, False)
    done = zone(geo, odd, False)
    copy = pltpu.make_async_copy(acc_ref.at[done], out_ref.at[done], sems.at[0])
    copy.start()
    for which, width in ((CROSS_MANY, geo.slots), (CROSS_FEW, 2)):
        each_group(
            geo,
            meta_ref,
            which,
            lambda chosen, width=width: add_columns(
                geo, chosen, width, meta_ref, ao_ref, h_ref, acc_ref
            ),
        )

    def write_quiet(up, down):
        run_copies(
            [
                pltpu.make_async_copy(
                    acc_ref.at[pl.ds(start, count)], out_ref.at[pl.ds(start, count)], sems.at[1 + i]
                )
                for i, (start, count) in enumerate(geo.quiet[0 if up else 1])
            ]
        )

    by_parity(odd, write_quiet, True, False)
    copy.wait()


def join_kernel(geo, packs, meta_ref, got_ref, acc_ref, out_in, out_ref, total, sems):
    def add(up, down):
        copies = []
        for start, place, count in packs[0 if up else 1]:
            spot = pl.ds(place, count)
            total[spot] = acc_ref[pl.ds(start, count)] + got_ref[spot].astype(jnp.float32)
            copy = pltpu.make_async_copy(
                total.at[spot], out_ref.at[pl.ds(start, count)], sems.at[len(copies)]
            )
            copy.start()
            copies.append(copy)
        for copy in copies:
            copy.wait()

    by_parity(meta_ref[geo.odd_at] == 1, add, False, True)


def call(kernel, out_shape, in_specs, out_specs, scratch, aliases=None, cost=None):
    return pl.pallas_call(
        kernel,
        out_shape=out_shape,
        in_specs=in_specs,
        out_specs=out_specs,
        scratch_shapes=scratch,
        input_output_aliases=aliases or {},
        cost_estimate=cost,
        compiler_params=pltpu.CompilerParams(vmem_limit_bytes=16 * MIB),
    )


def to_first(x, size):
    pairs = [(i, i + 1) for i in range(0, size - 1, 2)]
    got = lax.ppermute(x, "blk", pairs + [(j, i) for i, j in pairs])
    return pltpu.with_memory_space_constraint(got, pltpu.VMEM)


def to_second(x, size):
    pairs = [(i, i + 1) for i in range(1, size - 1, 2)]
    got = lax.ppermute(x, "blk", pairs + [(j, i) for i, j in pairs])
    return pltpu.with_memory_space_constraint(got, pltpu.VMEM)


def local(density, ao_values, kernel, grid_weights, centre, sig_offsets, counts):
    rows, band, nb, _ = density.shape
    batches, slots, _, pts = ao_values.shape
    size = lax.axis_size("blk")
    geo = Geometry(rows, band, batches, slots)
    in_hbm = lambda x: pltpu.with_memory_space_constraint(x, pltpu.HBM)
    tiles = density.reshape(geo.own, nb, nb)
    pack = lambda count: pltpu.VMEM((count, nb, nb), jnp.bfloat16)
    dma = pltpu.SemaphoreType.DMA
    acc_type = pltpu.VMEM((geo.spare + 1, nb, nb), jnp.float32)

    near_halo, cross_halo, meta, acc = call(
        functools.partial(pack_kernel, geo),
        (pack(geo.halo),) * 2 + (pltpu.SMEM((geo.meta_size,), jnp.int32), acc_type),
        [ANY_SPEC] * 4,
        (VMEM_SPEC,) * 2 + (SMEM_SPEC, VMEM_SPEC),
        [
            pltpu.SMEM((batches,), jnp.int32),
            pltpu.SMEM((slots, batches), jnp.int32),
            pltpu.SMEM((batches,), jnp.int32),
            dma((3, max(geo.reach, 3))),
        ],
        cost=pl.CostEstimate(flops=10**10, bytes_accessed=10**8, transcendentals=0),
    )(in_hbm(tiles), in_hbm(centre), in_hbm(sig_offsets.T), in_hbm(counts))
    cross_halo = to_second(cross_halo, size)
    near_halo = to_first(near_halo, size)

    panel = (tiles, ao_values, kernel, grid_weights)
    acc, early = call(
        functools.partial(early_kernel, geo),
        (acc_type, pack(geo.early)),
        [SMEM_SPEC] + [VMEM_SPEC] * 5,
        (VMEM_SPEC,) * 2,
        [],
        {5: 0},
    )(meta, *panel, acc)
    early = to_second(early, size)

    acc, first = call(
        functools.partial(near_kernel, geo),
        (acc_type, pack(geo.halo)),
        [SMEM_SPEC] + [VMEM_SPEC] * 6,
        (VMEM_SPEC,) * 2,
        [],
        {6: 0},
    )(meta, near_halo, *panel, acc)
    first = to_first(first, size)

    acc, done = call(
        functools.partial(waiting_kernel, geo),
        (acc_type, pltpu.SMEM((1,), jnp.int32)),
        [SMEM_SPEC] + [VMEM_SPEC] * 5,
        (VMEM_SPEC, SMEM_SPEC),
        [],
        {5: 0},
    )(meta, *panel, acc)

    h_type = pltpu.VMEM((batches + 1, geo.reach * nb, pts), jnp.bfloat16)
    h, late = call(
        functools.partial(late_kernel, geo),
        (h_type, pack(geo.late)),
        [SMEM_SPEC] * 2 + [VMEM_SPEC] * 4,
        (VMEM_SPEC,) * 2,
        [pltpu.VMEM((geo.reach * nb, geo.reach * nb), jnp.float32)],
    )(meta, done, cross_halo, *panel[1:])
    late = to_second(late, size)

    whole = jax.ShapeDtypeStruct((geo.own, nb, nb), jnp.float32)
    acc, out = call(
        functools.partial(inner_kernel, geo),
        (acc_type, whole),
        [SMEM_SPEC] + [VMEM_SPEC] * 7,
        (VMEM_SPEC, ANY_SPEC),
        [dma((1 + max(len(runs) for runs in geo.quiet),))],
        {7: 0},
    )(meta, first, *panel, h, acc)

    for packs, got in ((geo.early_packs, early), (geo.late_packs, late)):
        out = call(
            functools.partial(join_kernel, geo, packs),
            whole,
            [SMEM_SPEC] + [VMEM_SPEC] * 2 + [ANY_SPEC],
            ANY_SPEC,
            [pltpu.VMEM(got.shape, jnp.float32), dma((geo.reach,))],
            {3: 0},
        )(meta, got, acc, out)
    return out.reshape(rows, band, nb, nb)


def solution(mesh):
    placed = (
        P(("groups", "blk"), None, None, None),
        P(("groups", "blk"), None, None, None),
        P(("groups", "blk"), None, None),
        P(("groups", "blk"), None),
        P(("groups", "blk")),
        P(("groups", "blk"), None),
        P(("groups", "blk")),
    )
    return jax.shard_map(
        local,
        mesh=mesh,
        in_specs=placed,
        out_specs=P(("groups", "blk"), None, None, None),
        check_vma=False,
    )
```

```python
import functools

import jax
import jax.numpy as jnp
from jax import lax
from jax.experimental import pallas as pl
from jax.experimental.pallas import tpu as pltpu
from jax.sharding import PartitionSpec as P

MIB = 1 << 20
GROUP = 2
LATE_GROUP = 4
LISTS = 7
BUDGET = 43
WAIT = 18
COST = (10, 7)
SMEM_SPEC = pl.BlockSpec(memory_space=pltpu.SMEM)
VMEM_SPEC = pl.BlockSpec(memory_space=pltpu.VMEM)
ANY_SPEC = pl.BlockSpec(memory_space=pl.ANY)


class Geometry:
    def __init__(self, rows, band, batches, slots):
        self.rows, self.band, self.batches, self.slots = rows, band, batches, slots
        self.half = half = (band - 1) // 2
        self.reach = reach = half // 2
        self.own = rows * band
        low = [(-m, reach + m, band) for m in range(reach, 0, -1)]
        high = [(rows + m, 0, 3 * reach - m) for m in range(reach)]
        self.halo = sum(stop - start for _, start, stop in low)
        low_cut = [half - row for row, _, _ in low]
        high_cut = [rows - row + half for row, _, _ in high]
        early = (
            [(row, cut, stop) for (row, _, stop), cut in zip(low, low_cut)],
            [(row, start, cut) for (row, start, _), cut in zip(high, high_cut)],
        )
        late = (
            [(row, start, cut) for (row, start, _), cut in zip(low, low_cut)],
            [(row, cut, stop) for (row, _, stop), cut in zip(high, high_cut)],
        )
        self.early = sum(stop - start for _, start, stop in early[0])
        self.late = self.halo - self.early
        self.first_at = self.own
        self.early_at = self.own + self.halo
        self.spare = self.early_at + self.early
        self.halo_base = self.bases((low, high))
        self.early_base = self.bases(early)
        shifts = (rows, -rows)
        self.packs = [self.places(*pair) for pair in zip((low, high), shifts)]
        self.early_packs = [self.places(*pair) for pair in zip(early, shifts)]
        self.late_packs = [self.places(*pair) for pair in zip(late, shifts)]
        self.span = min(2 * reach, rows) * band
        self.quiet = [
            self.others(self.packs[1], 0, self.span),
            self.others(self.packs[0], self.own - self.span, self.own),
        ]
        self.list_size = batches + 2
        self.lengths_at = LISTS * self.list_size
        self.local_at = self.lengths_at + LISTS
        self.count_at = self.local_at + batches
        self.offsets_at = self.count_at + batches
        self.odd_at = self.offsets_at + slots * batches
        self.meta_size = self.odd_at + 1

    def bases(self, sides):
        found = {}
        for segments in sides:
            place = 0
            for row, start, stop in segments:
                found[row] = place - start
                place += stop - start
        return found

    def places(self, segments, shift):
        pack, place = ([], 0)
        for row, start, stop in segments:
            pack.append(((row + shift) * self.band + start, place, stop - start))
            place += stop - start
        return pack

    def others(self, pack, begin, end):
        touched = set()
        for start, _, count in pack:
            touched.update(range(start, start + count))
        runs = []
        for index in range(begin, end):
            if index in touched:
                continue
            if runs and sum(runs[-1]) == index:
                runs[-1] = (runs[-1][0], runs[-1][1] + 1)
            else:
                runs.append((index, 1))
        return runs

    def pick(self, bases, shift, row, otherwise):
        value = otherwise
        for at, base in bases.items():
            value = jnp.where(row == at, base + shift, value)
        return value


def run_copies(copies):
    for copy in copies:
        copy.start()
    for copy in copies:
        copy.wait()


def by_parity(odd, body, first, second):
    @pl.when(jnp.logical_not(odd))
    def _():
        body(first, second)

    @pl.when(odd)
    def _():
        body(second, first)


CROSS_MANY, CROSS_FEW, NEAR_MANY, NEAR_FEW, INNER_MANY, INNER_FEW, CROSS = range(LISTS)


def build_lists(geo, index, centre_ref, offsets_ref, counts_ref, meta_ref):
    first = index * geo.rows
    odd = index % 2 == 1
    meta_ref[geo.odd_at] = odd.astype(jnp.int32)
    lengths = [jnp.int32(0)] * LISTS
    for b in range(geo.batches):
        local = centre_ref[b] - first
        count = counts_ref[b]
        meta_ref[geo.local_at + b] = local
        meta_ref[geo.count_at + b] = count
        low = high = jnp.bool_(False)
        for k in range(geo.slots):
            offset = offsets_ref[k, b]
            meta_ref[geo.offsets_at + k * geo.batches + b] = offset
            row = local + offset
            low = low | ((k < count) & (row < 0))
            high = high | ((k < count) & (row >= geo.rows))
        cross = (odd & high) | (jnp.logical_not(odd) & low)
        near = (odd & low) | (jnp.logical_not(odd) & high)
        inner = jnp.logical_not(low | high)
        many = count > 2
        few = (count > 0) & jnp.logical_not(many)
        kinds = [kind & size for kind in (cross, near, inner) for size in (many, few)]
        for which, member in enumerate(kinds + [cross]):
            meta_ref[which * geo.list_size + lengths[which]] = b
            lengths[which] = lengths[which] + member.astype(jnp.int32)
    for which in range(LISTS):
        meta_ref[which * geo.list_size + lengths[which]] = geo.batches
        meta_ref[geo.lengths_at + which] = lengths[which]


def zone(geo, odd, cross):
    span = geo.span if cross else geo.own - geo.span
    return pl.ds(jnp.where(odd == cross, geo.own - span, 0), span)


def pack_kernel(
    geo, density_ref, centre_in, offsets_in, counts_in,
    near_ref, cross_ref, meta_ref, acc_ref,
    centre_ref, offsets_ref, counts_ref, sems,
):
    index = lax.axis_index("blk")
    odd = index % 2 == 1

    def copies(up, down):
        return [
            pltpu.make_async_copy(
                density_ref.at[pl.ds(start, count)], ref.at[pl.ds(place, count)], sems.at[side, i]
            )
            for side, (pack, ref) in enumerate(zip(geo.packs, (up, down)))
            for i, (start, place, count) in enumerate(pack)
        ]

    def start(up, down):
        for copy in copies(up, down):
            copy.start()

    by_parity(odd, start, near_ref, cross_ref)
    scalars = [
        pltpu.make_async_copy(*pair, sems.at[2, i])
        for i, pair in enumerate(
            ((centre_in, centre_ref), (offsets_in, offsets_ref), (counts_in, counts_ref))
        )
    ]
    for copy in scalars:
        copy.start()
    for where in (zone(geo, odd, False), pl.ds(geo.first_at, geo.halo)):
        acc_ref[where] = jnp.zeros_like(acc_ref[where])
    for copy in scalars:
        copy.wait()
    build_lists(geo, index, centre_ref, offsets_ref, counts_ref, meta_ref)
    for copy in copies(near_ref, cross_ref):
        copy.wait()


def group_count(geo, meta_ref, which):
    return (meta_ref[geo.lengths_at + which] + GROUP - 1) // GROUP


def inner_share(geo, meta_ref):
    before = BUDGET
    for which in (CROSS_MANY, CROSS_FEW, NEAR_MANY, NEAR_FEW):
        before = before - COST[which % 2] * group_count(geo, meta_ref, which)
    waiting = jnp.where((lax.axis_index("blk") + 1) // 2 % 2 == 1, WAIT, 0)
    share = []
    for which in (INNER_MANY, INNER_FEW):
        cost, count = COST[which % 2], group_count(geo, meta_ref, which)
        first = jnp.minimum(jnp.maximum(before, 0) // cost, count)
        second = jnp.minimum(jnp.maximum(waiting, 0) // cost, count - first)
        before = before - cost * first
        waiting = waiting - cost * second
        share.append((0, first, first + second, count))
    return share


def inner_part(geo, meta_ref, stage, refs):
    for which, width, bounds in zip(
        (INNER_MANY, INNER_FEW), (geo.slots, 2), inner_share(geo, meta_ref)
    ):
        work = lambda chosen, width=width: add_whole(geo, chosen, width, *refs)
        begin, end = bounds[stage], bounds[stage + 1]
        pairs = (end - begin) // 2
        each_group(geo, meta_ref, which, work, size=2 * GROUP, end=pairs, skip=begin * GROUP)
        each_group(geo, meta_ref, which, work, begin=begin + 2 * pairs, end=end)


def each_group(geo, meta_ref, which, body, size=GROUP, begin=0, end=None, skip=0):
    length = meta_ref[geo.lengths_at + which]

    def step(i, carry):
        chosen = []
        for n in range(size):
            place = skip + i * size + n
            there = place < length
            b = meta_ref[which * geo.list_size + jnp.minimum(place, length)]
            chosen.append((jnp.where(there, b, 0), there))
        body(chosen)
        return carry

    lax.fori_loop(begin, (length + size - 1) // size if end is None else end, step, 0)


class Slots:
    def __init__(self, geo, meta_ref, b, there, width):
        local = meta_ref[geo.local_at + b]
        count = jnp.where(there, meta_ref[geo.count_at + b], 0)
        self.offset = [meta_ref[geo.offsets_at + k * geo.batches + b] for k in range(width)]
        self.local = local
        self.row = [local + offset for offset in self.offset]
        self.live = [k < count for k in range(width)]
        self.own = [(row >= 0) & (row < geo.rows) for row in self.row]
        self.width = width


def panels(slots, ao_ref, b):
    return jnp.concatenate(
        [
            ao_ref[b, k] * jnp.where(slots.live[k], 1.0, 0.0).astype(ao_ref.dtype)
            for k in range(slots.width)
        ],
        axis=0,
    )


def gathered(tiles_ref, places):
    return jnp.concatenate(
        [jnp.concatenate([tiles_ref[place] for place in row], axis=1) for row in places], axis=0
    )


def potentials(xs, tiles, batches, kernel_ref):
    fs = [
        jnp.dot(t, x, preferred_element_type=jnp.float32).astype(jnp.bfloat16)
        for t, x in zip(tiles, xs)
    ]
    return [
        jnp.dot(f, kernel_ref[b], preferred_element_type=jnp.float32) for f, b in zip(fs, batches)
    ]


def outer_product(x, h):
    return lax.dot_general(x, h, (((1,), (1,)), ((), ())), preferred_element_type=jnp.float32)


def chain(xs, tiles, batches, kernel_ref, weights_ref):
    gs = potentials(xs, tiles, batches, kernel_ref)
    hs = [(g * weights_ref[pl.ds(b, 1), :]).astype(jnp.bfloat16) for g, b in zip(gs, batches)]
    return [outer_product(x, h) for x, h in zip(xs, hs)]


def scatter(part, target, nb, acc_ref):
    for k, row in enumerate(target):
        for j, place in enumerate(row):
            acc_ref[place] += part[k * nb : (k + 1) * nb, j * nb : (j + 1) * nb]


def add_whole(
    geo, chosen, width, meta_ref, tiles_ref, ao_ref, kernel_ref, weights_ref, acc_ref, halo_ref=None
):
    xs, tiles, targets = ([], [], [])
    for b, there in chosen:
        slots = Slots(geo, meta_ref, b, there, width)
        xs.append(panels(slots, ao_ref, b))
        rows, target = ([], [])
        for k in range(width):
            band = [slots.offset[j] - slots.offset[k] + geo.half for j in range(width)]
            own = slots.own[k]
            base = jnp.where(slots.live[k] & own, slots.row[k], 0) * geo.band
            row = jnp.concatenate([tiles_ref[base + o] for o in band], axis=1)
            if halo_ref is not None:
                away = slots.live[k] & jnp.logical_not(own)
                outside = jnp.where(away, geo.pick(geo.halo_base, 0, slots.row[k], 0), 0)
                other = [halo_ref[jnp.where(away, outside + o, 0)] for o in band]
                row = jnp.where(away, jnp.concatenate(other, axis=1), row)
                base = jnp.where(away, outside + geo.first_at, base)
            rows.append(row)
            target.append(
                [
                    jnp.where(slots.live[k] & slots.live[j], base + band[j], geo.spare)
                    for j in range(width)
                ]
            )
        tiles.append(jnp.concatenate(rows, axis=0))
        targets.append(target)
    parts = chain(xs, tiles, [b for b, _ in chosen], kernel_ref, weights_ref)
    for part, target in zip(parts, targets):
        scatter(part, target, ao_ref.shape[2], acc_ref)


def add_own(geo, chosen, width, meta_ref, tiles_ref, ao_ref, kernel_ref, weights_ref, acc_ref):
    xs, tiles, targets = ([], [], [])
    for b, there in chosen:
        slots = Slots(geo, meta_ref, b, there, width)
        xs.append(panels(slots, ao_ref, b))
        places, target = ([], [])
        for k in range(width):
            row = slots.row[k]
            band = [slots.offset[j] - slots.offset[k] + geo.half for j in range(width)]
            base = jnp.where(slots.own[k], row, 0) * geo.band
            places.append([base + o for o in band])
            base = geo.pick(geo.early_base, geo.early_at, row, base)
            target.append(
                [
                    jnp.where(
                        slots.live[k] & slots.live[j] & slots.own[j], base + band[j], geo.spare
                    )
                    for j in range(width)
                ]
            )
        tiles.append(gathered(tiles_ref, places))
        targets.append(target)
    parts = chain(xs, tiles, [b for b, _ in chosen], kernel_ref, weights_ref)
    for part, target in zip(parts, targets):
        scatter(part, target, ao_ref.shape[2], acc_ref)


def halo_rows(geo, meta_ref, slots):
    odd = meta_ref[geo.odd_at] == 1
    rows, places, present = ([], [], [])
    for i in range(geo.reach):
        row = jnp.where(odd, geo.rows + i, i - geo.reach)
        place, found = (jnp.int32(0), jnp.bool_(False))
        for k in range(slots.width):
            hit = slots.live[k] & (slots.row[k] == row)
            place = jnp.where(hit, k, place)
            found = found | hit
        rows.append(row)
        places.append(place)
        present.append(found)
    return rows, places, present


def add_corner(geo, chosen, meta_ref, halo_ref, ao_ref, kernel_ref, weights_ref, h_ref, total_ref):
    nb = ao_ref.shape[2]
    factor = lambda flag: jnp.where(flag, 1.0, 0.0)
    xs, sides, tiles, masks = ([], [], [], [])
    for b, there in chosen:
        slots = Slots(geo, meta_ref, b, there, geo.slots)
        rows, places, present = halo_rows(geo, meta_ref, slots)
        xs.append(panels(slots, ao_ref, b))
        sides.append(
            jnp.concatenate(
                [
                    ao_ref[b, place] * factor(found).astype(ao_ref.dtype)
                    for place, found in zip(places, present)
                ],
                axis=0,
            )
        )
        picked = []
        for row, found in zip(rows, present):
            base = geo.pick(geo.halo_base, 0, row, 0) - row + geo.half
            picked.append([jnp.where(found, base + column, 0) for column in slots.row])
        tiles.append(gathered(halo_ref, picked))
        masks.append([factor(found) for found in present])
    gs = potentials(xs, tiles, [b for b, _ in chosen], kernel_ref)
    hs = []
    for g, mask, (b, there) in zip(gs, masks, chosen):
        weights = weights_ref[pl.ds(b, 1), :]
        h = jnp.concatenate(
            [g[i * nb : (i + 1) * nb] * (weights * mask[i]) for i in range(geo.reach)], axis=0
        ).astype(jnp.bfloat16)
        h_ref[jnp.where(there, b, geo.batches)] = h
        hs.append(h)
    total_ref[...] += outer_product(
        jnp.concatenate(sides, axis=1), jnp.concatenate(hs, axis=1)
    )


def add_columns(geo, chosen, width, meta_ref, ao_ref, h_ref, acc_ref):
    parts, targets = ([], [])
    for b, there in chosen:
        slots = Slots(geo, meta_ref, b, there, width)
        rows, _, present = halo_rows(geo, meta_ref, slots)
        parts.append(outer_product(ao_ref[b, pl.ds(0, width)].reshape(-1, ao_ref.shape[3]), h_ref[b]))
        targets.append(
            [
                [
                    jnp.where(
                        slots.live[k] & slots.own[k] & found,
                        slots.row[k] * geo.band + row - slots.row[k] + geo.half,
                        geo.spare,
                    )
                    for row, found in zip(rows, present)
                ]
                for k in range(width)
            ]
        )
    for part, target in zip(parts, targets):
        scatter(part, target, ao_ref.shape[2], acc_ref)


def early_kernel(
    geo, meta_ref, tiles_ref, ao_ref, kernel_ref, weights_ref, acc_in, acc_ref, early_out
):
    odd = meta_ref[geo.odd_at] == 1
    for where in (zone(geo, odd, True), pl.ds(geo.early_at, geo.early), pl.ds(geo.spare, 1)):
        acc_ref[where] = jnp.zeros_like(acc_ref[where])
    refs = (meta_ref, tiles_ref, ao_ref, kernel_ref, weights_ref, acc_ref)
    for which, width in ((CROSS_MANY, geo.slots), (CROSS_FEW, 2)):
        each_group(
            geo, meta_ref, which, lambda chosen, width=width: add_own(geo, chosen, width, *refs)
        )
    early_out[...] = acc_ref[pl.ds(geo.early_at, geo.early)].astype(early_out.dtype)


def near_kernel(
    geo, meta_ref, halo_ref, tiles_ref, ao_ref, kernel_ref, weights_ref, acc_in, acc_ref, first_out
):
    refs = (meta_ref, tiles_ref, ao_ref, kernel_ref, weights_ref, acc_ref, halo_ref)
    for which, width in ((NEAR_MANY, geo.slots), (NEAR_FEW, 2)):
        each_group(
            geo, meta_ref, which, lambda chosen, width=width: add_whole(geo, chosen, width, *refs)
        )
    first_out[...] = acc_ref[pl.ds(geo.first_at, geo.halo)].astype(first_out.dtype)
    inner_part(geo, meta_ref, 0, refs[:-1])


def waiting_kernel(
    geo, meta_ref, tiles_ref, ao_ref, kernel_ref, weights_ref, acc_in, acc_ref, done_ref
):
    inner_part(geo, meta_ref, 1, (meta_ref, tiles_ref, ao_ref, kernel_ref, weights_ref, acc_ref))
    done_ref[0] = 1


def late_kernel(
    geo, meta_ref, done_ref, halo_ref, ao_ref, kernel_ref, weights_ref, h_ref, late_out, total_ref
):
    nb = ao_ref.shape[2]
    total_ref[...] = jnp.zeros_like(total_ref)

    def work(chosen):
        add_corner(
            geo, chosen, meta_ref, halo_ref, ao_ref, kernel_ref, weights_ref, h_ref, total_ref
        )

    groups = (meta_ref[geo.lengths_at + CROSS] + 1) // LATE_GROUP
    each_group(geo, meta_ref, CROSS, work, size=LATE_GROUP, end=groups)
    each_group(geo, meta_ref, CROSS, work, size=LATE_GROUP // 2, begin=2 * groups)
    for i in range(geo.reach):
        for j in range(geo.reach):
            late_out[i * geo.reach + j] = total_ref[
                i * nb : (i + 1) * nb, j * nb : (j + 1) * nb
            ].astype(late_out.dtype)


def inner_kernel(
    geo, meta_ref, first_ref, tiles_ref, ao_ref, kernel_ref, weights_ref, h_ref, acc_in,
    acc_ref, out_ref, sems,
):
    odd = meta_ref[geo.odd_at] == 1
    refs = (meta_ref, tiles_ref, ao_ref, kernel_ref, weights_ref, acc_ref)
    inner_part(geo, meta_ref, 2, refs)

    def add_near(up, down):
        for start, place, count in geo.packs[0 if up else 1]:
            acc_ref[pl.ds(start, count)] += first_ref[pl.ds(place, count)].astype(jnp.float32)

    by_parity(odd, add_near, True, False)
    done = zone(geo, odd, False)
    copy = pltpu.make_async_copy(acc_ref.at[done], out_ref.at[done], sems.at[0])
    copy.start()
    for which, width in ((CROSS_MANY, geo.slots), (CROSS_FEW, 2)):
        each_group(
            geo,
            meta_ref,
            which,
            lambda chosen, width=width: add_columns(
                geo, chosen, width, meta_ref, ao_ref, h_ref, acc_ref
            ),
        )

    def write_quiet(up, down):
        run_copies(
            [
                pltpu.make_async_copy(
                    acc_ref.at[pl.ds(start, count)], out_ref.at[pl.ds(start, count)], sems.at[1 + i]
                )
                for i, (start, count) in enumerate(geo.quiet[0 if up else 1])
            ]
        )

    by_parity(odd, write_quiet, True, False)
    copy.wait()


def finish_kernel(geo, meta_ref, early_ref, late_ref, acc_ref, out_in, out_ref, total, sems):
    def add(up, down):
        copies = []
        for packs, ref in ((geo.early_packs, early_ref), (geo.late_packs, late_ref)):
            for start, place, count in packs[0 if up else 1]:
                spot = pl.ds(len(copies) * geo.band, count)
                total[spot] = acc_ref[pl.ds(start, count)] + ref[pl.ds(place, count)].astype(
                    jnp.float32
                )
                copy = pltpu.make_async_copy(
                    total.at[spot], out_ref.at[pl.ds(start, count)], sems.at[len(copies)]
                )
                copy.start()
                copies.append(copy)
        for copy in copies:
            copy.wait()

    by_parity(meta_ref[geo.odd_at] == 1, add, False, True)


def call(kernel, out_shape, in_specs, out_specs, scratch, aliases=None, cost=None):
    return pl.pallas_call(
        kernel,
        out_shape=out_shape,
        in_specs=in_specs,
        out_specs=out_specs,
        scratch_shapes=scratch,
        input_output_aliases=aliases or {},
        cost_estimate=cost,
        compiler_params=pltpu.CompilerParams(vmem_limit_bytes=16 * MIB),
    )


def to_first(x, size):
    pairs = [(i, i + 1) for i in range(0, size - 1, 2)]
    got = lax.ppermute(x, "blk", pairs + [(j, i) for i, j in pairs])
    return pltpu.with_memory_space_constraint(got, pltpu.VMEM)


def to_second(x, size):
    pairs = [(i, i + 1) for i in range(1, size - 1, 2)]
    got = lax.ppermute(x, "blk", pairs + [(j, i) for i, j in pairs])
    return pltpu.with_memory_space_constraint(got, pltpu.VMEM)


def local(density, ao_values, kernel, grid_weights, centre, sig_offsets, counts):
    rows, band, nb, _ = density.shape
    batches, slots, _, pts = ao_values.shape
    size = lax.axis_size("blk")
    geo = Geometry(rows, band, batches, slots)
    in_hbm = lambda x: pltpu.with_memory_space_constraint(x, pltpu.HBM)
    tiles = density.reshape(geo.own, nb, nb)
    pack = lambda count: pltpu.VMEM((count, nb, nb), jnp.bfloat16)
    dma = pltpu.SemaphoreType.DMA
    acc_type = pltpu.VMEM((geo.spare + 1, nb, nb), jnp.float32)

    near_halo, cross_halo, meta, acc = call(
        functools.partial(pack_kernel, geo),
        (pack(geo.halo),) * 2 + (pltpu.SMEM((geo.meta_size,), jnp.int32), acc_type),
        [ANY_SPEC] * 4,
        (VMEM_SPEC,) * 2 + (SMEM_SPEC, VMEM_SPEC),
        [
            pltpu.SMEM((batches,), jnp.int32),
            pltpu.SMEM((slots, batches), jnp.int32),
            pltpu.SMEM((batches,), jnp.int32),
            dma((3, max(geo.reach, 3))),
        ],
        cost=pl.CostEstimate(flops=10**10, bytes_accessed=10**8, transcendentals=0),
    )(in_hbm(tiles), in_hbm(centre), in_hbm(sig_offsets.T), in_hbm(counts))
    cross_halo = to_second(cross_halo, size)
    near_halo = to_first(near_halo, size)

    panel = (tiles, ao_values, kernel, grid_weights)
    acc, early = call(
        functools.partial(early_kernel, geo),
        (acc_type, pack(geo.early)),
        [SMEM_SPEC] + [VMEM_SPEC] * 5,
        (VMEM_SPEC,) * 2,
        [],
        {5: 0},
    )(meta, *panel, acc)
    early = to_second(early, size)

    acc, first = call(
        functools.partial(near_kernel, geo),
        (acc_type, pack(geo.halo)),
        [SMEM_SPEC] + [VMEM_SPEC] * 6,
        (VMEM_SPEC,) * 2,
        [],
        {6: 0},
    )(meta, near_halo, *panel, acc)
    first = to_first(first, size)

    acc, done = call(
        functools.partial(waiting_kernel, geo),
        (acc_type, pltpu.SMEM((1,), jnp.int32)),
        [SMEM_SPEC] + [VMEM_SPEC] * 5,
        (VMEM_SPEC, SMEM_SPEC),
        [],
        {5: 0},
    )(meta, *panel, acc)

    h_type = pltpu.VMEM((batches + 1, geo.reach * nb, pts), jnp.bfloat16)
    h, late = call(
        functools.partial(late_kernel, geo),
        (h_type, pack(geo.late)),
        [SMEM_SPEC] * 2 + [VMEM_SPEC] * 4,
        (VMEM_SPEC,) * 2,
        [pltpu.VMEM((geo.reach * nb, geo.reach * nb), jnp.float32)],
    )(meta, done, cross_halo, *panel[1:])
    late = to_second(late, size)

    whole = jax.ShapeDtypeStruct((geo.own, nb, nb), jnp.float32)
    acc, out = call(
        functools.partial(inner_kernel, geo),
        (acc_type, whole),
        [SMEM_SPEC] + [VMEM_SPEC] * 7,
        (VMEM_SPEC, ANY_SPEC),
        [dma((1 + max(len(runs) for runs in geo.quiet),))],
        {7: 0},
    )(meta, first, *panel, h, acc)

    parts = 2 * geo.reach
    out = call(
        functools.partial(finish_kernel, geo),
        whole,
        [SMEM_SPEC] + [VMEM_SPEC] * 3 + [ANY_SPEC],
        ANY_SPEC,
        [pltpu.VMEM((parts * band, nb, nb), jnp.float32), dma((parts,))],
        {4: 0},
    )(meta, early, late, acc, out)
    return out.reshape(rows, band, nb, nb)


def solution(mesh):
    placed = (
        P(("groups", "blk"), None, None, None),
        P(("groups", "blk"), None, None, None),
        P(("groups", "blk"), None, None),
        P(("groups", "blk"), None),
        P(("groups", "blk")),
        P(("groups", "blk"), None),
        P(("groups", "blk")),
    )
    return jax.shard_map(
        local,
        mesh=mesh,
        in_specs=placed,
        out_specs=P(("groups", "blk"), None, None, None),
        check_vma=False,
    )
```

```python
import functools

import jax
import jax.numpy as jnp
from jax import lax
from jax.experimental import pallas as pl
from jax.experimental.pallas import tpu as pltpu
from jax.sharding import PartitionSpec as P

MIB = 1 << 20
GROUP = 2
LATE_GROUP = 4
LISTS = 7
BUDGET = 43
WAIT = 18
COST = (10, 7)
SMEM_SPEC = pl.BlockSpec(memory_space=pltpu.SMEM)
VMEM_SPEC = pl.BlockSpec(memory_space=pltpu.VMEM)
ANY_SPEC = pl.BlockSpec(memory_space=pl.ANY)


class Geometry:
    def __init__(self, rows, band, batches, slots):
        self.rows, self.band, self.batches, self.slots = rows, band, batches, slots
        self.half = half = (band - 1) // 2
        self.reach = reach = half // 2
        self.own = rows * band
        low = [(-m, reach + m, band) for m in range(reach, 0, -1)]
        high = [(rows + m, 0, 3 * reach - m) for m in range(reach)]
        self.halo = sum(stop - start for _, start, stop in low)
        low_cut = [half - row for row, _, _ in low]
        high_cut = [rows - row + half for row, _, _ in high]
        early = (
            [(row, cut, stop) for (row, _, stop), cut in zip(low, low_cut)],
            [(row, start, cut) for (row, start, _), cut in zip(high, high_cut)],
        )
        late = (
            [(row, start, cut) for (row, start, _), cut in zip(low, low_cut)],
            [(row, cut, stop) for (row, _, stop), cut in zip(high, high_cut)],
        )
        self.early = sum(stop - start for _, start, stop in early[0])
        self.late = self.halo - self.early
        self.first_at = self.own
        self.early_at = self.own + self.halo
        self.spare = self.early_at + self.early
        self.halo_base = self.bases((low, high))
        self.early_base = self.bases(early)
        shifts = (rows, -rows)
        self.packs = [self.places(*pair) for pair in zip((low, high), shifts)]
        self.early_packs = [self.places(*pair) for pair in zip(early, shifts)]
        self.late_packs = [self.places(*pair) for pair in zip(late, shifts)]
        self.span = min(2 * reach, rows) * band
        self.quiet = [
            self.others(self.packs[1], 0, self.span),
            self.others(self.packs[0], self.own - self.span, self.own),
        ]
        self.list_size = batches + 2
        self.lengths_at = LISTS * self.list_size
        self.local_at = self.lengths_at + LISTS
        self.count_at = self.local_at + batches
        self.offsets_at = self.count_at + batches
        self.odd_at = self.offsets_at + slots * batches
        self.meta_size = self.odd_at + 1

    def bases(self, sides):
        found = {}
        for segments in sides:
            place = 0
            for row, start, stop in segments:
                found[row] = place - start
                place += stop - start
        return found

    def places(self, segments, shift):
        pack, place = ([], 0)
        for row, start, stop in segments:
            pack.append(((row + shift) * self.band + start, place, stop - start))
            place += stop - start
        return pack

    def others(self, pack, begin, end):
        touched = set()
        for start, _, count in pack:
            touched.update(range(start, start + count))
        runs = []
        for index in range(begin, end):
            if index in touched:
                continue
            if runs and sum(runs[-1]) == index:
                runs[-1] = (runs[-1][0], runs[-1][1] + 1)
            else:
                runs.append((index, 1))
        return runs

    def pick(self, bases, shift, row, otherwise):
        value = otherwise
        for at, base in bases.items():
            value = jnp.where(row == at, base + shift, value)
        return value


def run_copies(copies):
    for copy in copies:
        copy.start()
    for copy in copies:
        copy.wait()


def by_parity(odd, body, first, second):
    @pl.when(jnp.logical_not(odd))
    def _():
        body(first, second)

    @pl.when(odd)
    def _():
        body(second, first)


CROSS_MANY, CROSS_FEW, NEAR_MANY, NEAR_FEW, INNER_MANY, INNER_FEW, CROSS = range(LISTS)


def build_lists(geo, index, centre_ref, offsets_ref, counts_ref, meta_ref):
    first = index * geo.rows
    odd = index % 2 == 1
    meta_ref[geo.odd_at] = odd.astype(jnp.int32)
    lengths = [jnp.int32(0)] * LISTS
    for b in range(geo.batches):
        local = centre_ref[b] - first
        count = counts_ref[b]
        meta_ref[geo.local_at + b] = local
        meta_ref[geo.count_at + b] = count
        low = high = jnp.bool_(False)
        for k in range(geo.slots):
            offset = offsets_ref[k, b]
            meta_ref[geo.offsets_at + k * geo.batches + b] = offset
            row = local + offset
            low = low | ((k < count) & (row < 0))
            high = high | ((k < count) & (row >= geo.rows))
        cross = (odd & high) | (jnp.logical_not(odd) & low)
        near = (odd & low) | (jnp.logical_not(odd) & high)
        inner = jnp.logical_not(low | high)
        many = count > 2
        few = (count > 0) & jnp.logical_not(many)
        kinds = [kind & size for kind in (cross, near, inner) for size in (many, few)]
        for which, member in enumerate(kinds + [cross]):
            meta_ref[which * geo.list_size + lengths[which]] = b
            lengths[which] = lengths[which] + member.astype(jnp.int32)
    for which in range(LISTS):
        meta_ref[which * geo.list_size + lengths[which]] = geo.batches
        meta_ref[geo.lengths_at + which] = lengths[which]


def zone(geo, odd, cross):
    span = geo.span if cross else geo.own - geo.span
    return pl.ds(jnp.where(odd == cross, geo.own - span, 0), span)


def pack_kernel(
    geo, density_ref, centre_in, offsets_in, counts_in,
    near_ref, cross_ref, meta_ref, acc_ref,
    centre_ref, offsets_ref, counts_ref, sems,
):
    index = lax.axis_index("blk")
    odd = index % 2 == 1

    def copies(up, down):
        return [
            pltpu.make_async_copy(
                density_ref.at[pl.ds(start, count)], ref.at[pl.ds(place, count)], sems.at[side, i]
            )
            for side, (pack, ref) in enumerate(zip(geo.packs, (up, down)))
            for i, (start, place, count) in enumerate(pack)
        ]

    def start(up, down):
        for copy in copies(up, down):
            copy.start()

    by_parity(odd, start, near_ref, cross_ref)
    scalars = [
        pltpu.make_async_copy(*pair, sems.at[2, i])
        for i, pair in enumerate(
            ((centre_in, centre_ref), (offsets_in, offsets_ref), (counts_in, counts_ref))
        )
    ]
    for copy in scalars:
        copy.start()
    for where in (zone(geo, odd, False), pl.ds(geo.first_at, geo.halo)):
        acc_ref[where] = jnp.zeros_like(acc_ref[where])
    for copy in scalars:
        copy.wait()
    build_lists(geo, index, centre_ref, offsets_ref, counts_ref, meta_ref)
    for copy in copies(near_ref, cross_ref):
        copy.wait()


def listed(geo, meta_ref, which, skip=0):
    return lambda place: meta_ref[which * geo.list_size + skip + place]


def length_of(geo, meta_ref, which):
    return meta_ref[geo.lengths_at + which]


def groups_in(length):
    return (length + GROUP - 1) // GROUP


def inner_share(geo, meta_ref):
    room = BUDGET
    for which in (CROSS_MANY, CROSS_FEW):
        room = room - COST[which % 2] * groups_in(length_of(geo, meta_ref, which))
    room = room - COST[1] * groups_in(length_of(geo, meta_ref, NEAR_FEW))
    taken = []
    for near, inner in ((NEAR_MANY, INNER_MANY), (NEAR_FEW, INNER_FEW)):
        cost = COST[near % 2]
        near = length_of(geo, meta_ref, near)
        whole = near + length_of(geo, meta_ref, inner)
        groups = jnp.maximum(groups_in(near), jnp.maximum(room, 0) // cost)
        together = jnp.minimum(groups * GROUP, whole)
        room = room - cost * groups_in(together)
        taken.append(together - near)
        room = room + COST[1] * groups_in(length_of(geo, meta_ref, NEAR_FEW))
    waiting = jnp.where((lax.axis_index("blk") + 1) // 2 % 2 == 1, WAIT // COST[0] * GROUP, 0)
    rest = length_of(geo, meta_ref, INNER_MANY) - taken[0]
    return taken[0], taken[1], jnp.minimum(waiting, rest)


def each_group(length, get, body, size=GROUP):
    def step(i, carry):
        chosen = []
        for n in range(size):
            place = i * size + n
            there = place < length
            b = get(jnp.where(there, place, 0))
            chosen.append((jnp.where(there, b, 0), there))
        body(chosen)
        return carry

    lax.fori_loop(0, (length + size - 1) // size, step, 0)


def each_listed(geo, meta_ref, which, body, size=GROUP):
    each_group(length_of(geo, meta_ref, which), listed(geo, meta_ref, which), body, size)


class Slots:
    def __init__(self, geo, meta_ref, b, there, width):
        local = meta_ref[geo.local_at + b]
        count = jnp.where(there, meta_ref[geo.count_at + b], 0)
        self.offset = [meta_ref[geo.offsets_at + k * geo.batches + b] for k in range(width)]
        self.local = local
        self.row = [local + offset for offset in self.offset]
        self.live = [k < count for k in range(width)]
        self.own = [(row >= 0) & (row < geo.rows) for row in self.row]
        self.width = width


def panels(slots, ao_ref, b):
    return jnp.concatenate(
        [
            ao_ref[b, k] * jnp.where(slots.live[k], 1.0, 0.0).astype(ao_ref.dtype)
            for k in range(slots.width)
        ],
        axis=0,
    )


def gathered(tiles_ref, places):
    return jnp.concatenate(
        [jnp.concatenate([tiles_ref[place] for place in row], axis=1) for row in places], axis=0
    )


def potentials(xs, tiles, batches, kernel_ref):
    fs = [
        jnp.dot(t, x, preferred_element_type=jnp.float32).astype(jnp.bfloat16)
        for t, x in zip(tiles, xs)
    ]
    return [
        jnp.dot(f, kernel_ref[b], preferred_element_type=jnp.float32) for f, b in zip(fs, batches)
    ]


def outer_product(x, h):
    return lax.dot_general(x, h, (((1,), (1,)), ((), ())), preferred_element_type=jnp.float32)


def chain(xs, tiles, batches, kernel_ref, weights_ref):
    gs = potentials(xs, tiles, batches, kernel_ref)
    hs = [(g * weights_ref[pl.ds(b, 1), :]).astype(jnp.bfloat16) for g, b in zip(gs, batches)]
    return [outer_product(x, h) for x, h in zip(xs, hs)]


def scatter(part, target, nb, acc_ref):
    for k, row in enumerate(target):
        for j, place in enumerate(row):
            acc_ref[place] += part[k * nb : (k + 1) * nb, j * nb : (j + 1) * nb]


def add_whole(
    geo, chosen, width, meta_ref, tiles_ref, ao_ref, kernel_ref, weights_ref, acc_ref, halo_ref=None
):
    xs, tiles, targets = ([], [], [])
    for b, there in chosen:
        slots = Slots(geo, meta_ref, b, there, width)
        xs.append(panels(slots, ao_ref, b))
        rows, target = ([], [])
        for k in range(width):
            band = [slots.offset[j] - slots.offset[k] + geo.half for j in range(width)]
            own = slots.own[k]
            base = jnp.where(slots.live[k] & own, slots.row[k], 0) * geo.band
            row = jnp.concatenate([tiles_ref[base + o] for o in band], axis=1)
            if halo_ref is not None:
                away = slots.live[k] & jnp.logical_not(own)
                outside = jnp.where(away, geo.pick(geo.halo_base, 0, slots.row[k], 0), 0)
                other = [halo_ref[jnp.where(away, outside + o, 0)] for o in band]
                row = jnp.where(away, jnp.concatenate(other, axis=1), row)
                base = jnp.where(away, outside + geo.first_at, base)
            rows.append(row)
            target.append(
                [
                    jnp.where(slots.live[k] & slots.live[j], base + band[j], geo.spare)
                    for j in range(width)
                ]
            )
        tiles.append(jnp.concatenate(rows, axis=0))
        targets.append(target)
    parts = chain(xs, tiles, [b for b, _ in chosen], kernel_ref, weights_ref)
    for part, target in zip(parts, targets):
        scatter(part, target, ao_ref.shape[2], acc_ref)


def add_own(geo, chosen, width, meta_ref, tiles_ref, ao_ref, kernel_ref, weights_ref, acc_ref):
    xs, tiles, targets = ([], [], [])
    for b, there in chosen:
        slots = Slots(geo, meta_ref, b, there, width)
        xs.append(panels(slots, ao_ref, b))
        places, target = ([], [])
        for k in range(width):
            row = slots.row[k]
            band = [slots.offset[j] - slots.offset[k] + geo.half for j in range(width)]
            base = jnp.where(slots.own[k], row, 0) * geo.band
            places.append([base + o for o in band])
            base = geo.pick(geo.early_base, geo.early_at, row, base)
            target.append(
                [
                    jnp.where(
                        slots.live[k] & slots.live[j] & slots.own[j], base + band[j], geo.spare
                    )
                    for j in range(width)
                ]
            )
        tiles.append(gathered(tiles_ref, places))
        targets.append(target)
    parts = chain(xs, tiles, [b for b, _ in chosen], kernel_ref, weights_ref)
    for part, target in zip(parts, targets):
        scatter(part, target, ao_ref.shape[2], acc_ref)


def halo_rows(geo, meta_ref, slots):
    odd = meta_ref[geo.odd_at] == 1
    rows, places, present = ([], [], [])
    for i in range(geo.reach):
        row = jnp.where(odd, geo.rows + i, i - geo.reach)
        place, found = (jnp.int32(0), jnp.bool_(False))
        for k in range(slots.width):
            hit = slots.live[k] & (slots.row[k] == row)
            place = jnp.where(hit, k, place)
            found = found | hit
        rows.append(row)
        places.append(place)
        present.append(found)
    return rows, places, present


def add_corner(geo, chosen, meta_ref, halo_ref, ao_ref, kernel_ref, weights_ref, h_ref, total_ref):
    nb = ao_ref.shape[2]
    factor = lambda flag: jnp.where(flag, 1.0, 0.0)
    xs, sides, tiles, masks = ([], [], [], [])
    for b, there in chosen:
        slots = Slots(geo, meta_ref, b, there, geo.slots)
        rows, places, present = halo_rows(geo, meta_ref, slots)
        xs.append(panels(slots, ao_ref, b))
        sides.append(
            jnp.concatenate(
                [
                    ao_ref[b, place] * factor(found).astype(ao_ref.dtype)
                    for place, found in zip(places, present)
                ],
                axis=0,
            )
        )
        picked = []
        for row, found in zip(rows, present):
            base = geo.pick(geo.halo_base, 0, row, 0) - row + geo.half
            picked.append([jnp.where(found, base + column, 0) for column in slots.row])
        tiles.append(gathered(halo_ref, picked))
        masks.append([factor(found) for found in present])
    gs = potentials(xs, tiles, [b for b, _ in chosen], kernel_ref)
    hs = []
    for g, mask, (b, there) in zip(gs, masks, chosen):
        weights = weights_ref[pl.ds(b, 1), :]
        h = jnp.concatenate(
            [g[i * nb : (i + 1) * nb] * (weights * mask[i]) for i in range(geo.reach)], axis=0
        ).astype(jnp.bfloat16)
        h_ref[jnp.where(there, b, geo.batches)] = h
        hs.append(h)
    total_ref[...] += outer_product(
        jnp.concatenate(sides, axis=1), jnp.concatenate(hs, axis=1)
    )


def add_columns(geo, chosen, width, meta_ref, ao_ref, h_ref, acc_ref):
    parts, targets = ([], [])
    for b, there in chosen:
        slots = Slots(geo, meta_ref, b, there, width)
        rows, _, present = halo_rows(geo, meta_ref, slots)
        parts.append(outer_product(ao_ref[b, pl.ds(0, width)].reshape(-1, ao_ref.shape[3]), h_ref[b]))
        targets.append(
            [
                [
                    jnp.where(
                        slots.live[k] & slots.own[k] & found,
                        slots.row[k] * geo.band + row - slots.row[k] + geo.half,
                        geo.spare,
                    )
                    for row, found in zip(rows, present)
                ]
                for k in range(width)
            ]
        )
    for part, target in zip(parts, targets):
        scatter(part, target, ao_ref.shape[2], acc_ref)


def early_kernel(
    geo, meta_ref, tiles_ref, ao_ref, kernel_ref, weights_ref, acc_in, acc_ref, early_out
):
    odd = meta_ref[geo.odd_at] == 1
    for where in (zone(geo, odd, True), pl.ds(geo.early_at, geo.early), pl.ds(geo.spare, 1)):
        acc_ref[where] = jnp.zeros_like(acc_ref[where])
    refs = (meta_ref, tiles_ref, ao_ref, kernel_ref, weights_ref, acc_ref)
    for which, width in ((CROSS_MANY, geo.slots), (CROSS_FEW, 2)):
        each_listed(
            geo, meta_ref, which, lambda chosen, width=width: add_own(geo, chosen, width, *refs)
        )
    early_out[...] = acc_ref[pl.ds(geo.early_at, geo.early)].astype(early_out.dtype)


def near_kernel(
    geo, meta_ref, halo_ref, tiles_ref, ao_ref, kernel_ref, weights_ref, acc_in, acc_ref, first_out
):
    refs = (meta_ref, tiles_ref, ao_ref, kernel_ref, weights_ref, acc_ref, halo_ref)
    many, few, _ = inner_share(geo, meta_ref)
    for near, inner, taken, width in (
        (NEAR_MANY, INNER_MANY, many, geo.slots),
        (NEAR_FEW, INNER_FEW, few, 2),
    ):
        length = length_of(geo, meta_ref, near)
        begin = jnp.int32(inner * geo.list_size) - length

        def get(place, length=length, begin=begin, near=near):
            return meta_ref[jnp.where(place < length, near * geo.list_size, begin) + place]

        each_group(
            length + taken, get, lambda chosen, width=width: add_whole(geo, chosen, width, *refs)
        )
    first_out[...] = acc_ref[pl.ds(geo.first_at, geo.halo)].astype(first_out.dtype)


def waiting_kernel(
    geo, meta_ref, tiles_ref, ao_ref, kernel_ref, weights_ref, acc_in, acc_ref, done_ref
):
    refs = (meta_ref, tiles_ref, ao_ref, kernel_ref, weights_ref, acc_ref)
    many, _, waiting = inner_share(geo, meta_ref)
    each_group(
        waiting,
        listed(geo, meta_ref, INNER_MANY, many),
        lambda chosen: add_whole(geo, chosen, geo.slots, *refs),
    )
    done_ref[0] = 1


def late_kernel(
    geo, meta_ref, done_ref, halo_ref, ao_ref, kernel_ref, weights_ref, h_ref, late_out, total_ref
):
    nb = ao_ref.shape[2]
    total_ref[...] = jnp.zeros_like(total_ref)

    def work(chosen):
        add_corner(
            geo, chosen, meta_ref, halo_ref, ao_ref, kernel_ref, weights_ref, h_ref, total_ref
        )

    each_listed(geo, meta_ref, CROSS, work, LATE_GROUP)
    for i in range(geo.reach):
        for j in range(geo.reach):
            late_out[i * geo.reach + j] = total_ref[
                i * nb : (i + 1) * nb, j * nb : (j + 1) * nb
            ].astype(late_out.dtype)


def inner_kernel(
    geo, meta_ref, first_ref, tiles_ref, ao_ref, kernel_ref, weights_ref, h_ref, acc_in,
    acc_ref, out_ref, sems,
):
    odd = meta_ref[geo.odd_at] == 1
    refs = (meta_ref, tiles_ref, ao_ref, kernel_ref, weights_ref, acc_ref)
    many, few, waiting = inner_share(geo, meta_ref)
    for which, done, width in ((INNER_MANY, many + waiting, geo.slots), (INNER_FEW, few, 2)):
        each_group(
            length_of(geo, meta_ref, which) - done,
            listed(geo, meta_ref, which, done),
            lambda chosen, width=width: add_whole(geo, chosen, width, *refs),
        )

    def add_near(up, down):
        for start, place, count in geo.packs[0 if up else 1]:
            acc_ref[pl.ds(start, count)] += first_ref[pl.ds(place, count)].astype(jnp.float32)

    by_parity(odd, add_near, True, False)
    done = zone(geo, odd, False)
    copy = pltpu.make_async_copy(acc_ref.at[done], out_ref.at[done], sems.at[0])
    copy.start()
    for which, width in ((CROSS_MANY, geo.slots), (CROSS_FEW, 2)):
        each_listed(
            geo,
            meta_ref,
            which,
            lambda chosen, width=width: add_columns(
                geo, chosen, width, meta_ref, ao_ref, h_ref, acc_ref
            ),
        )

    def write_quiet(up, down):
        run_copies(
            [
                pltpu.make_async_copy(
                    acc_ref.at[pl.ds(start, count)], out_ref.at[pl.ds(start, count)], sems.at[1 + i]
                )
                for i, (start, count) in enumerate(geo.quiet[0 if up else 1])
            ]
        )

    by_parity(odd, write_quiet, True, False)
    copy.wait()


def finish_kernel(geo, meta_ref, early_ref, late_ref, acc_ref, out_in, out_ref, total, sems):
    def add(up, down):
        copies = []
        for packs, ref in ((geo.early_packs, early_ref), (geo.late_packs, late_ref)):
            for start, place, count in packs[0 if up else 1]:
                spot = pl.ds(len(copies) * geo.band, count)
                total[spot] = acc_ref[pl.ds(start, count)] + ref[pl.ds(place, count)].astype(
                    jnp.float32
                )
                copy = pltpu.make_async_copy(
                    total.at[spot], out_ref.at[pl.ds(start, count)], sems.at[len(copies)]
                )
                copy.start()
                copies.append(copy)
        for copy in copies:
            copy.wait()

    by_parity(meta_ref[geo.odd_at] == 1, add, False, True)


def call(kernel, out_shape, in_specs, out_specs, scratch, aliases=None, cost=None):
    return pl.pallas_call(
        kernel,
        out_shape=out_shape,
        in_specs=in_specs,
        out_specs=out_specs,
        scratch_shapes=scratch,
        input_output_aliases=aliases or {},
        cost_estimate=cost,
        compiler_params=pltpu.CompilerParams(vmem_limit_bytes=16 * MIB),
    )


def to_first(x, size):
    pairs = [(i, i + 1) for i in range(0, size - 1, 2)]
    got = lax.ppermute(x, "blk", pairs + [(j, i) for i, j in pairs])
    return pltpu.with_memory_space_constraint(got, pltpu.VMEM)


def to_second(x, size):
    pairs = [(i, i + 1) for i in range(1, size - 1, 2)]
    got = lax.ppermute(x, "blk", pairs + [(j, i) for i, j in pairs])
    return pltpu.with_memory_space_constraint(got, pltpu.VMEM)


def local(density, ao_values, kernel, grid_weights, centre, sig_offsets, counts):
    rows, band, nb, _ = density.shape
    batches, slots, _, pts = ao_values.shape
    size = lax.axis_size("blk")
    geo = Geometry(rows, band, batches, slots)
    in_hbm = lambda x: pltpu.with_memory_space_constraint(x, pltpu.HBM)
    tiles = density.reshape(geo.own, nb, nb)
    pack = lambda count: pltpu.VMEM((count, nb, nb), jnp.bfloat16)
    dma = pltpu.SemaphoreType.DMA
    acc_type = pltpu.VMEM((geo.spare + 1, nb, nb), jnp.float32)

    near_halo, cross_halo, meta, acc = call(
        functools.partial(pack_kernel, geo),
        (pack(geo.halo),) * 2 + (pltpu.SMEM((geo.meta_size,), jnp.int32), acc_type),
        [ANY_SPEC] * 4,
        (VMEM_SPEC,) * 2 + (SMEM_SPEC, VMEM_SPEC),
        [
            pltpu.SMEM((batches,), jnp.int32),
            pltpu.SMEM((slots, batches), jnp.int32),
            pltpu.SMEM((batches,), jnp.int32),
            dma((3, max(geo.reach, 3))),
        ],
        cost=pl.CostEstimate(flops=10**10, bytes_accessed=10**8, transcendentals=0),
    )(in_hbm(tiles), in_hbm(centre), in_hbm(sig_offsets.T), in_hbm(counts))
    cross_halo = to_second(cross_halo, size)
    near_halo = to_first(near_halo, size)

    panel = (tiles, ao_values, kernel, grid_weights)
    acc, early = call(
        functools.partial(early_kernel, geo),
        (acc_type, pack(geo.early)),
        [SMEM_SPEC] + [VMEM_SPEC] * 5,
        (VMEM_SPEC,) * 2,
        [],
        {5: 0},
    )(meta, *panel, acc)
    early = to_second(early, size)

    acc, first = call(
        functools.partial(near_kernel, geo),
        (acc_type, pack(geo.halo)),
        [SMEM_SPEC] + [VMEM_SPEC] * 6,
        (VMEM_SPEC,) * 2,
        [],
        {6: 0},
    )(meta, near_halo, *panel, acc)
    first = to_first(first, size)

    acc, done = call(
        functools.partial(waiting_kernel, geo),
        (acc_type, pltpu.SMEM((1,), jnp.int32)),
        [SMEM_SPEC] + [VMEM_SPEC] * 5,
        (VMEM_SPEC, SMEM_SPEC),
        [],
        {5: 0},
    )(meta, *panel, acc)

    h_type = pltpu.VMEM((batches + 1, geo.reach * nb, pts), jnp.bfloat16)
    h, late = call(
        functools.partial(late_kernel, geo),
        (h_type, pack(geo.late)),
        [SMEM_SPEC] * 2 + [VMEM_SPEC] * 4,
        (VMEM_SPEC,) * 2,
        [pltpu.VMEM((geo.reach * nb, geo.reach * nb), jnp.float32)],
    )(meta, done, cross_halo, *panel[1:])
    late = to_second(late, size)

    whole = jax.ShapeDtypeStruct((geo.own, nb, nb), jnp.float32)
    acc, out = call(
        functools.partial(inner_kernel, geo),
        (acc_type, whole),
        [SMEM_SPEC] + [VMEM_SPEC] * 7,
        (VMEM_SPEC, ANY_SPEC),
        [dma((1 + max(len(runs) for runs in geo.quiet),))],
        {7: 0},
    )(meta, first, *panel, h, acc)

    parts = 2 * geo.reach
    out = call(
        functools.partial(finish_kernel, geo),
        whole,
        [SMEM_SPEC] + [VMEM_SPEC] * 3 + [ANY_SPEC],
        ANY_SPEC,
        [pltpu.VMEM((parts * band, nb, nb), jnp.float32), dma((parts,))],
        {4: 0},
    )(meta, early, late, acc, out)
    return out.reshape(rows, band, nb, nb)


def solution(mesh):
    placed = (
        P(("groups", "blk"), None, None, None),
        P(("groups", "blk"), None, None, None),
        P(("groups", "blk"), None, None),
        P(("groups", "blk"), None),
        P(("groups", "blk")),
        P(("groups", "blk"), None),
        P(("groups", "blk")),
    )
    return jax.shard_map(
        local,
        mesh=mesh,
        in_specs=placed,
        out_specs=P(("groups", "blk"), None, None, None),
        check_vma=False,
    )
```

```python
import functools

import jax
import jax.numpy as jnp
from jax import lax
from jax.experimental import pallas as pl
from jax.experimental.pallas import tpu as pltpu
from jax.sharding import PartitionSpec as P

MIB = 1 << 20
GROUP = 2
LATE_GROUP = 4
LISTS = 7
BUDGET = 43
WAIT = 18
COST = (10, 7)
SMEM_SPEC = pl.BlockSpec(memory_space=pltpu.SMEM)
VMEM_SPEC = pl.BlockSpec(memory_space=pltpu.VMEM)
ANY_SPEC = pl.BlockSpec(memory_space=pl.ANY)


class Geometry:
    def __init__(self, rows, band, batches, slots):
        self.rows, self.band, self.batches, self.slots = rows, band, batches, slots
        self.half = half = (band - 1) // 2
        self.reach = reach = half // 2
        self.own = rows * band
        low = [(-m, reach + m, band) for m in range(reach, 0, -1)]
        high = [(rows + m, 0, 3 * reach - m) for m in range(reach)]
        self.halo = sum(stop - start for _, start, stop in low)
        low_cut = [half - row for row, _, _ in low]
        high_cut = [rows - row + half for row, _, _ in high]
        early = (
            [(row, cut, stop) for (row, _, stop), cut in zip(low, low_cut)],
            [(row, start, cut) for (row, start, _), cut in zip(high, high_cut)],
        )
        late = (
            [(row, start, cut) for (row, start, _), cut in zip(low, low_cut)],
            [(row, cut, stop) for (row, _, stop), cut in zip(high, high_cut)],
        )
        self.early = sum(stop - start for _, start, stop in early[0])
        self.late = self.halo - self.early
        self.first_at = self.own
        self.early_at = self.own + self.halo
        self.spare = self.early_at + self.early
        self.halo_base = self.bases((low, high))
        self.early_base = self.bases(early)
        shifts = (rows, -rows)
        self.packs = [self.places(*pair) for pair in zip((low, high), shifts)]
        self.early_packs = [self.places(*pair) for pair in zip(early, shifts)]
        self.late_packs = [self.places(*pair) for pair in zip(late, shifts)]
        self.span = min(2 * reach, rows) * band
        self.quiet = [
            self.others(self.packs[1], 0, self.span),
            self.others(self.packs[0], self.own - self.span, self.own),
        ]
        self.list_size = batches + 2
        self.lengths_at = LISTS * self.list_size
        self.local_at = self.lengths_at + LISTS
        self.count_at = self.local_at + batches
        self.offsets_at = self.count_at + batches
        self.odd_at = self.offsets_at + slots * batches
        self.meta_size = self.odd_at + 1

    def bases(self, sides):
        found = {}
        for segments in sides:
            place = 0
            for row, start, stop in segments:
                found[row] = place - start
                place += stop - start
        return found

    def places(self, segments, shift):
        pack, place = ([], 0)
        for row, start, stop in segments:
            pack.append(((row + shift) * self.band + start, place, stop - start))
            place += stop - start
        return pack

    def others(self, pack, begin, end):
        touched = set()
        for start, _, count in pack:
            touched.update(range(start, start + count))
        runs = []
        for index in range(begin, end):
            if index in touched:
                continue
            if runs and sum(runs[-1]) == index:
                runs[-1] = (runs[-1][0], runs[-1][1] + 1)
            else:
                runs.append((index, 1))
        return runs

    def pick(self, bases, shift, row, otherwise):
        value = otherwise
        for at, base in bases.items():
            value = jnp.where(row == at, base + shift, value)
        return value


def run_copies(copies):
    for copy in copies:
        copy.start()
    for copy in copies:
        copy.wait()


def by_parity(odd, body, first, second):
    @pl.when(jnp.logical_not(odd))
    def _():
        body(first, second)

    @pl.when(odd)
    def _():
        body(second, first)


CROSS_MANY, CROSS_FEW, NEAR_MANY, NEAR_FEW, INNER_MANY, INNER_FEW, CROSS = range(LISTS)


def build_lists(geo, index, centre_ref, offsets_ref, counts_ref, meta_ref):
    first = index * geo.rows
    odd = index % 2 == 1
    meta_ref[geo.odd_at] = odd.astype(jnp.int32)
    lengths = [jnp.int32(0)] * LISTS
    for b in range(geo.batches):
        local = centre_ref[b] - first
        count = counts_ref[b]
        meta_ref[geo.local_at + b] = local
        meta_ref[geo.count_at + b] = count
        low = high = jnp.bool_(False)
        for k in range(geo.slots):
            offset = offsets_ref[k, b]
            meta_ref[geo.offsets_at + k * geo.batches + b] = offset
            row = local + offset
            low = low | ((k < count) & (row < 0))
            high = high | ((k < count) & (row >= geo.rows))
        cross = (odd & high) | (jnp.logical_not(odd) & low)
        near = (odd & low) | (jnp.logical_not(odd) & high)
        inner = jnp.logical_not(low | high)
        many = count > 2
        few = (count > 0) & jnp.logical_not(many)
        kinds = [kind & size for kind in (cross, near, inner) for size in (many, few)]
        for which, member in enumerate(kinds + [cross]):
            meta_ref[which * geo.list_size + lengths[which]] = b
            lengths[which] = lengths[which] + member.astype(jnp.int32)
    for which in range(LISTS):
        meta_ref[which * geo.list_size + lengths[which]] = geo.batches
        meta_ref[geo.lengths_at + which] = lengths[which]


def zone(geo, odd, cross):
    span = geo.span if cross else geo.own - geo.span
    return pl.ds(jnp.where(odd == cross, geo.own - span, 0), span)


def pack_kernel(
    geo, density_ref, centre_in, offsets_in, counts_in,
    near_ref, cross_ref, meta_ref, acc_ref,
    centre_ref, offsets_ref, counts_ref, sems,
):
    index = lax.axis_index("blk")
    odd = index % 2 == 1

    def copies(up, down):
        return [
            pltpu.make_async_copy(
                density_ref.at[pl.ds(start, count)], ref.at[pl.ds(place, count)], sems.at[side, i]
            )
            for side, (pack, ref) in enumerate(zip(geo.packs, (up, down)))
            for i, (start, place, count) in enumerate(pack)
        ]

    def start(up, down):
        for copy in copies(up, down):
            copy.start()

    by_parity(odd, start, near_ref, cross_ref)
    scalars = [
        pltpu.make_async_copy(*pair, sems.at[2, i])
        for i, pair in enumerate(
            ((centre_in, centre_ref), (offsets_in, offsets_ref), (counts_in, counts_ref))
        )
    ]
    for copy in scalars:
        copy.start()
    for where in (zone(geo, odd, False), pl.ds(geo.first_at, geo.halo)):
        acc_ref[where] = jnp.zeros_like(acc_ref[where])
    for copy in scalars:
        copy.wait()
    build_lists(geo, index, centre_ref, offsets_ref, counts_ref, meta_ref)
    for copy in copies(near_ref, cross_ref):
        copy.wait()


def group_count(geo, meta_ref, which):
    return (meta_ref[geo.lengths_at + which] + GROUP - 1) // GROUP


def waits():
    return (lax.axis_index("blk") + 1) // 2 % 2 == 1


def inner_share(geo, meta_ref):
    before = BUDGET
    for which in (CROSS_MANY, CROSS_FEW, NEAR_MANY, NEAR_FEW):
        before = before - COST[which % 2] * group_count(geo, meta_ref, which)
    waiting = jnp.where(waits(), WAIT, 0)
    share = []
    for which in (INNER_MANY, INNER_FEW):
        cost, count = COST[which % 2], group_count(geo, meta_ref, which)
        first = jnp.minimum(jnp.maximum(before, 0) // cost, count)
        second = jnp.minimum(jnp.maximum(waiting, 0) // cost, count - first)
        before = before - cost * first
        waiting = waiting - cost * second
        share.append((0, first, first + second, count))
    return share


def inner_part(geo, meta_ref, stage, refs):
    for which, width, bounds in zip(
        (INNER_MANY, INNER_FEW), (geo.slots, 2), inner_share(geo, meta_ref)
    ):
        each_group(
            geo,
            meta_ref,
            which,
            lambda chosen, width=width: add_whole(geo, chosen, width, *refs),
            begin=bounds[stage],
            end=bounds[stage + 1],
        )


def each_group(geo, meta_ref, which, body, size=GROUP, begin=0, end=None):
    length = meta_ref[geo.lengths_at + which]

    def step(i, carry):
        chosen = []
        for n in range(size):
            place = i * size + n
            there = place < length
            b = meta_ref[which * geo.list_size + jnp.minimum(place, length)]
            chosen.append((jnp.where(there, b, 0), there))
        body(chosen)
        return carry

    lax.fori_loop(begin, (length + size - 1) // size if end is None else end, step, 0)


class Slots:
    def __init__(self, geo, meta_ref, b, there, width):
        local = meta_ref[geo.local_at + b]
        count = jnp.where(there, meta_ref[geo.count_at + b], 0)
        self.offset = [meta_ref[geo.offsets_at + k * geo.batches + b] for k in range(width)]
        self.local = local
        self.row = [local + offset for offset in self.offset]
        self.live = [k < count for k in range(width)]
        self.own = [(row >= 0) & (row < geo.rows) for row in self.row]
        self.width = width


def panels(slots, ao_ref, b):
    return jnp.concatenate(
        [
            ao_ref[b, k] * jnp.where(slots.live[k], 1.0, 0.0).astype(ao_ref.dtype)
            for k in range(slots.width)
        ],
        axis=0,
    )


def gathered(tiles_ref, places):
    return jnp.concatenate(
        [jnp.concatenate([tiles_ref[place] for place in row], axis=1) for row in places], axis=0
    )


def potentials(xs, tiles, batches, kernel_ref):
    fs = [
        jnp.dot(t, x, preferred_element_type=jnp.float32).astype(jnp.bfloat16)
        for t, x in zip(tiles, xs)
    ]
    return [
        jnp.dot(f, kernel_ref[b], preferred_element_type=jnp.float32) for f, b in zip(fs, batches)
    ]


def outer_product(x, h):
    return lax.dot_general(x, h, (((1,), (1,)), ((), ())), preferred_element_type=jnp.float32)


def chain(xs, tiles, batches, kernel_ref, weights_ref):
    gs = potentials(xs, tiles, batches, kernel_ref)
    hs = [(g * weights_ref[pl.ds(b, 1), :]).astype(jnp.bfloat16) for g, b in zip(gs, batches)]
    return [outer_product(x, h) for x, h in zip(xs, hs)]


def scatter(part, target, nb, acc_ref):
    for k, row in enumerate(target):
        for j, place in enumerate(row):
            acc_ref[place] += part[k * nb : (k + 1) * nb, j * nb : (j + 1) * nb]


def add_whole(
    geo, chosen, width, meta_ref, tiles_ref, ao_ref, kernel_ref, weights_ref, acc_ref, halo_ref=None
):
    xs, tiles, targets = ([], [], [])
    for b, there in chosen:
        slots = Slots(geo, meta_ref, b, there, width)
        xs.append(panels(slots, ao_ref, b))
        rows, target = ([], [])
        for k in range(width):
            band = [slots.offset[j] - slots.offset[k] + geo.half for j in range(width)]
            own = slots.own[k]
            base = jnp.where(slots.live[k] & own, slots.row[k], 0) * geo.band
            row = jnp.concatenate([tiles_ref[base + o] for o in band], axis=1)
            if halo_ref is not None:
                away = slots.live[k] & jnp.logical_not(own)
                outside = jnp.where(away, geo.pick(geo.halo_base, 0, slots.row[k], 0), 0)
                other = [halo_ref[jnp.where(away, outside + o, 0)] for o in band]
                row = jnp.where(away, jnp.concatenate(other, axis=1), row)
                base = jnp.where(away, outside + geo.first_at, base)
            rows.append(row)
            target.append(
                [
                    jnp.where(slots.live[k] & slots.live[j], base + band[j], geo.spare)
                    for j in range(width)
                ]
            )
        tiles.append(jnp.concatenate(rows, axis=0))
        targets.append(target)
    parts = chain(xs, tiles, [b for b, _ in chosen], kernel_ref, weights_ref)
    for part, target in zip(parts, targets):
        scatter(part, target, ao_ref.shape[2], acc_ref)


def add_own(geo, chosen, width, meta_ref, tiles_ref, ao_ref, kernel_ref, weights_ref, acc_ref):
    xs, tiles, targets = ([], [], [])
    for b, there in chosen:
        slots = Slots(geo, meta_ref, b, there, width)
        xs.append(panels(slots, ao_ref, b))
        places, target = ([], [])
        for k in range(width):
            row = slots.row[k]
            band = [slots.offset[j] - slots.offset[k] + geo.half for j in range(width)]
            base = jnp.where(slots.own[k], row, 0) * geo.band
            places.append([base + o for o in band])
            base = geo.pick(geo.early_base, geo.early_at, row, base)
            target.append(
                [
                    jnp.where(
                        slots.live[k] & slots.live[j] & slots.own[j], base + band[j], geo.spare
                    )
                    for j in range(width)
                ]
            )
        tiles.append(gathered(tiles_ref, places))
        targets.append(target)
    parts = chain(xs, tiles, [b for b, _ in chosen], kernel_ref, weights_ref)
    for part, target in zip(parts, targets):
        scatter(part, target, ao_ref.shape[2], acc_ref)


def halo_rows(geo, meta_ref, slots):
    odd = meta_ref[geo.odd_at] == 1
    rows, places, present = ([], [], [])
    for i in range(geo.reach):
        row = jnp.where(odd, geo.rows + i, i - geo.reach)
        place, found = (jnp.int32(0), jnp.bool_(False))
        for k in range(slots.width):
            hit = slots.live[k] & (slots.row[k] == row)
            place = jnp.where(hit, k, place)
            found = found | hit
        rows.append(row)
        places.append(place)
        present.append(found)
    return rows, places, present


def add_corner(geo, chosen, meta_ref, halo_ref, ao_ref, kernel_ref, weights_ref, h_ref, total_ref):
    nb = ao_ref.shape[2]
    factor = lambda flag: jnp.where(flag, 1.0, 0.0)
    xs, sides, tiles, masks = ([], [], [], [])
    for b, there in chosen:
        slots = Slots(geo, meta_ref, b, there, geo.slots)
        rows, places, present = halo_rows(geo, meta_ref, slots)
        xs.append(panels(slots, ao_ref, b))
        sides.append(
            jnp.concatenate(
                [
                    ao_ref[b, place] * factor(found).astype(ao_ref.dtype)
                    for place, found in zip(places, present)
                ],
                axis=0,
            )
        )
        picked = []
        for row, found in zip(rows, present):
            base = geo.pick(geo.halo_base, 0, row, 0) - row + geo.half
            picked.append([jnp.where(found, base + column, 0) for column in slots.row])
        tiles.append(gathered(halo_ref, picked))
        masks.append([factor(found) for found in present])
    gs = potentials(xs, tiles, [b for b, _ in chosen], kernel_ref)
    hs = []
    for g, mask, (b, there) in zip(gs, masks, chosen):
        weights = weights_ref[pl.ds(b, 1), :]
        h = jnp.concatenate(
            [g[i * nb : (i + 1) * nb] * (weights * mask[i]) for i in range(geo.reach)], axis=0
        ).astype(jnp.bfloat16)
        h_ref[jnp.where(there, b, geo.batches)] = h
        hs.append(h)
    total_ref[...] += outer_product(
        jnp.concatenate(sides, axis=1), jnp.concatenate(hs, axis=1)
    )


def add_columns(geo, chosen, width, meta_ref, ao_ref, h_ref, acc_ref):
    parts, targets = ([], [])
    for b, there in chosen:
        slots = Slots(geo, meta_ref, b, there, width)
        rows, _, present = halo_rows(geo, meta_ref, slots)
        parts.append(outer_product(ao_ref[b, pl.ds(0, width)].reshape(-1, ao_ref.shape[3]), h_ref[b]))
        targets.append(
            [
                [
                    jnp.where(
                        slots.live[k] & slots.own[k] & found,
                        slots.row[k] * geo.band + row - slots.row[k] + geo.half,
                        geo.spare,
                    )
                    for row, found in zip(rows, present)
                ]
                for k in range(width)
            ]
        )
    for part, target in zip(parts, targets):
        scatter(part, target, ao_ref.shape[2], acc_ref)


def early_kernel(
    geo, meta_ref, tiles_ref, ao_ref, kernel_ref, weights_ref, acc_in, acc_ref, early_out
):
    odd = meta_ref[geo.odd_at] == 1
    for where in (zone(geo, odd, True), pl.ds(geo.early_at, geo.early), pl.ds(geo.spare, 1)):
        acc_ref[where] = jnp.zeros_like(acc_ref[where])
    refs = (meta_ref, tiles_ref, ao_ref, kernel_ref, weights_ref, acc_ref)
    for which, width in ((CROSS_MANY, geo.slots), (CROSS_FEW, 2)):
        each_group(
            geo, meta_ref, which, lambda chosen, width=width: add_own(geo, chosen, width, *refs)
        )
    early_out[...] = acc_ref[pl.ds(geo.early_at, geo.early)].astype(early_out.dtype)


def near_kernel(
    geo, meta_ref, halo_ref, tiles_ref, ao_ref, kernel_ref, weights_ref, acc_in, acc_ref, first_out
):
    refs = (meta_ref, tiles_ref, ao_ref, kernel_ref, weights_ref, acc_ref, halo_ref)
    for which, width in ((NEAR_MANY, geo.slots), (NEAR_FEW, 2)):
        each_group(
            geo, meta_ref, which, lambda chosen, width=width: add_whole(geo, chosen, width, *refs)
        )
    first_out[...] = acc_ref[pl.ds(geo.first_at, geo.halo)].astype(first_out.dtype)
    inner_part(geo, meta_ref, 0, refs[:-1])


def waiting_kernel(
    geo, meta_ref, tiles_ref, ao_ref, kernel_ref, weights_ref, acc_in, acc_ref, done_ref
):
    inner_part(geo, meta_ref, 1, (meta_ref, tiles_ref, ao_ref, kernel_ref, weights_ref, acc_ref))
    done_ref[0] = 1


def late_kernel(
    geo, meta_ref, done_ref, halo_ref, ao_ref, kernel_ref, weights_ref, h_ref, late_out, total_ref
):
    nb = ao_ref.shape[2]
    total_ref[...] = jnp.zeros_like(total_ref)

    def work(chosen):
        add_corner(
            geo, chosen, meta_ref, halo_ref, ao_ref, kernel_ref, weights_ref, h_ref, total_ref
        )

    groups = (meta_ref[geo.lengths_at + CROSS] + 1) // LATE_GROUP
    each_group(geo, meta_ref, CROSS, work, size=LATE_GROUP, end=groups)
    each_group(geo, meta_ref, CROSS, work, size=LATE_GROUP // 2, begin=2 * groups)
    for i in range(geo.reach):
        for j in range(geo.reach):
            late_out[i * geo.reach + j] = total_ref[
                i * nb : (i + 1) * nb, j * nb : (j + 1) * nb
            ].astype(late_out.dtype)


def inner_kernel(
    geo, meta_ref, first_ref, tiles_ref, ao_ref, kernel_ref, weights_ref, h_ref, acc_in,
    acc_ref, out_ref, sems,
):
    odd = meta_ref[geo.odd_at] == 1
    refs = (meta_ref, tiles_ref, ao_ref, kernel_ref, weights_ref, acc_ref)
    inner_part(geo, meta_ref, 2, refs)

    def add_near(up, down):
        for start, place, count in geo.packs[0 if up else 1]:
            acc_ref[pl.ds(start, count)] += first_ref[pl.ds(place, count)].astype(jnp.float32)

    by_parity(odd, add_near, True, False)
    done = zone(geo, odd, False)
    copy = pltpu.make_async_copy(acc_ref.at[done], out_ref.at[done], sems.at[0])
    copy.start()
    for which, width in ((CROSS_MANY, geo.slots), (CROSS_FEW, 2)):
        each_group(
            geo,
            meta_ref,
            which,
            lambda chosen, width=width: add_columns(
                geo, chosen, width, meta_ref, ao_ref, h_ref, acc_ref
            ),
        )

    def write_quiet(up, down):
        run_copies(
            [
                pltpu.make_async_copy(
                    acc_ref.at[pl.ds(start, count)], out_ref.at[pl.ds(start, count)], sems.at[1 + i]
                )
                for i, (start, count) in enumerate(geo.quiet[0 if up else 1])
            ]
        )

    by_parity(odd, write_quiet, True, False)
    copy.wait()


def finish_cross(geo, odd, parts, acc_ref, out_ref, total, sems):
    def add(up, down):
        copies = []
        for packs, ref in parts:
            for start, place, count in packs[0 if up else 1]:
                spot = pl.ds(len(copies) * geo.band, count)
                total[spot] = acc_ref[pl.ds(start, count)] + ref[pl.ds(place, count)].astype(
                    jnp.float32
                )
                copy = pltpu.make_async_copy(
                    total.at[spot], out_ref.at[pl.ds(start, count)], sems.at[len(copies)]
                )
                copy.start()
                copies.append(copy)
        for copy in copies:
            copy.wait()

    by_parity(odd, add, False, True)


def early_join_kernel(geo, meta_ref, early_ref, acc_ref, out_in, out_ref, total, sems):
    @pl.when(waits())
    def _():
        odd = meta_ref[geo.odd_at] == 1
        finish_cross(geo, odd, ((geo.early_packs, early_ref),), acc_ref, out_ref, total, sems)


def finish_kernel(geo, meta_ref, late_ref, early_ref, acc_ref, out_in, out_ref, total, sems):
    odd = meta_ref[geo.odd_at] == 1
    late = (geo.late_packs, late_ref)

    @pl.when(waits())
    def _():
        finish_cross(geo, odd, (late,), acc_ref, out_ref, total, sems)

    @pl.when(jnp.logical_not(waits()))
    def _():
        parts = ((geo.early_packs, early_ref), late)
        finish_cross(geo, odd, parts, acc_ref, out_ref, total, sems)


def call(kernel, out_shape, in_specs, out_specs, scratch, aliases=None, cost=None):
    return pl.pallas_call(
        kernel,
        out_shape=out_shape,
        in_specs=in_specs,
        out_specs=out_specs,
        scratch_shapes=scratch,
        input_output_aliases=aliases or {},
        cost_estimate=cost,
        compiler_params=pltpu.CompilerParams(vmem_limit_bytes=16 * MIB),
    )


def to_first(x, size):
    pairs = [(i, i + 1) for i in range(0, size - 1, 2)]
    got = lax.ppermute(x, "blk", pairs + [(j, i) for i, j in pairs])
    return pltpu.with_memory_space_constraint(got, pltpu.VMEM)


def to_second(x, size):
    pairs = [(i, i + 1) for i in range(1, size - 1, 2)]
    got = lax.ppermute(x, "blk", pairs + [(j, i) for i, j in pairs])
    return pltpu.with_memory_space_constraint(got, pltpu.VMEM)


def local(density, ao_values, kernel, grid_weights, centre, sig_offsets, counts):
    rows, band, nb, _ = density.shape
    batches, slots, _, pts = ao_values.shape
    size = lax.axis_size("blk")
    geo = Geometry(rows, band, batches, slots)
    in_hbm = lambda x: pltpu.with_memory_space_constraint(x, pltpu.HBM)
    tiles = density.reshape(geo.own, nb, nb)
    pack = lambda count: pltpu.VMEM((count, nb, nb), jnp.bfloat16)
    dma = pltpu.SemaphoreType.DMA
    acc_type = pltpu.VMEM((geo.spare + 1, nb, nb), jnp.float32)

    near_halo, cross_halo, meta, acc = call(
        functools.partial(pack_kernel, geo),
        (pack(geo.halo),) * 2 + (pltpu.SMEM((geo.meta_size,), jnp.int32), acc_type),
        [ANY_SPEC] * 4,
        (VMEM_SPEC,) * 2 + (SMEM_SPEC, VMEM_SPEC),
        [
            pltpu.SMEM((batches,), jnp.int32),
            pltpu.SMEM((slots, batches), jnp.int32),
            pltpu.SMEM((batches,), jnp.int32),
            dma((3, max(geo.reach, 3))),
        ],
        cost=pl.CostEstimate(flops=10**10, bytes_accessed=10**8, transcendentals=0),
    )(in_hbm(tiles), in_hbm(centre), in_hbm(sig_offsets.T), in_hbm(counts))
    cross_halo = to_second(cross_halo, size)
    near_halo = to_first(near_halo, size)

    panel = (tiles, ao_values, kernel, grid_weights)
    acc, early = call(
        functools.partial(early_kernel, geo),
        (acc_type, pack(geo.early)),
        [SMEM_SPEC] + [VMEM_SPEC] * 5,
        (VMEM_SPEC,) * 2,
        [],
        {5: 0},
    )(meta, *panel, acc)
    early = to_second(early, size)

    acc, first = call(
        functools.partial(near_kernel, geo),
        (acc_type, pack(geo.halo)),
        [SMEM_SPEC] + [VMEM_SPEC] * 6,
        (VMEM_SPEC,) * 2,
        [],
        {6: 0},
    )(meta, near_halo, *panel, acc)
    first = to_first(first, size)

    acc, done = call(
        functools.partial(waiting_kernel, geo),
        (acc_type, pltpu.SMEM((1,), jnp.int32)),
        [SMEM_SPEC] + [VMEM_SPEC] * 5,
        (VMEM_SPEC, SMEM_SPEC),
        [],
        {5: 0},
    )(meta, *panel, acc)

    h_type = pltpu.VMEM((batches + 1, geo.reach * nb, pts), jnp.bfloat16)
    h, late = call(
        functools.partial(late_kernel, geo),
        (h_type, pack(geo.late)),
        [SMEM_SPEC] * 2 + [VMEM_SPEC] * 4,
        (VMEM_SPEC,) * 2,
        [pltpu.VMEM((geo.reach * nb, geo.reach * nb), jnp.float32)],
    )(meta, done, cross_halo, *panel[1:])
    late = to_second(late, size)

    whole = jax.ShapeDtypeStruct((geo.own, nb, nb), jnp.float32)
    acc, out = call(
        functools.partial(inner_kernel, geo),
        (acc_type, whole),
        [SMEM_SPEC] + [VMEM_SPEC] * 7,
        (VMEM_SPEC, ANY_SPEC),
        [dma((1 + max(len(runs) for runs in geo.quiet),))],
        {7: 0},
    )(meta, first, *panel, h, acc)

    for kernel_of, got, parts in (
        (early_join_kernel, (early,), geo.reach),
        (finish_kernel, (late, early), 2 * geo.reach),
    ):
        out = call(
            functools.partial(kernel_of, geo),
            whole,
            [SMEM_SPEC] + [VMEM_SPEC] * (len(got) + 1) + [ANY_SPEC],
            ANY_SPEC,
            [pltpu.VMEM((parts * band, nb, nb), jnp.float32), dma((parts,))],
            {len(got) + 2: 0},
        )(meta, *got, acc, out)
    return out.reshape(rows, band, nb, nb)


def solution(mesh):
    placed = (
        P(("groups", "blk"), None, None, None),
        P(("groups", "blk"), None, None, None),
        P(("groups", "blk"), None, None),
        P(("groups", "blk"), None),
        P(("groups", "blk")),
        P(("groups", "blk"), None),
        P(("groups", "blk")),
    )
    return jax.shard_map(
        local,
        mesh=mesh,
        in_specs=placed,
        out_specs=P(("groups", "blk"), None, None, None),
        check_vma=False,
    )
```

```python
import functools

import jax
import jax.numpy as jnp
from jax import lax
from jax.experimental import pallas as pl
from jax.experimental.pallas import tpu as pltpu
from jax.sharding import PartitionSpec as P

MIB = 1 << 20
GROUP = 2
LATE_GROUP = 4
LISTS = 7
BUDGET = 43
WAIT = 18
COST = (10, 7)
SMEM_SPEC = pl.BlockSpec(memory_space=pltpu.SMEM)
VMEM_SPEC = pl.BlockSpec(memory_space=pltpu.VMEM)
ANY_SPEC = pl.BlockSpec(memory_space=pl.ANY)


class Geometry:
    def __init__(self, rows, band, batches, slots):
        self.rows, self.band, self.batches, self.slots = rows, band, batches, slots
        self.half = half = (band - 1) // 2
        self.reach = reach = half // 2
        self.own = rows * band
        low = [(-m, reach + m, band) for m in range(reach, 0, -1)]
        high = [(rows + m, 0, 3 * reach - m) for m in range(reach)]
        self.halo = sum(stop - start for _, start, stop in low)
        low_cut = [half - row for row, _, _ in low]
        high_cut = [rows - row + half for row, _, _ in high]
        early = (
            [(row, cut, stop) for (row, _, stop), cut in zip(low, low_cut)],
            [(row, start, cut) for (row, start, _), cut in zip(high, high_cut)],
        )
        late = (
            [(row, start, cut) for (row, start, _), cut in zip(low, low_cut)],
            [(row, cut, stop) for (row, _, stop), cut in zip(high, high_cut)],
        )
        self.early = sum(stop - start for _, start, stop in early[0])
        self.late = self.halo - self.early
        self.first_at = self.own
        self.early_at = self.own + self.halo
        self.spare = self.early_at + self.early
        self.halo_base = self.bases((low, high))
        self.early_base = self.bases(early)
        shifts = (rows, -rows)
        self.packs = [self.places(*pair) for pair in zip((low, high), shifts)]
        self.early_packs = [self.places(*pair) for pair in zip(early, shifts)]
        self.late_packs = [self.places(*pair) for pair in zip(late, shifts)]
        self.span = min(2 * reach, rows) * band
        self.quiet = [
            self.others(self.packs[1], 0, self.span),
            self.others(self.packs[0], self.own - self.span, self.own),
        ]
        self.list_size = batches + 2
        self.lengths_at = LISTS * self.list_size
        self.local_at = self.lengths_at + LISTS
        self.count_at = self.local_at + batches
        self.offsets_at = self.count_at + batches
        self.odd_at = self.offsets_at + slots * batches
        self.meta_size = self.odd_at + 1

    def bases(self, sides):
        found = {}
        for segments in sides:
            place = 0
            for row, start, stop in segments:
                found[row] = place - start
                place += stop - start
        return found

    def places(self, segments, shift):
        pack, place = ([], 0)
        for row, start, stop in segments:
            pack.append(((row + shift) * self.band + start, place, stop - start))
            place += stop - start
        return pack

    def others(self, pack, begin, end):
        touched = set()
        for start, _, count in pack:
            touched.update(range(start, start + count))
        runs = []
        for index in range(begin, end):
            if index in touched:
                continue
            if runs and sum(runs[-1]) == index:
                runs[-1] = (runs[-1][0], runs[-1][1] + 1)
            else:
                runs.append((index, 1))
        return runs

    def pick(self, bases, shift, row, otherwise):
        value = otherwise
        for at, base in bases.items():
            value = jnp.where(row == at, base + shift, value)
        return value


def run_copies(copies):
    for copy in copies:
        copy.start()
    for copy in copies:
        copy.wait()


def by_parity(odd, body, first, second):
    @pl.when(jnp.logical_not(odd))
    def _():
        body(first, second)

    @pl.when(odd)
    def _():
        body(second, first)


CROSS_MANY, CROSS_FEW, NEAR_MANY, NEAR_FEW, INNER_MANY, INNER_FEW, CROSS = range(LISTS)


def build_lists(geo, index, centre_ref, offsets_ref, counts_ref, meta_ref):
    first = index * geo.rows
    odd = index % 2 == 1
    meta_ref[geo.odd_at] = odd.astype(jnp.int32)
    lengths = [jnp.int32(0)] * LISTS
    for b in range(geo.batches):
        local = centre_ref[b] - first
        count = counts_ref[b]
        meta_ref[geo.local_at + b] = local
        meta_ref[geo.count_at + b] = count
        low = high = jnp.bool_(False)
        for k in range(geo.slots):
            offset = offsets_ref[k, b]
            meta_ref[geo.offsets_at + k * geo.batches + b] = offset
            row = local + offset
            low = low | ((k < count) & (row < 0))
            high = high | ((k < count) & (row >= geo.rows))
        cross = (odd & high) | (jnp.logical_not(odd) & low)
        near = (odd & low) | (jnp.logical_not(odd) & high)
        inner = jnp.logical_not(low | high)
        many = count > 2
        few = (count > 0) & jnp.logical_not(many)
        kinds = [kind & size for kind in (cross, near, inner) for size in (many, few)]
        for which, member in enumerate(kinds + [cross]):
            meta_ref[which * geo.list_size + lengths[which]] = b
            lengths[which] = lengths[which] + member.astype(jnp.int32)
    for which in range(LISTS):
        meta_ref[which * geo.list_size + lengths[which]] = geo.batches
        meta_ref[geo.lengths_at + which] = lengths[which]


def zone(geo, odd, cross):
    span = geo.span if cross else geo.own - geo.span
    return pl.ds(jnp.where(odd == cross, geo.own - span, 0), span)


def pack_kernel(
    geo, density_ref, centre_in, offsets_in, counts_in,
    near_ref, cross_ref, meta_ref, acc_ref,
    centre_ref, offsets_ref, counts_ref, sems,
):
    index = lax.axis_index("blk")
    odd = index % 2 == 1

    def copies(up, down):
        return [
            pltpu.make_async_copy(
                density_ref.at[pl.ds(start, count)], ref.at[pl.ds(place, count)], sems.at[side, i]
            )
            for side, (pack, ref) in enumerate(zip(geo.packs, (up, down)))
            for i, (start, place, count) in enumerate(pack)
        ]

    def start(up, down):
        for copy in copies(up, down):
            copy.start()

    by_parity(odd, start, near_ref, cross_ref)
    scalars = [
        pltpu.make_async_copy(*pair, sems.at[2, i])
        for i, pair in enumerate(
            ((centre_in, centre_ref), (offsets_in, offsets_ref), (counts_in, counts_ref))
        )
    ]
    for copy in scalars:
        copy.start()
    for where in (zone(geo, odd, False), pl.ds(geo.first_at, geo.halo)):
        acc_ref[where] = jnp.zeros_like(acc_ref[where])
    for copy in scalars:
        copy.wait()
    build_lists(geo, index, centre_ref, offsets_ref, counts_ref, meta_ref)
    for copy in copies(near_ref, cross_ref):
        copy.wait()


def group_count(geo, meta_ref, which):
    return (meta_ref[geo.lengths_at + which] + GROUP - 1) // GROUP


def waits():
    return (lax.axis_index("blk") + 1) // 2 % 2 == 1


def inner_share(geo, meta_ref):
    before = BUDGET
    for which in (CROSS_MANY, CROSS_FEW, NEAR_MANY, NEAR_FEW):
        before = before - COST[which % 2] * group_count(geo, meta_ref, which)
    waiting = jnp.where(waits(), WAIT, 0)
    share = []
    for which in (INNER_MANY, INNER_FEW):
        cost, count = COST[which % 2], group_count(geo, meta_ref, which)
        first = jnp.minimum(jnp.maximum(before, 0) // cost, count)
        second = jnp.minimum(jnp.maximum(waiting, 0) // cost, count - first)
        before = before - cost * first
        waiting = waiting - cost * second
        share.append((0, first, first + second, count))
    return share


def inner_part(geo, meta_ref, stage, refs):
    for which, width, bounds in zip(
        (INNER_MANY, INNER_FEW), (geo.slots, 2), inner_share(geo, meta_ref)
    ):
        each_group(
            geo,
            meta_ref,
            which,
            lambda chosen, width=width: add_whole(geo, chosen, width, *refs),
            begin=bounds[stage],
            end=bounds[stage + 1],
        )


def each_group(geo, meta_ref, which, body, size=GROUP, begin=0, end=None):
    length = meta_ref[geo.lengths_at + which]

    def step(i, carry):
        chosen = []
        for n in range(size):
            place = i * size + n
            there = place < length
            b = meta_ref[which * geo.list_size + jnp.minimum(place, length)]
            chosen.append((jnp.where(there, b, 0), there))
        body(chosen)
        return carry

    lax.fori_loop(begin, (length + size - 1) // size if end is None else end, step, 0)


class Slots:
    def __init__(self, geo, meta_ref, b, there, width):
        local = meta_ref[geo.local_at + b]
        count = jnp.where(there, meta_ref[geo.count_at + b], 0)
        self.offset = [meta_ref[geo.offsets_at + k * geo.batches + b] for k in range(width)]
        self.local = local
        self.row = [local + offset for offset in self.offset]
        self.live = [k < count for k in range(width)]
        self.own = [(row >= 0) & (row < geo.rows) for row in self.row]
        self.width = width


def panels(slots, ao_ref, b):
    return jnp.concatenate(
        [
            ao_ref[b, k] * jnp.where(slots.live[k], 1.0, 0.0).astype(ao_ref.dtype)
            for k in range(slots.width)
        ],
        axis=0,
    )


def gathered(tiles_ref, places):
    return jnp.concatenate(
        [jnp.concatenate([tiles_ref[place] for place in row], axis=1) for row in places], axis=0
    )


def potentials(xs, tiles, batches, kernel_ref):
    fs = [
        jnp.dot(t, x, preferred_element_type=jnp.float32).astype(jnp.bfloat16)
        for t, x in zip(tiles, xs)
    ]
    return [
        jnp.dot(f, kernel_ref[b], preferred_element_type=jnp.float32) for f, b in zip(fs, batches)
    ]


def outer_product(x, h):
    return lax.dot_general(x, h, (((1,), (1,)), ((), ())), preferred_element_type=jnp.float32)


def chain(xs, tiles, batches, kernel_ref, weights_ref):
    gs = potentials(xs, tiles, batches, kernel_ref)
    hs = [(g * weights_ref[pl.ds(b, 1), :]).astype(jnp.bfloat16) for g, b in zip(gs, batches)]
    return [outer_product(x, h) for x, h in zip(xs, hs)]


def scatter(part, target, nb, acc_ref):
    for k, row in enumerate(target):
        for j, place in enumerate(row):
            acc_ref[place] += part[k * nb : (k + 1) * nb, j * nb : (j + 1) * nb]


def add_whole(
    geo, chosen, width, meta_ref, tiles_ref, ao_ref, kernel_ref, weights_ref, acc_ref, halo_ref=None
):
    xs, tiles, targets = ([], [], [])
    for b, there in chosen:
        slots = Slots(geo, meta_ref, b, there, width)
        xs.append(panels(slots, ao_ref, b))
        rows, target = ([], [])
        for k in range(width):
            band = [slots.offset[j] - slots.offset[k] + geo.half for j in range(width)]
            own = slots.own[k]
            base = jnp.where(slots.live[k] & own, slots.row[k], 0) * geo.band
            row = jnp.concatenate([tiles_ref[base + o] for o in band], axis=1)
            if halo_ref is not None:
                away = slots.live[k] & jnp.logical_not(own)
                outside = jnp.where(away, geo.pick(geo.halo_base, 0, slots.row[k], 0), 0)
                other = [halo_ref[jnp.where(away, outside + o, 0)] for o in band]
                row = jnp.where(away, jnp.concatenate(other, axis=1), row)
                base = jnp.where(away, outside + geo.first_at, base)
            rows.append(row)
            target.append(
                [
                    jnp.where(slots.live[k] & slots.live[j], base + band[j], geo.spare)
                    for j in range(width)
                ]
            )
        tiles.append(jnp.concatenate(rows, axis=0))
        targets.append(target)
    parts = chain(xs, tiles, [b for b, _ in chosen], kernel_ref, weights_ref)
    for part, target in zip(parts, targets):
        scatter(part, target, ao_ref.shape[2], acc_ref)


def add_own(geo, chosen, width, meta_ref, tiles_ref, ao_ref, kernel_ref, weights_ref, acc_ref):
    xs, tiles, targets = ([], [], [])
    for b, there in chosen:
        slots = Slots(geo, meta_ref, b, there, width)
        xs.append(panels(slots, ao_ref, b))
        places, target = ([], [])
        for k in range(width):
            row = slots.row[k]
            band = [slots.offset[j] - slots.offset[k] + geo.half for j in range(width)]
            base = jnp.where(slots.own[k], row, 0) * geo.band
            places.append([base + o for o in band])
            base = geo.pick(geo.early_base, geo.early_at, row, base)
            target.append(
                [
                    jnp.where(
                        slots.live[k] & slots.live[j] & slots.own[j], base + band[j], geo.spare
                    )
                    for j in range(width)
                ]
            )
        tiles.append(gathered(tiles_ref, places))
        targets.append(target)
    parts = chain(xs, tiles, [b for b, _ in chosen], kernel_ref, weights_ref)
    for part, target in zip(parts, targets):
        scatter(part, target, ao_ref.shape[2], acc_ref)


def halo_rows(geo, meta_ref, slots):
    odd = meta_ref[geo.odd_at] == 1
    rows, places, present = ([], [], [])
    for i in range(geo.reach):
        row = jnp.where(odd, geo.rows + i, i - geo.reach)
        place, found = (jnp.int32(0), jnp.bool_(False))
        for k in range(slots.width):
            hit = slots.live[k] & (slots.row[k] == row)
            place = jnp.where(hit, k, place)
            found = found | hit
        rows.append(row)
        places.append(place)
        present.append(found)
    return rows, places, present


def add_corner(geo, chosen, meta_ref, halo_ref, ao_ref, kernel_ref, weights_ref, h_ref, total_ref):
    nb = ao_ref.shape[2]
    factor = lambda flag: jnp.where(flag, 1.0, 0.0)
    xs, sides, tiles, masks = ([], [], [], [])
    for b, there in chosen:
        slots = Slots(geo, meta_ref, b, there, geo.slots)
        rows, places, present = halo_rows(geo, meta_ref, slots)
        xs.append(panels(slots, ao_ref, b))
        sides.append(
            jnp.concatenate(
                [
                    ao_ref[b, place] * factor(found).astype(ao_ref.dtype)
                    for place, found in zip(places, present)
                ],
                axis=0,
            )
        )
        picked = []
        for row, found in zip(rows, present):
            base = geo.pick(geo.halo_base, 0, row, 0) - row + geo.half
            picked.append([jnp.where(found, base + column, 0) for column in slots.row])
        tiles.append(gathered(halo_ref, picked))
        masks.append([factor(found) for found in present])
    gs = potentials(xs, tiles, [b for b, _ in chosen], kernel_ref)
    hs = []
    for g, mask, (b, there) in zip(gs, masks, chosen):
        weights = weights_ref[pl.ds(b, 1), :]
        h = jnp.concatenate(
            [g[i * nb : (i + 1) * nb] * (weights * mask[i]) for i in range(geo.reach)], axis=0
        ).astype(jnp.bfloat16)
        h_ref[jnp.where(there, b, geo.batches)] = h
        hs.append(h)
    total_ref[...] += outer_product(
        jnp.concatenate(sides, axis=1), jnp.concatenate(hs, axis=1)
    )


def add_columns(geo, chosen, width, meta_ref, ao_ref, h_ref, acc_ref):
    parts, targets = ([], [])
    for b, there in chosen:
        slots = Slots(geo, meta_ref, b, there, width)
        rows, _, present = halo_rows(geo, meta_ref, slots)
        parts.append(outer_product(ao_ref[b, pl.ds(0, width)].reshape(-1, ao_ref.shape[3]), h_ref[b]))
        targets.append(
            [
                [
                    jnp.where(
                        slots.live[k] & slots.own[k] & found,
                        slots.row[k] * geo.band + row - slots.row[k] + geo.half,
                        geo.spare,
                    )
                    for row, found in zip(rows, present)
                ]
                for k in range(width)
            ]
        )
    for part, target in zip(parts, targets):
        scatter(part, target, ao_ref.shape[2], acc_ref)


def early_kernel(
    geo, meta_ref, tiles_ref, ao_ref, kernel_ref, weights_ref, acc_in, acc_ref, early_out
):
    odd = meta_ref[geo.odd_at] == 1
    for where in (zone(geo, odd, True), pl.ds(geo.early_at, geo.early), pl.ds(geo.spare, 1)):
        acc_ref[where] = jnp.zeros_like(acc_ref[where])
    refs = (meta_ref, tiles_ref, ao_ref, kernel_ref, weights_ref, acc_ref)
    for which, width in ((CROSS_MANY, geo.slots), (CROSS_FEW, 2)):
        each_group(
            geo, meta_ref, which, lambda chosen, width=width: add_own(geo, chosen, width, *refs)
        )
    early_out[...] = acc_ref[pl.ds(geo.early_at, geo.early)].astype(early_out.dtype)


def near_kernel(
    geo, meta_ref, halo_ref, tiles_ref, ao_ref, kernel_ref, weights_ref, acc_in, acc_ref, first_out
):
    refs = (meta_ref, tiles_ref, ao_ref, kernel_ref, weights_ref, acc_ref, halo_ref)
    for which, width in ((NEAR_MANY, geo.slots), (NEAR_FEW, 2)):
        each_group(
            geo, meta_ref, which, lambda chosen, width=width: add_whole(geo, chosen, width, *refs)
        )
    first_out[...] = acc_ref[pl.ds(geo.first_at, geo.halo)].astype(first_out.dtype)
    inner_part(geo, meta_ref, 0, refs[:-1])


def waiting_kernel(
    geo, meta_ref, tiles_ref, ao_ref, kernel_ref, weights_ref, acc_in, acc_ref, done_ref
):
    inner_part(geo, meta_ref, 1, (meta_ref, tiles_ref, ao_ref, kernel_ref, weights_ref, acc_ref))
    done_ref[0] = 1


def late_kernel(
    geo, meta_ref, done_ref, halo_ref, ao_ref, kernel_ref, weights_ref, h_ref, late_out, total_ref
):
    nb = ao_ref.shape[2]
    total_ref[...] = jnp.zeros_like(total_ref)

    def work(chosen):
        add_corner(
            geo, chosen, meta_ref, halo_ref, ao_ref, kernel_ref, weights_ref, h_ref, total_ref
        )

    groups = (meta_ref[geo.lengths_at + CROSS] + 1) // LATE_GROUP
    each_group(geo, meta_ref, CROSS, work, size=LATE_GROUP, end=groups)
    each_group(geo, meta_ref, CROSS, work, size=LATE_GROUP // 2, begin=2 * groups)
    for i in range(geo.reach):
        for j in range(geo.reach):
            late_out[i * geo.reach + j] = total_ref[
                i * nb : (i + 1) * nb, j * nb : (j + 1) * nb
            ].astype(late_out.dtype)


def inner_kernel(
    geo, meta_ref, first_ref, tiles_ref, ao_ref, kernel_ref, weights_ref, h_ref, acc_in,
    acc_ref, out_ref, sems,
):
    odd = meta_ref[geo.odd_at] == 1
    refs = (meta_ref, tiles_ref, ao_ref, kernel_ref, weights_ref, acc_ref)
    inner_part(geo, meta_ref, 2, refs)

    def add_near(up, down):
        for start, place, count in geo.packs[0 if up else 1]:
            acc_ref[pl.ds(start, count)] += first_ref[pl.ds(place, count)].astype(jnp.float32)

    by_parity(odd, add_near, True, False)
    done = zone(geo, odd, False)
    copy = pltpu.make_async_copy(acc_ref.at[done], out_ref.at[done], sems.at[0])
    copy.start()
    for which, width in ((CROSS_MANY, geo.slots), (CROSS_FEW, 2)):
        each_group(
            geo,
            meta_ref,
            which,
            lambda chosen, width=width: add_columns(
                geo, chosen, width, meta_ref, ao_ref, h_ref, acc_ref
            ),
        )

    def write_quiet(up, down):
        run_copies(
            [
                pltpu.make_async_copy(
                    acc_ref.at[pl.ds(start, count)], out_ref.at[pl.ds(start, count)], sems.at[1 + i]
                )
                for i, (start, count) in enumerate(geo.quiet[0 if up else 1])
            ]
        )

    by_parity(odd, write_quiet, True, False)
    copy.wait()


def finish_cross(geo, odd, parts, acc_ref, out_ref, total, sems):
    def add(up, down):
        copies = []
        for packs, ref in parts:
            for start, place, count in packs[0 if up else 1]:
                spot = pl.ds(len(copies) * geo.band, count)
                total[spot] = acc_ref[pl.ds(start, count)] + ref[pl.ds(place, count)].astype(
                    jnp.float32
                )
                copy = pltpu.make_async_copy(
                    total.at[spot], out_ref.at[pl.ds(start, count)], sems.at[len(copies)]
                )
                copy.start()
                copies.append(copy)
        for copy in copies:
            copy.wait()

    by_parity(odd, add, False, True)


def has_time(geo, meta_ref):
    left = [bounds[3] - bounds[2] for bounds in inner_share(geo, meta_ref)]
    return waits() & (left[0] + left[1] == 0)


def early_join_kernel(geo, meta_ref, early_ref, acc_ref, out_in, out_ref, total, sems):
    @pl.when(has_time(geo, meta_ref))
    def _():
        odd = meta_ref[geo.odd_at] == 1
        finish_cross(geo, odd, ((geo.early_packs, early_ref),), acc_ref, out_ref, total, sems)


def finish_kernel(geo, meta_ref, late_ref, early_ref, acc_ref, out_in, out_ref, total, sems):
    odd = meta_ref[geo.odd_at] == 1
    late = (geo.late_packs, late_ref)
    joined = has_time(geo, meta_ref)

    @pl.when(joined)
    def _():
        finish_cross(geo, odd, (late,), acc_ref, out_ref, total, sems)

    @pl.when(jnp.logical_not(joined))
    def _():
        parts = ((geo.early_packs, early_ref), late)
        finish_cross(geo, odd, parts, acc_ref, out_ref, total, sems)


def call(kernel, out_shape, in_specs, out_specs, scratch, aliases=None, cost=None):
    return pl.pallas_call(
        kernel,
        out_shape=out_shape,
        in_specs=in_specs,
        out_specs=out_specs,
        scratch_shapes=scratch,
        input_output_aliases=aliases or {},
        cost_estimate=cost,
        compiler_params=pltpu.CompilerParams(vmem_limit_bytes=16 * MIB),
    )


def to_first(x, size):
    pairs = [(i, i + 1) for i in range(0, size - 1, 2)]
    got = lax.ppermute(x, "blk", pairs + [(j, i) for i, j in pairs])
    return pltpu.with_memory_space_constraint(got, pltpu.VMEM)


def to_second(x, size):
    pairs = [(i, i + 1) for i in range(1, size - 1, 2)]
    got = lax.ppermute(x, "blk", pairs + [(j, i) for i, j in pairs])
    return pltpu.with_memory_space_constraint(got, pltpu.VMEM)


def local(density, ao_values, kernel, grid_weights, centre, sig_offsets, counts):
    rows, band, nb, _ = density.shape
    batches, slots, _, pts = ao_values.shape
    size = lax.axis_size("blk")
    geo = Geometry(rows, band, batches, slots)
    in_hbm = lambda x: pltpu.with_memory_space_constraint(x, pltpu.HBM)
    tiles = density.reshape(geo.own, nb, nb)
    pack = lambda count: pltpu.VMEM((count, nb, nb), jnp.bfloat16)
    dma = pltpu.SemaphoreType.DMA
    acc_type = pltpu.VMEM((geo.spare + 1, nb, nb), jnp.float32)

    near_halo, cross_halo, meta, acc = call(
        functools.partial(pack_kernel, geo),
        (pack(geo.halo),) * 2 + (pltpu.SMEM((geo.meta_size,), jnp.int32), acc_type),
        [ANY_SPEC] * 4,
        (VMEM_SPEC,) * 2 + (SMEM_SPEC, VMEM_SPEC),
        [
            pltpu.SMEM((batches,), jnp.int32),
            pltpu.SMEM((slots, batches), jnp.int32),
            pltpu.SMEM((batches,), jnp.int32),
            dma((3, max(geo.reach, 3))),
        ],
        cost=pl.CostEstimate(flops=10**10, bytes_accessed=10**8, transcendentals=0),
    )(in_hbm(tiles), in_hbm(centre), in_hbm(sig_offsets.T), in_hbm(counts))
    cross_halo = to_second(cross_halo, size)
    near_halo = to_first(near_halo, size)

    panel = (tiles, ao_values, kernel, grid_weights)
    acc, early = call(
        functools.partial(early_kernel, geo),
        (acc_type, pack(geo.early)),
        [SMEM_SPEC] + [VMEM_SPEC] * 5,
        (VMEM_SPEC,) * 2,
        [],
        {5: 0},
    )(meta, *panel, acc)
    early = to_second(early, size)

    acc, first = call(
        functools.partial(near_kernel, geo),
        (acc_type, pack(geo.halo)),
        [SMEM_SPEC] + [VMEM_SPEC] * 6,
        (VMEM_SPEC,) * 2,
        [],
        {6: 0},
    )(meta, near_halo, *panel, acc)
    first = to_first(first, size)

    acc, done = call(
        functools.partial(waiting_kernel, geo),
        (acc_type, pltpu.SMEM((1,), jnp.int32)),
        [SMEM_SPEC] + [VMEM_SPEC] * 5,
        (VMEM_SPEC, SMEM_SPEC),
        [],
        {5: 0},
    )(meta, *panel, acc)

    h_type = pltpu.VMEM((batches + 1, geo.reach * nb, pts), jnp.bfloat16)
    h, late = call(
        functools.partial(late_kernel, geo),
        (h_type, pack(geo.late)),
        [SMEM_SPEC] * 2 + [VMEM_SPEC] * 4,
        (VMEM_SPEC,) * 2,
        [pltpu.VMEM((geo.reach * nb, geo.reach * nb), jnp.float32)],
    )(meta, done, cross_halo, *panel[1:])
    late = to_second(late, size)

    whole = jax.ShapeDtypeStruct((geo.own, nb, nb), jnp.float32)
    acc, out = call(
        functools.partial(inner_kernel, geo),
        (acc_type, whole),
        [SMEM_SPEC] + [VMEM_SPEC] * 7,
        (VMEM_SPEC, ANY_SPEC),
        [dma((1 + max(len(runs) for runs in geo.quiet),))],
        {7: 0},
    )(meta, first, *panel, h, acc)

    for kernel_of, got, parts in (
        (early_join_kernel, (early,), geo.reach),
        (finish_kernel, (late, early), 2 * geo.reach),
    ):
        out = call(
            functools.partial(kernel_of, geo),
            whole,
            [SMEM_SPEC] + [VMEM_SPEC] * (len(got) + 1) + [ANY_SPEC],
            ANY_SPEC,
            [pltpu.VMEM((parts * band, nb, nb), jnp.float32), dma((parts,))],
            {len(got) + 2: 0},
        )(meta, *got, acc, out)
    return out.reshape(rows, band, nb, nb)


def solution(mesh):
    placed = (
        P(("groups", "blk"), None, None, None),
        P(("groups", "blk"), None, None, None),
        P(("groups", "blk"), None, None),
        P(("groups", "blk"), None),
        P(("groups", "blk")),
        P(("groups", "blk"), None),
        P(("groups", "blk")),
    )
    return jax.shard_map(
        local,
        mesh=mesh,
        in_specs=placed,
        out_specs=P(("groups", "blk"), None, None, None),
        check_vma=False,
    )
```

```python
import functools

import jax
import jax.numpy as jnp
from jax import lax
from jax.experimental import pallas as pl
from jax.experimental.pallas import tpu as pltpu
from jax.sharding import PartitionSpec as P

MIB = 1 << 20
GROUP = 2
LATE_GROUP = 4
LISTS = 7
BUDGET = 43
WAIT = (18, 27)
COST = (10, 7)
SMEM_SPEC = pl.BlockSpec(memory_space=pltpu.SMEM)
VMEM_SPEC = pl.BlockSpec(memory_space=pltpu.VMEM)
ANY_SPEC = pl.BlockSpec(memory_space=pl.ANY)


class Geometry:
    def __init__(self, rows, band, batches, slots):
        self.rows, self.band, self.batches, self.slots = rows, band, batches, slots
        self.half = half = (band - 1) // 2
        self.reach = reach = half // 2
        self.own = rows * band
        low = [(-m, reach + m, band) for m in range(reach, 0, -1)]
        high = [(rows + m, 0, 3 * reach - m) for m in range(reach)]
        self.halo = sum(stop - start for _, start, stop in low)
        low_cut = [half - row for row, _, _ in low]
        high_cut = [rows - row + half for row, _, _ in high]
        early = (
            [(row, cut, stop) for (row, _, stop), cut in zip(low, low_cut)],
            [(row, start, cut) for (row, start, _), cut in zip(high, high_cut)],
        )
        late = (
            [(row, start, cut) for (row, start, _), cut in zip(low, low_cut)],
            [(row, cut, stop) for (row, _, stop), cut in zip(high, high_cut)],
        )
        self.early = sum(stop - start for _, start, stop in early[0])
        self.late = self.halo - self.early
        self.first_at = self.own
        self.early_at = self.own + self.halo
        self.spare = self.early_at + self.early
        self.halo_base = self.bases((low, high))
        self.early_base = self.bases(early)
        shifts = (rows, -rows)
        self.packs = [self.places(*pair) for pair in zip((low, high), shifts)]
        self.early_packs = [self.places(*pair) for pair in zip(early, shifts)]
        self.late_packs = [self.places(*pair) for pair in zip(late, shifts)]
        self.span = min(2 * reach, rows) * band
        self.quiet = [
            self.others(self.packs[1], 0, self.span),
            self.others(self.packs[0], self.own - self.span, self.own),
        ]
        self.list_size = batches + 2
        self.lengths_at = LISTS * self.list_size
        self.local_at = self.lengths_at + LISTS
        self.count_at = self.local_at + batches
        self.offsets_at = self.count_at + batches
        self.odd_at = self.offsets_at + slots * batches
        self.meta_size = self.odd_at + 1

    def bases(self, sides):
        found = {}
        for segments in sides:
            place = 0
            for row, start, stop in segments:
                found[row] = place - start
                place += stop - start
        return found

    def places(self, segments, shift):
        pack, place = ([], 0)
        for row, start, stop in segments:
            pack.append(((row + shift) * self.band + start, place, stop - start))
            place += stop - start
        return pack

    def others(self, pack, begin, end):
        touched = set()
        for start, _, count in pack:
            touched.update(range(start, start + count))
        runs = []
        for index in range(begin, end):
            if index in touched:
                continue
            if runs and sum(runs[-1]) == index:
                runs[-1] = (runs[-1][0], runs[-1][1] + 1)
            else:
                runs.append((index, 1))
        return runs

    def pick(self, bases, shift, row, otherwise):
        value = otherwise
        for at, base in bases.items():
            value = jnp.where(row == at, base + shift, value)
        return value


def run_copies(copies):
    for copy in copies:
        copy.start()
    for copy in copies:
        copy.wait()


def by_parity(odd, body, first, second):
    @pl.when(jnp.logical_not(odd))
    def _():
        body(first, second)

    @pl.when(odd)
    def _():
        body(second, first)


CROSS_MANY, CROSS_FEW, NEAR_MANY, NEAR_FEW, INNER_MANY, INNER_FEW, CROSS = range(LISTS)


def build_lists(geo, index, centre_ref, offsets_ref, counts_ref, meta_ref):
    first = index * geo.rows
    odd = index % 2 == 1
    meta_ref[geo.odd_at] = odd.astype(jnp.int32)
    lengths = [jnp.int32(0)] * LISTS
    for b in range(geo.batches):
        local = centre_ref[b] - first
        count = counts_ref[b]
        meta_ref[geo.local_at + b] = local
        meta_ref[geo.count_at + b] = count
        low = high = jnp.bool_(False)
        for k in range(geo.slots):
            offset = offsets_ref[k, b]
            meta_ref[geo.offsets_at + k * geo.batches + b] = offset
            row = local + offset
            low = low | ((k < count) & (row < 0))
            high = high | ((k < count) & (row >= geo.rows))
        cross = (odd & high) | (jnp.logical_not(odd) & low)
        near = (odd & low) | (jnp.logical_not(odd) & high)
        inner = jnp.logical_not(low | high)
        many = count > 2
        few = (count > 0) & jnp.logical_not(many)
        kinds = [kind & size for kind in (cross, near, inner) for size in (many, few)]
        for which, member in enumerate(kinds + [cross]):
            meta_ref[which * geo.list_size + lengths[which]] = b
            lengths[which] = lengths[which] + member.astype(jnp.int32)
    for which in range(LISTS):
        meta_ref[which * geo.list_size + lengths[which]] = geo.batches
        meta_ref[geo.lengths_at + which] = lengths[which]


def zone(geo, odd, cross):
    span = geo.span if cross else geo.own - geo.span
    return pl.ds(jnp.where(odd == cross, geo.own - span, 0), span)


def pack_kernel(
    geo, density_ref, centre_in, offsets_in, counts_in,
    near_ref, cross_ref, meta_ref, acc_ref,
    centre_ref, offsets_ref, counts_ref, sems,
):
    index = lax.axis_index("blk")
    odd = index % 2 == 1

    def copies(up, down):
        return [
            pltpu.make_async_copy(
                density_ref.at[pl.ds(start, count)], ref.at[pl.ds(place, count)], sems.at[side, i]
            )
            for side, (pack, ref) in enumerate(zip(geo.packs, (up, down)))
            for i, (start, place, count) in enumerate(pack)
        ]

    def start(up, down):
        for copy in copies(up, down):
            copy.start()

    by_parity(odd, start, near_ref, cross_ref)
    scalars = [
        pltpu.make_async_copy(*pair, sems.at[2, i])
        for i, pair in enumerate(
            ((centre_in, centre_ref), (offsets_in, offsets_ref), (counts_in, counts_ref))
        )
    ]
    for copy in scalars:
        copy.start()
    for where in (zone(geo, odd, False), pl.ds(geo.first_at, geo.halo)):
        acc_ref[where] = jnp.zeros_like(acc_ref[where])
    for copy in scalars:
        copy.wait()
    build_lists(geo, index, centre_ref, offsets_ref, counts_ref, meta_ref)
    for copy in copies(near_ref, cross_ref):
        copy.wait()


def group_count(geo, meta_ref, which):
    return (meta_ref[geo.lengths_at + which] + GROUP - 1) // GROUP


def waits():
    return (lax.axis_index("blk") + 1) // 2 % 2 == 1


def inner_share(geo, meta_ref):
    before = BUDGET
    for which in (CROSS_MANY, CROSS_FEW, NEAR_MANY, NEAR_FEW):
        before = before - COST[which % 2] * group_count(geo, meta_ref, which)
    odd = meta_ref[geo.odd_at] == 1
    waiting = jnp.where(waits(), jnp.where(odd, WAIT[1], WAIT[0]), 0)
    share = []
    for which in (INNER_MANY, INNER_FEW):
        cost, count = COST[which % 2], group_count(geo, meta_ref, which)
        first = jnp.minimum(jnp.maximum(before, 0) // cost, count)
        second = jnp.minimum(jnp.maximum(waiting, 0) // cost, count - first)
        before = before - cost * first
        waiting = waiting - cost * second
        share.append((0, first, first + second, count))
    return share


def inner_part(geo, meta_ref, stage, refs):
    for which, width, bounds in zip(
        (INNER_MANY, INNER_FEW), (geo.slots, 2), inner_share(geo, meta_ref)
    ):
        each_group(
            geo,
            meta_ref,
            which,
            lambda chosen, width=width: add_whole(geo, chosen, width, *refs),
            begin=bounds[stage],
            end=bounds[stage + 1],
        )


def each_group(geo, meta_ref, which, body, size=GROUP, begin=0, end=None):
    length = meta_ref[geo.lengths_at + which]

    def step(i, carry):
        chosen = []
        for n in range(size):
            place = i * size + n
            there = place < length
            b = meta_ref[which * geo.list_size + jnp.minimum(place, length)]
            chosen.append((jnp.where(there, b, 0), there))
        body(chosen)
        return carry

    lax.fori_loop(begin, (length + size - 1) // size if end is None else end, step, 0)


class Slots:
    def __init__(self, geo, meta_ref, b, there, width):
        local = meta_ref[geo.local_at + b]
        count = jnp.where(there, meta_ref[geo.count_at + b], 0)
        self.offset = [meta_ref[geo.offsets_at + k * geo.batches + b] for k in range(width)]
        self.local = local
        self.row = [local + offset for offset in self.offset]
        self.live = [k < count for k in range(width)]
        self.own = [(row >= 0) & (row < geo.rows) for row in self.row]
        self.width = width


def panels(slots, ao_ref, b):
    return jnp.concatenate(
        [
            ao_ref[b, k] * jnp.where(slots.live[k], 1.0, 0.0).astype(ao_ref.dtype)
            for k in range(slots.width)
        ],
        axis=0,
    )


def gathered(tiles_ref, places):
    return jnp.concatenate(
        [jnp.concatenate([tiles_ref[place] for place in row], axis=1) for row in places], axis=0
    )


def potentials(xs, tiles, batches, kernel_ref):
    fs = [
        jnp.dot(t, x, preferred_element_type=jnp.float32).astype(jnp.bfloat16)
        for t, x in zip(tiles, xs)
    ]
    return [
        jnp.dot(f, kernel_ref[b], preferred_element_type=jnp.float32) for f, b in zip(fs, batches)
    ]


def outer_product(x, h):
    return lax.dot_general(x, h, (((1,), (1,)), ((), ())), preferred_element_type=jnp.float32)


def chain(xs, tiles, batches, kernel_ref, weights_ref):
    gs = potentials(xs, tiles, batches, kernel_ref)
    hs = [(g * weights_ref[pl.ds(b, 1), :]).astype(jnp.bfloat16) for g, b in zip(gs, batches)]
    return [outer_product(x, h) for x, h in zip(xs, hs)]


def scatter(part, target, nb, acc_ref):
    for k, row in enumerate(target):
        for j, place in enumerate(row):
            acc_ref[place] += part[k * nb : (k + 1) * nb, j * nb : (j + 1) * nb]


def add_whole(
    geo, chosen, width, meta_ref, tiles_ref, ao_ref, kernel_ref, weights_ref, acc_ref, halo_ref=None
):
    xs, tiles, targets = ([], [], [])
    for b, there in chosen:
        slots = Slots(geo, meta_ref, b, there, width)
        xs.append(panels(slots, ao_ref, b))
        rows, target = ([], [])
        for k in range(width):
            band = [slots.offset[j] - slots.offset[k] + geo.half for j in range(width)]
            own = slots.own[k]
            base = jnp.where(slots.live[k] & own, slots.row[k], 0) * geo.band
            row = jnp.concatenate([tiles_ref[base + o] for o in band], axis=1)
            if halo_ref is not None:
                away = slots.live[k] & jnp.logical_not(own)
                outside = jnp.where(away, geo.pick(geo.halo_base, 0, slots.row[k], 0), 0)
                other = [halo_ref[jnp.where(away, outside + o, 0)] for o in band]
                row = jnp.where(away, jnp.concatenate(other, axis=1), row)
                base = jnp.where(away, outside + geo.first_at, base)
            rows.append(row)
            target.append(
                [
                    jnp.where(slots.live[k] & slots.live[j], base + band[j], geo.spare)
                    for j in range(width)
                ]
            )
        tiles.append(jnp.concatenate(rows, axis=0))
        targets.append(target)
    parts = chain(xs, tiles, [b for b, _ in chosen], kernel_ref, weights_ref)
    for part, target in zip(parts, targets):
        scatter(part, target, ao_ref.shape[2], acc_ref)


def add_own(geo, chosen, width, meta_ref, tiles_ref, ao_ref, kernel_ref, weights_ref, acc_ref):
    xs, tiles, targets = ([], [], [])
    for b, there in chosen:
        slots = Slots(geo, meta_ref, b, there, width)
        xs.append(panels(slots, ao_ref, b))
        places, target = ([], [])
        for k in range(width):
            row = slots.row[k]
            band = [slots.offset[j] - slots.offset[k] + geo.half for j in range(width)]
            base = jnp.where(slots.own[k], row, 0) * geo.band
            places.append([base + o for o in band])
            base = geo.pick(geo.early_base, geo.early_at, row, base)
            target.append(
                [
                    jnp.where(
                        slots.live[k] & slots.live[j] & slots.own[j], base + band[j], geo.spare
                    )
                    for j in range(width)
                ]
            )
        tiles.append(gathered(tiles_ref, places))
        targets.append(target)
    parts = chain(xs, tiles, [b for b, _ in chosen], kernel_ref, weights_ref)
    for part, target in zip(parts, targets):
        scatter(part, target, ao_ref.shape[2], acc_ref)


def halo_rows(geo, meta_ref, slots):
    odd = meta_ref[geo.odd_at] == 1
    rows, places, present = ([], [], [])
    for i in range(geo.reach):
        row = jnp.where(odd, geo.rows + i, i - geo.reach)
        place, found = (jnp.int32(0), jnp.bool_(False))
        for k in range(slots.width):
            hit = slots.live[k] & (slots.row[k] == row)
            place = jnp.where(hit, k, place)
            found = found | hit
        rows.append(row)
        places.append(place)
        present.append(found)
    return rows, places, present


def add_corner(geo, chosen, meta_ref, halo_ref, ao_ref, kernel_ref, weights_ref, h_ref, total_ref):
    nb = ao_ref.shape[2]
    factor = lambda flag: jnp.where(flag, 1.0, 0.0)
    xs, sides, tiles, masks = ([], [], [], [])
    for b, there in chosen:
        slots = Slots(geo, meta_ref, b, there, geo.slots)
        rows, places, present = halo_rows(geo, meta_ref, slots)
        xs.append(panels(slots, ao_ref, b))
        sides.append(
            jnp.concatenate(
                [
                    ao_ref[b, place] * factor(found).astype(ao_ref.dtype)
                    for place, found in zip(places, present)
                ],
                axis=0,
            )
        )
        picked = []
        for row, found in zip(rows, present):
            base = geo.pick(geo.halo_base, 0, row, 0) - row + geo.half
            picked.append([jnp.where(found, base + column, 0) for column in slots.row])
        tiles.append(gathered(halo_ref, picked))
        masks.append([factor(found) for found in present])
    gs = potentials(xs, tiles, [b for b, _ in chosen], kernel_ref)
    hs = []
    for g, mask, (b, there) in zip(gs, masks, chosen):
        weights = weights_ref[pl.ds(b, 1), :]
        h = jnp.concatenate(
            [g[i * nb : (i + 1) * nb] * (weights * mask[i]) for i in range(geo.reach)], axis=0
        ).astype(jnp.bfloat16)
        h_ref[jnp.where(there, b, geo.batches)] = h
        hs.append(h)
    total_ref[...] += outer_product(
        jnp.concatenate(sides, axis=1), jnp.concatenate(hs, axis=1)
    )


def add_columns(geo, chosen, width, meta_ref, ao_ref, h_ref, acc_ref):
    parts, targets = ([], [])
    for b, there in chosen:
        slots = Slots(geo, meta_ref, b, there, width)
        rows, _, present = halo_rows(geo, meta_ref, slots)
        parts.append(outer_product(ao_ref[b, pl.ds(0, width)].reshape(-1, ao_ref.shape[3]), h_ref[b]))
        targets.append(
            [
                [
                    jnp.where(
                        slots.live[k] & slots.own[k] & found,
                        slots.row[k] * geo.band + row - slots.row[k] + geo.half,
                        geo.spare,
                    )
                    for row, found in zip(rows, present)
                ]
                for k in range(width)
            ]
        )
    for part, target in zip(parts, targets):
        scatter(part, target, ao_ref.shape[2], acc_ref)


def early_kernel(
    geo, meta_ref, tiles_ref, ao_ref, kernel_ref, weights_ref, acc_in, acc_ref, early_out
):
    odd = meta_ref[geo.odd_at] == 1
    for where in (zone(geo, odd, True), pl.ds(geo.early_at, geo.early), pl.ds(geo.spare, 1)):
        acc_ref[where] = jnp.zeros_like(acc_ref[where])
    refs = (meta_ref, tiles_ref, ao_ref, kernel_ref, weights_ref, acc_ref)
    for which, width in ((CROSS_MANY, geo.slots), (CROSS_FEW, 2)):
        each_group(
            geo, meta_ref, which, lambda chosen, width=width: add_own(geo, chosen, width, *refs)
        )
    early_out[...] = acc_ref[pl.ds(geo.early_at, geo.early)].astype(early_out.dtype)


def near_kernel(
    geo, meta_ref, halo_ref, tiles_ref, ao_ref, kernel_ref, weights_ref, acc_in, acc_ref, first_out
):
    refs = (meta_ref, tiles_ref, ao_ref, kernel_ref, weights_ref, acc_ref, halo_ref)
    for which, width in ((NEAR_MANY, geo.slots), (NEAR_FEW, 2)):
        each_group(
            geo, meta_ref, which, lambda chosen, width=width: add_whole(geo, chosen, width, *refs)
        )
    first_out[...] = acc_ref[pl.ds(geo.first_at, geo.halo)].astype(first_out.dtype)
    inner_part(geo, meta_ref, 0, refs[:-1])


def waiting_kernel(
    geo, meta_ref, tiles_ref, ao_ref, kernel_ref, weights_ref, acc_in, acc_ref, done_ref
):
    inner_part(geo, meta_ref, 1, (meta_ref, tiles_ref, ao_ref, kernel_ref, weights_ref, acc_ref))
    done_ref[0] = 1


def late_kernel(
    geo, meta_ref, done_ref, halo_ref, ao_ref, kernel_ref, weights_ref, h_ref, late_out, total_ref
):
    nb = ao_ref.shape[2]
    total_ref[...] = jnp.zeros_like(total_ref)

    def work(chosen):
        add_corner(
            geo, chosen, meta_ref, halo_ref, ao_ref, kernel_ref, weights_ref, h_ref, total_ref
        )

    groups = (meta_ref[geo.lengths_at + CROSS] + 1) // LATE_GROUP
    each_group(geo, meta_ref, CROSS, work, size=LATE_GROUP, end=groups)
    each_group(geo, meta_ref, CROSS, work, size=LATE_GROUP // 2, begin=2 * groups)
    for i in range(geo.reach):
        for j in range(geo.reach):
            late_out[i * geo.reach + j] = total_ref[
                i * nb : (i + 1) * nb, j * nb : (j + 1) * nb
            ].astype(late_out.dtype)


def inner_kernel(
    geo, meta_ref, first_ref, tiles_ref, ao_ref, kernel_ref, weights_ref, h_ref, acc_in,
    acc_ref, out_ref, sems,
):
    odd = meta_ref[geo.odd_at] == 1
    refs = (meta_ref, tiles_ref, ao_ref, kernel_ref, weights_ref, acc_ref)
    inner_part(geo, meta_ref, 2, refs)

    def add_near(up, down):
        for start, place, count in geo.packs[0 if up else 1]:
            acc_ref[pl.ds(start, count)] += first_ref[pl.ds(place, count)].astype(jnp.float32)

    by_parity(odd, add_near, True, False)
    done = zone(geo, odd, False)
    copy = pltpu.make_async_copy(acc_ref.at[done], out_ref.at[done], sems.at[0])
    copy.start()
    for which, width in ((CROSS_MANY, geo.slots), (CROSS_FEW, 2)):
        each_group(
            geo,
            meta_ref,
            which,
            lambda chosen, width=width: add_columns(
                geo, chosen, width, meta_ref, ao_ref, h_ref, acc_ref
            ),
        )

    def write_quiet(up, down):
        run_copies(
            [
                pltpu.make_async_copy(
                    acc_ref.at[pl.ds(start, count)], out_ref.at[pl.ds(start, count)], sems.at[1 + i]
                )
                for i, (start, count) in enumerate(geo.quiet[0 if up else 1])
            ]
        )

    by_parity(odd, write_quiet, True, False)
    copy.wait()


def finish_cross(geo, odd, parts, acc_ref, out_ref, total, sems):
    def add(up, down):
        copies = []
        for packs, ref in parts:
            for start, place, count in packs[0 if up else 1]:
                spot = pl.ds(len(copies) * geo.band, count)
                total[spot] = acc_ref[pl.ds(start, count)] + ref[pl.ds(place, count)].astype(
                    jnp.float32
                )
                copy = pltpu.make_async_copy(
                    total.at[spot], out_ref.at[pl.ds(start, count)], sems.at[len(copies)]
                )
                copy.start()
                copies.append(copy)
        for copy in copies:
            copy.wait()

    by_parity(odd, add, False, True)


def has_time(geo, meta_ref):
    left = [bounds[3] - bounds[2] for bounds in inner_share(geo, meta_ref)]
    return waits() & (left[0] + left[1] == 0)


def early_join_kernel(geo, meta_ref, early_ref, acc_ref, out_in, out_ref, total, sems):
    @pl.when(has_time(geo, meta_ref))
    def _():
        odd = meta_ref[geo.odd_at] == 1
        finish_cross(geo, odd, ((geo.early_packs, early_ref),), acc_ref, out_ref, total, sems)


def finish_kernel(geo, meta_ref, late_ref, early_ref, acc_ref, out_in, out_ref, total, sems):
    odd = meta_ref[geo.odd_at] == 1
    late = (geo.late_packs, late_ref)
    joined = has_time(geo, meta_ref)

    @pl.when(joined)
    def _():
        finish_cross(geo, odd, (late,), acc_ref, out_ref, total, sems)

    @pl.when(jnp.logical_not(joined))
    def _():
        parts = ((geo.early_packs, early_ref), late)
        finish_cross(geo, odd, parts, acc_ref, out_ref, total, sems)


def call(kernel, out_shape, in_specs, out_specs, scratch, aliases=None, cost=None):
    return pl.pallas_call(
        kernel,
        out_shape=out_shape,
        in_specs=in_specs,
        out_specs=out_specs,
        scratch_shapes=scratch,
        input_output_aliases=aliases or {},
        cost_estimate=cost,
        compiler_params=pltpu.CompilerParams(vmem_limit_bytes=16 * MIB),
    )


def to_first(x, size):
    pairs = [(i, i + 1) for i in range(0, size - 1, 2)]
    got = lax.ppermute(x, "blk", pairs + [(j, i) for i, j in pairs])
    return pltpu.with_memory_space_constraint(got, pltpu.VMEM)


def to_second(x, size):
    pairs = [(i, i + 1) for i in range(1, size - 1, 2)]
    got = lax.ppermute(x, "blk", pairs + [(j, i) for i, j in pairs])
    return pltpu.with_memory_space_constraint(got, pltpu.VMEM)


def local(density, ao_values, kernel, grid_weights, centre, sig_offsets, counts):
    rows, band, nb, _ = density.shape
    batches, slots, _, pts = ao_values.shape
    size = lax.axis_size("blk")
    geo = Geometry(rows, band, batches, slots)
    in_hbm = lambda x: pltpu.with_memory_space_constraint(x, pltpu.HBM)
    tiles = density.reshape(geo.own, nb, nb)
    pack = lambda count: pltpu.VMEM((count, nb, nb), jnp.bfloat16)
    dma = pltpu.SemaphoreType.DMA
    acc_type = pltpu.VMEM((geo.spare + 1, nb, nb), jnp.float32)

    near_halo, cross_halo, meta, acc = call(
        functools.partial(pack_kernel, geo),
        (pack(geo.halo),) * 2 + (pltpu.SMEM((geo.meta_size,), jnp.int32), acc_type),
        [ANY_SPEC] * 4,
        (VMEM_SPEC,) * 2 + (SMEM_SPEC, VMEM_SPEC),
        [
            pltpu.SMEM((batches,), jnp.int32),
            pltpu.SMEM((slots, batches), jnp.int32),
            pltpu.SMEM((batches,), jnp.int32),
            dma((3, max(geo.reach, 3))),
        ],
        cost=pl.CostEstimate(flops=10**10, bytes_accessed=10**8, transcendentals=0),
    )(in_hbm(tiles), in_hbm(centre), in_hbm(sig_offsets.T), in_hbm(counts))
    cross_halo = to_second(cross_halo, size)
    near_halo = to_first(near_halo, size)

    panel = (tiles, ao_values, kernel, grid_weights)
    acc, early = call(
        functools.partial(early_kernel, geo),
        (acc_type, pack(geo.early)),
        [SMEM_SPEC] + [VMEM_SPEC] * 5,
        (VMEM_SPEC,) * 2,
        [],
        {5: 0},
    )(meta, *panel, acc)
    early = to_second(early, size)

    acc, first = call(
        functools.partial(near_kernel, geo),
        (acc_type, pack(geo.halo)),
        [SMEM_SPEC] + [VMEM_SPEC] * 6,
        (VMEM_SPEC,) * 2,
        [],
        {6: 0},
    )(meta, near_halo, *panel, acc)
    first = to_first(first, size)

    acc, done = call(
        functools.partial(waiting_kernel, geo),
        (acc_type, pltpu.SMEM((1,), jnp.int32)),
        [SMEM_SPEC] + [VMEM_SPEC] * 5,
        (VMEM_SPEC, SMEM_SPEC),
        [],
        {5: 0},
    )(meta, *panel, acc)

    h_type = pltpu.VMEM((batches + 1, geo.reach * nb, pts), jnp.bfloat16)
    h, late = call(
        functools.partial(late_kernel, geo),
        (h_type, pack(geo.late)),
        [SMEM_SPEC] * 2 + [VMEM_SPEC] * 4,
        (VMEM_SPEC,) * 2,
        [pltpu.VMEM((geo.reach * nb, geo.reach * nb), jnp.float32)],
    )(meta, done, cross_halo, *panel[1:])
    late = to_second(late, size)

    whole = jax.ShapeDtypeStruct((geo.own, nb, nb), jnp.float32)
    acc, out = call(
        functools.partial(inner_kernel, geo),
        (acc_type, whole),
        [SMEM_SPEC] + [VMEM_SPEC] * 7,
        (VMEM_SPEC, ANY_SPEC),
        [dma((1 + max(len(runs) for runs in geo.quiet),))],
        {7: 0},
    )(meta, first, *panel, h, acc)

    for kernel_of, got, parts in (
        (early_join_kernel, (early,), geo.reach),
        (finish_kernel, (late, early), 2 * geo.reach),
    ):
        out = call(
            functools.partial(kernel_of, geo),
            whole,
            [SMEM_SPEC] + [VMEM_SPEC] * (len(got) + 1) + [ANY_SPEC],
            ANY_SPEC,
            [pltpu.VMEM((parts * band, nb, nb), jnp.float32), dma((parts,))],
            {len(got) + 2: 0},
        )(meta, *got, acc, out)
    return out.reshape(rows, band, nb, nb)


def solution(mesh):
    placed = (
        P(("groups", "blk"), None, None, None),
        P(("groups", "blk"), None, None, None),
        P(("groups", "blk"), None, None),
        P(("groups", "blk"), None),
        P(("groups", "blk")),
        P(("groups", "blk"), None),
        P(("groups", "blk")),
    )
    return jax.shard_map(
        local,
        mesh=mesh,
        in_specs=placed,
        out_specs=P(("groups", "blk"), None, None, None),
        check_vma=False,
    )
```

```python
import functools

import jax
import jax.numpy as jnp
from jax import lax
from jax.experimental import pallas as pl
from jax.experimental.pallas import tpu as pltpu
from jax.sharding import PartitionSpec as P

MIB = 1 << 20
GROUP = 2
LATE_GROUP = 4
LISTS = 7
BUDGET = 48
WAIT = (18, 27)
COST = (10, 7)
SMEM_SPEC = pl.BlockSpec(memory_space=pltpu.SMEM)
VMEM_SPEC = pl.BlockSpec(memory_space=pltpu.VMEM)
ANY_SPEC = pl.BlockSpec(memory_space=pl.ANY)


class Geometry:
    def __init__(self, rows, band, batches, slots):
        self.rows, self.band, self.batches, self.slots = rows, band, batches, slots
        self.half = half = (band - 1) // 2
        self.reach = reach = half // 2
        self.own = rows * band
        low = [(-m, reach + m, band) for m in range(reach, 0, -1)]
        high = [(rows + m, 0, 3 * reach - m) for m in range(reach)]
        self.halo = sum(stop - start for _, start, stop in low)
        low_cut = [half - row for row, _, _ in low]
        high_cut = [rows - row + half for row, _, _ in high]
        early = (
            [(row, cut, stop) for (row, _, stop), cut in zip(low, low_cut)],
            [(row, start, cut) for (row, start, _), cut in zip(high, high_cut)],
        )
        late = (
            [(row, start, cut) for (row, start, _), cut in zip(low, low_cut)],
            [(row, cut, stop) for (row, _, stop), cut in zip(high, high_cut)],
        )
        self.early = sum(stop - start for _, start, stop in early[0])
        self.late = self.halo - self.early
        self.first_at = self.own
        self.early_at = self.own + self.halo
        self.spare = self.early_at + self.early
        cut = 6
        self.pieces = ((0, cut), (cut, self.halo - cut))
        self.halo_base = self.bases((low, high))
        self.early_base = self.bases(early)
        shifts = (rows, -rows)
        self.packs = [self.places(*pair) for pair in zip((low, high), shifts)]
        self.early_packs = [self.places(*pair) for pair in zip(early, shifts)]
        self.late_packs = [self.places(*pair) for pair in zip(late, shifts)]
        self.span = min(2 * reach, rows) * band
        self.quiet = [
            self.others(self.packs[1], 0, self.span),
            self.others(self.packs[0], self.own - self.span, self.own),
        ]
        self.list_size = batches + 2
        self.lengths_at = LISTS * self.list_size
        self.local_at = self.lengths_at + LISTS
        self.count_at = self.local_at + batches
        self.offsets_at = self.count_at + batches
        self.odd_at = self.offsets_at + slots * batches
        self.meta_size = self.odd_at + 1

    def bases(self, sides):
        found = {}
        for segments in sides:
            place = 0
            for row, start, stop in segments:
                found[row] = place - start
                place += stop - start
        return found

    def places(self, segments, shift):
        pack, place = ([], 0)
        for row, start, stop in segments:
            pack.append(((row + shift) * self.band + start, place, stop - start))
            place += stop - start
        return pack

    def others(self, pack, begin, end):
        touched = set()
        for start, _, count in pack:
            touched.update(range(start, start + count))
        runs = []
        for index in range(begin, end):
            if index in touched:
                continue
            if runs and sum(runs[-1]) == index:
                runs[-1] = (runs[-1][0], runs[-1][1] + 1)
            else:
                runs.append((index, 1))
        return runs

    def near_packs(self, piece):
        begin, count = self.pieces[piece]
        found = []
        for pack in self.packs:
            part = []
            for start, place, size in pack:
                low, high = max(place, begin), min(place + size, begin + count)
                if low < high:
                    part.append((start + low - place, low - begin, high - low))
            found.append(part)
        return found

    def pick(self, bases, shift, row, otherwise):
        value = otherwise
        for at, base in bases.items():
            value = jnp.where(row == at, base + shift, value)
        return value


def run_copies(copies):
    for copy in copies:
        copy.start()
    for copy in copies:
        copy.wait()


def by_parity(odd, body, first, second):
    @pl.when(jnp.logical_not(odd))
    def _():
        body(first, second)

    @pl.when(odd)
    def _():
        body(second, first)


CROSS_MANY, CROSS_FEW, NEAR_MANY, NEAR_FEW, INNER_MANY, INNER_FEW, CROSS = range(LISTS)


def build_lists(geo, index, centre_ref, offsets_ref, counts_ref, meta_ref):
    first = index * geo.rows
    odd = index % 2 == 1
    meta_ref[geo.odd_at] = odd.astype(jnp.int32)
    lengths = [jnp.int32(0)] * LISTS
    for b in range(geo.batches):
        local = centre_ref[b] - first
        count = counts_ref[b]
        meta_ref[geo.local_at + b] = local
        meta_ref[geo.count_at + b] = count
        low = high = jnp.bool_(False)
        for k in range(geo.slots):
            offset = offsets_ref[k, b]
            meta_ref[geo.offsets_at + k * geo.batches + b] = offset
            row = local + offset
            low = low | ((k < count) & (row < 0))
            high = high | ((k < count) & (row >= geo.rows))
        cross = (odd & high) | (jnp.logical_not(odd) & low)
        near = (odd & low) | (jnp.logical_not(odd) & high)
        inner = jnp.logical_not(low | high)
        many = count > 2
        few = (count > 0) & jnp.logical_not(many)
        kinds = [kind & size for kind in (cross, near, inner) for size in (many, few)]
        for which, member in enumerate(kinds + [cross]):
            meta_ref[which * geo.list_size + lengths[which]] = b
            lengths[which] = lengths[which] + member.astype(jnp.int32)
    for which in range(LISTS):
        meta_ref[which * geo.list_size + lengths[which]] = geo.batches
        meta_ref[geo.lengths_at + which] = lengths[which]


def zone(geo, odd, cross):
    span = geo.span if cross else geo.own - geo.span
    return pl.ds(jnp.where(odd == cross, geo.own - span, 0), span)


def pack_kernel(
    geo, density_ref, centre_in, offsets_in, counts_in,
    near_ref, cross_ref, meta_ref, acc_ref,
    centre_ref, offsets_ref, counts_ref, sems,
):
    index = lax.axis_index("blk")
    odd = index % 2 == 1

    def copies(up, down):
        return [
            pltpu.make_async_copy(
                density_ref.at[pl.ds(start, count)], ref.at[pl.ds(place, count)], sems.at[side, i]
            )
            for side, (pack, ref) in enumerate(zip(geo.packs, (up, down)))
            for i, (start, place, count) in enumerate(pack)
        ]

    def start(up, down):
        for copy in copies(up, down):
            copy.start()

    by_parity(odd, start, near_ref, cross_ref)
    scalars = [
        pltpu.make_async_copy(*pair, sems.at[2, i])
        for i, pair in enumerate(
            ((centre_in, centre_ref), (offsets_in, offsets_ref), (counts_in, counts_ref))
        )
    ]
    for copy in scalars:
        copy.start()
    for where in (zone(geo, odd, False), pl.ds(geo.first_at, geo.halo)):
        acc_ref[where] = jnp.zeros_like(acc_ref[where])
    for copy in scalars:
        copy.wait()
    build_lists(geo, index, centre_ref, offsets_ref, counts_ref, meta_ref)
    for copy in copies(near_ref, cross_ref):
        copy.wait()


def group_count(geo, meta_ref, which):
    return (meta_ref[geo.lengths_at + which] + GROUP - 1) // GROUP


def waits():
    return (lax.axis_index("blk") + 1) // 2 % 2 == 1


def inner_share(geo, meta_ref):
    before = BUDGET
    for which in (CROSS_MANY, CROSS_FEW, NEAR_MANY, NEAR_FEW):
        before = before - COST[which % 2] * group_count(geo, meta_ref, which)
    odd = meta_ref[geo.odd_at] == 1
    waiting = jnp.where(waits(), jnp.where(odd, WAIT[1], WAIT[0]), 0)
    share = []
    for which in (INNER_MANY, INNER_FEW):
        cost, count = COST[which % 2], group_count(geo, meta_ref, which)
        first = jnp.minimum(jnp.maximum(before, 0) // cost, count)
        second = jnp.minimum(jnp.maximum(waiting, 0) // cost, count - first)
        before = before - cost * first
        waiting = waiting - cost * second
        share.append((0, first, first + second, count))
    return share


def inner_part(geo, meta_ref, stage, refs):
    for which, width, bounds in zip(
        (INNER_MANY, INNER_FEW), (geo.slots, 2), inner_share(geo, meta_ref)
    ):
        each_group(
            geo,
            meta_ref,
            which,
            lambda chosen, width=width: add_whole(geo, chosen, width, *refs),
            begin=bounds[stage],
            end=bounds[stage + 1],
        )


def each_group(geo, meta_ref, which, body, size=GROUP, begin=0, end=None):
    length = meta_ref[geo.lengths_at + which]

    def step(i, carry):
        chosen = []
        for n in range(size):
            place = i * size + n
            there = place < length
            b = meta_ref[which * geo.list_size + jnp.minimum(place, length)]
            chosen.append((jnp.where(there, b, 0), there))
        body(chosen)
        return carry

    lax.fori_loop(begin, (length + size - 1) // size if end is None else end, step, 0)


class Slots:
    def __init__(self, geo, meta_ref, b, there, width):
        local = meta_ref[geo.local_at + b]
        count = jnp.where(there, meta_ref[geo.count_at + b], 0)
        self.offset = [meta_ref[geo.offsets_at + k * geo.batches + b] for k in range(width)]
        self.local = local
        self.row = [local + offset for offset in self.offset]
        self.live = [k < count for k in range(width)]
        self.own = [(row >= 0) & (row < geo.rows) for row in self.row]
        self.width = width


def panels(slots, ao_ref, b):
    return jnp.concatenate(
        [
            ao_ref[b, k] * jnp.where(slots.live[k], 1.0, 0.0).astype(ao_ref.dtype)
            for k in range(slots.width)
        ],
        axis=0,
    )


def gathered(tiles_ref, places):
    return jnp.concatenate(
        [jnp.concatenate([tiles_ref[place] for place in row], axis=1) for row in places], axis=0
    )


def potentials(xs, tiles, batches, kernel_ref):
    fs = [
        jnp.dot(t, x, preferred_element_type=jnp.float32).astype(jnp.bfloat16)
        for t, x in zip(tiles, xs)
    ]
    return [
        jnp.dot(f, kernel_ref[b], preferred_element_type=jnp.float32) for f, b in zip(fs, batches)
    ]


def outer_product(x, h):
    return lax.dot_general(x, h, (((1,), (1,)), ((), ())), preferred_element_type=jnp.float32)


def chain(xs, tiles, batches, kernel_ref, weights_ref):
    gs = potentials(xs, tiles, batches, kernel_ref)
    hs = [(g * weights_ref[pl.ds(b, 1), :]).astype(jnp.bfloat16) for g, b in zip(gs, batches)]
    return [outer_product(x, h) for x, h in zip(xs, hs)]


def scatter(part, target, nb, acc_ref):
    for k, row in enumerate(target):
        for j, place in enumerate(row):
            acc_ref[place] += part[k * nb : (k + 1) * nb, j * nb : (j + 1) * nb]


def add_whole(
    geo, chosen, width, meta_ref, tiles_ref, ao_ref, kernel_ref, weights_ref, acc_ref, halo_ref=None
):
    xs, tiles, targets = ([], [], [])
    for b, there in chosen:
        slots = Slots(geo, meta_ref, b, there, width)
        xs.append(panels(slots, ao_ref, b))
        rows, target = ([], [])
        for k in range(width):
            band = [slots.offset[j] - slots.offset[k] + geo.half for j in range(width)]
            own = slots.own[k]
            base = jnp.where(slots.live[k] & own, slots.row[k], 0) * geo.band
            row = jnp.concatenate([tiles_ref[base + o] for o in band], axis=1)
            if halo_ref is not None:
                away = slots.live[k] & jnp.logical_not(own)
                outside = jnp.where(away, geo.pick(geo.halo_base, 0, slots.row[k], 0), 0)
                other = [halo_ref[jnp.where(away, outside + o, 0)] for o in band]
                row = jnp.where(away, jnp.concatenate(other, axis=1), row)
                base = jnp.where(away, outside + geo.first_at, base)
            rows.append(row)
            target.append(
                [
                    jnp.where(slots.live[k] & slots.live[j], base + band[j], geo.spare)
                    for j in range(width)
                ]
            )
        tiles.append(jnp.concatenate(rows, axis=0))
        targets.append(target)
    parts = chain(xs, tiles, [b for b, _ in chosen], kernel_ref, weights_ref)
    for part, target in zip(parts, targets):
        scatter(part, target, ao_ref.shape[2], acc_ref)


def add_own(geo, chosen, width, meta_ref, tiles_ref, ao_ref, kernel_ref, weights_ref, acc_ref):
    xs, tiles, targets = ([], [], [])
    for b, there in chosen:
        slots = Slots(geo, meta_ref, b, there, width)
        xs.append(panels(slots, ao_ref, b))
        places, target = ([], [])
        for k in range(width):
            row = slots.row[k]
            band = [slots.offset[j] - slots.offset[k] + geo.half for j in range(width)]
            base = jnp.where(slots.own[k], row, 0) * geo.band
            places.append([base + o for o in band])
            base = geo.pick(geo.early_base, geo.early_at, row, base)
            target.append(
                [
                    jnp.where(
                        slots.live[k] & slots.live[j] & slots.own[j], base + band[j], geo.spare
                    )
                    for j in range(width)
                ]
            )
        tiles.append(gathered(tiles_ref, places))
        targets.append(target)
    parts = chain(xs, tiles, [b for b, _ in chosen], kernel_ref, weights_ref)
    for part, target in zip(parts, targets):
        scatter(part, target, ao_ref.shape[2], acc_ref)


def halo_rows(geo, meta_ref, slots):
    odd = meta_ref[geo.odd_at] == 1
    rows, places, present = ([], [], [])
    for i in range(geo.reach):
        row = jnp.where(odd, geo.rows + i, i - geo.reach)
        place, found = (jnp.int32(0), jnp.bool_(False))
        for k in range(slots.width):
            hit = slots.live[k] & (slots.row[k] == row)
            place = jnp.where(hit, k, place)
            found = found | hit
        rows.append(row)
        places.append(place)
        present.append(found)
    return rows, places, present


def add_corner(geo, chosen, meta_ref, halo_ref, ao_ref, kernel_ref, weights_ref, h_ref, total_ref):
    nb = ao_ref.shape[2]
    factor = lambda flag: jnp.where(flag, 1.0, 0.0)
    xs, sides, tiles, masks = ([], [], [], [])
    for b, there in chosen:
        slots = Slots(geo, meta_ref, b, there, geo.slots)
        rows, places, present = halo_rows(geo, meta_ref, slots)
        xs.append(panels(slots, ao_ref, b))
        sides.append(
            jnp.concatenate(
                [
                    ao_ref[b, place] * factor(found).astype(ao_ref.dtype)
                    for place, found in zip(places, present)
                ],
                axis=0,
            )
        )
        picked = []
        for row, found in zip(rows, present):
            base = geo.pick(geo.halo_base, 0, row, 0) - row + geo.half
            picked.append([jnp.where(found, base + column, 0) for column in slots.row])
        tiles.append(gathered(halo_ref, picked))
        masks.append([factor(found) for found in present])
    gs = potentials(xs, tiles, [b for b, _ in chosen], kernel_ref)
    hs = []
    for g, mask, (b, there) in zip(gs, masks, chosen):
        weights = weights_ref[pl.ds(b, 1), :]
        h = jnp.concatenate(
            [g[i * nb : (i + 1) * nb] * (weights * mask[i]) for i in range(geo.reach)], axis=0
        ).astype(jnp.bfloat16)
        h_ref[jnp.where(there, b, geo.batches)] = h
        hs.append(h)
    total_ref[...] += outer_product(
        jnp.concatenate(sides, axis=1), jnp.concatenate(hs, axis=1)
    )


def add_columns(geo, chosen, width, meta_ref, ao_ref, h_ref, acc_ref):
    parts, targets = ([], [])
    for b, there in chosen:
        slots = Slots(geo, meta_ref, b, there, width)
        rows, _, present = halo_rows(geo, meta_ref, slots)
        parts.append(outer_product(ao_ref[b, pl.ds(0, width)].reshape(-1, ao_ref.shape[3]), h_ref[b]))
        targets.append(
            [
                [
                    jnp.where(
                        slots.live[k] & slots.own[k] & found,
                        slots.row[k] * geo.band + row - slots.row[k] + geo.half,
                        geo.spare,
                    )
                    for row, found in zip(rows, present)
                ]
                for k in range(width)
            ]
        )
    for part, target in zip(parts, targets):
        scatter(part, target, ao_ref.shape[2], acc_ref)


def early_kernel(
    geo, meta_ref, tiles_ref, ao_ref, kernel_ref, weights_ref, acc_in, acc_ref
):
    odd = meta_ref[geo.odd_at] == 1
    for where in (zone(geo, odd, True), pl.ds(geo.early_at, geo.early), pl.ds(geo.spare, 1)):
        acc_ref[where] = jnp.zeros_like(acc_ref[where])
    refs = (meta_ref, tiles_ref, ao_ref, kernel_ref, weights_ref, acc_ref)
    for which, width in ((CROSS_MANY, geo.slots), (CROSS_FEW, 2)):
        each_group(
            geo, meta_ref, which, lambda chosen, width=width: add_own(geo, chosen, width, *refs)
        )


def near_kernel(
    geo, meta_ref, halo_ref, tiles_ref, ao_ref, kernel_ref, weights_ref, acc_in, acc_ref,
    early_out, *outs,
):
    early_out[...] = acc_ref[pl.ds(geo.early_at, geo.early)].astype(early_out.dtype)
    refs = (meta_ref, tiles_ref, ao_ref, kernel_ref, weights_ref, acc_ref, halo_ref)
    for which, width in ((NEAR_MANY, geo.slots), (NEAR_FEW, 2)):
        each_group(
            geo, meta_ref, which, lambda chosen, width=width: add_whole(geo, chosen, width, *refs)
        )
    for out, (start, count) in zip(outs, geo.pieces):
        out[...] = acc_ref[pl.ds(geo.first_at + start, count)].astype(out.dtype)
    inner_part(geo, meta_ref, 0, refs[:-1])


def waiting_kernel(
    geo, meta_ref, tiles_ref, ao_ref, kernel_ref, weights_ref, acc_in, acc_ref, done_ref
):
    inner_part(geo, meta_ref, 1, (meta_ref, tiles_ref, ao_ref, kernel_ref, weights_ref, acc_ref))
    done_ref[0] = 1


def late_kernel(
    geo, meta_ref, done_ref, halo_ref, ao_ref, kernel_ref, weights_ref, h_ref, late_out, total_ref
):
    nb = ao_ref.shape[2]
    total_ref[...] = jnp.zeros_like(total_ref)

    def work(chosen):
        add_corner(
            geo, chosen, meta_ref, halo_ref, ao_ref, kernel_ref, weights_ref, h_ref, total_ref
        )

    groups = (meta_ref[geo.lengths_at + CROSS] + 1) // LATE_GROUP
    each_group(geo, meta_ref, CROSS, work, size=LATE_GROUP, end=groups)
    each_group(geo, meta_ref, CROSS, work, size=LATE_GROUP // 2, begin=2 * groups)
    for i in range(geo.reach):
        for j in range(geo.reach):
            late_out[i * geo.reach + j] = total_ref[
                i * nb : (i + 1) * nb, j * nb : (j + 1) * nb
            ].astype(late_out.dtype)


def inner_kernel(
    geo, meta_ref, first_a, first_b, tiles_ref, ao_ref, kernel_ref, weights_ref, h_ref, acc_in,
    acc_ref, out_ref, sems,
):
    odd = meta_ref[geo.odd_at] == 1
    refs = (meta_ref, tiles_ref, ao_ref, kernel_ref, weights_ref, acc_ref)
    inner_part(geo, meta_ref, 2, refs)

    def add_near(up, down):
        for piece, ref in enumerate((first_a, first_b)):
            for start, place, count in geo.near_packs(piece)[0 if up else 1]:
                acc_ref[pl.ds(start, count)] += ref[pl.ds(place, count)].astype(jnp.float32)

    by_parity(odd, add_near, True, False)
    done = zone(geo, odd, False)
    copy = pltpu.make_async_copy(acc_ref.at[done], out_ref.at[done], sems.at[0])
    copy.start()
    for which, width in ((CROSS_MANY, geo.slots), (CROSS_FEW, 2)):
        each_group(
            geo,
            meta_ref,
            which,
            lambda chosen, width=width: add_columns(
                geo, chosen, width, meta_ref, ao_ref, h_ref, acc_ref
            ),
        )

    def write_quiet(up, down):
        run_copies(
            [
                pltpu.make_async_copy(
                    acc_ref.at[pl.ds(start, count)], out_ref.at[pl.ds(start, count)], sems.at[1 + i]
                )
                for i, (start, count) in enumerate(geo.quiet[0 if up else 1])
            ]
        )

    by_parity(odd, write_quiet, True, False)
    copy.wait()


def finish_cross(geo, odd, parts, acc_ref, out_ref, total, sems):
    def add(up, down):
        copies = []
        for packs, ref in parts:
            for start, place, count in packs[0 if up else 1]:
                spot = pl.ds(len(copies) * geo.band, count)
                total[spot] = acc_ref[pl.ds(start, count)] + ref[pl.ds(place, count)].astype(
                    jnp.float32
                )
                copy = pltpu.make_async_copy(
                    total.at[spot], out_ref.at[pl.ds(start, count)], sems.at[len(copies)]
                )
                copy.start()
                copies.append(copy)
        for copy in copies:
            copy.wait()

    by_parity(odd, add, False, True)


def has_time(geo, meta_ref):
    left = [bounds[3] - bounds[2] for bounds in inner_share(geo, meta_ref)]
    return waits() & (left[0] + left[1] == 0)


def early_join_kernel(geo, meta_ref, early_ref, acc_ref, out_in, out_ref, total, sems):
    @pl.when(has_time(geo, meta_ref))
    def _():
        odd = meta_ref[geo.odd_at] == 1
        finish_cross(geo, odd, ((geo.early_packs, early_ref),), acc_ref, out_ref, total, sems)


def finish_kernel(geo, meta_ref, late_ref, early_ref, acc_ref, out_in, out_ref, total, sems):
    odd = meta_ref[geo.odd_at] == 1
    late = (geo.late_packs, late_ref)
    joined = has_time(geo, meta_ref)

    @pl.when(joined)
    def _():
        finish_cross(geo, odd, (late,), acc_ref, out_ref, total, sems)

    @pl.when(jnp.logical_not(joined))
    def _():
        parts = ((geo.early_packs, early_ref), late)
        finish_cross(geo, odd, parts, acc_ref, out_ref, total, sems)


def call(kernel, out_shape, in_specs, out_specs, scratch, aliases=None, cost=None):
    return pl.pallas_call(
        kernel,
        out_shape=out_shape,
        in_specs=in_specs,
        out_specs=out_specs,
        scratch_shapes=scratch,
        input_output_aliases=aliases or {},
        cost_estimate=cost,
        compiler_params=pltpu.CompilerParams(vmem_limit_bytes=16 * MIB),
    )


def to_first(x, size):
    pairs = [(i, i + 1) for i in range(0, size - 1, 2)]
    got = lax.ppermute(x, "blk", pairs + [(j, i) for i, j in pairs])
    return pltpu.with_memory_space_constraint(got, pltpu.VMEM)


def to_second(x, size):
    pairs = [(i, i + 1) for i in range(1, size - 1, 2)]
    got = lax.ppermute(x, "blk", pairs + [(j, i) for i, j in pairs])
    return pltpu.with_memory_space_constraint(got, pltpu.VMEM)


def local(density, ao_values, kernel, grid_weights, centre, sig_offsets, counts):
    rows, band, nb, _ = density.shape
    batches, slots, _, pts = ao_values.shape
    size = lax.axis_size("blk")
    geo = Geometry(rows, band, batches, slots)
    in_hbm = lambda x: pltpu.with_memory_space_constraint(x, pltpu.HBM)
    tiles = density.reshape(geo.own, nb, nb)
    pack = lambda count: pltpu.VMEM((count, nb, nb), jnp.bfloat16)
    dma = pltpu.SemaphoreType.DMA
    acc_type = pltpu.VMEM((geo.spare + 1, nb, nb), jnp.float32)

    near_halo, cross_halo, meta, acc = call(
        functools.partial(pack_kernel, geo),
        (pack(geo.halo),) * 2 + (pltpu.SMEM((geo.meta_size,), jnp.int32), acc_type),
        [ANY_SPEC] * 4,
        (VMEM_SPEC,) * 2 + (SMEM_SPEC, VMEM_SPEC),
        [
            pltpu.SMEM((batches,), jnp.int32),
            pltpu.SMEM((slots, batches), jnp.int32),
            pltpu.SMEM((batches,), jnp.int32),
            dma((3, max(geo.reach, 3))),
        ],
        cost=pl.CostEstimate(flops=10**10, bytes_accessed=10**8, transcendentals=0),
    )(in_hbm(tiles), in_hbm(centre), in_hbm(sig_offsets.T), in_hbm(counts))
    cross_halo = to_second(cross_halo, size)
    near_halo = to_first(near_halo, size)

    panel = (tiles, ao_values, kernel, grid_weights)
    acc = call(
        functools.partial(early_kernel, geo),
        acc_type,
        [SMEM_SPEC] + [VMEM_SPEC] * 5,
        VMEM_SPEC,
        [],
        {5: 0},
    )(meta, *panel, acc)

    acc, early, *first = call(
        functools.partial(near_kernel, geo),
        (acc_type, pack(geo.early)) + tuple(pack(count) for _, count in geo.pieces),
        [SMEM_SPEC] + [VMEM_SPEC] * 6,
        (VMEM_SPEC,) * 4,
        [],
        {6: 0},
    )(meta, near_halo, *panel, acc)
    early = to_second(early, size)
    first = [to_first(piece, size) for piece in first]

    acc, done = call(
        functools.partial(waiting_kernel, geo),
        (acc_type, pltpu.SMEM((1,), jnp.int32)),
        [SMEM_SPEC] + [VMEM_SPEC] * 5,
        (VMEM_SPEC, SMEM_SPEC),
        [],
        {5: 0},
    )(meta, *panel, acc)

    h_type = pltpu.VMEM((batches + 1, geo.reach * nb, pts), jnp.bfloat16)
    h, late = call(
        functools.partial(late_kernel, geo),
        (h_type, pack(geo.late)),
        [SMEM_SPEC] * 2 + [VMEM_SPEC] * 4,
        (VMEM_SPEC,) * 2,
        [pltpu.VMEM((geo.reach * nb, geo.reach * nb), jnp.float32)],
    )(meta, done, cross_halo, *panel[1:])
    late = to_second(late, size)

    whole = jax.ShapeDtypeStruct((geo.own, nb, nb), jnp.float32)
    acc, out = call(
        functools.partial(inner_kernel, geo),
        (acc_type, whole),
        [SMEM_SPEC] + [VMEM_SPEC] * 8,
        (VMEM_SPEC, ANY_SPEC),
        [dma((1 + max(len(runs) for runs in geo.quiet),))],
        {8: 0},
    )(meta, *first, *panel, h, acc)

    for kernel_of, got, parts in (
        (early_join_kernel, (early,), geo.reach),
        (finish_kernel, (late, early), 2 * geo.reach),
    ):
        out = call(
            functools.partial(kernel_of, geo),
            whole,
            [SMEM_SPEC] + [VMEM_SPEC] * (len(got) + 1) + [ANY_SPEC],
            ANY_SPEC,
            [pltpu.VMEM((parts * band, nb, nb), jnp.float32), dma((parts,))],
            {len(got) + 2: 0},
        )(meta, *got, acc, out)
    return out.reshape(rows, band, nb, nb)


def solution(mesh):
    placed = (
        P(("groups", "blk"), None, None, None),
        P(("groups", "blk"), None, None, None),
        P(("groups", "blk"), None, None),
        P(("groups", "blk"), None),
        P(("groups", "blk")),
        P(("groups", "blk"), None),
        P(("groups", "blk")),
    )
    return jax.shard_map(
        local,
        mesh=mesh,
        in_specs=placed,
        out_specs=P(("groups", "blk"), None, None, None),
        check_vma=False,
    )
```

```python
import functools

import jax
import jax.numpy as jnp
from jax import lax
from jax.experimental import pallas as pl
from jax.experimental.pallas import tpu as pltpu
from jax.sharding import PartitionSpec as P

MIB = 1 << 20
GROUP = 2
LATE_GROUP = 4
LISTS = 7
BUDGET = 40
WAIT = (18, 27)
COST = (10, 7)
SMEM_SPEC = pl.BlockSpec(memory_space=pltpu.SMEM)
VMEM_SPEC = pl.BlockSpec(memory_space=pltpu.VMEM)
ANY_SPEC = pl.BlockSpec(memory_space=pl.ANY)


class Geometry:
    def __init__(self, rows, band, batches, slots):
        self.rows, self.band, self.batches, self.slots = rows, band, batches, slots
        self.half = half = (band - 1) // 2
        self.reach = reach = half // 2
        self.own = rows * band
        low = [(-m, reach + m, band) for m in range(reach, 0, -1)]
        high = [(rows + m, 0, 3 * reach - m) for m in range(reach)]
        self.halo = sum(stop - start for _, start, stop in low)
        low_cut = [half - row for row, _, _ in low]
        high_cut = [rows - row + half for row, _, _ in high]
        early = (
            [(row, cut, stop) for (row, _, stop), cut in zip(low, low_cut)],
            [(row, start, cut) for (row, start, _), cut in zip(high, high_cut)],
        )
        late = (
            [(row, start, cut) for (row, start, _), cut in zip(low, low_cut)],
            [(row, cut, stop) for (row, _, stop), cut in zip(high, high_cut)],
        )
        self.early = sum(stop - start for _, start, stop in early[0])
        self.late = self.halo - self.early
        self.first_at = self.own
        self.early_at = self.own + self.halo
        self.spare = self.early_at + self.early
        cut = 6
        self.pieces = ((0, cut), (cut, self.halo - cut))
        self.halo_base = self.bases((low, high))
        self.early_base = self.bases(early)
        shifts = (rows, -rows)
        self.packs = [self.places(*pair) for pair in zip((low, high), shifts)]
        self.early_packs = [self.places(*pair) for pair in zip(early, shifts)]
        self.late_packs = [self.places(*pair) for pair in zip(late, shifts)]
        self.span = min(2 * reach, rows) * band
        self.quiet = [
            self.others(self.packs[1], 0, self.span),
            self.others(self.packs[0], self.own - self.span, self.own),
        ]
        self.list_size = batches + 2
        self.lengths_at = LISTS * self.list_size
        self.local_at = self.lengths_at + LISTS
        self.count_at = self.local_at + batches
        self.offsets_at = self.count_at + batches
        self.odd_at = self.offsets_at + slots * batches
        self.meta_size = self.odd_at + 1

    def bases(self, sides):
        found = {}
        for segments in sides:
            place = 0
            for row, start, stop in segments:
                found[row] = place - start
                place += stop - start
        return found

    def places(self, segments, shift):
        pack, place = ([], 0)
        for row, start, stop in segments:
            pack.append(((row + shift) * self.band + start, place, stop - start))
            place += stop - start
        return pack

    def others(self, pack, begin, end):
        touched = set()
        for start, _, count in pack:
            touched.update(range(start, start + count))
        runs = []
        for index in range(begin, end):
            if index in touched:
                continue
            if runs and sum(runs[-1]) == index:
                runs[-1] = (runs[-1][0], runs[-1][1] + 1)
            else:
                runs.append((index, 1))
        return runs

    def near_packs(self, piece):
        begin, count = self.pieces[piece]
        found = []
        for pack in self.packs:
            part = []
            for start, place, size in pack:
                low, high = max(place, begin), min(place + size, begin + count)
                if low < high:
                    part.append((start + low - place, low - begin, high - low))
            found.append(part)
        return found

    def pick(self, bases, shift, row, otherwise):
        value = otherwise
        for at, base in bases.items():
            value = jnp.where(row == at, base + shift, value)
        return value


def run_copies(copies):
    for copy in copies:
        copy.start()
    for copy in copies:
        copy.wait()


def by_parity(odd, body, first, second):
    @pl.when(jnp.logical_not(odd))
    def _():
        body(first, second)

    @pl.when(odd)
    def _():
        body(second, first)


CROSS_MANY, CROSS_FEW, NEAR_MANY, NEAR_FEW, INNER_MANY, INNER_FEW, CROSS = range(LISTS)


def build_lists(geo, index, centre_ref, offsets_ref, counts_ref, meta_ref):
    first = index * geo.rows
    odd = index % 2 == 1
    meta_ref[geo.odd_at] = odd.astype(jnp.int32)
    lengths = [jnp.int32(0)] * LISTS
    for b in range(geo.batches):
        local = centre_ref[b] - first
        count = counts_ref[b]
        meta_ref[geo.local_at + b] = local
        meta_ref[geo.count_at + b] = count
        low = high = jnp.bool_(False)
        for k in range(geo.slots):
            offset = offsets_ref[k, b]
            meta_ref[geo.offsets_at + k * geo.batches + b] = offset
            row = local + offset
            low = low | ((k < count) & (row < 0))
            high = high | ((k < count) & (row >= geo.rows))
        cross = (odd & high) | (jnp.logical_not(odd) & low)
        near = (odd & low) | (jnp.logical_not(odd) & high)
        inner = jnp.logical_not(low | high)
        many = count > 2
        few = (count > 0) & jnp.logical_not(many)
        kinds = [kind & size for kind in (cross, near, inner) for size in (many, few)]
        for which, member in enumerate(kinds + [cross]):
            meta_ref[which * geo.list_size + lengths[which]] = b
            lengths[which] = lengths[which] + member.astype(jnp.int32)
    for which in range(LISTS):
        meta_ref[which * geo.list_size + lengths[which]] = geo.batches
        meta_ref[geo.lengths_at + which] = lengths[which]


def zone(geo, odd, cross):
    span = geo.span if cross else geo.own - geo.span
    return pl.ds(jnp.where(odd == cross, geo.own - span, 0), span)


def pack_kernel(
    geo, density_ref, centre_in, offsets_in, counts_in,
    near_ref, cross_ref, meta_ref, acc_ref,
    centre_ref, offsets_ref, counts_ref, sems,
):
    index = lax.axis_index("blk")
    odd = index % 2 == 1

    def copies(up, down):
        return [
            pltpu.make_async_copy(
                density_ref.at[pl.ds(start, count)], ref.at[pl.ds(place, count)], sems.at[side, i]
            )
            for side, (pack, ref) in enumerate(zip(geo.packs, (up, down)))
            for i, (start, place, count) in enumerate(pack)
        ]

    def start(up, down):
        for copy in copies(up, down):
            copy.start()

    by_parity(odd, start, near_ref, cross_ref)
    scalars = [
        pltpu.make_async_copy(*pair, sems.at[2, i])
        for i, pair in enumerate(
            ((centre_in, centre_ref), (offsets_in, offsets_ref), (counts_in, counts_ref))
        )
    ]
    for copy in scalars:
        copy.start()
    for where in (zone(geo, odd, False), pl.ds(geo.first_at, geo.halo)):
        acc_ref[where] = jnp.zeros_like(acc_ref[where])
    for copy in scalars:
        copy.wait()
    build_lists(geo, index, centre_ref, offsets_ref, counts_ref, meta_ref)
    for copy in copies(near_ref, cross_ref):
        copy.wait()


def group_count(geo, meta_ref, which):
    return (meta_ref[geo.lengths_at + which] + GROUP - 1) // GROUP


def waits():
    return (lax.axis_index("blk") + 1) // 2 % 2 == 1


def inner_share(geo, meta_ref):
    before = BUDGET
    for which in (CROSS_MANY, CROSS_FEW, NEAR_MANY, NEAR_FEW):
        before = before - COST[which % 2] * group_count(geo, meta_ref, which)
    odd = meta_ref[geo.odd_at] == 1
    waiting = jnp.where(waits(), jnp.where(odd, WAIT[1], WAIT[0]), 0)
    share = []
    for which in (INNER_MANY, INNER_FEW):
        cost, count = COST[which % 2], group_count(geo, meta_ref, which)
        first = jnp.minimum(jnp.maximum(before, 0) // cost, count)
        second = jnp.minimum(jnp.maximum(waiting, 0) // cost, count - first)
        before = before - cost * first
        waiting = waiting - cost * second
        share.append((0, first, first + second, count))
    return share


def inner_part(geo, meta_ref, stage, refs):
    for which, width, bounds in zip(
        (INNER_MANY, INNER_FEW), (geo.slots, 2), inner_share(geo, meta_ref)
    ):
        each_group(
            geo,
            meta_ref,
            which,
            lambda chosen, width=width: add_whole(geo, chosen, width, *refs),
            begin=bounds[stage],
            end=bounds[stage + 1],
        )


def each_group(geo, meta_ref, which, body, size=GROUP, begin=0, end=None):
    length = meta_ref[geo.lengths_at + which]

    def step(i, carry):
        chosen = []
        for n in range(size):
            place = i * size + n
            there = place < length
            b = meta_ref[which * geo.list_size + jnp.minimum(place, length)]
            chosen.append((jnp.where(there, b, 0), there))
        body(chosen)
        return carry

    lax.fori_loop(begin, (length + size - 1) // size if end is None else end, step, 0)


class Slots:
    def __init__(self, geo, meta_ref, b, there, width):
        local = meta_ref[geo.local_at + b]
        count = jnp.where(there, meta_ref[geo.count_at + b], 0)
        self.offset = [meta_ref[geo.offsets_at + k * geo.batches + b] for k in range(width)]
        self.local = local
        self.row = [local + offset for offset in self.offset]
        self.live = [k < count for k in range(width)]
        self.own = [(row >= 0) & (row < geo.rows) for row in self.row]
        self.width = width


def panels(slots, ao_ref, b):
    return jnp.concatenate(
        [
            ao_ref[b, k] * jnp.where(slots.live[k], 1.0, 0.0).astype(ao_ref.dtype)
            for k in range(slots.width)
        ],
        axis=0,
    )


def gathered(tiles_ref, places):
    return jnp.concatenate(
        [jnp.concatenate([tiles_ref[place] for place in row], axis=1) for row in places], axis=0
    )


def potentials(xs, tiles, batches, kernel_ref):
    fs = [
        jnp.dot(t, x, preferred_element_type=jnp.float32).astype(jnp.bfloat16)
        for t, x in zip(tiles, xs)
    ]
    return [
        jnp.dot(f, kernel_ref[b], preferred_element_type=jnp.float32) for f, b in zip(fs, batches)
    ]


def outer_product(x, h):
    return lax.dot_general(x, h, (((1,), (1,)), ((), ())), preferred_element_type=jnp.float32)


def chain(xs, tiles, batches, kernel_ref, weights_ref):
    gs = potentials(xs, tiles, batches, kernel_ref)
    hs = [(g * weights_ref[pl.ds(b, 1), :]).astype(jnp.bfloat16) for g, b in zip(gs, batches)]
    return [outer_product(x, h) for x, h in zip(xs, hs)]


def scatter(part, target, nb, acc_ref):
    for k, row in enumerate(target):
        for j, place in enumerate(row):
            acc_ref[place] += part[k * nb : (k + 1) * nb, j * nb : (j + 1) * nb]


def add_whole(
    geo, chosen, width, meta_ref, tiles_ref, ao_ref, kernel_ref, weights_ref, acc_ref, halo_ref=None
):
    xs, tiles, targets = ([], [], [])
    for b, there in chosen:
        slots = Slots(geo, meta_ref, b, there, width)
        xs.append(panels(slots, ao_ref, b))
        rows, target = ([], [])
        for k in range(width):
            band = [slots.offset[j] - slots.offset[k] + geo.half for j in range(width)]
            own = slots.own[k]
            base = jnp.where(slots.live[k] & own, slots.row[k], 0) * geo.band
            row = jnp.concatenate([tiles_ref[base + o] for o in band], axis=1)
            if halo_ref is not None:
                away = slots.live[k] & jnp.logical_not(own)
                outside = jnp.where(away, geo.pick(geo.halo_base, 0, slots.row[k], 0), 0)
                other = [halo_ref[jnp.where(away, outside + o, 0)] for o in band]
                row = jnp.where(away, jnp.concatenate(other, axis=1), row)
                base = jnp.where(away, outside + geo.first_at, base)
            rows.append(row)
            target.append(
                [
                    jnp.where(slots.live[k] & slots.live[j], base + band[j], geo.spare)
                    for j in range(width)
                ]
            )
        tiles.append(jnp.concatenate(rows, axis=0))
        targets.append(target)
    parts = chain(xs, tiles, [b for b, _ in chosen], kernel_ref, weights_ref)
    for part, target in zip(parts, targets):
        scatter(part, target, ao_ref.shape[2], acc_ref)


def add_own(geo, chosen, width, meta_ref, tiles_ref, ao_ref, kernel_ref, weights_ref, acc_ref):
    xs, tiles, targets = ([], [], [])
    for b, there in chosen:
        slots = Slots(geo, meta_ref, b, there, width)
        xs.append(panels(slots, ao_ref, b))
        places, target = ([], [])
        for k in range(width):
            row = slots.row[k]
            band = [slots.offset[j] - slots.offset[k] + geo.half for j in range(width)]
            base = jnp.where(slots.own[k], row, 0) * geo.band
            places.append([base + o for o in band])
            base = geo.pick(geo.early_base, geo.early_at, row, base)
            target.append(
                [
                    jnp.where(
                        slots.live[k] & slots.live[j] & slots.own[j], base + band[j], geo.spare
                    )
                    for j in range(width)
                ]
            )
        tiles.append(gathered(tiles_ref, places))
        targets.append(target)
    parts = chain(xs, tiles, [b for b, _ in chosen], kernel_ref, weights_ref)
    for part, target in zip(parts, targets):
        scatter(part, target, ao_ref.shape[2], acc_ref)


def halo_rows(geo, meta_ref, slots):
    odd = meta_ref[geo.odd_at] == 1
    rows, places, present = ([], [], [])
    for i in range(geo.reach):
        row = jnp.where(odd, geo.rows + i, i - geo.reach)
        place, found = (jnp.int32(0), jnp.bool_(False))
        for k in range(slots.width):
            hit = slots.live[k] & (slots.row[k] == row)
            place = jnp.where(hit, k, place)
            found = found | hit
        rows.append(row)
        places.append(place)
        present.append(found)
    return rows, places, present


def add_corner(geo, chosen, meta_ref, halo_ref, ao_ref, kernel_ref, weights_ref, h_ref, total_ref):
    nb = ao_ref.shape[2]
    factor = lambda flag: jnp.where(flag, 1.0, 0.0)
    xs, sides, tiles, masks = ([], [], [], [])
    for b, there in chosen:
        slots = Slots(geo, meta_ref, b, there, geo.slots)
        rows, places, present = halo_rows(geo, meta_ref, slots)
        xs.append(panels(slots, ao_ref, b))
        sides.append(
            jnp.concatenate(
                [
                    ao_ref[b, place] * factor(found).astype(ao_ref.dtype)
                    for place, found in zip(places, present)
                ],
                axis=0,
            )
        )
        picked = []
        for row, found in zip(rows, present):
            base = geo.pick(geo.halo_base, 0, row, 0) - row + geo.half
            picked.append([jnp.where(found, base + column, 0) for column in slots.row])
        tiles.append(gathered(halo_ref, picked))
        masks.append([factor(found) for found in present])
    gs = potentials(xs, tiles, [b for b, _ in chosen], kernel_ref)
    hs = []
    for g, mask, (b, there) in zip(gs, masks, chosen):
        weights = weights_ref[pl.ds(b, 1), :]
        h = jnp.concatenate(
            [g[i * nb : (i + 1) * nb] * (weights * mask[i]) for i in range(geo.reach)], axis=0
        ).astype(jnp.bfloat16)
        h_ref[jnp.where(there, b, geo.batches)] = h
        hs.append(h)
    total_ref[...] += outer_product(
        jnp.concatenate(sides, axis=1), jnp.concatenate(hs, axis=1)
    )


def add_columns(geo, chosen, width, meta_ref, ao_ref, h_ref, acc_ref):
    parts, targets = ([], [])
    for b, there in chosen:
        slots = Slots(geo, meta_ref, b, there, width)
        rows, _, present = halo_rows(geo, meta_ref, slots)
        parts.append(outer_product(ao_ref[b, pl.ds(0, width)].reshape(-1, ao_ref.shape[3]), h_ref[b]))
        targets.append(
            [
                [
                    jnp.where(
                        slots.live[k] & slots.own[k] & found,
                        slots.row[k] * geo.band + row - slots.row[k] + geo.half,
                        geo.spare,
                    )
                    for row, found in zip(rows, present)
                ]
                for k in range(width)
            ]
        )
    for part, target in zip(parts, targets):
        scatter(part, target, ao_ref.shape[2], acc_ref)


def early_kernel(
    geo, meta_ref, tiles_ref, ao_ref, kernel_ref, weights_ref, acc_in, acc_ref
):
    odd = meta_ref[geo.odd_at] == 1
    for where in (zone(geo, odd, True), pl.ds(geo.early_at, geo.early), pl.ds(geo.spare, 1)):
        acc_ref[where] = jnp.zeros_like(acc_ref[where])
    refs = (meta_ref, tiles_ref, ao_ref, kernel_ref, weights_ref, acc_ref)
    for which, width in ((CROSS_MANY, geo.slots), (CROSS_FEW, 2)):
        each_group(
            geo, meta_ref, which, lambda chosen, width=width: add_own(geo, chosen, width, *refs)
        )


def near_kernel(
    geo, meta_ref, halo_ref, tiles_ref, ao_ref, kernel_ref, weights_ref, acc_in, acc_ref,
    early_out, *outs,
):
    early_out[...] = acc_ref[pl.ds(geo.early_at, geo.early)].astype(early_out.dtype)
    refs = (meta_ref, tiles_ref, ao_ref, kernel_ref, weights_ref, acc_ref, halo_ref)
    for which, width in ((NEAR_MANY, geo.slots), (NEAR_FEW, 2)):
        each_group(
            geo, meta_ref, which, lambda chosen, width=width: add_whole(geo, chosen, width, *refs)
        )
    for out, (start, count) in zip(outs, geo.pieces):
        out[...] = acc_ref[pl.ds(geo.first_at + start, count)].astype(out.dtype)
    inner_part(geo, meta_ref, 0, refs[:-1])


def waiting_kernel(
    geo, meta_ref, tiles_ref, ao_ref, kernel_ref, weights_ref, acc_in, acc_ref, done_ref
):
    inner_part(geo, meta_ref, 1, (meta_ref, tiles_ref, ao_ref, kernel_ref, weights_ref, acc_ref))
    done_ref[0] = 1


def late_kernel(
    geo, meta_ref, done_ref, halo_ref, ao_ref, kernel_ref, weights_ref, h_ref, late_out, total_ref
):
    nb = ao_ref.shape[2]
    total_ref[...] = jnp.zeros_like(total_ref)

    def work(chosen):
        add_corner(
            geo, chosen, meta_ref, halo_ref, ao_ref, kernel_ref, weights_ref, h_ref, total_ref
        )

    groups = (meta_ref[geo.lengths_at + CROSS] + 1) // LATE_GROUP
    each_group(geo, meta_ref, CROSS, work, size=LATE_GROUP, end=groups)
    each_group(geo, meta_ref, CROSS, work, size=LATE_GROUP // 2, begin=2 * groups)
    for i in range(geo.reach):
        for j in range(geo.reach):
            late_out[i * geo.reach + j] = total_ref[
                i * nb : (i + 1) * nb, j * nb : (j + 1) * nb
            ].astype(late_out.dtype)


def inner_kernel(
    geo, meta_ref, first_a, first_b, tiles_ref, ao_ref, kernel_ref, weights_ref, h_ref, acc_in,
    acc_ref, out_ref, sems,
):
    odd = meta_ref[geo.odd_at] == 1
    refs = (meta_ref, tiles_ref, ao_ref, kernel_ref, weights_ref, acc_ref)
    inner_part(geo, meta_ref, 2, refs)

    def add_near(up, down):
        for piece, ref in enumerate((first_a, first_b)):
            for start, place, count in geo.near_packs(piece)[0 if up else 1]:
                acc_ref[pl.ds(start, count)] += ref[pl.ds(place, count)].astype(jnp.float32)

    by_parity(odd, add_near, True, False)
    done = zone(geo, odd, False)
    copy = pltpu.make_async_copy(acc_ref.at[done], out_ref.at[done], sems.at[0])
    copy.start()
    for which, width in ((CROSS_MANY, geo.slots), (CROSS_FEW, 2)):
        each_group(
            geo,
            meta_ref,
            which,
            lambda chosen, width=width: add_columns(
                geo, chosen, width, meta_ref, ao_ref, h_ref, acc_ref
            ),
        )

    def write_quiet(up, down):
        run_copies(
            [
                pltpu.make_async_copy(
                    acc_ref.at[pl.ds(start, count)], out_ref.at[pl.ds(start, count)], sems.at[1 + i]
                )
                for i, (start, count) in enumerate(geo.quiet[0 if up else 1])
            ]
        )

    by_parity(odd, write_quiet, True, False)
    copy.wait()


def finish_cross(geo, odd, parts, acc_ref, out_ref, total, sems):
    def add(up, down):
        copies = []
        for packs, ref in parts:
            for start, place, count in packs[0 if up else 1]:
                spot = pl.ds(len(copies) * geo.band, count)
                total[spot] = acc_ref[pl.ds(start, count)] + ref[pl.ds(place, count)].astype(
                    jnp.float32
                )
                copy = pltpu.make_async_copy(
                    total.at[spot], out_ref.at[pl.ds(start, count)], sems.at[len(copies)]
                )
                copy.start()
                copies.append(copy)
        for copy in copies:
            copy.wait()

    by_parity(odd, add, False, True)


def has_time(geo, meta_ref):
    left = [bounds[3] - bounds[2] for bounds in inner_share(geo, meta_ref)]
    return waits() & (left[0] + left[1] == 0)


def early_join_kernel(geo, meta_ref, early_ref, acc_ref, out_in, out_ref, total, sems):
    @pl.when(has_time(geo, meta_ref))
    def _():
        odd = meta_ref[geo.odd_at] == 1
        finish_cross(geo, odd, ((geo.early_packs, early_ref),), acc_ref, out_ref, total, sems)


def finish_kernel(geo, meta_ref, late_ref, early_ref, acc_ref, out_in, out_ref, total, sems):
    odd = meta_ref[geo.odd_at] == 1
    late = (geo.late_packs, late_ref)
    joined = has_time(geo, meta_ref)

    @pl.when(joined)
    def _():
        finish_cross(geo, odd, (late,), acc_ref, out_ref, total, sems)

    @pl.when(jnp.logical_not(joined))
    def _():
        parts = ((geo.early_packs, early_ref), late)
        finish_cross(geo, odd, parts, acc_ref, out_ref, total, sems)


def call(kernel, out_shape, in_specs, out_specs, scratch, aliases=None, cost=None):
    return pl.pallas_call(
        kernel,
        out_shape=out_shape,
        in_specs=in_specs,
        out_specs=out_specs,
        scratch_shapes=scratch,
        input_output_aliases=aliases or {},
        cost_estimate=cost,
        compiler_params=pltpu.CompilerParams(vmem_limit_bytes=16 * MIB),
    )


def to_first(x, size):
    pairs = [(i, i + 1) for i in range(0, size - 1, 2)]
    got = lax.ppermute(x, "blk", pairs + [(j, i) for i, j in pairs])
    return pltpu.with_memory_space_constraint(got, pltpu.VMEM)


def to_second(x, size):
    pairs = [(i, i + 1) for i in range(1, size - 1, 2)]
    got = lax.ppermute(x, "blk", pairs + [(j, i) for i, j in pairs])
    return pltpu.with_memory_space_constraint(got, pltpu.VMEM)


def local(density, ao_values, kernel, grid_weights, centre, sig_offsets, counts):
    rows, band, nb, _ = density.shape
    batches, slots, _, pts = ao_values.shape
    size = lax.axis_size("blk")
    geo = Geometry(rows, band, batches, slots)
    in_hbm = lambda x: pltpu.with_memory_space_constraint(x, pltpu.HBM)
    tiles = density.reshape(geo.own, nb, nb)
    pack = lambda count: pltpu.VMEM((count, nb, nb), jnp.bfloat16)
    dma = pltpu.SemaphoreType.DMA
    acc_type = pltpu.VMEM((geo.spare + 1, nb, nb), jnp.float32)

    near_halo, cross_halo, meta, acc = call(
        functools.partial(pack_kernel, geo),
        (pack(geo.halo),) * 2 + (pltpu.SMEM((geo.meta_size,), jnp.int32), acc_type),
        [ANY_SPEC] * 4,
        (VMEM_SPEC,) * 2 + (SMEM_SPEC, VMEM_SPEC),
        [
            pltpu.SMEM((batches,), jnp.int32),
            pltpu.SMEM((slots, batches), jnp.int32),
            pltpu.SMEM((batches,), jnp.int32),
            dma((3, max(geo.reach, 3))),
        ],
        cost=pl.CostEstimate(flops=10**10, bytes_accessed=10**8, transcendentals=0),
    )(in_hbm(tiles), in_hbm(centre), in_hbm(sig_offsets.T), in_hbm(counts))
    cross_halo = to_second(cross_halo, size)
    near_halo = to_first(near_halo, size)

    panel = (tiles, ao_values, kernel, grid_weights)
    acc = call(
        functools.partial(early_kernel, geo),
        acc_type,
        [SMEM_SPEC] + [VMEM_SPEC] * 5,
        VMEM_SPEC,
        [],
        {5: 0},
    )(meta, *panel, acc)

    acc, early, *first = call(
        functools.partial(near_kernel, geo),
        (acc_type, pack(geo.early)) + tuple(pack(count) for _, count in geo.pieces),
        [SMEM_SPEC] + [VMEM_SPEC] * 6,
        (VMEM_SPEC,) * 4,
        [],
        {6: 0},
    )(meta, near_halo, *panel, acc)
    early = to_second(early, size)
    first = [to_first(piece, size) for piece in first]

    acc, done = call(
        functools.partial(waiting_kernel, geo),
        (acc_type, pltpu.SMEM((1,), jnp.int32)),
        [SMEM_SPEC] + [VMEM_SPEC] * 5,
        (VMEM_SPEC, SMEM_SPEC),
        [],
        {5: 0},
    )(meta, *panel, acc)

    h_type = pltpu.VMEM((batches + 1, geo.reach * nb, pts), jnp.bfloat16)
    h, late = call(
        functools.partial(late_kernel, geo),
        (h_type, pack(geo.late)),
        [SMEM_SPEC] * 2 + [VMEM_SPEC] * 4,
        (VMEM_SPEC,) * 2,
        [pltpu.VMEM((geo.reach * nb, geo.reach * nb), jnp.float32)],
    )(meta, done, cross_halo, *panel[1:])
    late = to_second(late, size)

    whole = jax.ShapeDtypeStruct((geo.own, nb, nb), jnp.float32)
    acc, out = call(
        functools.partial(inner_kernel, geo),
        (acc_type, whole),
        [SMEM_SPEC] + [VMEM_SPEC] * 8,
        (VMEM_SPEC, ANY_SPEC),
        [dma((1 + max(len(runs) for runs in geo.quiet),))],
        {8: 0},
    )(meta, *first, *panel, h, acc)

    for kernel_of, got, parts in (
        (early_join_kernel, (early,), geo.reach),
        (finish_kernel, (late, early), 2 * geo.reach),
    ):
        out = call(
            functools.partial(kernel_of, geo),
            whole,
            [SMEM_SPEC] + [VMEM_SPEC] * (len(got) + 1) + [ANY_SPEC],
            ANY_SPEC,
            [pltpu.VMEM((parts * band, nb, nb), jnp.float32), dma((parts,))],
            {len(got) + 2: 0},
        )(meta, *got, acc, out)
    return out.reshape(rows, band, nb, nb)


def solution(mesh):
    placed = (
        P(("groups", "blk"), None, None, None),
        P(("groups", "blk"), None, None, None),
        P(("groups", "blk"), None, None),
        P(("groups", "blk"), None),
        P(("groups", "blk")),
        P(("groups", "blk"), None),
        P(("groups", "blk")),
    )
    return jax.shard_map(
        local,
        mesh=mesh,
        in_specs=placed,
        out_specs=P(("groups", "blk"), None, None, None),
        check_vma=False,
    )
```

```python
import functools

import jax
import jax.numpy as jnp
from jax import lax
from jax.experimental import pallas as pl
from jax.experimental.pallas import tpu as pltpu
from jax.sharding import PartitionSpec as P

MIB = 1 << 20
GROUP = 2
LATE_GROUP = 4
LISTS = 7
BUDGET = 44
WAIT = (18, 20)
COST = (10, 7)
SMEM_SPEC = pl.BlockSpec(memory_space=pltpu.SMEM)
VMEM_SPEC = pl.BlockSpec(memory_space=pltpu.VMEM)
ANY_SPEC = pl.BlockSpec(memory_space=pl.ANY)


class Geometry:
    def __init__(self, rows, band, batches, slots):
        self.rows, self.band, self.batches, self.slots = rows, band, batches, slots
        self.half = half = (band - 1) // 2
        self.reach = reach = half // 2
        self.own = rows * band
        low = [(-m, reach + m, band) for m in range(reach, 0, -1)]
        high = [(rows + m, 0, 3 * reach - m) for m in range(reach)]
        self.halo = sum(stop - start for _, start, stop in low)
        low_cut = [half - row for row, _, _ in low]
        high_cut = [rows - row + half for row, _, _ in high]
        early = (
            [(row, cut, stop) for (row, _, stop), cut in zip(low, low_cut)],
            [(row, start, cut) for (row, start, _), cut in zip(high, high_cut)],
        )
        late = (
            [(row, start, cut) for (row, start, _), cut in zip(low, low_cut)],
            [(row, cut, stop) for (row, _, stop), cut in zip(high, high_cut)],
        )
        self.early = sum(stop - start for _, start, stop in early[0])
        self.late = self.halo - self.early
        self.first_at = self.own
        self.early_at = self.own + self.halo
        self.spare = self.early_at + self.early
        cut = 6
        self.pieces = ((0, cut), (cut, self.halo - cut))
        self.halo_base = self.bases((low, high))
        self.early_base = self.bases(early)
        shifts = (rows, -rows)
        self.packs = [self.places(*pair) for pair in zip((low, high), shifts)]
        self.early_packs = [self.places(*pair) for pair in zip(early, shifts)]
        self.late_packs = [self.places(*pair) for pair in zip(late, shifts)]
        self.span = min(2 * reach, rows) * band
        self.quiet = [
            self.others(self.packs[1], 0, self.span),
            self.others(self.packs[0], self.own - self.span, self.own),
        ]
        self.list_size = batches + 2
        self.lengths_at = LISTS * self.list_size
        self.local_at = self.lengths_at + LISTS
        self.count_at = self.local_at + batches
        self.offsets_at = self.count_at + batches
        self.odd_at = self.offsets_at + slots * batches
        self.meta_size = self.odd_at + 1

    def bases(self, sides):
        found = {}
        for segments in sides:
            place = 0
            for row, start, stop in segments:
                found[row] = place - start
                place += stop - start
        return found

    def places(self, segments, shift):
        pack, place = ([], 0)
        for row, start, stop in segments:
            pack.append(((row + shift) * self.band + start, place, stop - start))
            place += stop - start
        return pack

    def others(self, pack, begin, end):
        touched = set()
        for start, _, count in pack:
            touched.update(range(start, start + count))
        runs = []
        for index in range(begin, end):
            if index in touched:
                continue
            if runs and sum(runs[-1]) == index:
                runs[-1] = (runs[-1][0], runs[-1][1] + 1)
            else:
                runs.append((index, 1))
        return runs

    def near_packs(self, piece):
        begin, count = self.pieces[piece]
        found = []
        for pack in self.packs:
            part = []
            for start, place, size in pack:
                low, high = max(place, begin), min(place + size, begin + count)
                if low < high:
                    part.append((start + low - place, low - begin, high - low))
            found.append(part)
        return found

    def pick(self, bases, shift, row, otherwise):
        value = otherwise
        for at, base in bases.items():
            value = jnp.where(row == at, base + shift, value)
        return value


def run_copies(copies):
    for copy in copies:
        copy.start()
    for copy in copies:
        copy.wait()


def by_parity(odd, body, first, second):
    @pl.when(jnp.logical_not(odd))
    def _():
        body(first, second)

    @pl.when(odd)
    def _():
        body(second, first)


CROSS_MANY, CROSS_FEW, NEAR_MANY, NEAR_FEW, INNER_MANY, INNER_FEW, CROSS = range(LISTS)


def build_lists(geo, index, centre_ref, offsets_ref, counts_ref, meta_ref):
    first = index * geo.rows
    odd = index % 2 == 1
    meta_ref[geo.odd_at] = odd.astype(jnp.int32)
    lengths = [jnp.int32(0)] * LISTS
    for b in range(geo.batches):
        local = centre_ref[b] - first
        count = counts_ref[b]
        meta_ref[geo.local_at + b] = local
        meta_ref[geo.count_at + b] = count
        low = high = jnp.bool_(False)
        for k in range(geo.slots):
            offset = offsets_ref[k, b]
            meta_ref[geo.offsets_at + k * geo.batches + b] = offset
            row = local + offset
            low = low | ((k < count) & (row < 0))
            high = high | ((k < count) & (row >= geo.rows))
        cross = (odd & high) | (jnp.logical_not(odd) & low)
        near = (odd & low) | (jnp.logical_not(odd) & high)
        inner = jnp.logical_not(low | high)
        many = count > 2
        few = (count > 0) & jnp.logical_not(many)
        kinds = [kind & size for kind in (cross, near, inner) for size in (many, few)]
        for which, member in enumerate(kinds + [cross]):
            meta_ref[which * geo.list_size + lengths[which]] = b
            lengths[which] = lengths[which] + member.astype(jnp.int32)
    for which in range(LISTS):
        meta_ref[which * geo.list_size + lengths[which]] = geo.batches
        meta_ref[geo.lengths_at + which] = lengths[which]


def zone(geo, odd, cross):
    span = geo.span if cross else geo.own - geo.span
    return pl.ds(jnp.where(odd == cross, geo.own - span, 0), span)


def pack_kernel(
    geo, density_ref, centre_in, offsets_in, counts_in,
    near_ref, cross_ref, meta_ref, acc_ref,
    centre_ref, offsets_ref, counts_ref, sems,
):
    index = lax.axis_index("blk")
    odd = index % 2 == 1

    def copies(up, down):
        return [
            pltpu.make_async_copy(
                density_ref.at[pl.ds(start, count)], ref.at[pl.ds(place, count)], sems.at[side, i]
            )
            for side, (pack, ref) in enumerate(zip(geo.packs, (up, down)))
            for i, (start, place, count) in enumerate(pack)
        ]

    def start(up, down):
        for copy in copies(up, down):
            copy.start()

    by_parity(odd, start, near_ref, cross_ref)
    scalars = [
        pltpu.make_async_copy(*pair, sems.at[2, i])
        for i, pair in enumerate(
            ((centre_in, centre_ref), (offsets_in, offsets_ref), (counts_in, counts_ref))
        )
    ]
    for copy in scalars:
        copy.start()
    for where in (zone(geo, odd, False), pl.ds(geo.first_at, geo.halo)):
        acc_ref[where] = jnp.zeros_like(acc_ref[where])
    for copy in scalars:
        copy.wait()
    build_lists(geo, index, centre_ref, offsets_ref, counts_ref, meta_ref)
    for copy in copies(near_ref, cross_ref):
        copy.wait()


def group_count(geo, meta_ref, which):
    return (meta_ref[geo.lengths_at + which] + GROUP - 1) // GROUP


def waits():
    return (lax.axis_index("blk") + 1) // 2 % 2 == 1


def inner_share(geo, meta_ref):
    before = BUDGET
    for which in (CROSS_MANY, CROSS_FEW, NEAR_MANY, NEAR_FEW):
        before = before - COST[which % 2] * group_count(geo, meta_ref, which)
    odd = meta_ref[geo.odd_at] == 1
    waiting = jnp.where(waits(), jnp.where(odd, WAIT[1], WAIT[0]), 0)
    share = []
    for which in (INNER_MANY, INNER_FEW):
        cost, count = COST[which % 2], group_count(geo, meta_ref, which)
        first = jnp.minimum(jnp.maximum(before, 0) // cost, count)
        second = jnp.minimum(jnp.maximum(waiting, 0) // cost, count - first)
        before = before - cost * first
        waiting = waiting - cost * second
        share.append((0, first, first + second, count))
    return share


def inner_part(geo, meta_ref, stage, refs):
    for which, width, bounds in zip(
        (INNER_MANY, INNER_FEW), (geo.slots, 2), inner_share(geo, meta_ref)
    ):
        each_group(
            geo,
            meta_ref,
            which,
            lambda chosen, width=width: add_whole(geo, chosen, width, *refs),
            begin=bounds[stage],
            end=bounds[stage + 1],
        )


def each_group(geo, meta_ref, which, body, size=GROUP, begin=0, end=None):
    length = meta_ref[geo.lengths_at + which]

    def step(i, carry):
        chosen = []
        for n in range(size):
            place = i * size + n
            there = place < length
            b = meta_ref[which * geo.list_size + jnp.minimum(place, length)]
            chosen.append((jnp.where(there, b, 0), there))
        body(chosen)
        return carry

    lax.fori_loop(begin, (length + size - 1) // size if end is None else end, step, 0)


class Slots:
    def __init__(self, geo, meta_ref, b, there, width):
        local = meta_ref[geo.local_at + b]
        count = jnp.where(there, meta_ref[geo.count_at + b], 0)
        self.offset = [meta_ref[geo.offsets_at + k * geo.batches + b] for k in range(width)]
        self.local = local
        self.row = [local + offset for offset in self.offset]
        self.live = [k < count for k in range(width)]
        self.own = [(row >= 0) & (row < geo.rows) for row in self.row]
        self.width = width


def panels(slots, ao_ref, b):
    return jnp.concatenate(
        [
            ao_ref[b, k] * jnp.where(slots.live[k], 1.0, 0.0).astype(ao_ref.dtype)
            for k in range(slots.width)
        ],
        axis=0,
    )


def gathered(tiles_ref, places):
    return jnp.concatenate(
        [jnp.concatenate([tiles_ref[place] for place in row], axis=1) for row in places], axis=0
    )


def potentials(xs, tiles, batches, kernel_ref):
    fs = [
        jnp.dot(t, x, preferred_element_type=jnp.float32).astype(jnp.bfloat16)
        for t, x in zip(tiles, xs)
    ]
    return [
        jnp.dot(f, kernel_ref[b], preferred_element_type=jnp.float32) for f, b in zip(fs, batches)
    ]


def outer_product(x, h):
    return lax.dot_general(x, h, (((1,), (1,)), ((), ())), preferred_element_type=jnp.float32)


def chain(xs, tiles, batches, kernel_ref, weights_ref):
    gs = potentials(xs, tiles, batches, kernel_ref)
    hs = [(g * weights_ref[pl.ds(b, 1), :]).astype(jnp.bfloat16) for g, b in zip(gs, batches)]
    return [outer_product(x, h) for x, h in zip(xs, hs)]


def scatter(part, target, nb, acc_ref):
    for k, row in enumerate(target):
        for j, place in enumerate(row):
            acc_ref[place] += part[k * nb : (k + 1) * nb, j * nb : (j + 1) * nb]


def add_whole(
    geo, chosen, width, meta_ref, tiles_ref, ao_ref, kernel_ref, weights_ref, acc_ref, halo_ref=None
):
    xs, tiles, targets = ([], [], [])
    for b, there in chosen:
        slots = Slots(geo, meta_ref, b, there, width)
        xs.append(panels(slots, ao_ref, b))
        rows, target = ([], [])
        for k in range(width):
            band = [slots.offset[j] - slots.offset[k] + geo.half for j in range(width)]
            own = slots.own[k]
            base = jnp.where(slots.live[k] & own, slots.row[k], 0) * geo.band
            row = jnp.concatenate([tiles_ref[base + o] for o in band], axis=1)
            if halo_ref is not None:
                away = slots.live[k] & jnp.logical_not(own)
                outside = jnp.where(away, geo.pick(geo.halo_base, 0, slots.row[k], 0), 0)
                other = [halo_ref[jnp.where(away, outside + o, 0)] for o in band]
                row = jnp.where(away, jnp.concatenate(other, axis=1), row)
                base = jnp.where(away, outside + geo.first_at, base)
            rows.append(row)
            target.append(
                [
                    jnp.where(slots.live[k] & slots.live[j], base + band[j], geo.spare)
                    for j in range(width)
                ]
            )
        tiles.append(jnp.concatenate(rows, axis=0))
        targets.append(target)
    parts = chain(xs, tiles, [b for b, _ in chosen], kernel_ref, weights_ref)
    for part, target in zip(parts, targets):
        scatter(part, target, ao_ref.shape[2], acc_ref)


def add_own(geo, chosen, width, meta_ref, tiles_ref, ao_ref, kernel_ref, weights_ref, acc_ref):
    xs, tiles, targets = ([], [], [])
    for b, there in chosen:
        slots = Slots(geo, meta_ref, b, there, width)
        xs.append(panels(slots, ao_ref, b))
        places, target = ([], [])
        for k in range(width):
            row = slots.row[k]
            band = [slots.offset[j] - slots.offset[k] + geo.half for j in range(width)]
            base = jnp.where(slots.own[k], row, 0) * geo.band
            places.append([base + o for o in band])
            base = geo.pick(geo.early_base, geo.early_at, row, base)
            target.append(
                [
                    jnp.where(
                        slots.live[k] & slots.live[j] & slots.own[j], base + band[j], geo.spare
                    )
                    for j in range(width)
                ]
            )
        tiles.append(gathered(tiles_ref, places))
        targets.append(target)
    parts = chain(xs, tiles, [b for b, _ in chosen], kernel_ref, weights_ref)
    for part, target in zip(parts, targets):
        scatter(part, target, ao_ref.shape[2], acc_ref)


def halo_rows(geo, meta_ref, slots):
    odd = meta_ref[geo.odd_at] == 1
    rows, places, present = ([], [], [])
    for i in range(geo.reach):
        row = jnp.where(odd, geo.rows + i, i - geo.reach)
        place, found = (jnp.int32(0), jnp.bool_(False))
        for k in range(slots.width):
            hit = slots.live[k] & (slots.row[k] == row)
            place = jnp.where(hit, k, place)
            found = found | hit
        rows.append(row)
        places.append(place)
        present.append(found)
    return rows, places, present


def add_corner(geo, chosen, meta_ref, halo_ref, ao_ref, kernel_ref, weights_ref, h_ref, total_ref):
    nb = ao_ref.shape[2]
    factor = lambda flag: jnp.where(flag, 1.0, 0.0)
    xs, sides, tiles, masks = ([], [], [], [])
    for b, there in chosen:
        slots = Slots(geo, meta_ref, b, there, geo.slots)
        rows, places, present = halo_rows(geo, meta_ref, slots)
        xs.append(panels(slots, ao_ref, b))
        sides.append(
            jnp.concatenate(
                [
                    ao_ref[b, place] * factor(found).astype(ao_ref.dtype)
                    for place, found in zip(places, present)
                ],
                axis=0,
            )
        )
        picked = []
        for row, found in zip(rows, present):
            base = geo.pick(geo.halo_base, 0, row, 0) - row + geo.half
            picked.append([jnp.where(found, base + column, 0) for column in slots.row])
        tiles.append(gathered(halo_ref, picked))
        masks.append([factor(found) for found in present])
    gs = potentials(xs, tiles, [b for b, _ in chosen], kernel_ref)
    hs = []
    for g, mask, (b, there) in zip(gs, masks, chosen):
        weights = weights_ref[pl.ds(b, 1), :]
        h = jnp.concatenate(
            [g[i * nb : (i + 1) * nb] * (weights * mask[i]) for i in range(geo.reach)], axis=0
        ).astype(jnp.bfloat16)
        h_ref[jnp.where(there, b, geo.batches)] = h
        hs.append(h)
    total_ref[...] += outer_product(
        jnp.concatenate(sides, axis=1), jnp.concatenate(hs, axis=1)
    )


def add_columns(geo, chosen, width, meta_ref, ao_ref, h_ref, acc_ref):
    parts, targets = ([], [])
    for b, there in chosen:
        slots = Slots(geo, meta_ref, b, there, width)
        rows, _, present = halo_rows(geo, meta_ref, slots)
        parts.append(outer_product(ao_ref[b, pl.ds(0, width)].reshape(-1, ao_ref.shape[3]), h_ref[b]))
        targets.append(
            [
                [
                    jnp.where(
                        slots.live[k] & slots.own[k] & found,
                        slots.row[k] * geo.band + row - slots.row[k] + geo.half,
                        geo.spare,
                    )
                    for row, found in zip(rows, present)
                ]
                for k in range(width)
            ]
        )
    for part, target in zip(parts, targets):
        scatter(part, target, ao_ref.shape[2], acc_ref)


def early_kernel(
    geo, meta_ref, tiles_ref, ao_ref, kernel_ref, weights_ref, acc_in, acc_ref
):
    odd = meta_ref[geo.odd_at] == 1
    for where in (zone(geo, odd, True), pl.ds(geo.early_at, geo.early), pl.ds(geo.spare, 1)):
        acc_ref[where] = jnp.zeros_like(acc_ref[where])
    refs = (meta_ref, tiles_ref, ao_ref, kernel_ref, weights_ref, acc_ref)
    for which, width in ((CROSS_MANY, geo.slots), (CROSS_FEW, 2)):
        each_group(
            geo, meta_ref, which, lambda chosen, width=width: add_own(geo, chosen, width, *refs)
        )


def near_kernel(
    geo, meta_ref, halo_ref, tiles_ref, ao_ref, kernel_ref, weights_ref, acc_in, acc_ref,
    early_out, *outs,
):
    early_out[...] = acc_ref[pl.ds(geo.early_at, geo.early)].astype(early_out.dtype)
    refs = (meta_ref, tiles_ref, ao_ref, kernel_ref, weights_ref, acc_ref, halo_ref)
    for which, width in ((NEAR_MANY, geo.slots), (NEAR_FEW, 2)):
        each_group(
            geo, meta_ref, which, lambda chosen, width=width: add_whole(geo, chosen, width, *refs)
        )
    for out, (start, count) in zip(outs, geo.pieces):
        out[...] = acc_ref[pl.ds(geo.first_at + start, count)].astype(out.dtype)
    inner_part(geo, meta_ref, 0, refs[:-1])


def waiting_kernel(
    geo, meta_ref, tiles_ref, ao_ref, kernel_ref, weights_ref, acc_in, acc_ref, done_ref
):
    inner_part(geo, meta_ref, 1, (meta_ref, tiles_ref, ao_ref, kernel_ref, weights_ref, acc_ref))
    done_ref[0] = 1


def late_kernel(
    geo, meta_ref, done_ref, halo_ref, ao_ref, kernel_ref, weights_ref, h_ref, late_out, total_ref
):
    nb = ao_ref.shape[2]
    total_ref[...] = jnp.zeros_like(total_ref)

    def work(chosen):
        add_corner(
            geo, chosen, meta_ref, halo_ref, ao_ref, kernel_ref, weights_ref, h_ref, total_ref
        )

    groups = (meta_ref[geo.lengths_at + CROSS] + 1) // LATE_GROUP
    each_group(geo, meta_ref, CROSS, work, size=LATE_GROUP, end=groups)
    each_group(geo, meta_ref, CROSS, work, size=LATE_GROUP // 2, begin=2 * groups)
    for i in range(geo.reach):
        for j in range(geo.reach):
            late_out[i * geo.reach + j] = total_ref[
                i * nb : (i + 1) * nb, j * nb : (j + 1) * nb
            ].astype(late_out.dtype)


def inner_kernel(
    geo, meta_ref, first_a, first_b, tiles_ref, ao_ref, kernel_ref, weights_ref, h_ref, acc_in,
    acc_ref, out_ref, sems,
):
    odd = meta_ref[geo.odd_at] == 1
    refs = (meta_ref, tiles_ref, ao_ref, kernel_ref, weights_ref, acc_ref)
    inner_part(geo, meta_ref, 2, refs)

    def add_near(up, down):
        for piece, ref in enumerate((first_a, first_b)):
            for start, place, count in geo.near_packs(piece)[0 if up else 1]:
                acc_ref[pl.ds(start, count)] += ref[pl.ds(place, count)].astype(jnp.float32)

    by_parity(odd, add_near, True, False)
    done = zone(geo, odd, False)
    copy = pltpu.make_async_copy(acc_ref.at[done], out_ref.at[done], sems.at[0])
    copy.start()
    for which, width in ((CROSS_MANY, geo.slots), (CROSS_FEW, 2)):
        each_group(
            geo,
            meta_ref,
            which,
            lambda chosen, width=width: add_columns(
                geo, chosen, width, meta_ref, ao_ref, h_ref, acc_ref
            ),
        )

    def write_quiet(up, down):
        run_copies(
            [
                pltpu.make_async_copy(
                    acc_ref.at[pl.ds(start, count)], out_ref.at[pl.ds(start, count)], sems.at[1 + i]
                )
                for i, (start, count) in enumerate(geo.quiet[0 if up else 1])
            ]
        )

    by_parity(odd, write_quiet, True, False)
    copy.wait()


def finish_cross(geo, odd, parts, acc_ref, out_ref, total, sems):
    def add(up, down):
        copies = []
        for packs, ref in parts:
            for start, place, count in packs[0 if up else 1]:
                spot = pl.ds(len(copies) * geo.band, count)
                total[spot] = acc_ref[pl.ds(start, count)] + ref[pl.ds(place, count)].astype(
                    jnp.float32
                )
                copy = pltpu.make_async_copy(
                    total.at[spot], out_ref.at[pl.ds(start, count)], sems.at[len(copies)]
                )
                copy.start()
                copies.append(copy)
        for copy in copies:
            copy.wait()

    by_parity(odd, add, False, True)


def has_time(geo, meta_ref):
    left = [bounds[3] - bounds[2] for bounds in inner_share(geo, meta_ref)]
    return waits() & (left[0] + left[1] == 0)


def early_join_kernel(geo, meta_ref, early_ref, acc_ref, out_in, out_ref, total, sems):
    @pl.when(has_time(geo, meta_ref))
    def _():
        odd = meta_ref[geo.odd_at] == 1
        finish_cross(geo, odd, ((geo.early_packs, early_ref),), acc_ref, out_ref, total, sems)


def finish_kernel(geo, meta_ref, late_ref, early_ref, acc_ref, out_in, out_ref, total, sems):
    odd = meta_ref[geo.odd_at] == 1
    late = (geo.late_packs, late_ref)
    joined = has_time(geo, meta_ref)

    @pl.when(joined)
    def _():
        finish_cross(geo, odd, (late,), acc_ref, out_ref, total, sems)

    @pl.when(jnp.logical_not(joined))
    def _():
        parts = ((geo.early_packs, early_ref), late)
        finish_cross(geo, odd, parts, acc_ref, out_ref, total, sems)


def call(kernel, out_shape, in_specs, out_specs, scratch, aliases=None, cost=None):
    return pl.pallas_call(
        kernel,
        out_shape=out_shape,
        in_specs=in_specs,
        out_specs=out_specs,
        scratch_shapes=scratch,
        input_output_aliases=aliases or {},
        cost_estimate=cost,
        compiler_params=pltpu.CompilerParams(vmem_limit_bytes=16 * MIB),
    )


def to_first(x, size):
    pairs = [(i, i + 1) for i in range(0, size - 1, 2)]
    got = lax.ppermute(x, "blk", pairs + [(j, i) for i, j in pairs])
    return pltpu.with_memory_space_constraint(got, pltpu.VMEM)


def to_second(x, size):
    pairs = [(i, i + 1) for i in range(1, size - 1, 2)]
    got = lax.ppermute(x, "blk", pairs + [(j, i) for i, j in pairs])
    return pltpu.with_memory_space_constraint(got, pltpu.VMEM)


def local(density, ao_values, kernel, grid_weights, centre, sig_offsets, counts):
    rows, band, nb, _ = density.shape
    batches, slots, _, pts = ao_values.shape
    size = lax.axis_size("blk")
    geo = Geometry(rows, band, batches, slots)
    in_hbm = lambda x: pltpu.with_memory_space_constraint(x, pltpu.HBM)
    tiles = density.reshape(geo.own, nb, nb)
    pack = lambda count: pltpu.VMEM((count, nb, nb), jnp.bfloat16)
    dma = pltpu.SemaphoreType.DMA
    acc_type = pltpu.VMEM((geo.spare + 1, nb, nb), jnp.float32)

    near_halo, cross_halo, meta, acc = call(
        functools.partial(pack_kernel, geo),
        (pack(geo.halo),) * 2 + (pltpu.SMEM((geo.meta_size,), jnp.int32), acc_type),
        [ANY_SPEC] * 4,
        (VMEM_SPEC,) * 2 + (SMEM_SPEC, VMEM_SPEC),
        [
            pltpu.SMEM((batches,), jnp.int32),
            pltpu.SMEM((slots, batches), jnp.int32),
            pltpu.SMEM((batches,), jnp.int32),
            dma((3, max(geo.reach, 3))),
        ],
        cost=pl.CostEstimate(flops=10**10, bytes_accessed=10**8, transcendentals=0),
    )(in_hbm(tiles), in_hbm(centre), in_hbm(sig_offsets.T), in_hbm(counts))
    cross_halo = to_second(cross_halo, size)
    near_halo = to_first(near_halo, size)

    panel = (tiles, ao_values, kernel, grid_weights)
    acc = call(
        functools.partial(early_kernel, geo),
        acc_type,
        [SMEM_SPEC] + [VMEM_SPEC] * 5,
        VMEM_SPEC,
        [],
        {5: 0},
    )(meta, *panel, acc)

    acc, early, *first = call(
        functools.partial(near_kernel, geo),
        (acc_type, pack(geo.early)) + tuple(pack(count) for _, count in geo.pieces),
        [SMEM_SPEC] + [VMEM_SPEC] * 6,
        (VMEM_SPEC,) * 4,
        [],
        {6: 0},
    )(meta, near_halo, *panel, acc)
    early = to_second(early, size)
    first = [to_first(piece, size) for piece in first]

    acc, done = call(
        functools.partial(waiting_kernel, geo),
        (acc_type, pltpu.SMEM((1,), jnp.int32)),
        [SMEM_SPEC] + [VMEM_SPEC] * 5,
        (VMEM_SPEC, SMEM_SPEC),
        [],
        {5: 0},
    )(meta, *panel, acc)

    h_type = pltpu.VMEM((batches + 1, geo.reach * nb, pts), jnp.bfloat16)
    h, late = call(
        functools.partial(late_kernel, geo),
        (h_type, pack(geo.late)),
        [SMEM_SPEC] * 2 + [VMEM_SPEC] * 4,
        (VMEM_SPEC,) * 2,
        [pltpu.VMEM((geo.reach * nb, geo.reach * nb), jnp.float32)],
    )(meta, done, cross_halo, *panel[1:])
    late = to_second(late, size)

    whole = jax.ShapeDtypeStruct((geo.own, nb, nb), jnp.float32)
    acc, out = call(
        functools.partial(inner_kernel, geo),
        (acc_type, whole),
        [SMEM_SPEC] + [VMEM_SPEC] * 8,
        (VMEM_SPEC, ANY_SPEC),
        [dma((1 + max(len(runs) for runs in geo.quiet),))],
        {8: 0},
    )(meta, *first, *panel, h, acc)

    for kernel_of, got, parts in (
        (early_join_kernel, (early,), geo.reach),
        (finish_kernel, (late, early), 2 * geo.reach),
    ):
        out = call(
            functools.partial(kernel_of, geo),
            whole,
            [SMEM_SPEC] + [VMEM_SPEC] * (len(got) + 1) + [ANY_SPEC],
            ANY_SPEC,
            [pltpu.VMEM((parts * band, nb, nb), jnp.float32), dma((parts,))],
            {len(got) + 2: 0},
        )(meta, *got, acc, out)
    return out.reshape(rows, band, nb, nb)


def solution(mesh):
    placed = (
        P(("groups", "blk"), None, None, None),
        P(("groups", "blk"), None, None, None),
        P(("groups", "blk"), None, None),
        P(("groups", "blk"), None),
        P(("groups", "blk")),
        P(("groups", "blk"), None),
        P(("groups", "blk")),
    )
    return jax.shard_map(
        local,
        mesh=mesh,
        in_specs=placed,
        out_specs=P(("groups", "blk"), None, None, None),
        check_vma=False,
    )
```

```python
import functools

import jax
import jax.numpy as jnp
from jax import lax
from jax.experimental import pallas as pl
from jax.experimental.pallas import tpu as pltpu
from jax.sharding import PartitionSpec as P

MIB = 1 << 20
GROUP = 2
LATE_GROUP = 4
LISTS = 7
BUDGET = 43
WAIT = 18
COST = (10, 7)
SMEM_SPEC = pl.BlockSpec(memory_space=pltpu.SMEM)
VMEM_SPEC = pl.BlockSpec(memory_space=pltpu.VMEM)
ANY_SPEC = pl.BlockSpec(memory_space=pl.ANY)


class Geometry:
    def __init__(self, rows, band, batches, slots):
        self.rows, self.band, self.batches, self.slots = rows, band, batches, slots
        self.half = half = (band - 1) // 2
        self.reach = reach = half // 2
        self.own = rows * band
        low = [(-m, reach + m, band) for m in range(reach, 0, -1)]
        high = [(rows + m, 0, 3 * reach - m) for m in range(reach)]
        self.halo = sum(stop - start for _, start, stop in low)
        low_cut = [half - row for row, _, _ in low]
        high_cut = [rows - row + half for row, _, _ in high]
        early = (
            [(row, cut, stop) for (row, _, stop), cut in zip(low, low_cut)],
            [(row, start, cut) for (row, start, _), cut in zip(high, high_cut)],
        )
        late = (
            [(row, start, cut) for (row, start, _), cut in zip(low, low_cut)],
            [(row, cut, stop) for (row, _, stop), cut in zip(high, high_cut)],
        )
        self.early = sum(stop - start for _, start, stop in early[0])
        self.late = self.halo - self.early
        self.first_at = self.own
        self.early_at = self.own + self.halo
        self.spare = self.early_at + self.early
        self.halo_base = self.bases((low, high))
        self.early_base = self.bases(early)
        shifts = (rows, -rows)
        self.packs = [self.places(*pair) for pair in zip((low, high), shifts)]
        self.early_packs = [self.places(*pair) for pair in zip(early, shifts)]
        self.late_packs = [self.places(*pair) for pair in zip(late, shifts)]
        self.span = min(2 * reach, rows) * band
        self.quiet = [
            self.others(self.packs[1], 0, self.span),
            self.others(self.packs[0], self.own - self.span, self.own),
        ]
        self.list_size = batches + 2
        self.lengths_at = LISTS * self.list_size
        self.local_at = self.lengths_at + LISTS
        self.count_at = self.local_at + batches
        self.offsets_at = self.count_at + batches
        self.odd_at = self.offsets_at + slots * batches
        self.meta_size = self.odd_at + 1

    def bases(self, sides):
        found = {}
        for segments in sides:
            place = 0
            for row, start, stop in segments:
                found[row] = place - start
                place += stop - start
        return found

    def places(self, segments, shift):
        pack, place = ([], 0)
        for row, start, stop in segments:
            pack.append(((row + shift) * self.band + start, place, stop - start))
            place += stop - start
        return pack

    def others(self, pack, begin, end):
        touched = set()
        for start, _, count in pack:
            touched.update(range(start, start + count))
        runs = []
        for index in range(begin, end):
            if index in touched:
                continue
            if runs and sum(runs[-1]) == index:
                runs[-1] = (runs[-1][0], runs[-1][1] + 1)
            else:
                runs.append((index, 1))
        return runs

    def pick(self, bases, shift, row, otherwise):
        value = otherwise
        for at, base in bases.items():
            value = jnp.where(row == at, base + shift, value)
        return value


def run_copies(copies):
    for copy in copies:
        copy.start()
    for copy in copies:
        copy.wait()


def by_parity(odd, body, first, second):
    @pl.when(jnp.logical_not(odd))
    def _():
        body(first, second)

    @pl.when(odd)
    def _():
        body(second, first)


CROSS_MANY, CROSS_FEW, NEAR_MANY, NEAR_FEW, INNER_MANY, INNER_FEW, CROSS = range(LISTS)


def build_lists(geo, index, centre_ref, offsets_ref, counts_ref, meta_ref):
    first = index * geo.rows
    odd = index % 2 == 1
    meta_ref[geo.odd_at] = odd.astype(jnp.int32)
    lengths = [jnp.int32(0)] * LISTS
    for b in range(geo.batches):
        local = centre_ref[b] - first
        count = counts_ref[b]
        meta_ref[geo.local_at + b] = local
        meta_ref[geo.count_at + b] = count
        low = high = jnp.bool_(False)
        for k in range(geo.slots):
            offset = offsets_ref[k, b]
            meta_ref[geo.offsets_at + k * geo.batches + b] = offset
            row = local + offset
            low = low | ((k < count) & (row < 0))
            high = high | ((k < count) & (row >= geo.rows))
        cross = (odd & high) | (jnp.logical_not(odd) & low)
        near = (odd & low) | (jnp.logical_not(odd) & high)
        inner = jnp.logical_not(low | high)
        many = count > 2
        few = (count > 0) & jnp.logical_not(many)
        kinds = [kind & size for kind in (cross, near, inner) for size in (many, few)]
        for which, member in enumerate(kinds + [cross]):
            meta_ref[which * geo.list_size + lengths[which]] = b
            lengths[which] = lengths[which] + member.astype(jnp.int32)
    for which in range(LISTS):
        meta_ref[which * geo.list_size + lengths[which]] = geo.batches
        meta_ref[geo.lengths_at + which] = lengths[which]


def zone(geo, odd, cross):
    span = geo.span if cross else geo.own - geo.span
    return pl.ds(jnp.where(odd == cross, geo.own - span, 0), span)


def pack_kernel(
    geo, density_ref, centre_in, offsets_in, counts_in,
    near_ref, cross_ref, meta_ref, acc_ref,
    centre_ref, offsets_ref, counts_ref, sems,
):
    index = lax.axis_index("blk")
    odd = index % 2 == 1

    def copies(up, down):
        return [
            pltpu.make_async_copy(
                density_ref.at[pl.ds(start, count)], ref.at[pl.ds(place, count)], sems.at[side, i]
            )
            for side, (pack, ref) in enumerate(zip(geo.packs, (up, down)))
            for i, (start, place, count) in enumerate(pack)
        ]

    def start(up, down):
        for copy in copies(up, down):
            copy.start()

    by_parity(odd, start, near_ref, cross_ref)
    scalars = [
        pltpu.make_async_copy(*pair, sems.at[2, i])
        for i, pair in enumerate(
            ((centre_in, centre_ref), (offsets_in, offsets_ref), (counts_in, counts_ref))
        )
    ]
    for copy in scalars:
        copy.start()
    for where in (zone(geo, odd, False), pl.ds(geo.first_at, geo.halo)):
        acc_ref[where] = jnp.zeros_like(acc_ref[where])
    for copy in scalars:
        copy.wait()
    build_lists(geo, index, centre_ref, offsets_ref, counts_ref, meta_ref)
    for copy in copies(near_ref, cross_ref):
        copy.wait()


def group_count(geo, meta_ref, which):
    return (meta_ref[geo.lengths_at + which] + GROUP - 1) // GROUP


def inner_share(geo, meta_ref):
    before = BUDGET
    for which in (CROSS_MANY, CROSS_FEW, NEAR_MANY, NEAR_FEW):
        before = before - COST[which % 2] * group_count(geo, meta_ref, which)
    waiting = jnp.where((lax.axis_index("blk") + 1) // 2 % 2 == 1, WAIT, 0)
    share = []
    for which in (INNER_MANY, INNER_FEW):
        cost, count = COST[which % 2], group_count(geo, meta_ref, which)
        first = jnp.minimum(jnp.maximum(before, 0) // cost, count)
        second = jnp.minimum(jnp.maximum(waiting, 0) // cost, count - first)
        before = before - cost * first
        waiting = waiting - cost * second
        share.append((0, first, first + second, count))
    return share


def inner_part(geo, meta_ref, stage, refs):
    for which, width, bounds in zip(
        (INNER_MANY, INNER_FEW), (geo.slots, 2), inner_share(geo, meta_ref)
    ):
        each_group(
            geo,
            meta_ref,
            which,
            lambda chosen, width=width: add_whole(geo, chosen, width, *refs),
            begin=bounds[stage],
            end=bounds[stage + 1],
        )


def each_group(geo, meta_ref, which, body, size=GROUP, begin=0, end=None):
    length = meta_ref[geo.lengths_at + which]

    def step(i, carry):
        chosen = []
        for n in range(size):
            place = i * size + n
            there = place < length
            b = meta_ref[which * geo.list_size + jnp.minimum(place, length)]
            chosen.append((jnp.where(there, b, 0), there))
        body(chosen)
        return carry

    lax.fori_loop(begin, (length + size - 1) // size if end is None else end, step, 0)


class Slots:
    def __init__(self, geo, meta_ref, b, there, width):
        local = meta_ref[geo.local_at + b]
        count = jnp.where(there, meta_ref[geo.count_at + b], 0)
        self.offset = [meta_ref[geo.offsets_at + k * geo.batches + b] for k in range(width)]
        self.local = local
        self.row = [local + offset for offset in self.offset]
        self.live = [k < count for k in range(width)]
        self.own = [(row >= 0) & (row < geo.rows) for row in self.row]
        self.width = width


def panels(slots, ao_ref, b):
    return jnp.concatenate(
        [
            ao_ref[b, k] * jnp.where(slots.live[k], 1.0, 0.0).astype(ao_ref.dtype)
            for k in range(slots.width)
        ],
        axis=0,
    )


def gathered(tiles_ref, places):
    return jnp.concatenate(
        [jnp.concatenate([tiles_ref[place] for place in row], axis=1) for row in places], axis=0
    )


def potentials(xs, tiles, batches, kernel_ref):
    fs = [
        jnp.dot(t, x, preferred_element_type=jnp.float32).astype(jnp.bfloat16)
        for t, x in zip(tiles, xs)
    ]
    return [
        jnp.dot(f, kernel_ref[b], preferred_element_type=jnp.float32) for f, b in zip(fs, batches)
    ]


def outer_product(x, h):
    return lax.dot_general(x, h, (((1,), (1,)), ((), ())), preferred_element_type=jnp.float32)


def chain(xs, tiles, batches, kernel_ref, weights_ref):
    gs = potentials(xs, tiles, batches, kernel_ref)
    hs = [(g * weights_ref[pl.ds(b, 1), :]).astype(jnp.bfloat16) for g, b in zip(gs, batches)]
    return [outer_product(x, h) for x, h in zip(xs, hs)]


def scatter(part, target, nb, acc_ref):
    for k, row in enumerate(target):
        for j, place in enumerate(row):
            acc_ref[place] += part[k * nb : (k + 1) * nb, j * nb : (j + 1) * nb]


def add_whole(
    geo, chosen, width, meta_ref, tiles_ref, ao_ref, kernel_ref, weights_ref, acc_ref, halo_ref=None
):
    xs, tiles, targets = ([], [], [])
    for b, there in chosen:
        slots = Slots(geo, meta_ref, b, there, width)
        xs.append(panels(slots, ao_ref, b))
        rows, target = ([], [])
        for k in range(width):
            band = [slots.offset[j] - slots.offset[k] + geo.half for j in range(width)]
            own = slots.own[k]
            base = jnp.where(slots.live[k] & own, slots.row[k], 0) * geo.band
            row = jnp.concatenate([tiles_ref[base + o] for o in band], axis=1)
            if halo_ref is not None:
                away = slots.live[k] & jnp.logical_not(own)
                outside = jnp.where(away, geo.pick(geo.halo_base, 0, slots.row[k], 0), 0)
                other = [halo_ref[jnp.where(away, outside + o, 0)] for o in band]
                row = jnp.where(away, jnp.concatenate(other, axis=1), row)
                base = jnp.where(away, outside + geo.first_at, base)
            rows.append(row)
            target.append(
                [
                    jnp.where(slots.live[k] & slots.live[j], base + band[j], geo.spare)
                    for j in range(width)
                ]
            )
        tiles.append(jnp.concatenate(rows, axis=0))
        targets.append(target)
    parts = chain(xs, tiles, [b for b, _ in chosen], kernel_ref, weights_ref)
    for part, target in zip(parts, targets):
        scatter(part, target, ao_ref.shape[2], acc_ref)


def add_own(geo, chosen, width, meta_ref, tiles_ref, ao_ref, kernel_ref, weights_ref, acc_ref):
    xs, tiles, targets = ([], [], [])
    for b, there in chosen:
        slots = Slots(geo, meta_ref, b, there, width)
        xs.append(panels(slots, ao_ref, b))
        places, target = ([], [])
        for k in range(width):
            row = slots.row[k]
            band = [slots.offset[j] - slots.offset[k] + geo.half for j in range(width)]
            base = jnp.where(slots.own[k], row, 0) * geo.band
            places.append([base + o for o in band])
            base = geo.pick(geo.early_base, geo.early_at, row, base)
            target.append(
                [
                    jnp.where(
                        slots.live[k] & slots.live[j] & slots.own[j], base + band[j], geo.spare
                    )
                    for j in range(width)
                ]
            )
        tiles.append(gathered(tiles_ref, places))
        targets.append(target)
    parts = chain(xs, tiles, [b for b, _ in chosen], kernel_ref, weights_ref)
    for part, target in zip(parts, targets):
        scatter(part, target, ao_ref.shape[2], acc_ref)


def halo_rows(geo, meta_ref, slots):
    odd = meta_ref[geo.odd_at] == 1
    rows, places, present = ([], [], [])
    for i in range(geo.reach):
        row = jnp.where(odd, geo.rows + i, i - geo.reach)
        place, found = (jnp.int32(0), jnp.bool_(False))
        for k in range(slots.width):
            hit = slots.live[k] & (slots.row[k] == row)
            place = jnp.where(hit, k, place)
            found = found | hit
        rows.append(row)
        places.append(place)
        present.append(found)
    return rows, places, present


def add_corner(geo, chosen, meta_ref, halo_ref, ao_ref, kernel_ref, weights_ref, h_ref, total_ref):
    nb = ao_ref.shape[2]
    factor = lambda flag: jnp.where(flag, 1.0, 0.0)
    xs, sides, tiles, masks = ([], [], [], [])
    for b, there in chosen:
        slots = Slots(geo, meta_ref, b, there, geo.slots)
        rows, places, present = halo_rows(geo, meta_ref, slots)
        xs.append(panels(slots, ao_ref, b))
        sides.append(
            jnp.concatenate(
                [
                    ao_ref[b, place] * factor(found).astype(ao_ref.dtype)
                    for place, found in zip(places, present)
                ],
                axis=0,
            )
        )
        picked = []
        for row, found in zip(rows, present):
            base = geo.pick(geo.halo_base, 0, row, 0) - row + geo.half
            picked.append([jnp.where(found, base + column, 0) for column in slots.row])
        tiles.append(gathered(halo_ref, picked))
        masks.append([factor(found) for found in present])
    gs = potentials(xs, tiles, [b for b, _ in chosen], kernel_ref)
    hs = []
    for g, mask, (b, there) in zip(gs, masks, chosen):
        weights = weights_ref[pl.ds(b, 1), :]
        h = jnp.concatenate(
            [g[i * nb : (i + 1) * nb] * (weights * mask[i]) for i in range(geo.reach)], axis=0
        ).astype(jnp.bfloat16)
        h_ref[jnp.where(there, b, geo.batches)] = h
        hs.append(h)
    total_ref[...] += outer_product(
        jnp.concatenate(sides, axis=1), jnp.concatenate(hs, axis=1)
    )


def add_columns(geo, chosen, width, meta_ref, ao_ref, h_ref, acc_ref):
    parts, targets = ([], [])
    for b, there in chosen:
        slots = Slots(geo, meta_ref, b, there, width)
        rows, _, present = halo_rows(geo, meta_ref, slots)
        parts.append(outer_product(ao_ref[b, pl.ds(0, width)].reshape(-1, ao_ref.shape[3]), h_ref[b]))
        targets.append(
            [
                [
                    jnp.where(
                        slots.live[k] & slots.own[k] & found,
                        slots.row[k] * geo.band + row - slots.row[k] + geo.half,
                        geo.spare,
                    )
                    for row, found in zip(rows, present)
                ]
                for k in range(width)
            ]
        )
    for part, target in zip(parts, targets):
        scatter(part, target, ao_ref.shape[2], acc_ref)


def early_kernel(
    geo, meta_ref, tiles_ref, ao_ref, kernel_ref, weights_ref, acc_in, acc_ref, early_out
):
    odd = meta_ref[geo.odd_at] == 1
    for where in (zone(geo, odd, True), pl.ds(geo.early_at, geo.early), pl.ds(geo.spare, 1)):
        acc_ref[where] = jnp.zeros_like(acc_ref[where])
    refs = (meta_ref, tiles_ref, ao_ref, kernel_ref, weights_ref, acc_ref)
    for which, width in ((CROSS_MANY, geo.slots), (CROSS_FEW, 2)):
        each_group(
            geo, meta_ref, which, lambda chosen, width=width: add_own(geo, chosen, width, *refs)
        )
    early_out[...] = acc_ref[pl.ds(geo.early_at, geo.early)].astype(early_out.dtype)


def near_kernel(
    geo, meta_ref, halo_ref, tiles_ref, ao_ref, kernel_ref, weights_ref, acc_in, acc_ref, first_out
):
    refs = (meta_ref, tiles_ref, ao_ref, kernel_ref, weights_ref, acc_ref, halo_ref)
    for which, width in ((NEAR_MANY, geo.slots), (NEAR_FEW, 2)):
        each_group(
            geo, meta_ref, which, lambda chosen, width=width: add_whole(geo, chosen, width, *refs)
        )
    first_out[...] = acc_ref[pl.ds(geo.first_at, geo.halo)].astype(first_out.dtype)
    inner_part(geo, meta_ref, 0, refs[:-1])


def waiting_kernel(
    geo, meta_ref, tiles_ref, ao_ref, kernel_ref, weights_ref, acc_in, acc_ref, done_ref
):
    inner_part(geo, meta_ref, 1, (meta_ref, tiles_ref, ao_ref, kernel_ref, weights_ref, acc_ref))
    done_ref[0] = 1


def late_kernel(
    geo, meta_ref, done_ref, halo_ref, ao_ref, kernel_ref, weights_ref, h_ref, late_out, total_ref
):
    nb = ao_ref.shape[2]
    total_ref[...] = jnp.zeros_like(total_ref)

    def work(chosen):
        add_corner(
            geo, chosen, meta_ref, halo_ref, ao_ref, kernel_ref, weights_ref, h_ref, total_ref
        )

    groups = (meta_ref[geo.lengths_at + CROSS] + 1) // LATE_GROUP
    each_group(geo, meta_ref, CROSS, work, size=LATE_GROUP, end=groups)
    each_group(geo, meta_ref, CROSS, work, size=LATE_GROUP // 2, begin=2 * groups)
    for i in range(geo.reach):
        for j in range(geo.reach):
            late_out[i * geo.reach + j] = total_ref[
                i * nb : (i + 1) * nb, j * nb : (j + 1) * nb
            ].astype(late_out.dtype)


def inner_kernel(
    geo, meta_ref, first_ref, tiles_ref, ao_ref, kernel_ref, weights_ref, h_ref, acc_in,
    acc_ref, out_ref, early_ref, late_ref, sems,
):
    odd = meta_ref[geo.odd_at] == 1
    refs = (meta_ref, tiles_ref, ao_ref, kernel_ref, weights_ref, acc_ref)
    inner_part(geo, meta_ref, 2, refs)

    def add_near(up, down):
        for start, place, count in geo.packs[0 if up else 1]:
            acc_ref[pl.ds(start, count)] += first_ref[pl.ds(place, count)].astype(jnp.float32)

    by_parity(odd, add_near, True, False)
    done = zone(geo, odd, False)
    copy = pltpu.make_async_copy(acc_ref.at[done], out_ref.at[done], sems.at[0])
    copy.start()
    for which, width in ((CROSS_MANY, geo.slots), (CROSS_FEW, 2)):
        each_group(
            geo,
            meta_ref,
            which,
            lambda chosen, width=width: add_columns(
                geo, chosen, width, meta_ref, ao_ref, h_ref, acc_ref
            ),
        )

    def write_quiet(up, down):
        side = 1 if up else 0
        for packs, ref in ((geo.early_packs, early_ref), (geo.late_packs, late_ref)):
            for start, place, count in packs[side]:
                ref[pl.ds(place, count)] = acc_ref[pl.ds(start, count)]
        run_copies(
            [
                pltpu.make_async_copy(
                    acc_ref.at[pl.ds(start, count)], out_ref.at[pl.ds(start, count)], sems.at[1 + i]
                )
                for i, (start, count) in enumerate(geo.quiet[0 if up else 1])
            ]
        )

    by_parity(odd, write_quiet, True, False)
    copy.wait()


def finish_cross(odd, packs, got, own, out):
    total = own + got.astype(jnp.float32)
    by_size = lambda pack: sorted(pack, key=lambda segment: segment[2])
    for upper, lower in zip(*(by_size(pack) for pack in packs)):
        start = jnp.where(odd, upper[0], lower[0])
        place = jnp.where(odd, upper[1], lower[1])
        part = lax.dynamic_slice_in_dim(total, place, upper[2])
        out = lax.dynamic_update_slice_in_dim(out, part, start, axis=0)
    return out


def call(kernel, out_shape, in_specs, out_specs, scratch, aliases=None, cost=None):
    return pl.pallas_call(
        kernel,
        out_shape=out_shape,
        in_specs=in_specs,
        out_specs=out_specs,
        scratch_shapes=scratch,
        input_output_aliases=aliases or {},
        cost_estimate=cost,
        compiler_params=pltpu.CompilerParams(vmem_limit_bytes=16 * MIB),
    )


def to_first(x, size):
    pairs = [(i, i + 1) for i in range(0, size - 1, 2)]
    got = lax.ppermute(x, "blk", pairs + [(j, i) for i, j in pairs])
    return pltpu.with_memory_space_constraint(got, pltpu.VMEM)


def to_second(x, size, for_kernel=True):
    pairs = [(i, i + 1) for i in range(1, size - 1, 2)]
    got = lax.ppermute(x, "blk", pairs + [(j, i) for i, j in pairs])
    return pltpu.with_memory_space_constraint(got, pltpu.VMEM) if for_kernel else got


def local(density, ao_values, kernel, grid_weights, centre, sig_offsets, counts):
    rows, band, nb, _ = density.shape
    batches, slots, _, pts = ao_values.shape
    size = lax.axis_size("blk")
    geo = Geometry(rows, band, batches, slots)
    in_hbm = lambda x: pltpu.with_memory_space_constraint(x, pltpu.HBM)
    tiles = density.reshape(geo.own, nb, nb)
    pack = lambda count: pltpu.VMEM((count, nb, nb), jnp.bfloat16)
    dma = pltpu.SemaphoreType.DMA
    acc_type = pltpu.VMEM((geo.spare + 1, nb, nb), jnp.float32)

    near_halo, cross_halo, meta, acc = call(
        functools.partial(pack_kernel, geo),
        (pack(geo.halo),) * 2 + (pltpu.SMEM((geo.meta_size,), jnp.int32), acc_type),
        [ANY_SPEC] * 4,
        (VMEM_SPEC,) * 2 + (SMEM_SPEC, VMEM_SPEC),
        [
            pltpu.SMEM((batches,), jnp.int32),
            pltpu.SMEM((slots, batches), jnp.int32),
            pltpu.SMEM((batches,), jnp.int32),
            dma((3, max(geo.reach, 3))),
        ],
        cost=pl.CostEstimate(flops=10**10, bytes_accessed=10**8, transcendentals=0),
    )(in_hbm(tiles), in_hbm(centre), in_hbm(sig_offsets.T), in_hbm(counts))
    cross_halo = to_second(cross_halo, size)
    near_halo = to_first(near_halo, size)

    panel = (tiles, ao_values, kernel, grid_weights)
    acc, early = call(
        functools.partial(early_kernel, geo),
        (acc_type, pack(geo.early)),
        [SMEM_SPEC] + [VMEM_SPEC] * 5,
        (VMEM_SPEC,) * 2,
        [],
        {5: 0},
    )(meta, *panel, acc)
    early = to_second(early, size, False)

    acc, first = call(
        functools.partial(near_kernel, geo),
        (acc_type, pack(geo.halo)),
        [SMEM_SPEC] + [VMEM_SPEC] * 6,
        (VMEM_SPEC,) * 2,
        [],
        {6: 0},
    )(meta, near_halo, *panel, acc)
    first = to_first(first, size)

    acc, done = call(
        functools.partial(waiting_kernel, geo),
        (acc_type, pltpu.SMEM((1,), jnp.int32)),
        [SMEM_SPEC] + [VMEM_SPEC] * 5,
        (VMEM_SPEC, SMEM_SPEC),
        [],
        {5: 0},
    )(meta, *panel, acc)

    h_type = pltpu.VMEM((batches + 1, geo.reach * nb, pts), jnp.bfloat16)
    h, late = call(
        functools.partial(late_kernel, geo),
        (h_type, pack(geo.late)),
        [SMEM_SPEC] * 2 + [VMEM_SPEC] * 4,
        (VMEM_SPEC,) * 2,
        [pltpu.VMEM((geo.reach * nb, geo.reach * nb), jnp.float32)],
    )(meta, done, cross_halo, *panel[1:])
    late = to_second(late, size, False)

    whole = jax.ShapeDtypeStruct((geo.own, nb, nb), jnp.float32)
    sums = [jax.ShapeDtypeStruct((count, nb, nb), jnp.float32) for count in (geo.early, geo.late)]
    _, out, *own = call(
        functools.partial(inner_kernel, geo),
        (acc_type, whole, *sums),
        [SMEM_SPEC] + [VMEM_SPEC] * 7,
        (VMEM_SPEC, ANY_SPEC, VMEM_SPEC, VMEM_SPEC),
        [dma((1 + max(len(runs) for runs in geo.quiet),))],
        {7: 0},
    )(meta, first, *panel, h, acc)

    odd = lax.axis_index("blk") % 2 == 1
    out = finish_cross(odd, geo.early_packs, early, own[0], out)
    out = finish_cross(odd, geo.late_packs, late, own[1], out)
    return out.reshape(rows, band, nb, nb)


def solution(mesh):
    placed = (
        P(("groups", "blk"), None, None, None),
        P(("groups", "blk"), None, None, None),
        P(("groups", "blk"), None, None),
        P(("groups", "blk"), None),
        P(("groups", "blk")),
        P(("groups", "blk"), None),
        P(("groups", "blk")),
    )
    return jax.shard_map(
        local,
        mesh=mesh,
        in_specs=placed,
        out_specs=P(("groups", "blk"), None, None, None),
        check_vma=False,
    )
```

```python
import functools

import jax
import jax.numpy as jnp
from jax import lax
from jax.experimental import pallas as pl
from jax.experimental.pallas import tpu as pltpu
from jax.sharding import PartitionSpec as P

MIB = 1 << 20
GROUP = 2
LATE_GROUP = 4
LISTS = 7
BUDGET = 43
WAIT = 18
COST = (10, 7)
SMEM_SPEC = pl.BlockSpec(memory_space=pltpu.SMEM)
VMEM_SPEC = pl.BlockSpec(memory_space=pltpu.VMEM)
ANY_SPEC = pl.BlockSpec(memory_space=pl.ANY)


class Geometry:
    def __init__(self, rows, band, batches, slots):
        self.rows, self.band, self.batches, self.slots = rows, band, batches, slots
        self.half = half = (band - 1) // 2
        self.reach = reach = half // 2
        self.own = rows * band
        low = [(-m, reach + m, band) for m in range(reach, 0, -1)]
        high = [(rows + m, 0, 3 * reach - m) for m in range(reach)]
        self.halo = sum(stop - start for _, start, stop in low)
        low_cut = [half - row for row, _, _ in low]
        high_cut = [rows - row + half for row, _, _ in high]
        early = (
            [(row, cut, stop) for (row, _, stop), cut in zip(low, low_cut)],
            [(row, start, cut) for (row, start, _), cut in zip(high, high_cut)],
        )
        late = (
            [(row, start, cut) for (row, start, _), cut in zip(low, low_cut)],
            [(row, cut, stop) for (row, _, stop), cut in zip(high, high_cut)],
        )
        self.early = sum(stop - start for _, start, stop in early[0])
        self.late = self.halo - self.early
        self.first_at = self.own
        self.early_at = self.own + self.halo
        self.spare = self.early_at + self.early
        self.halo_base = self.bases((low, high))
        self.early_base = self.bases(early)
        shifts = (rows, -rows)
        self.packs = [self.places(*pair) for pair in zip((low, high), shifts)]
        self.early_packs = [self.places(*pair) for pair in zip(early, shifts)]
        self.late_packs = [self.places(*pair) for pair in zip(late, shifts)]
        self.span = min(2 * reach, rows) * band
        self.quiet = [
            self.others(self.packs[1], 0, self.span),
            self.others(self.packs[0], self.own - self.span, self.own),
        ]
        self.list_size = batches + 2
        self.lengths_at = LISTS * self.list_size
        self.local_at = self.lengths_at + LISTS
        self.count_at = self.local_at + batches
        self.offsets_at = self.count_at + batches
        self.odd_at = self.offsets_at + slots * batches
        self.meta_size = self.odd_at + 1

    def bases(self, sides):
        found = {}
        for segments in sides:
            place = 0
            for row, start, stop in segments:
                found[row] = place - start
                place += stop - start
        return found

    def places(self, segments, shift):
        pack, place = ([], 0)
        for row, start, stop in segments:
            pack.append(((row + shift) * self.band + start, place, stop - start))
            place += stop - start
        return pack

    def others(self, pack, begin, end):
        touched = set()
        for start, _, count in pack:
            touched.update(range(start, start + count))
        runs = []
        for index in range(begin, end):
            if index in touched:
                continue
            if runs and sum(runs[-1]) == index:
                runs[-1] = (runs[-1][0], runs[-1][1] + 1)
            else:
                runs.append((index, 1))
        return runs

    def pick(self, bases, shift, row, otherwise):
        value = otherwise
        for at, base in bases.items():
            value = jnp.where(row == at, base + shift, value)
        return value


def run_copies(copies):
    for copy in copies:
        copy.start()
    for copy in copies:
        copy.wait()


def by_parity(odd, body, first, second):
    @pl.when(jnp.logical_not(odd))
    def _():
        body(first, second)

    @pl.when(odd)
    def _():
        body(second, first)


CROSS_MANY, CROSS_FEW, NEAR_MANY, NEAR_FEW, INNER_MANY, INNER_FEW, CROSS = range(LISTS)


def build_lists(geo, index, centre_ref, offsets_ref, counts_ref, meta_ref):
    first = index * geo.rows
    odd = index % 2 == 1
    meta_ref[geo.odd_at] = odd.astype(jnp.int32)
    lengths = [jnp.int32(0)] * LISTS
    for b in range(geo.batches):
        local = centre_ref[b] - first
        count = counts_ref[b]
        meta_ref[geo.local_at + b] = local
        meta_ref[geo.count_at + b] = count
        low = high = jnp.bool_(False)
        for k in range(geo.slots):
            offset = offsets_ref[k, b]
            meta_ref[geo.offsets_at + k * geo.batches + b] = offset
            row = local + offset
            low = low | ((k < count) & (row < 0))
            high = high | ((k < count) & (row >= geo.rows))
        cross = (odd & high) | (jnp.logical_not(odd) & low)
        near = (odd & low) | (jnp.logical_not(odd) & high)
        inner = jnp.logical_not(low | high)
        many = count > 2
        few = (count > 0) & jnp.logical_not(many)
        kinds = [kind & size for kind in (cross, near, inner) for size in (many, few)]
        for which, member in enumerate(kinds + [cross]):
            meta_ref[which * geo.list_size + lengths[which]] = b
            lengths[which] = lengths[which] + member.astype(jnp.int32)
    for which in range(LISTS):
        meta_ref[which * geo.list_size + lengths[which]] = geo.batches
        meta_ref[geo.lengths_at + which] = lengths[which]


def zone(geo, odd, cross):
    span = geo.span if cross else geo.own - geo.span
    return pl.ds(jnp.where(odd == cross, geo.own - span, 0), span)


def pack_kernel(
    geo, density_ref, centre_in, offsets_in, counts_in,
    near_ref, cross_ref, meta_ref, acc_ref,
    centre_ref, offsets_ref, counts_ref, sems,
):
    index = lax.axis_index("blk")
    odd = index % 2 == 1

    by_size = lambda pack: sorted(pack, key=lambda segment: segment[2])
    copies = []
    for side, (ref, upper) in enumerate(((cross_ref, odd), (near_ref, jnp.logical_not(odd)))):
        for i, (up, down) in enumerate(zip(*(by_size(pack) for pack in geo.packs))):
            start = jnp.where(upper, up[0], down[0])
            place = jnp.where(upper, up[1], down[1])
            copies.append(
                pltpu.make_async_copy(
                    density_ref.at[pl.ds(start, up[2])], ref.at[pl.ds(place, up[2])], sems.at[side, i]
                )
            )
    for copy in copies:
        copy.start()
    scalars = [
        pltpu.make_async_copy(*pair, sems.at[2, i])
        for i, pair in enumerate(
            ((centre_in, centre_ref), (offsets_in, offsets_ref), (counts_in, counts_ref))
        )
    ]
    for copy in scalars:
        copy.start()
    for where in (zone(geo, odd, False), pl.ds(geo.first_at, geo.halo)):
        acc_ref[where] = jnp.zeros_like(acc_ref[where])
    for copy in scalars:
        copy.wait()
    build_lists(geo, index, centre_ref, offsets_ref, counts_ref, meta_ref)
    for copy in copies:
        copy.wait()


def group_count(geo, meta_ref, which):
    return (meta_ref[geo.lengths_at + which] + GROUP - 1) // GROUP


def inner_share(geo, meta_ref):
    before = BUDGET
    for which in (CROSS_MANY, CROSS_FEW, NEAR_MANY, NEAR_FEW):
        before = before - COST[which % 2] * group_count(geo, meta_ref, which)
    waiting = jnp.where((lax.axis_index("blk") + 1) // 2 % 2 == 1, WAIT, 0)
    share = []
    for which in (INNER_MANY, INNER_FEW):
        cost, count = COST[which % 2], group_count(geo, meta_ref, which)
        first = jnp.minimum(jnp.maximum(before, 0) // cost, count)
        second = jnp.minimum(jnp.maximum(waiting, 0) // cost, count - first)
        before = before - cost * first
        waiting = waiting - cost * second
        share.append((0, first, first + second, count))
    return share


def inner_part(geo, meta_ref, stage, refs):
    for which, width, bounds in zip(
        (INNER_MANY, INNER_FEW), (geo.slots, 2), inner_share(geo, meta_ref)
    ):
        each_group(
            geo,
            meta_ref,
            which,
            lambda chosen, width=width: add_whole(geo, chosen, width, *refs),
            begin=bounds[stage],
            end=bounds[stage + 1],
        )


def each_group(geo, meta_ref, which, body, size=GROUP, begin=0, end=None):
    length = meta_ref[geo.lengths_at + which]

    def step(i, carry):
        chosen = []
        for n in range(size):
            place = i * size + n
            there = place < length
            b = meta_ref[which * geo.list_size + jnp.minimum(place, length)]
            chosen.append((jnp.where(there, b, 0), there))
        body(chosen)
        return carry

    lax.fori_loop(begin, (length + size - 1) // size if end is None else end, step, 0)


class Slots:
    def __init__(self, geo, meta_ref, b, there, width):
        local = meta_ref[geo.local_at + b]
        count = jnp.where(there, meta_ref[geo.count_at + b], 0)
        self.offset = [meta_ref[geo.offsets_at + k * geo.batches + b] for k in range(width)]
        self.local = local
        self.row = [local + offset for offset in self.offset]
        self.live = [k < count for k in range(width)]
        self.own = [(row >= 0) & (row < geo.rows) for row in self.row]
        self.width = width


def panels(slots, ao_ref, b):
    return jnp.concatenate(
        [
            ao_ref[b, k] * jnp.where(slots.live[k], 1.0, 0.0).astype(ao_ref.dtype)
            for k in range(slots.width)
        ],
        axis=0,
    )


def gathered(tiles_ref, places):
    return jnp.concatenate(
        [jnp.concatenate([tiles_ref[place] for place in row], axis=1) for row in places], axis=0
    )


def potentials(xs, tiles, batches, kernel_ref):
    fs = [
        jnp.dot(t, x, preferred_element_type=jnp.float32).astype(jnp.bfloat16)
        for t, x in zip(tiles, xs)
    ]
    return [
        jnp.dot(f, kernel_ref[b], preferred_element_type=jnp.float32) for f, b in zip(fs, batches)
    ]


def outer_product(x, h):
    return lax.dot_general(x, h, (((1,), (1,)), ((), ())), preferred_element_type=jnp.float32)


def chain(xs, tiles, batches, kernel_ref, weights_ref):
    gs = potentials(xs, tiles, batches, kernel_ref)
    hs = [(g * weights_ref[pl.ds(b, 1), :]).astype(jnp.bfloat16) for g, b in zip(gs, batches)]
    return [outer_product(x, h) for x, h in zip(xs, hs)]


def scatter(part, target, nb, acc_ref):
    for k, row in enumerate(target):
        for j, place in enumerate(row):
            acc_ref[place] += part[k * nb : (k + 1) * nb, j * nb : (j + 1) * nb]


def add_whole(
    geo, chosen, width, meta_ref, tiles_ref, ao_ref, kernel_ref, weights_ref, acc_ref, halo_ref=None
):
    xs, tiles, targets = ([], [], [])
    for b, there in chosen:
        slots = Slots(geo, meta_ref, b, there, width)
        xs.append(panels(slots, ao_ref, b))
        rows, target = ([], [])
        for k in range(width):
            band = [slots.offset[j] - slots.offset[k] + geo.half for j in range(width)]
            own = slots.own[k]
            base = jnp.where(slots.live[k] & own, slots.row[k], 0) * geo.band
            row = jnp.concatenate([tiles_ref[base + o] for o in band], axis=1)
            if halo_ref is not None:
                away = slots.live[k] & jnp.logical_not(own)
                outside = jnp.where(away, geo.pick(geo.halo_base, 0, slots.row[k], 0), 0)
                other = [halo_ref[jnp.where(away, outside + o, 0)] for o in band]
                row = jnp.where(away, jnp.concatenate(other, axis=1), row)
                base = jnp.where(away, outside + geo.first_at, base)
            rows.append(row)
            target.append(
                [
                    jnp.where(slots.live[k] & slots.live[j], base + band[j], geo.spare)
                    for j in range(width)
                ]
            )
        tiles.append(jnp.concatenate(rows, axis=0))
        targets.append(target)
    parts = chain(xs, tiles, [b for b, _ in chosen], kernel_ref, weights_ref)
    for part, target in zip(parts, targets):
        scatter(part, target, ao_ref.shape[2], acc_ref)


def add_own(geo, chosen, width, meta_ref, tiles_ref, ao_ref, kernel_ref, weights_ref, acc_ref):
    xs, tiles, targets = ([], [], [])
    for b, there in chosen:
        slots = Slots(geo, meta_ref, b, there, width)
        xs.append(panels(slots, ao_ref, b))
        places, target = ([], [])
        for k in range(width):
            row = slots.row[k]
            band = [slots.offset[j] - slots.offset[k] + geo.half for j in range(width)]
            base = jnp.where(slots.own[k], row, 0) * geo.band
            places.append([base + o for o in band])
            base = geo.pick(geo.early_base, geo.early_at, row, base)
            target.append(
                [
                    jnp.where(
                        slots.live[k] & slots.live[j] & slots.own[j], base + band[j], geo.spare
                    )
                    for j in range(width)
                ]
            )
        tiles.append(gathered(tiles_ref, places))
        targets.append(target)
    parts = chain(xs, tiles, [b for b, _ in chosen], kernel_ref, weights_ref)
    for part, target in zip(parts, targets):
        scatter(part, target, ao_ref.shape[2], acc_ref)


def halo_rows(geo, meta_ref, slots):
    odd = meta_ref[geo.odd_at] == 1
    rows, places, present = ([], [], [])
    for i in range(geo.reach):
        row = jnp.where(odd, geo.rows + i, i - geo.reach)
        place, found = (jnp.int32(0), jnp.bool_(False))
        for k in range(slots.width):
            hit = slots.live[k] & (slots.row[k] == row)
            place = jnp.where(hit, k, place)
            found = found | hit
        rows.append(row)
        places.append(place)
        present.append(found)
    return rows, places, present


def add_corner(geo, chosen, meta_ref, halo_ref, ao_ref, kernel_ref, weights_ref, h_ref, total_ref):
    nb = ao_ref.shape[2]
    factor = lambda flag: jnp.where(flag, 1.0, 0.0)
    xs, sides, tiles, masks = ([], [], [], [])
    for b, there in chosen:
        slots = Slots(geo, meta_ref, b, there, geo.slots)
        rows, places, present = halo_rows(geo, meta_ref, slots)
        xs.append(panels(slots, ao_ref, b))
        sides.append(
            jnp.concatenate(
                [
                    ao_ref[b, place] * factor(found).astype(ao_ref.dtype)
                    for place, found in zip(places, present)
                ],
                axis=0,
            )
        )
        picked = []
        for row, found in zip(rows, present):
            base = geo.pick(geo.halo_base, 0, row, 0) - row + geo.half
            picked.append([jnp.where(found, base + column, 0) for column in slots.row])
        tiles.append(gathered(halo_ref, picked))
        masks.append([factor(found) for found in present])
    gs = potentials(xs, tiles, [b for b, _ in chosen], kernel_ref)
    hs = []
    for g, mask, (b, there) in zip(gs, masks, chosen):
        weights = weights_ref[pl.ds(b, 1), :]
        h = jnp.concatenate(
            [g[i * nb : (i + 1) * nb] * (weights * mask[i]) for i in range(geo.reach)], axis=0
        ).astype(jnp.bfloat16)
        h_ref[jnp.where(there, b, geo.batches)] = h
        hs.append(h)
    total_ref[...] += outer_product(
        jnp.concatenate(sides, axis=1), jnp.concatenate(hs, axis=1)
    )


def add_columns(geo, chosen, width, meta_ref, ao_ref, h_ref, acc_ref):
    parts, targets = ([], [])
    for b, there in chosen:
        slots = Slots(geo, meta_ref, b, there, width)
        rows, _, present = halo_rows(geo, meta_ref, slots)
        parts.append(outer_product(ao_ref[b, pl.ds(0, width)].reshape(-1, ao_ref.shape[3]), h_ref[b]))
        targets.append(
            [
                [
                    jnp.where(
                        slots.live[k] & slots.own[k] & found,
                        slots.row[k] * geo.band + row - slots.row[k] + geo.half,
                        geo.spare,
                    )
                    for row, found in zip(rows, present)
                ]
                for k in range(width)
            ]
        )
    for part, target in zip(parts, targets):
        scatter(part, target, ao_ref.shape[2], acc_ref)


def early_kernel(
    geo, meta_ref, tiles_ref, ao_ref, kernel_ref, weights_ref, acc_in, acc_ref, early_out
):
    odd = meta_ref[geo.odd_at] == 1
    for where in (zone(geo, odd, True), pl.ds(geo.early_at, geo.early), pl.ds(geo.spare, 1)):
        acc_ref[where] = jnp.zeros_like(acc_ref[where])
    refs = (meta_ref, tiles_ref, ao_ref, kernel_ref, weights_ref, acc_ref)
    for which, width in ((CROSS_MANY, geo.slots), (CROSS_FEW, 2)):
        each_group(
            geo, meta_ref, which, lambda chosen, width=width: add_own(geo, chosen, width, *refs)
        )
    early_out[...] = acc_ref[pl.ds(geo.early_at, geo.early)].astype(early_out.dtype)


def near_kernel(
    geo, meta_ref, halo_ref, tiles_ref, ao_ref, kernel_ref, weights_ref, acc_in, acc_ref, first_out
):
    refs = (meta_ref, tiles_ref, ao_ref, kernel_ref, weights_ref, acc_ref, halo_ref)
    for which, width in ((NEAR_MANY, geo.slots), (NEAR_FEW, 2)):
        each_group(
            geo, meta_ref, which, lambda chosen, width=width: add_whole(geo, chosen, width, *refs)
        )
    first_out[...] = acc_ref[pl.ds(geo.first_at, geo.halo)].astype(first_out.dtype)
    inner_part(geo, meta_ref, 0, refs[:-1])


def waiting_kernel(
    geo, meta_ref, tiles_ref, ao_ref, kernel_ref, weights_ref, acc_in, acc_ref, done_ref
):
    inner_part(geo, meta_ref, 1, (meta_ref, tiles_ref, ao_ref, kernel_ref, weights_ref, acc_ref))
    done_ref[0] = 1


def late_kernel(
    geo, meta_ref, done_ref, halo_ref, ao_ref, kernel_ref, weights_ref, h_ref, late_out, total_ref
):
    nb = ao_ref.shape[2]
    total_ref[...] = jnp.zeros_like(total_ref)

    def work(chosen):
        add_corner(
            geo, chosen, meta_ref, halo_ref, ao_ref, kernel_ref, weights_ref, h_ref, total_ref
        )

    groups = (meta_ref[geo.lengths_at + CROSS] + 1) // LATE_GROUP
    each_group(geo, meta_ref, CROSS, work, size=LATE_GROUP, end=groups)
    each_group(geo, meta_ref, CROSS, work, size=LATE_GROUP // 2, begin=2 * groups)
    for i in range(geo.reach):
        for j in range(geo.reach):
            late_out[i * geo.reach + j] = total_ref[
                i * nb : (i + 1) * nb, j * nb : (j + 1) * nb
            ].astype(late_out.dtype)


def inner_kernel(
    geo, meta_ref, first_ref, tiles_ref, ao_ref, kernel_ref, weights_ref, h_ref, acc_in,
    acc_ref, out_ref, sems,
):
    odd = meta_ref[geo.odd_at] == 1
    refs = (meta_ref, tiles_ref, ao_ref, kernel_ref, weights_ref, acc_ref)
    inner_part(geo, meta_ref, 2, refs)

    def add_near(up, down):
        for start, place, count in geo.packs[0 if up else 1]:
            acc_ref[pl.ds(start, count)] += first_ref[pl.ds(place, count)].astype(jnp.float32)

    by_parity(odd, add_near, True, False)
    done = zone(geo, odd, False)
    copy = pltpu.make_async_copy(acc_ref.at[done], out_ref.at[done], sems.at[0])
    copy.start()
    for which, width in ((CROSS_MANY, geo.slots), (CROSS_FEW, 2)):
        each_group(
            geo,
            meta_ref,
            which,
            lambda chosen, width=width: add_columns(
                geo, chosen, width, meta_ref, ao_ref, h_ref, acc_ref
            ),
        )

    def write_quiet(up, down):
        run_copies(
            [
                pltpu.make_async_copy(
                    acc_ref.at[pl.ds(start, count)], out_ref.at[pl.ds(start, count)], sems.at[1 + i]
                )
                for i, (start, count) in enumerate(geo.quiet[0 if up else 1])
            ]
        )

    by_parity(odd, write_quiet, True, False)
    copy.wait()


def finish_kernel(geo, meta_ref, early_ref, late_ref, acc_ref, out_in, out_ref, total, sems):
    def add(up, down):
        copies = []
        for packs, ref in ((geo.early_packs, early_ref), (geo.late_packs, late_ref)):
            for start, place, count in packs[0 if up else 1]:
                spot = pl.ds(len(copies) * geo.band, count)
                total[spot] = acc_ref[pl.ds(start, count)] + ref[pl.ds(place, count)].astype(
                    jnp.float32
                )
                copy = pltpu.make_async_copy(
                    total.at[spot], out_ref.at[pl.ds(start, count)], sems.at[len(copies)]
                )
                copy.start()
                copies.append(copy)
        for copy in copies:
            copy.wait()

    by_parity(meta_ref[geo.odd_at] == 1, add, False, True)


def call(kernel, out_shape, in_specs, out_specs, scratch, aliases=None, cost=None):
    return pl.pallas_call(
        kernel,
        out_shape=out_shape,
        in_specs=in_specs,
        out_specs=out_specs,
        scratch_shapes=scratch,
        input_output_aliases=aliases or {},
        cost_estimate=cost,
        compiler_params=pltpu.CompilerParams(vmem_limit_bytes=16 * MIB),
    )


def to_first(x, size):
    pairs = [(i, i + 1) for i in range(0, size - 1, 2)]
    got = lax.ppermute(x, "blk", pairs + [(j, i) for i, j in pairs])
    return pltpu.with_memory_space_constraint(got, pltpu.VMEM)


def to_second(x, size):
    pairs = [(i, i + 1) for i in range(1, size - 1, 2)]
    got = lax.ppermute(x, "blk", pairs + [(j, i) for i, j in pairs])
    return pltpu.with_memory_space_constraint(got, pltpu.VMEM)


def local(density, ao_values, kernel, grid_weights, centre, sig_offsets, counts):
    rows, band, nb, _ = density.shape
    batches, slots, _, pts = ao_values.shape
    size = lax.axis_size("blk")
    geo = Geometry(rows, band, batches, slots)
    in_hbm = lambda x: pltpu.with_memory_space_constraint(x, pltpu.HBM)
    tiles = density.reshape(geo.own, nb, nb)
    pack = lambda count: pltpu.VMEM((count, nb, nb), jnp.bfloat16)
    dma = pltpu.SemaphoreType.DMA
    acc_type = pltpu.VMEM((geo.spare + 1, nb, nb), jnp.float32)

    near_halo, cross_halo, meta, acc = call(
        functools.partial(pack_kernel, geo),
        (pack(geo.halo),) * 2 + (pltpu.SMEM((geo.meta_size,), jnp.int32), acc_type),
        [ANY_SPEC] * 4,
        (VMEM_SPEC,) * 2 + (SMEM_SPEC, VMEM_SPEC),
        [
            pltpu.SMEM((batches,), jnp.int32),
            pltpu.SMEM((slots, batches), jnp.int32),
            pltpu.SMEM((batches,), jnp.int32),
            dma((3, max(geo.reach, 3))),
        ],
        cost=pl.CostEstimate(flops=10**10, bytes_accessed=10**8, transcendentals=0),
    )(in_hbm(tiles), in_hbm(centre), in_hbm(sig_offsets.T), in_hbm(counts))
    cross_halo = to_second(cross_halo, size)
    near_halo = to_first(near_halo, size)

    panel = (tiles, ao_values, kernel, grid_weights)
    acc, early = call(
        functools.partial(early_kernel, geo),
        (acc_type, pack(geo.early)),
        [SMEM_SPEC] + [VMEM_SPEC] * 5,
        (VMEM_SPEC,) * 2,
        [],
        {5: 0},
    )(meta, *panel, acc)
    early = to_second(early, size)

    acc, first = call(
        functools.partial(near_kernel, geo),
        (acc_type, pack(geo.halo)),
        [SMEM_SPEC] + [VMEM_SPEC] * 6,
        (VMEM_SPEC,) * 2,
        [],
        {6: 0},
    )(meta, near_halo, *panel, acc)
    first = to_first(first, size)

    acc, done = call(
        functools.partial(waiting_kernel, geo),
        (acc_type, pltpu.SMEM((1,), jnp.int32)),
        [SMEM_SPEC] + [VMEM_SPEC] * 5,
        (VMEM_SPEC, SMEM_SPEC),
        [],
        {5: 0},
    )(meta, *panel, acc)

    h_type = pltpu.VMEM((batches + 1, geo.reach * nb, pts), jnp.bfloat16)
    h, late = call(
        functools.partial(late_kernel, geo),
        (h_type, pack(geo.late)),
        [SMEM_SPEC] * 2 + [VMEM_SPEC] * 4,
        (VMEM_SPEC,) * 2,
        [pltpu.VMEM((geo.reach * nb, geo.reach * nb), jnp.float32)],
    )(meta, done, cross_halo, *panel[1:])
    late = to_second(late, size)

    whole = jax.ShapeDtypeStruct((geo.own, nb, nb), jnp.float32)
    acc, out = call(
        functools.partial(inner_kernel, geo),
        (acc_type, whole),
        [SMEM_SPEC] + [VMEM_SPEC] * 7,
        (VMEM_SPEC, ANY_SPEC),
        [dma((1 + max(len(runs) for runs in geo.quiet),))],
        {7: 0},
    )(meta, first, *panel, h, acc)

    parts = 2 * geo.reach
    out = call(
        functools.partial(finish_kernel, geo),
        whole,
        [SMEM_SPEC] + [VMEM_SPEC] * 3 + [ANY_SPEC],
        ANY_SPEC,
        [pltpu.VMEM((parts * band, nb, nb), jnp.float32), dma((parts,))],
        {4: 0},
    )(meta, early, late, acc, out)
    return out.reshape(rows, band, nb, nb)


def solution(mesh):
    placed = (
        P(("groups", "blk"), None, None, None),
        P(("groups", "blk"), None, None, None),
        P(("groups", "blk"), None, None),
        P(("groups", "blk"), None),
        P(("groups", "blk")),
        P(("groups", "blk"), None),
        P(("groups", "blk")),
    )
    return jax.shard_map(
        local,
        mesh=mesh,
        in_specs=placed,
        out_specs=P(("groups", "blk"), None, None, None),
        check_vma=False,
    )
```

```python
import functools

import jax
import jax.numpy as jnp
from jax import lax
from jax.experimental import pallas as pl
from jax.experimental.pallas import tpu as pltpu
from jax.sharding import PartitionSpec as P

MIB = 1 << 20
GROUP = 2
LATE_GROUP = 4
LISTS = 7
BUDGET = 43
WAIT = 18
COST = (10, 7)
SMEM_SPEC = pl.BlockSpec(memory_space=pltpu.SMEM)
VMEM_SPEC = pl.BlockSpec(memory_space=pltpu.VMEM)
ANY_SPEC = pl.BlockSpec(memory_space=pl.ANY)


class Geometry:
    def __init__(self, rows, band, batches, slots):
        self.rows, self.band, self.batches, self.slots = rows, band, batches, slots
        self.half = half = (band - 1) // 2
        self.reach = reach = half // 2
        self.own = rows * band
        low = [(-m, reach + m, band) for m in range(reach, 0, -1)]
        high = [(rows + m, 0, 3 * reach - m) for m in range(reach)]
        self.halo = sum(stop - start for _, start, stop in low)
        low_cut = [half - row for row, _, _ in low]
        high_cut = [rows - row + half for row, _, _ in high]
        early = (
            [(row, cut, stop) for (row, _, stop), cut in zip(low, low_cut)],
            [(row, start, cut) for (row, start, _), cut in zip(high, high_cut)],
        )
        late = (
            [(row, start, cut) for (row, start, _), cut in zip(low, low_cut)],
            [(row, cut, stop) for (row, _, stop), cut in zip(high, high_cut)],
        )
        self.early = sum(stop - start for _, start, stop in early[0])
        self.late = self.halo - self.early
        self.first_at = self.own
        self.early_at = self.own + self.halo
        self.spare = self.early_at + self.early
        self.halo_base = self.bases((low, high))
        self.early_base = self.bases(early)
        shifts = (rows, -rows)
        self.packs = [self.places(*pair) for pair in zip((low, high), shifts)]
        self.early_packs = [self.places(*pair) for pair in zip(early, shifts)]
        self.late_packs = [self.places(*pair) for pair in zip(late, shifts)]
        self.span = min(2 * reach, rows) * band
        self.quiet = [
            self.others(self.packs[1], 0, self.span),
            self.others(self.packs[0], self.own - self.span, self.own),
        ]
        self.list_size = batches + 2
        self.lengths_at = LISTS * self.list_size
        self.local_at = self.lengths_at + LISTS
        self.count_at = self.local_at + batches
        self.offsets_at = self.count_at + batches
        self.odd_at = self.offsets_at + slots * batches
        self.meta_size = self.odd_at + 1

    def bases(self, sides):
        found = {}
        for segments in sides:
            place = 0
            for row, start, stop in segments:
                found[row] = place - start
                place += stop - start
        return found

    def places(self, segments, shift):
        pack, place = ([], 0)
        for row, start, stop in segments:
            pack.append(((row + shift) * self.band + start, place, stop - start))
            place += stop - start
        return pack

    def others(self, pack, begin, end):
        touched = set()
        for start, _, count in pack:
            touched.update(range(start, start + count))
        runs = []
        for index in range(begin, end):
            if index in touched:
                continue
            if runs and sum(runs[-1]) == index:
                runs[-1] = (runs[-1][0], runs[-1][1] + 1)
            else:
                runs.append((index, 1))
        return runs

    def pick(self, bases, shift, row, otherwise):
        value = otherwise
        for at, base in bases.items():
            value = jnp.where(row == at, base + shift, value)
        return value


def run_copies(copies):
    for copy in copies:
        copy.start()
    for copy in copies:
        copy.wait()


def by_parity(odd, body, first, second):
    @pl.when(jnp.logical_not(odd))
    def _():
        body(first, second)

    @pl.when(odd)
    def _():
        body(second, first)


CROSS_MANY, CROSS_FEW, NEAR_MANY, NEAR_FEW, INNER_MANY, INNER_FEW, CROSS = range(LISTS)


def build_lists(geo, index, centre_ref, offsets_ref, counts_ref, meta_ref):
    first = index * geo.rows
    odd = index % 2 == 1
    meta_ref[geo.odd_at] = odd.astype(jnp.int32)
    lengths = [jnp.int32(0)] * LISTS
    for b in range(geo.batches):
        local = centre_ref[b] - first
        count = counts_ref[b]
        meta_ref[geo.local_at + b] = local
        meta_ref[geo.count_at + b] = count
        low = high = jnp.bool_(False)
        for k in range(geo.slots):
            offset = offsets_ref[k, b]
            meta_ref[geo.offsets_at + k * geo.batches + b] = offset
            row = local + offset
            low = low | ((k < count) & (row < 0))
            high = high | ((k < count) & (row >= geo.rows))
        cross = (odd & high) | (jnp.logical_not(odd) & low)
        near = (odd & low) | (jnp.logical_not(odd) & high)
        inner = jnp.logical_not(low | high)
        many = count > 2
        few = (count > 0) & jnp.logical_not(many)
        kinds = [kind & size for kind in (cross, near, inner) for size in (many, few)]
        for which, member in enumerate(kinds + [cross]):
            meta_ref[which * geo.list_size + lengths[which]] = b
            lengths[which] = lengths[which] + member.astype(jnp.int32)
    for which in range(LISTS):
        meta_ref[which * geo.list_size + lengths[which]] = geo.batches
        meta_ref[geo.lengths_at + which] = lengths[which]


def zone(geo, odd, cross):
    span = geo.span if cross else geo.own - geo.span
    return pl.ds(jnp.where(odd == cross, geo.own - span, 0), span)


def pack_kernel(
    geo, density_ref, centre_in, offsets_in, counts_in,
    near_ref, cross_ref, meta_ref, acc_ref,
    centre_ref, offsets_ref, counts_ref, sems,
):
    index = lax.axis_index("blk")
    odd = index % 2 == 1

    by_size = lambda pack: sorted(pack, key=lambda segment: segment[2])
    copies = []
    for side, (ref, upper) in enumerate(((cross_ref, odd), (near_ref, jnp.logical_not(odd)))):
        for i, (up, down) in enumerate(zip(*(by_size(pack) for pack in geo.packs))):
            start = jnp.where(upper, up[0], down[0])
            place = jnp.where(upper, up[1], down[1])
            copies.append(
                pltpu.make_async_copy(
                    density_ref.at[pl.ds(start, up[2])], ref.at[pl.ds(place, up[2])], sems.at[side, i]
                )
            )
    for copy in copies:
        copy.start()
    scalars = [
        pltpu.make_async_copy(*pair, sems.at[2, i])
        for i, pair in enumerate(
            ((centre_in, centre_ref), (offsets_in, offsets_ref), (counts_in, counts_ref))
        )
    ]
    for copy in scalars:
        copy.start()
    for where in (zone(geo, odd, False), pl.ds(geo.first_at, geo.halo)):
        acc_ref[where] = jnp.zeros_like(acc_ref[where])
    for copy in scalars:
        copy.wait()
    build_lists(geo, index, centre_ref, offsets_ref, counts_ref, meta_ref)
    for copy in copies:
        copy.wait()


def group_count(geo, meta_ref, which):
    return (meta_ref[geo.lengths_at + which] + GROUP - 1) // GROUP


def waits():
    return (lax.axis_index("blk") + 1) // 2 % 2 == 1


def inner_share(geo, meta_ref):
    before = BUDGET
    for which in (CROSS_MANY, CROSS_FEW, NEAR_MANY, NEAR_FEW):
        before = before - COST[which % 2] * group_count(geo, meta_ref, which)
    waiting = jnp.where(waits(), WAIT, 0)
    share = []
    for which in (INNER_MANY, INNER_FEW):
        cost, count = COST[which % 2], group_count(geo, meta_ref, which)
        first = jnp.minimum(jnp.maximum(before, 0) // cost, count)
        second = jnp.minimum(jnp.maximum(waiting, 0) // cost, count - first)
        before = before - cost * first
        waiting = waiting - cost * second
        share.append((0, first, first + second, count))
    return share


def inner_part(geo, meta_ref, stage, refs):
    for which, width, bounds in zip(
        (INNER_MANY, INNER_FEW), (geo.slots, 2), inner_share(geo, meta_ref)
    ):
        each_group(
            geo,
            meta_ref,
            which,
            lambda chosen, width=width: add_whole(geo, chosen, width, *refs),
            begin=bounds[stage],
            end=bounds[stage + 1],
        )


def each_group(geo, meta_ref, which, body, size=GROUP, begin=0, end=None):
    length = meta_ref[geo.lengths_at + which]

    def step(i, carry):
        chosen = []
        for n in range(size):
            place = i * size + n
            there = place < length
            b = meta_ref[which * geo.list_size + jnp.minimum(place, length)]
            chosen.append((jnp.where(there, b, 0), there))
        body(chosen)
        return carry

    lax.fori_loop(begin, (length + size - 1) // size if end is None else end, step, 0)


class Slots:
    def __init__(self, geo, meta_ref, b, there, width):
        local = meta_ref[geo.local_at + b]
        count = jnp.where(there, meta_ref[geo.count_at + b], 0)
        self.offset = [meta_ref[geo.offsets_at + k * geo.batches + b] for k in range(width)]
        self.local = local
        self.row = [local + offset for offset in self.offset]
        self.live = [k < count for k in range(width)]
        self.own = [(row >= 0) & (row < geo.rows) for row in self.row]
        self.width = width


def panels(slots, ao_ref, b):
    return jnp.concatenate(
        [
            ao_ref[b, k] * jnp.where(slots.live[k], 1.0, 0.0).astype(ao_ref.dtype)
            for k in range(slots.width)
        ],
        axis=0,
    )


def gathered(tiles_ref, places):
    return jnp.concatenate(
        [jnp.concatenate([tiles_ref[place] for place in row], axis=1) for row in places], axis=0
    )


def potentials(xs, tiles, batches, kernel_ref):
    fs = [
        jnp.dot(t, x, preferred_element_type=jnp.float32).astype(jnp.bfloat16)
        for t, x in zip(tiles, xs)
    ]
    return [
        jnp.dot(f, kernel_ref[b], preferred_element_type=jnp.float32) for f, b in zip(fs, batches)
    ]


def outer_product(x, h):
    return lax.dot_general(x, h, (((1,), (1,)), ((), ())), preferred_element_type=jnp.float32)


def chain(xs, tiles, batches, kernel_ref, weights_ref):
    gs = potentials(xs, tiles, batches, kernel_ref)
    hs = [(g * weights_ref[pl.ds(b, 1), :]).astype(jnp.bfloat16) for g, b in zip(gs, batches)]
    return [outer_product(x, h) for x, h in zip(xs, hs)]


def scatter(part, target, nb, acc_ref):
    for k, row in enumerate(target):
        for j, place in enumerate(row):
            acc_ref[place] += part[k * nb : (k + 1) * nb, j * nb : (j + 1) * nb]


def add_whole(
    geo, chosen, width, meta_ref, tiles_ref, ao_ref, kernel_ref, weights_ref, acc_ref, halo_ref=None
):
    xs, tiles, targets = ([], [], [])
    for b, there in chosen:
        slots = Slots(geo, meta_ref, b, there, width)
        xs.append(panels(slots, ao_ref, b))
        rows, target = ([], [])
        for k in range(width):
            band = [slots.offset[j] - slots.offset[k] + geo.half for j in range(width)]
            own = slots.own[k]
            base = jnp.where(slots.live[k] & own, slots.row[k], 0) * geo.band
            row = jnp.concatenate([tiles_ref[base + o] for o in band], axis=1)
            if halo_ref is not None:
                away = slots.live[k] & jnp.logical_not(own)
                outside = jnp.where(away, geo.pick(geo.halo_base, 0, slots.row[k], 0), 0)
                other = [halo_ref[jnp.where(away, outside + o, 0)] for o in band]
                row = jnp.where(away, jnp.concatenate(other, axis=1), row)
                base = jnp.where(away, outside + geo.first_at, base)
            rows.append(row)
            target.append(
                [
                    jnp.where(slots.live[k] & slots.live[j], base + band[j], geo.spare)
                    for j in range(width)
                ]
            )
        tiles.append(jnp.concatenate(rows, axis=0))
        targets.append(target)
    parts = chain(xs, tiles, [b for b, _ in chosen], kernel_ref, weights_ref)
    for part, target in zip(parts, targets):
        scatter(part, target, ao_ref.shape[2], acc_ref)


def add_own(geo, chosen, width, meta_ref, tiles_ref, ao_ref, kernel_ref, weights_ref, acc_ref):
    xs, tiles, targets = ([], [], [])
    for b, there in chosen:
        slots = Slots(geo, meta_ref, b, there, width)
        xs.append(panels(slots, ao_ref, b))
        places, target = ([], [])
        for k in range(width):
            row = slots.row[k]
            band = [slots.offset[j] - slots.offset[k] + geo.half for j in range(width)]
            base = jnp.where(slots.own[k], row, 0) * geo.band
            places.append([base + o for o in band])
            base = geo.pick(geo.early_base, geo.early_at, row, base)
            target.append(
                [
                    jnp.where(
                        slots.live[k] & slots.live[j] & slots.own[j], base + band[j], geo.spare
                    )
                    for j in range(width)
                ]
            )
        tiles.append(gathered(tiles_ref, places))
        targets.append(target)
    parts = chain(xs, tiles, [b for b, _ in chosen], kernel_ref, weights_ref)
    for part, target in zip(parts, targets):
        scatter(part, target, ao_ref.shape[2], acc_ref)


def halo_rows(geo, meta_ref, slots):
    odd = meta_ref[geo.odd_at] == 1
    rows, places, present = ([], [], [])
    for i in range(geo.reach):
        row = jnp.where(odd, geo.rows + i, i - geo.reach)
        place, found = (jnp.int32(0), jnp.bool_(False))
        for k in range(slots.width):
            hit = slots.live[k] & (slots.row[k] == row)
            place = jnp.where(hit, k, place)
            found = found | hit
        rows.append(row)
        places.append(place)
        present.append(found)
    return rows, places, present


def add_corner(geo, chosen, meta_ref, halo_ref, ao_ref, kernel_ref, weights_ref, h_ref, total_ref):
    nb = ao_ref.shape[2]
    factor = lambda flag: jnp.where(flag, 1.0, 0.0)
    xs, sides, tiles, masks = ([], [], [], [])
    for b, there in chosen:
        slots = Slots(geo, meta_ref, b, there, geo.slots)
        rows, places, present = halo_rows(geo, meta_ref, slots)
        xs.append(panels(slots, ao_ref, b))
        sides.append(
            jnp.concatenate(
                [
                    ao_ref[b, place] * factor(found).astype(ao_ref.dtype)
                    for place, found in zip(places, present)
                ],
                axis=0,
            )
        )
        picked = []
        for row, found in zip(rows, present):
            base = geo.pick(geo.halo_base, 0, row, 0) - row + geo.half
            picked.append([jnp.where(found, base + column, 0) for column in slots.row])
        tiles.append(gathered(halo_ref, picked))
        masks.append([factor(found) for found in present])
    gs = potentials(xs, tiles, [b for b, _ in chosen], kernel_ref)
    hs = []
    for g, mask, (b, there) in zip(gs, masks, chosen):
        weights = weights_ref[pl.ds(b, 1), :]
        h = jnp.concatenate(
            [g[i * nb : (i + 1) * nb] * (weights * mask[i]) for i in range(geo.reach)], axis=0
        ).astype(jnp.bfloat16)
        h_ref[jnp.where(there, b, geo.batches)] = h
        hs.append(h)
    total_ref[...] += outer_product(
        jnp.concatenate(sides, axis=1), jnp.concatenate(hs, axis=1)
    )


def add_columns(geo, chosen, width, meta_ref, ao_ref, h_ref, acc_ref):
    parts, targets = ([], [])
    for b, there in chosen:
        slots = Slots(geo, meta_ref, b, there, width)
        rows, _, present = halo_rows(geo, meta_ref, slots)
        parts.append(outer_product(ao_ref[b, pl.ds(0, width)].reshape(-1, ao_ref.shape[3]), h_ref[b]))
        targets.append(
            [
                [
                    jnp.where(
                        slots.live[k] & slots.own[k] & found,
                        slots.row[k] * geo.band + row - slots.row[k] + geo.half,
                        geo.spare,
                    )
                    for row, found in zip(rows, present)
                ]
                for k in range(width)
            ]
        )
    for part, target in zip(parts, targets):
        scatter(part, target, ao_ref.shape[2], acc_ref)


def early_kernel(
    geo, meta_ref, tiles_ref, ao_ref, kernel_ref, weights_ref, acc_in, acc_ref, early_out
):
    odd = meta_ref[geo.odd_at] == 1
    for where in (zone(geo, odd, True), pl.ds(geo.early_at, geo.early), pl.ds(geo.spare, 1)):
        acc_ref[where] = jnp.zeros_like(acc_ref[where])
    refs = (meta_ref, tiles_ref, ao_ref, kernel_ref, weights_ref, acc_ref)
    for which, width in ((CROSS_MANY, geo.slots), (CROSS_FEW, 2)):
        each_group(
            geo, meta_ref, which, lambda chosen, width=width: add_own(geo, chosen, width, *refs)
        )
    early_out[...] = acc_ref[pl.ds(geo.early_at, geo.early)].astype(early_out.dtype)


def near_kernel(
    geo, meta_ref, halo_ref, tiles_ref, ao_ref, kernel_ref, weights_ref, acc_in, acc_ref, first_out
):
    refs = (meta_ref, tiles_ref, ao_ref, kernel_ref, weights_ref, acc_ref, halo_ref)
    for which, width in ((NEAR_MANY, geo.slots), (NEAR_FEW, 2)):
        each_group(
            geo, meta_ref, which, lambda chosen, width=width: add_whole(geo, chosen, width, *refs)
        )
    first_out[...] = acc_ref[pl.ds(geo.first_at, geo.halo)].astype(first_out.dtype)
    inner_part(geo, meta_ref, 0, refs[:-1])


def waiting_kernel(
    geo, meta_ref, tiles_ref, ao_ref, kernel_ref, weights_ref, acc_in, acc_ref, done_ref
):
    inner_part(geo, meta_ref, 1, (meta_ref, tiles_ref, ao_ref, kernel_ref, weights_ref, acc_ref))
    done_ref[0] = 1


def late_kernel(
    geo, meta_ref, done_ref, halo_ref, ao_ref, kernel_ref, weights_ref, h_ref, late_out, total_ref
):
    nb = ao_ref.shape[2]
    total_ref[...] = jnp.zeros_like(total_ref)

    def work(chosen):
        add_corner(
            geo, chosen, meta_ref, halo_ref, ao_ref, kernel_ref, weights_ref, h_ref, total_ref
        )

    groups = (meta_ref[geo.lengths_at + CROSS] + 1) // LATE_GROUP
    each_group(geo, meta_ref, CROSS, work, size=LATE_GROUP, end=groups)
    each_group(geo, meta_ref, CROSS, work, size=LATE_GROUP // 2, begin=2 * groups)
    for i in range(geo.reach):
        for j in range(geo.reach):
            late_out[i * geo.reach + j] = total_ref[
                i * nb : (i + 1) * nb, j * nb : (j + 1) * nb
            ].astype(late_out.dtype)


def inner_kernel(
    geo, meta_ref, first_ref, tiles_ref, ao_ref, kernel_ref, weights_ref, h_ref, acc_in,
    acc_ref, out_ref, sems,
):
    odd = meta_ref[geo.odd_at] == 1
    refs = (meta_ref, tiles_ref, ao_ref, kernel_ref, weights_ref, acc_ref)
    inner_part(geo, meta_ref, 2, refs)

    def add_near(up, down):
        for start, place, count in geo.packs[0 if up else 1]:
            acc_ref[pl.ds(start, count)] += first_ref[pl.ds(place, count)].astype(jnp.float32)

    by_parity(odd, add_near, True, False)
    done = zone(geo, odd, False)
    copy = pltpu.make_async_copy(acc_ref.at[done], out_ref.at[done], sems.at[0])
    copy.start()
    for which, width in ((CROSS_MANY, geo.slots), (CROSS_FEW, 2)):
        each_group(
            geo,
            meta_ref,
            which,
            lambda chosen, width=width: add_columns(
                geo, chosen, width, meta_ref, ao_ref, h_ref, acc_ref
            ),
        )

    def write_quiet(up, down):
        run_copies(
            [
                pltpu.make_async_copy(
                    acc_ref.at[pl.ds(start, count)], out_ref.at[pl.ds(start, count)], sems.at[1 + i]
                )
                for i, (start, count) in enumerate(geo.quiet[0 if up else 1])
            ]
        )

    by_parity(odd, write_quiet, True, False)
    copy.wait()


def finish_cross(geo, odd, parts, acc_ref, out_ref, total, sems):
    def add(up, down):
        copies = []
        for packs, ref in parts:
            for start, place, count in packs[0 if up else 1]:
                spot = pl.ds(len(copies) * geo.band, count)
                total[spot] = acc_ref[pl.ds(start, count)] + ref[pl.ds(place, count)].astype(
                    jnp.float32
                )
                copy = pltpu.make_async_copy(
                    total.at[spot], out_ref.at[pl.ds(start, count)], sems.at[len(copies)]
                )
                copy.start()
                copies.append(copy)
        for copy in copies:
            copy.wait()

    by_parity(odd, add, False, True)


def has_time(geo, meta_ref):
    left = [bounds[3] - bounds[2] for bounds in inner_share(geo, meta_ref)]
    return waits() & (left[0] + left[1] == 0)


def early_join_kernel(geo, meta_ref, early_ref, acc_ref, out_in, out_ref, total, sems):
    @pl.when(has_time(geo, meta_ref))
    def _():
        odd = meta_ref[geo.odd_at] == 1
        finish_cross(geo, odd, ((geo.early_packs, early_ref),), acc_ref, out_ref, total, sems)


def finish_kernel(geo, meta_ref, late_ref, early_ref, acc_ref, out_in, out_ref, total, sems):
    odd = meta_ref[geo.odd_at] == 1
    late = (geo.late_packs, late_ref)
    joined = has_time(geo, meta_ref)

    @pl.when(joined)
    def _():
        finish_cross(geo, odd, (late,), acc_ref, out_ref, total, sems)

    @pl.when(jnp.logical_not(joined))
    def _():
        parts = ((geo.early_packs, early_ref), late)
        finish_cross(geo, odd, parts, acc_ref, out_ref, total, sems)


def call(kernel, out_shape, in_specs, out_specs, scratch, aliases=None, cost=None):
    return pl.pallas_call(
        kernel,
        out_shape=out_shape,
        in_specs=in_specs,
        out_specs=out_specs,
        scratch_shapes=scratch,
        input_output_aliases=aliases or {},
        cost_estimate=cost,
        compiler_params=pltpu.CompilerParams(vmem_limit_bytes=16 * MIB),
    )


def to_first(x, size):
    pairs = [(i, i + 1) for i in range(0, size - 1, 2)]
    got = lax.ppermute(x, "blk", pairs + [(j, i) for i, j in pairs])
    return pltpu.with_memory_space_constraint(got, pltpu.VMEM)


def to_second(x, size):
    pairs = [(i, i + 1) for i in range(1, size - 1, 2)]
    got = lax.ppermute(x, "blk", pairs + [(j, i) for i, j in pairs])
    return pltpu.with_memory_space_constraint(got, pltpu.VMEM)


def local(density, ao_values, kernel, grid_weights, centre, sig_offsets, counts):
    rows, band, nb, _ = density.shape
    batches, slots, _, pts = ao_values.shape
    size = lax.axis_size("blk")
    geo = Geometry(rows, band, batches, slots)
    in_hbm = lambda x: pltpu.with_memory_space_constraint(x, pltpu.HBM)
    tiles = density.reshape(geo.own, nb, nb)
    pack = lambda count: pltpu.VMEM((count, nb, nb), jnp.bfloat16)
    dma = pltpu.SemaphoreType.DMA
    acc_type = pltpu.VMEM((geo.spare + 1, nb, nb), jnp.float32)

    near_halo, cross_halo, meta, acc = call(
        functools.partial(pack_kernel, geo),
        (pack(geo.halo),) * 2 + (pltpu.SMEM((geo.meta_size,), jnp.int32), acc_type),
        [ANY_SPEC] * 4,
        (VMEM_SPEC,) * 2 + (SMEM_SPEC, VMEM_SPEC),
        [
            pltpu.SMEM((batches,), jnp.int32),
            pltpu.SMEM((slots, batches), jnp.int32),
            pltpu.SMEM((batches,), jnp.int32),
            dma((3, max(geo.reach, 3))),
        ],
        cost=pl.CostEstimate(flops=10**10, bytes_accessed=10**8, transcendentals=0),
    )(in_hbm(tiles), in_hbm(centre), in_hbm(sig_offsets.T), in_hbm(counts))
    cross_halo = to_second(cross_halo, size)
    near_halo = to_first(near_halo, size)

    panel = (tiles, ao_values, kernel, grid_weights)
    acc, early = call(
        functools.partial(early_kernel, geo),
        (acc_type, pack(geo.early)),
        [SMEM_SPEC] + [VMEM_SPEC] * 5,
        (VMEM_SPEC,) * 2,
        [],
        {5: 0},
    )(meta, *panel, acc)
    early = to_second(early, size)

    acc, first = call(
        functools.partial(near_kernel, geo),
        (acc_type, pack(geo.halo)),
        [SMEM_SPEC] + [VMEM_SPEC] * 6,
        (VMEM_SPEC,) * 2,
        [],
        {6: 0},
    )(meta, near_halo, *panel, acc)
    first = to_first(first, size)

    acc, done = call(
        functools.partial(waiting_kernel, geo),
        (acc_type, pltpu.SMEM((1,), jnp.int32)),
        [SMEM_SPEC] + [VMEM_SPEC] * 5,
        (VMEM_SPEC, SMEM_SPEC),
        [],
        {5: 0},
    )(meta, *panel, acc)

    h_type = pltpu.VMEM((batches + 1, geo.reach * nb, pts), jnp.bfloat16)
    h, late = call(
        functools.partial(late_kernel, geo),
        (h_type, pack(geo.late)),
        [SMEM_SPEC] * 2 + [VMEM_SPEC] * 4,
        (VMEM_SPEC,) * 2,
        [pltpu.VMEM((geo.reach * nb, geo.reach * nb), jnp.float32)],
    )(meta, done, cross_halo, *panel[1:])
    late = to_second(late, size)

    whole = jax.ShapeDtypeStruct((geo.own, nb, nb), jnp.float32)
    acc, out = call(
        functools.partial(inner_kernel, geo),
        (acc_type, whole),
        [SMEM_SPEC] + [VMEM_SPEC] * 7,
        (VMEM_SPEC, ANY_SPEC),
        [dma((1 + max(len(runs) for runs in geo.quiet),))],
        {7: 0},
    )(meta, first, *panel, h, acc)

    for kernel_of, got, parts in (
        (early_join_kernel, (early,), geo.reach),
        (finish_kernel, (late, early), 2 * geo.reach),
    ):
        out = call(
            functools.partial(kernel_of, geo),
            whole,
            [SMEM_SPEC] + [VMEM_SPEC] * (len(got) + 1) + [ANY_SPEC],
            ANY_SPEC,
            [pltpu.VMEM((parts * band, nb, nb), jnp.float32), dma((parts,))],
            {len(got) + 2: 0},
        )(meta, *got, acc, out)
    return out.reshape(rows, band, nb, nb)


def solution(mesh):
    placed = (
        P(("groups", "blk"), None, None, None),
        P(("groups", "blk"), None, None, None),
        P(("groups", "blk"), None, None),
        P(("groups", "blk"), None),
        P(("groups", "blk")),
        P(("groups", "blk"), None),
        P(("groups", "blk")),
    )
    return jax.shard_map(
        local,
        mesh=mesh,
        in_specs=placed,
        out_specs=P(("groups", "blk"), None, None, None),
        check_vma=False,
    )
```

```python
import functools

import jax
import jax.numpy as jnp
from jax import lax
from jax.experimental import pallas as pl
from jax.experimental.pallas import tpu as pltpu
from jax.sharding import PartitionSpec as P

MIB = 1 << 20
GROUP = 2
LATE_GROUP = 4
LISTS = 7
BUDGET = 43
WAIT = 18
COST = (10, 7)
SMEM_SPEC = pl.BlockSpec(memory_space=pltpu.SMEM)
VMEM_SPEC = pl.BlockSpec(memory_space=pltpu.VMEM)
ANY_SPEC = pl.BlockSpec(memory_space=pl.ANY)


class Geometry:
    def __init__(self, rows, band, batches, slots):
        self.rows, self.band, self.batches, self.slots = rows, band, batches, slots
        self.half = half = (band - 1) // 2
        self.reach = reach = half // 2
        self.own = rows * band
        low = [(-m, reach + m, band) for m in range(reach, 0, -1)]
        high = [(rows + m, 0, 3 * reach - m) for m in range(reach)]
        self.halo = sum(stop - start for _, start, stop in low)
        low_cut = [half - row for row, _, _ in low]
        high_cut = [rows - row + half for row, _, _ in high]
        early = (
            [(row, cut, stop) for (row, _, stop), cut in zip(low, low_cut)],
            [(row, start, cut) for (row, start, _), cut in zip(high, high_cut)],
        )
        late = (
            [(row, start, cut) for (row, start, _), cut in zip(low, low_cut)],
            [(row, cut, stop) for (row, _, stop), cut in zip(high, high_cut)],
        )
        self.early = sum(stop - start for _, start, stop in early[0])
        self.late = self.halo - self.early
        self.first_at = self.own
        self.early_at = self.own + self.halo
        self.spare = self.early_at + self.early
        self.halo_base = self.bases((low, high))
        self.early_base = self.bases(early)
        shifts = (rows, -rows)
        self.packs = [self.places(*pair) for pair in zip((low, high), shifts)]
        self.early_packs = [self.places(*pair) for pair in zip(early, shifts)]
        self.late_packs = [self.places(*pair) for pair in zip(late, shifts)]
        self.span = min(2 * reach, rows) * band
        self.quiet = [
            self.others(self.packs[1], 0, self.span),
            self.others(self.packs[0], self.own - self.span, self.own),
        ]
        self.list_size = batches + 2
        self.lengths_at = LISTS * self.list_size
        self.local_at = self.lengths_at + LISTS
        self.count_at = self.local_at + batches
        self.offsets_at = self.count_at + batches
        self.odd_at = self.offsets_at + slots * batches
        self.meta_size = self.odd_at + 1

    def bases(self, sides):
        found = {}
        for segments in sides:
            place = 0
            for row, start, stop in segments:
                found[row] = place - start
                place += stop - start
        return found

    def places(self, segments, shift):
        pack, place = ([], 0)
        for row, start, stop in segments:
            pack.append(((row + shift) * self.band + start, place, stop - start))
            place += stop - start
        return pack

    def others(self, pack, begin, end):
        touched = set()
        for start, _, count in pack:
            touched.update(range(start, start + count))
        runs = []
        for index in range(begin, end):
            if index in touched:
                continue
            if runs and sum(runs[-1]) == index:
                runs[-1] = (runs[-1][0], runs[-1][1] + 1)
            else:
                runs.append((index, 1))
        return runs

    def pick(self, bases, shift, row, otherwise):
        value = otherwise
        for at, base in bases.items():
            value = jnp.where(row == at, base + shift, value)
        return value


def run_copies(copies):
    for copy in copies:
        copy.start()
    for copy in copies:
        copy.wait()


def by_parity(odd, body, first, second):
    @pl.when(jnp.logical_not(odd))
    def _():
        body(first, second)

    @pl.when(odd)
    def _():
        body(second, first)


CROSS_MANY, CROSS_FEW, NEAR_MANY, NEAR_FEW, INNER_MANY, INNER_FEW, CROSS = range(LISTS)


def build_lists(geo, index, centre_ref, offsets_ref, counts_ref, meta_ref):
    first = index * geo.rows
    odd = index % 2 == 1
    meta_ref[geo.odd_at] = odd.astype(jnp.int32)
    lengths = [jnp.int32(0)] * LISTS
    for b in range(geo.batches):
        local = centre_ref[b] - first
        count = counts_ref[b]
        meta_ref[geo.local_at + b] = local
        meta_ref[geo.count_at + b] = count
        low = high = jnp.bool_(False)
        for k in range(geo.slots):
            offset = offsets_ref[k, b]
            meta_ref[geo.offsets_at + k * geo.batches + b] = offset
            row = local + offset
            low = low | ((k < count) & (row < 0))
            high = high | ((k < count) & (row >= geo.rows))
        cross = (odd & high) | (jnp.logical_not(odd) & low)
        near = (odd & low) | (jnp.logical_not(odd) & high)
        inner = jnp.logical_not(low | high)
        many = count > 2
        few = (count > 0) & jnp.logical_not(many)
        kinds = [kind & size for kind in (cross, near, inner) for size in (many, few)]
        for which, member in enumerate(kinds + [cross]):
            meta_ref[which * geo.list_size + lengths[which]] = b
            lengths[which] = lengths[which] + member.astype(jnp.int32)
    for which in range(LISTS):
        meta_ref[which * geo.list_size + lengths[which]] = geo.batches
        meta_ref[geo.lengths_at + which] = lengths[which]


def zone(geo, odd, cross):
    span = geo.span if cross else geo.own - geo.span
    return pl.ds(jnp.where(odd == cross, geo.own - span, 0), span)


def pack_kernel(
    geo, density_ref, centre_in, offsets_in, counts_in,
    near_ref, cross_ref, meta_ref, acc_ref,
    centre_ref, offsets_ref, counts_ref, sems,
):
    index = lax.axis_index("blk")
    odd = index % 2 == 1

    by_size = lambda pack: sorted(pack, key=lambda segment: segment[2])
    copies = []
    for side, (ref, upper) in enumerate(((cross_ref, odd), (near_ref, jnp.logical_not(odd)))):
        for i, (up, down) in enumerate(zip(*(by_size(pack) for pack in geo.packs))):
            start = jnp.where(upper, up[0], down[0])
            place = jnp.where(upper, up[1], down[1])
            copies.append(
                pltpu.make_async_copy(
                    density_ref.at[pl.ds(start, up[2])], ref.at[pl.ds(place, up[2])], sems.at[side, i]
                )
            )
    for copy in copies:
        copy.start()
    scalars = [
        pltpu.make_async_copy(*pair, sems.at[2, i])
        for i, pair in enumerate(
            ((centre_in, centre_ref), (offsets_in, offsets_ref), (counts_in, counts_ref))
        )
    ]
    for copy in scalars:
        copy.start()
    for where in (zone(geo, odd, False), pl.ds(geo.first_at, geo.halo)):
        acc_ref[where] = jnp.zeros_like(acc_ref[where])
    for copy in scalars:
        copy.wait()
    build_lists(geo, index, centre_ref, offsets_ref, counts_ref, meta_ref)
    for copy in copies:
        copy.wait()


def group_count(geo, meta_ref, which):
    return (meta_ref[geo.lengths_at + which] + GROUP - 1) // GROUP


def waits():
    return (lax.axis_index("blk") + 1) // 2 % 2 == 1


def inner_share(geo, meta_ref):
    before = BUDGET
    for which in (CROSS_MANY, CROSS_FEW, NEAR_MANY, NEAR_FEW):
        before = before - COST[which % 2] * group_count(geo, meta_ref, which)
    rounds = (meta_ref[geo.lengths_at + CROSS] + LATE_GROUP - 1) // LATE_GROUP
    waiting = jnp.where(waits(), WAIT - COST[0] * jnp.maximum(rounds - 1, 0), 0)
    share = []
    for which in (INNER_MANY, INNER_FEW):
        cost, count = COST[which % 2], group_count(geo, meta_ref, which)
        first = jnp.minimum(jnp.maximum(before, 0) // cost, count)
        second = jnp.minimum(jnp.maximum(waiting, 0) // cost, count - first)
        before = before - cost * first
        waiting = waiting - cost * second
        share.append((0, first, first + second, count))
    return share


def inner_part(geo, meta_ref, stage, refs):
    for which, width, bounds in zip(
        (INNER_MANY, INNER_FEW), (geo.slots, 2), inner_share(geo, meta_ref)
    ):
        each_group(
            geo,
            meta_ref,
            which,
            lambda chosen, width=width: add_whole(geo, chosen, width, *refs),
            begin=bounds[stage],
            end=bounds[stage + 1],
        )


def each_group(geo, meta_ref, which, body, size=GROUP, begin=0, end=None):
    length = meta_ref[geo.lengths_at + which]

    def step(i, carry):
        chosen = []
        for n in range(size):
            place = i * size + n
            there = place < length
            b = meta_ref[which * geo.list_size + jnp.minimum(place, length)]
            chosen.append((jnp.where(there, b, 0), there))
        body(chosen)
        return carry

    lax.fori_loop(begin, (length + size - 1) // size if end is None else end, step, 0)


class Slots:
    def __init__(self, geo, meta_ref, b, there, width):
        local = meta_ref[geo.local_at + b]
        count = jnp.where(there, meta_ref[geo.count_at + b], 0)
        self.offset = [meta_ref[geo.offsets_at + k * geo.batches + b] for k in range(width)]
        self.local = local
        self.row = [local + offset for offset in self.offset]
        self.live = [k < count for k in range(width)]
        self.own = [(row >= 0) & (row < geo.rows) for row in self.row]
        self.width = width


def panels(slots, ao_ref, b):
    return jnp.concatenate(
        [
            ao_ref[b, k] * jnp.where(slots.live[k], 1.0, 0.0).astype(ao_ref.dtype)
            for k in range(slots.width)
        ],
        axis=0,
    )


def gathered(tiles_ref, places):
    return jnp.concatenate(
        [jnp.concatenate([tiles_ref[place] for place in row], axis=1) for row in places], axis=0
    )


def potentials(xs, tiles, batches, kernel_ref):
    fs = [
        jnp.dot(t, x, preferred_element_type=jnp.float32).astype(jnp.bfloat16)
        for t, x in zip(tiles, xs)
    ]
    return [
        jnp.dot(f, kernel_ref[b], preferred_element_type=jnp.float32) for f, b in zip(fs, batches)
    ]


def outer_product(x, h):
    return lax.dot_general(x, h, (((1,), (1,)), ((), ())), preferred_element_type=jnp.float32)


def chain(xs, tiles, batches, kernel_ref, weights_ref):
    gs = potentials(xs, tiles, batches, kernel_ref)
    hs = [(g * weights_ref[pl.ds(b, 1), :]).astype(jnp.bfloat16) for g, b in zip(gs, batches)]
    return [outer_product(x, h) for x, h in zip(xs, hs)]


def scatter(part, target, nb, acc_ref):
    for k, row in enumerate(target):
        for j, place in enumerate(row):
            acc_ref[place] += part[k * nb : (k + 1) * nb, j * nb : (j + 1) * nb]


def add_whole(
    geo, chosen, width, meta_ref, tiles_ref, ao_ref, kernel_ref, weights_ref, acc_ref, halo_ref=None
):
    xs, tiles, targets = ([], [], [])
    for b, there in chosen:
        slots = Slots(geo, meta_ref, b, there, width)
        xs.append(panels(slots, ao_ref, b))
        rows, target = ([], [])
        for k in range(width):
            band = [slots.offset[j] - slots.offset[k] + geo.half for j in range(width)]
            own = slots.own[k]
            base = jnp.where(slots.live[k] & own, slots.row[k], 0) * geo.band
            row = jnp.concatenate([tiles_ref[base + o] for o in band], axis=1)
            if halo_ref is not None:
                away = slots.live[k] & jnp.logical_not(own)
                outside = jnp.where(away, geo.pick(geo.halo_base, 0, slots.row[k], 0), 0)
                other = [halo_ref[jnp.where(away, outside + o, 0)] for o in band]
                row = jnp.where(away, jnp.concatenate(other, axis=1), row)
                base = jnp.where(away, outside + geo.first_at, base)
            rows.append(row)
            target.append(
                [
                    jnp.where(slots.live[k] & slots.live[j], base + band[j], geo.spare)
                    for j in range(width)
                ]
            )
        tiles.append(jnp.concatenate(rows, axis=0))
        targets.append(target)
    parts = chain(xs, tiles, [b for b, _ in chosen], kernel_ref, weights_ref)
    for part, target in zip(parts, targets):
        scatter(part, target, ao_ref.shape[2], acc_ref)


def add_own(geo, chosen, width, meta_ref, tiles_ref, ao_ref, kernel_ref, weights_ref, acc_ref):
    xs, tiles, targets = ([], [], [])
    for b, there in chosen:
        slots = Slots(geo, meta_ref, b, there, width)
        xs.append(panels(slots, ao_ref, b))
        places, target = ([], [])
        for k in range(width):
            row = slots.row[k]
            band = [slots.offset[j] - slots.offset[k] + geo.half for j in range(width)]
            base = jnp.where(slots.own[k], row, 0) * geo.band
            places.append([base + o for o in band])
            base = geo.pick(geo.early_base, geo.early_at, row, base)
            target.append(
                [
                    jnp.where(
                        slots.live[k] & slots.live[j] & slots.own[j], base + band[j], geo.spare
                    )
                    for j in range(width)
                ]
            )
        tiles.append(gathered(tiles_ref, places))
        targets.append(target)
    parts = chain(xs, tiles, [b for b, _ in chosen], kernel_ref, weights_ref)
    for part, target in zip(parts, targets):
        scatter(part, target, ao_ref.shape[2], acc_ref)


def halo_rows(geo, meta_ref, slots):
    odd = meta_ref[geo.odd_at] == 1
    rows, places, present = ([], [], [])
    for i in range(geo.reach):
        row = jnp.where(odd, geo.rows + i, i - geo.reach)
        place, found = (jnp.int32(0), jnp.bool_(False))
        for k in range(slots.width):
            hit = slots.live[k] & (slots.row[k] == row)
            place = jnp.where(hit, k, place)
            found = found | hit
        rows.append(row)
        places.append(place)
        present.append(found)
    return rows, places, present


def add_corner(geo, chosen, meta_ref, halo_ref, ao_ref, kernel_ref, weights_ref, h_ref, total_ref):
    nb = ao_ref.shape[2]
    factor = lambda flag: jnp.where(flag, 1.0, 0.0)
    xs, sides, tiles, masks = ([], [], [], [])
    for b, there in chosen:
        slots = Slots(geo, meta_ref, b, there, geo.slots)
        rows, places, present = halo_rows(geo, meta_ref, slots)
        xs.append(panels(slots, ao_ref, b))
        sides.append(
            jnp.concatenate(
                [
                    ao_ref[b, place] * factor(found).astype(ao_ref.dtype)
                    for place, found in zip(places, present)
                ],
                axis=0,
            )
        )
        picked = []
        for row, found in zip(rows, present):
            base = geo.pick(geo.halo_base, 0, row, 0) - row + geo.half
            picked.append([jnp.where(found, base + column, 0) for column in slots.row])
        tiles.append(gathered(halo_ref, picked))
        masks.append([factor(found) for found in present])
    gs = potentials(xs, tiles, [b for b, _ in chosen], kernel_ref)
    hs = []
    for g, mask, (b, there) in zip(gs, masks, chosen):
        weights = weights_ref[pl.ds(b, 1), :]
        h = jnp.concatenate(
            [g[i * nb : (i + 1) * nb] * (weights * mask[i]) for i in range(geo.reach)], axis=0
        ).astype(jnp.bfloat16)
        h_ref[jnp.where(there, b, geo.batches)] = h
        hs.append(h)
    total_ref[...] += outer_product(
        jnp.concatenate(sides, axis=1), jnp.concatenate(hs, axis=1)
    )


def add_columns(geo, chosen, width, meta_ref, ao_ref, h_ref, acc_ref):
    parts, targets = ([], [])
    for b, there in chosen:
        slots = Slots(geo, meta_ref, b, there, width)
        rows, _, present = halo_rows(geo, meta_ref, slots)
        parts.append(outer_product(ao_ref[b, pl.ds(0, width)].reshape(-1, ao_ref.shape[3]), h_ref[b]))
        targets.append(
            [
                [
                    jnp.where(
                        slots.live[k] & slots.own[k] & found,
                        slots.row[k] * geo.band + row - slots.row[k] + geo.half,
                        geo.spare,
                    )
                    for row, found in zip(rows, present)
                ]
                for k in range(width)
            ]
        )
    for part, target in zip(parts, targets):
        scatter(part, target, ao_ref.shape[2], acc_ref)


def early_kernel(
    geo, meta_ref, tiles_ref, ao_ref, kernel_ref, weights_ref, acc_in, acc_ref, early_out
):
    odd = meta_ref[geo.odd_at] == 1
    for where in (zone(geo, odd, True), pl.ds(geo.early_at, geo.early), pl.ds(geo.spare, 1)):
        acc_ref[where] = jnp.zeros_like(acc_ref[where])
    refs = (meta_ref, tiles_ref, ao_ref, kernel_ref, weights_ref, acc_ref)
    for which, width in ((CROSS_MANY, geo.slots), (CROSS_FEW, 2)):
        each_group(
            geo, meta_ref, which, lambda chosen, width=width: add_own(geo, chosen, width, *refs)
        )
    early_out[...] = acc_ref[pl.ds(geo.early_at, geo.early)].astype(early_out.dtype)


def near_kernel(
    geo, meta_ref, halo_ref, tiles_ref, ao_ref, kernel_ref, weights_ref, acc_in, acc_ref, first_out
):
    refs = (meta_ref, tiles_ref, ao_ref, kernel_ref, weights_ref, acc_ref, halo_ref)
    for which, width in ((NEAR_MANY, geo.slots), (NEAR_FEW, 2)):
        each_group(
            geo, meta_ref, which, lambda chosen, width=width: add_whole(geo, chosen, width, *refs)
        )
    first_out[...] = acc_ref[pl.ds(geo.first_at, geo.halo)].astype(first_out.dtype)
    inner_part(geo, meta_ref, 0, refs[:-1])


def waiting_kernel(
    geo, meta_ref, tiles_ref, ao_ref, kernel_ref, weights_ref, acc_in, acc_ref, done_ref
):
    inner_part(geo, meta_ref, 1, (meta_ref, tiles_ref, ao_ref, kernel_ref, weights_ref, acc_ref))
    done_ref[0] = 1


def late_kernel(
    geo, meta_ref, done_ref, halo_ref, ao_ref, kernel_ref, weights_ref, h_ref, late_out, total_ref
):
    nb = ao_ref.shape[2]
    total_ref[...] = jnp.zeros_like(total_ref)

    def work(chosen):
        add_corner(
            geo, chosen, meta_ref, halo_ref, ao_ref, kernel_ref, weights_ref, h_ref, total_ref
        )

    groups = (meta_ref[geo.lengths_at + CROSS] + 1) // LATE_GROUP
    each_group(geo, meta_ref, CROSS, work, size=LATE_GROUP, end=groups)
    each_group(geo, meta_ref, CROSS, work, size=LATE_GROUP // 2, begin=2 * groups)
    for i in range(geo.reach):
        for j in range(geo.reach):
            late_out[i * geo.reach + j] = total_ref[
                i * nb : (i + 1) * nb, j * nb : (j + 1) * nb
            ].astype(late_out.dtype)


def inner_kernel(
    geo, meta_ref, first_ref, tiles_ref, ao_ref, kernel_ref, weights_ref, h_ref, acc_in,
    acc_ref, out_ref, sems,
):
    odd = meta_ref[geo.odd_at] == 1
    refs = (meta_ref, tiles_ref, ao_ref, kernel_ref, weights_ref, acc_ref)
    inner_part(geo, meta_ref, 2, refs)

    def add_near(up, down):
        for start, place, count in geo.packs[0 if up else 1]:
            acc_ref[pl.ds(start, count)] += first_ref[pl.ds(place, count)].astype(jnp.float32)

    by_parity(odd, add_near, True, False)
    done = zone(geo, odd, False)
    copy = pltpu.make_async_copy(acc_ref.at[done], out_ref.at[done], sems.at[0])
    copy.start()
    for which, width in ((CROSS_MANY, geo.slots), (CROSS_FEW, 2)):
        each_group(
            geo,
            meta_ref,
            which,
            lambda chosen, width=width: add_columns(
                geo, chosen, width, meta_ref, ao_ref, h_ref, acc_ref
            ),
        )

    def write_quiet(up, down):
        run_copies(
            [
                pltpu.make_async_copy(
                    acc_ref.at[pl.ds(start, count)], out_ref.at[pl.ds(start, count)], sems.at[1 + i]
                )
                for i, (start, count) in enumerate(geo.quiet[0 if up else 1])
            ]
        )

    by_parity(odd, write_quiet, True, False)
    copy.wait()


def finish_cross(geo, odd, parts, acc_ref, out_ref, total, sems):
    def add(up, down):
        copies = []
        for packs, ref in parts:
            for start, place, count in packs[0 if up else 1]:
                spot = pl.ds(len(copies) * geo.band, count)
                total[spot] = acc_ref[pl.ds(start, count)] + ref[pl.ds(place, count)].astype(
                    jnp.float32
                )
                copy = pltpu.make_async_copy(
                    total.at[spot], out_ref.at[pl.ds(start, count)], sems.at[len(copies)]
                )
                copy.start()
                copies.append(copy)
        for copy in copies:
            copy.wait()

    by_parity(odd, add, False, True)


def has_time(geo, meta_ref):
    left = [bounds[3] - bounds[2] for bounds in inner_share(geo, meta_ref)]
    return waits() & (left[0] + left[1] == 0)


def early_join_kernel(geo, meta_ref, early_ref, acc_ref, out_in, out_ref, total, sems):
    @pl.when(has_time(geo, meta_ref))
    def _():
        odd = meta_ref[geo.odd_at] == 1
        finish_cross(geo, odd, ((geo.early_packs, early_ref),), acc_ref, out_ref, total, sems)


def finish_kernel(geo, meta_ref, late_ref, early_ref, acc_ref, out_in, out_ref, total, sems):
    odd = meta_ref[geo.odd_at] == 1
    late = (geo.late_packs, late_ref)
    joined = has_time(geo, meta_ref)

    @pl.when(joined)
    def _():
        finish_cross(geo, odd, (late,), acc_ref, out_ref, total, sems)

    @pl.when(jnp.logical_not(joined))
    def _():
        parts = ((geo.early_packs, early_ref), late)
        finish_cross(geo, odd, parts, acc_ref, out_ref, total, sems)


def call(kernel, out_shape, in_specs, out_specs, scratch, aliases=None, cost=None):
    return pl.pallas_call(
        kernel,
        out_shape=out_shape,
        in_specs=in_specs,
        out_specs=out_specs,
        scratch_shapes=scratch,
        input_output_aliases=aliases or {},
        cost_estimate=cost,
        compiler_params=pltpu.CompilerParams(vmem_limit_bytes=16 * MIB),
    )


def to_first(x, size):
    pairs = [(i, i + 1) for i in range(0, size - 1, 2)]
    got = lax.ppermute(x, "blk", pairs + [(j, i) for i, j in pairs])
    return pltpu.with_memory_space_constraint(got, pltpu.VMEM)


def to_second(x, size):
    pairs = [(i, i + 1) for i in range(1, size - 1, 2)]
    got = lax.ppermute(x, "blk", pairs + [(j, i) for i, j in pairs])
    return pltpu.with_memory_space_constraint(got, pltpu.VMEM)


def local(density, ao_values, kernel, grid_weights, centre, sig_offsets, counts):
    rows, band, nb, _ = density.shape
    batches, slots, _, pts = ao_values.shape
    size = lax.axis_size("blk")
    geo = Geometry(rows, band, batches, slots)
    in_hbm = lambda x: pltpu.with_memory_space_constraint(x, pltpu.HBM)
    tiles = density.reshape(geo.own, nb, nb)
    pack = lambda count: pltpu.VMEM((count, nb, nb), jnp.bfloat16)
    dma = pltpu.SemaphoreType.DMA
    acc_type = pltpu.VMEM((geo.spare + 1, nb, nb), jnp.float32)

    near_halo, cross_halo, meta, acc = call(
        functools.partial(pack_kernel, geo),
        (pack(geo.halo),) * 2 + (pltpu.SMEM((geo.meta_size,), jnp.int32), acc_type),
        [ANY_SPEC] * 4,
        (VMEM_SPEC,) * 2 + (SMEM_SPEC, VMEM_SPEC),
        [
            pltpu.SMEM((batches,), jnp.int32),
            pltpu.SMEM((slots, batches), jnp.int32),
            pltpu.SMEM((batches,), jnp.int32),
            dma((3, max(geo.reach, 3))),
        ],
        cost=pl.CostEstimate(flops=10**10, bytes_accessed=10**8, transcendentals=0),
    )(in_hbm(tiles), in_hbm(centre), in_hbm(sig_offsets.T), in_hbm(counts))
    cross_halo = to_second(cross_halo, size)
    near_halo = to_first(near_halo, size)

    panel = (tiles, ao_values, kernel, grid_weights)
    acc, early = call(
        functools.partial(early_kernel, geo),
        (acc_type, pack(geo.early)),
        [SMEM_SPEC] + [VMEM_SPEC] * 5,
        (VMEM_SPEC,) * 2,
        [],
        {5: 0},
    )(meta, *panel, acc)
    early = to_second(early, size)

    acc, first = call(
        functools.partial(near_kernel, geo),
        (acc_type, pack(geo.halo)),
        [SMEM_SPEC] + [VMEM_SPEC] * 6,
        (VMEM_SPEC,) * 2,
        [],
        {6: 0},
    )(meta, near_halo, *panel, acc)
    first = to_first(first, size)

    acc, done = call(
        functools.partial(waiting_kernel, geo),
        (acc_type, pltpu.SMEM((1,), jnp.int32)),
        [SMEM_SPEC] + [VMEM_SPEC] * 5,
        (VMEM_SPEC, SMEM_SPEC),
        [],
        {5: 0},
    )(meta, *panel, acc)

    h_type = pltpu.VMEM((batches + 1, geo.reach * nb, pts), jnp.bfloat16)
    h, late = call(
        functools.partial(late_kernel, geo),
        (h_type, pack(geo.late)),
        [SMEM_SPEC] * 2 + [VMEM_SPEC] * 4,
        (VMEM_SPEC,) * 2,
        [pltpu.VMEM((geo.reach * nb, geo.reach * nb), jnp.float32)],
    )(meta, done, cross_halo, *panel[1:])
    late = to_second(late, size)

    whole = jax.ShapeDtypeStruct((geo.own, nb, nb), jnp.float32)
    acc, out = call(
        functools.partial(inner_kernel, geo),
        (acc_type, whole),
        [SMEM_SPEC] + [VMEM_SPEC] * 7,
        (VMEM_SPEC, ANY_SPEC),
        [dma((1 + max(len(runs) for runs in geo.quiet),))],
        {7: 0},
    )(meta, first, *panel, h, acc)

    for kernel_of, got, parts in (
        (early_join_kernel, (early,), geo.reach),
        (finish_kernel, (late, early), 2 * geo.reach),
    ):
        out = call(
            functools.partial(kernel_of, geo),
            whole,
            [SMEM_SPEC] + [VMEM_SPEC] * (len(got) + 1) + [ANY_SPEC],
            ANY_SPEC,
            [pltpu.VMEM((parts * band, nb, nb), jnp.float32), dma((parts,))],
            {len(got) + 2: 0},
        )(meta, *got, acc, out)
    return out.reshape(rows, band, nb, nb)


def solution(mesh):
    placed = (
        P(("groups", "blk"), None, None, None),
        P(("groups", "blk"), None, None, None),
        P(("groups", "blk"), None, None),
        P(("groups", "blk"), None),
        P(("groups", "blk")),
        P(("groups", "blk"), None),
        P(("groups", "blk")),
    )
    return jax.shard_map(
        local,
        mesh=mesh,
        in_specs=placed,
        out_specs=P(("groups", "blk"), None, None, None),
        check_vma=False,
    )
```

```python
import functools

import jax
import jax.numpy as jnp
from jax import lax
from jax.experimental import pallas as pl
from jax.experimental.pallas import tpu as pltpu
from jax.sharding import PartitionSpec as P

MIB = 1 << 20
GROUP = 2
LATE_GROUP = 4
LISTS = 7
BUDGET = 41
WAIT = 18
COST = (10, 7)
SMEM_SPEC = pl.BlockSpec(memory_space=pltpu.SMEM)
VMEM_SPEC = pl.BlockSpec(memory_space=pltpu.VMEM)
ANY_SPEC = pl.BlockSpec(memory_space=pl.ANY)


class Geometry:
    def __init__(self, rows, band, batches, slots):
        self.rows, self.band, self.batches, self.slots = rows, band, batches, slots
        self.half = half = (band - 1) // 2
        self.reach = reach = half // 2
        self.own = rows * band
        low = [(-m, reach + m, band) for m in range(reach, 0, -1)]
        high = [(rows + m, 0, 3 * reach - m) for m in range(reach)]
        self.halo = sum(stop - start for _, start, stop in low)
        low_cut = [half - row for row, _, _ in low]
        high_cut = [rows - row + half for row, _, _ in high]
        early = (
            [(row, cut, stop) for (row, _, stop), cut in zip(low, low_cut)],
            [(row, start, cut) for (row, start, _), cut in zip(high, high_cut)],
        )
        late = (
            [(row, start, cut) for (row, start, _), cut in zip(low, low_cut)],
            [(row, cut, stop) for (row, _, stop), cut in zip(high, high_cut)],
        )
        self.early = sum(stop - start for _, start, stop in early[0])
        self.late = self.halo - self.early
        self.first_at = self.own
        self.early_at = self.own + self.halo
        self.spare = self.early_at + self.early
        cut = 6
        self.pieces = ((0, cut), (cut, self.halo - cut))
        self.halo_base = self.bases((low, high))
        self.early_base = self.bases(early)
        shifts = (rows, -rows)
        self.packs = [self.places(*pair) for pair in zip((low, high), shifts)]
        self.early_packs = [self.places(*pair) for pair in zip(early, shifts)]
        self.late_packs = [self.places(*pair) for pair in zip(late, shifts)]
        self.span = min(2 * reach, rows) * band
        self.quiet = [
            self.others(self.packs[1], 0, self.span),
            self.others(self.packs[0], self.own - self.span, self.own),
        ]
        self.list_size = batches + 2
        self.lengths_at = LISTS * self.list_size
        self.local_at = self.lengths_at + LISTS
        self.count_at = self.local_at + batches
        self.offsets_at = self.count_at + batches
        self.odd_at = self.offsets_at + slots * batches
        self.meta_size = self.odd_at + 1

    def bases(self, sides):
        found = {}
        for segments in sides:
            place = 0
            for row, start, stop in segments:
                found[row] = place - start
                place += stop - start
        return found

    def places(self, segments, shift):
        pack, place = ([], 0)
        for row, start, stop in segments:
            pack.append(((row + shift) * self.band + start, place, stop - start))
            place += stop - start
        return pack

    def others(self, pack, begin, end):
        touched = set()
        for start, _, count in pack:
            touched.update(range(start, start + count))
        runs = []
        for index in range(begin, end):
            if index in touched:
                continue
            if runs and sum(runs[-1]) == index:
                runs[-1] = (runs[-1][0], runs[-1][1] + 1)
            else:
                runs.append((index, 1))
        return runs

    def near_packs(self, piece):
        begin, count = self.pieces[piece]
        found = []
        for pack in self.packs:
            part = []
            for start, place, size in pack:
                low, high = max(place, begin), min(place + size, begin + count)
                if low < high:
                    part.append((start + low - place, low - begin, high - low))
            found.append(part)
        return found

    def pick(self, bases, shift, row, otherwise):
        value = otherwise
        for at, base in bases.items():
            value = jnp.where(row == at, base + shift, value)
        return value


def run_copies(copies):
    for copy in copies:
        copy.start()
    for copy in copies:
        copy.wait()


def by_parity(odd, body, first, second):
    @pl.when(jnp.logical_not(odd))
    def _():
        body(first, second)

    @pl.when(odd)
    def _():
        body(second, first)


CROSS_MANY, CROSS_FEW, NEAR_MANY, NEAR_FEW, INNER_MANY, INNER_FEW, CROSS = range(LISTS)


def build_lists(geo, index, centre_ref, offsets_ref, counts_ref, meta_ref):
    first = index * geo.rows
    odd = index % 2 == 1
    meta_ref[geo.odd_at] = odd.astype(jnp.int32)
    lengths = [jnp.int32(0)] * LISTS
    for b in range(geo.batches):
        local = centre_ref[b] - first
        count = counts_ref[b]
        meta_ref[geo.local_at + b] = local
        meta_ref[geo.count_at + b] = count
        low = high = jnp.bool_(False)
        for k in range(geo.slots):
            offset = offsets_ref[k, b]
            meta_ref[geo.offsets_at + k * geo.batches + b] = offset
            row = local + offset
            low = low | ((k < count) & (row < 0))
            high = high | ((k < count) & (row >= geo.rows))
        cross = (odd & high) | (jnp.logical_not(odd) & low)
        near = (odd & low) | (jnp.logical_not(odd) & high)
        inner = jnp.logical_not(low | high)
        many = count > 2
        few = (count > 0) & jnp.logical_not(many)
        kinds = [kind & size for kind in (cross, near, inner) for size in (many, few)]
        for which, member in enumerate(kinds + [cross]):
            meta_ref[which * geo.list_size + lengths[which]] = b
            lengths[which] = lengths[which] + member.astype(jnp.int32)
    for which in range(LISTS):
        meta_ref[which * geo.list_size + lengths[which]] = geo.batches
        meta_ref[geo.lengths_at + which] = lengths[which]


def zone(geo, odd, cross):
    span = geo.span if cross else geo.own - geo.span
    return pl.ds(jnp.where(odd == cross, geo.own - span, 0), span)


def pack_kernel(
    geo, density_ref, centre_in, offsets_in, counts_in,
    near_a, near_b, cross_ref, meta_ref, acc_ref,
    centre_ref, offsets_ref, counts_ref, sems,
):
    index = lax.axis_index("blk")
    odd = index % 2 == 1

    def copies(up, down):
        near = 0 if up else 1
        parts = [(cross_ref, geo.packs[1 - near])]
        parts += [(ref, geo.near_packs(i)[near]) for i, ref in enumerate((near_a, near_b))]
        return [
            pltpu.make_async_copy(
                density_ref.at[pl.ds(start, count)], ref.at[pl.ds(place, count)], sems.at[side, i]
            )
            for side, (ref, pack) in enumerate(parts)
            for i, (start, place, count) in enumerate(pack)
        ]

    def act(up, down, what):
        for copy in copies(up, down):
            what(copy)

    by_parity(odd, lambda up, down: act(up, down, lambda c: c.start()), True, False)
    scalars = [
        pltpu.make_async_copy(*pair, sems.at[3, i])
        for i, pair in enumerate(
            ((centre_in, centre_ref), (offsets_in, offsets_ref), (counts_in, counts_ref))
        )
    ]
    for copy in scalars:
        copy.start()
    for where in (zone(geo, odd, False), pl.ds(geo.first_at, geo.halo)):
        acc_ref[where] = jnp.zeros_like(acc_ref[where])
    for copy in scalars:
        copy.wait()
    build_lists(geo, index, centre_ref, offsets_ref, counts_ref, meta_ref)
    by_parity(odd, lambda up, down: act(up, down, lambda c: c.wait()), True, False)


def group_count(geo, meta_ref, which):
    return (meta_ref[geo.lengths_at + which] + GROUP - 1) // GROUP


def waits():
    return (lax.axis_index("blk") + 1) // 2 % 2 == 1


def inner_share(geo, meta_ref):
    before = BUDGET
    for which in (CROSS_MANY, CROSS_FEW, NEAR_MANY, NEAR_FEW):
        before = before - COST[which % 2] * group_count(geo, meta_ref, which)
    rounds = (meta_ref[geo.lengths_at + CROSS] + LATE_GROUP - 1) // LATE_GROUP
    waiting = jnp.where(waits(), WAIT - COST[0] * jnp.maximum(rounds - 1, 0), 0)
    share = []
    for which in (INNER_MANY, INNER_FEW):
        cost, count = COST[which % 2], group_count(geo, meta_ref, which)
        first = jnp.minimum(jnp.maximum(before, 0) // cost, count)
        second = jnp.minimum(jnp.maximum(waiting, 0) // cost, count - first)
        before = before - cost * first
        waiting = waiting - cost * second
        share.append((0, first, first + second, count))
    return share


def inner_part(geo, meta_ref, stage, refs):
    for which, width, bounds in zip(
        (INNER_MANY, INNER_FEW), (geo.slots, 2), inner_share(geo, meta_ref)
    ):
        each_group(
            geo,
            meta_ref,
            which,
            lambda chosen, width=width: add_whole(geo, chosen, width, *refs),
            begin=bounds[stage],
            end=bounds[stage + 1],
        )


def each_group(geo, meta_ref, which, body, size=GROUP, begin=0, end=None):
    length = meta_ref[geo.lengths_at + which]

    def step(i, carry):
        chosen = []
        for n in range(size):
            place = i * size + n
            there = place < length
            b = meta_ref[which * geo.list_size + jnp.minimum(place, length)]
            chosen.append((jnp.where(there, b, 0), there))
        body(chosen)
        return carry

    lax.fori_loop(begin, (length + size - 1) // size if end is None else end, step, 0)


class Slots:
    def __init__(self, geo, meta_ref, b, there, width):
        local = meta_ref[geo.local_at + b]
        count = jnp.where(there, meta_ref[geo.count_at + b], 0)
        self.offset = [meta_ref[geo.offsets_at + k * geo.batches + b] for k in range(width)]
        self.local = local
        self.row = [local + offset for offset in self.offset]
        self.live = [k < count for k in range(width)]
        self.own = [(row >= 0) & (row < geo.rows) for row in self.row]
        self.width = width


def panels(slots, ao_ref, b):
    return jnp.concatenate(
        [
            ao_ref[b, k] * jnp.where(slots.live[k], 1.0, 0.0).astype(ao_ref.dtype)
            for k in range(slots.width)
        ],
        axis=0,
    )


def gathered(tiles_ref, places):
    return jnp.concatenate(
        [jnp.concatenate([tiles_ref[place] for place in row], axis=1) for row in places], axis=0
    )


def potentials(xs, tiles, batches, kernel_ref):
    fs = [
        jnp.dot(t, x, preferred_element_type=jnp.float32).astype(jnp.bfloat16)
        for t, x in zip(tiles, xs)
    ]
    return [
        jnp.dot(f, kernel_ref[b], preferred_element_type=jnp.float32) for f, b in zip(fs, batches)
    ]


def outer_product(x, h):
    return lax.dot_general(x, h, (((1,), (1,)), ((), ())), preferred_element_type=jnp.float32)


def chain(xs, tiles, batches, kernel_ref, weights_ref):
    gs = potentials(xs, tiles, batches, kernel_ref)
    hs = [(g * weights_ref[pl.ds(b, 1), :]).astype(jnp.bfloat16) for g, b in zip(gs, batches)]
    return [outer_product(x, h) for x, h in zip(xs, hs)]


def scatter(part, target, nb, acc_ref):
    for k, row in enumerate(target):
        for j, place in enumerate(row):
            acc_ref[place] += part[k * nb : (k + 1) * nb, j * nb : (j + 1) * nb]


def add_whole(
    geo, chosen, width, meta_ref, tiles_ref, ao_ref, kernel_ref, weights_ref, acc_ref, halo_ref=None
):
    xs, tiles, targets = ([], [], [])
    for b, there in chosen:
        slots = Slots(geo, meta_ref, b, there, width)
        xs.append(panels(slots, ao_ref, b))
        rows, target = ([], [])
        for k in range(width):
            band = [slots.offset[j] - slots.offset[k] + geo.half for j in range(width)]
            own = slots.own[k]
            base = jnp.where(slots.live[k] & own, slots.row[k], 0) * geo.band
            row = jnp.concatenate([tiles_ref[base + o] for o in band], axis=1)
            if halo_ref is not None:
                away = slots.live[k] & jnp.logical_not(own)
                outside = jnp.where(away, geo.pick(geo.halo_base, 0, slots.row[k], 0), 0)
                other = [halo_ref[jnp.where(away, outside + o, 0)] for o in band]
                row = jnp.where(away, jnp.concatenate(other, axis=1), row)
                base = jnp.where(away, outside + geo.first_at, base)
            rows.append(row)
            target.append(
                [
                    jnp.where(slots.live[k] & slots.live[j], base + band[j], geo.spare)
                    for j in range(width)
                ]
            )
        tiles.append(jnp.concatenate(rows, axis=0))
        targets.append(target)
    parts = chain(xs, tiles, [b for b, _ in chosen], kernel_ref, weights_ref)
    for part, target in zip(parts, targets):
        scatter(part, target, ao_ref.shape[2], acc_ref)


def add_own(geo, chosen, width, meta_ref, tiles_ref, ao_ref, kernel_ref, weights_ref, acc_ref):
    xs, tiles, targets = ([], [], [])
    for b, there in chosen:
        slots = Slots(geo, meta_ref, b, there, width)
        xs.append(panels(slots, ao_ref, b))
        places, target = ([], [])
        for k in range(width):
            row = slots.row[k]
            band = [slots.offset[j] - slots.offset[k] + geo.half for j in range(width)]
            base = jnp.where(slots.own[k], row, 0) * geo.band
            places.append([base + o for o in band])
            base = geo.pick(geo.early_base, geo.early_at, row, base)
            target.append(
                [
                    jnp.where(
                        slots.live[k] & slots.live[j] & slots.own[j], base + band[j], geo.spare
                    )
                    for j in range(width)
                ]
            )
        tiles.append(gathered(tiles_ref, places))
        targets.append(target)
    parts = chain(xs, tiles, [b for b, _ in chosen], kernel_ref, weights_ref)
    for part, target in zip(parts, targets):
        scatter(part, target, ao_ref.shape[2], acc_ref)


def halo_rows(geo, meta_ref, slots):
    odd = meta_ref[geo.odd_at] == 1
    rows, places, present = ([], [], [])
    for i in range(geo.reach):
        row = jnp.where(odd, geo.rows + i, i - geo.reach)
        place, found = (jnp.int32(0), jnp.bool_(False))
        for k in range(slots.width):
            hit = slots.live[k] & (slots.row[k] == row)
            place = jnp.where(hit, k, place)
            found = found | hit
        rows.append(row)
        places.append(place)
        present.append(found)
    return rows, places, present


def add_corner(geo, chosen, meta_ref, halo_ref, ao_ref, kernel_ref, weights_ref, h_ref, total_ref):
    nb = ao_ref.shape[2]
    factor = lambda flag: jnp.where(flag, 1.0, 0.0)
    xs, sides, tiles, masks = ([], [], [], [])
    for b, there in chosen:
        slots = Slots(geo, meta_ref, b, there, geo.slots)
        rows, places, present = halo_rows(geo, meta_ref, slots)
        xs.append(panels(slots, ao_ref, b))
        sides.append(
            jnp.concatenate(
                [
                    ao_ref[b, place] * factor(found).astype(ao_ref.dtype)
                    for place, found in zip(places, present)
                ],
                axis=0,
            )
        )
        picked = []
        for row, found in zip(rows, present):
            base = geo.pick(geo.halo_base, 0, row, 0) - row + geo.half
            picked.append([jnp.where(found, base + column, 0) for column in slots.row])
        tiles.append(gathered(halo_ref, picked))
        masks.append([factor(found) for found in present])
    gs = potentials(xs, tiles, [b for b, _ in chosen], kernel_ref)
    hs = []
    for g, mask, (b, there) in zip(gs, masks, chosen):
        weights = weights_ref[pl.ds(b, 1), :]
        h = jnp.concatenate(
            [g[i * nb : (i + 1) * nb] * (weights * mask[i]) for i in range(geo.reach)], axis=0
        ).astype(jnp.bfloat16)
        h_ref[jnp.where(there, b, geo.batches)] = h
        hs.append(h)
    total_ref[...] += outer_product(
        jnp.concatenate(sides, axis=1), jnp.concatenate(hs, axis=1)
    )


def add_columns(geo, chosen, width, meta_ref, ao_ref, h_ref, acc_ref):
    parts, targets = ([], [])
    for b, there in chosen:
        slots = Slots(geo, meta_ref, b, there, width)
        rows, _, present = halo_rows(geo, meta_ref, slots)
        parts.append(outer_product(ao_ref[b, pl.ds(0, width)].reshape(-1, ao_ref.shape[3]), h_ref[b]))
        targets.append(
            [
                [
                    jnp.where(
                        slots.live[k] & slots.own[k] & found,
                        slots.row[k] * geo.band + row - slots.row[k] + geo.half,
                        geo.spare,
                    )
                    for row, found in zip(rows, present)
                ]
                for k in range(width)
            ]
        )
    for part, target in zip(parts, targets):
        scatter(part, target, ao_ref.shape[2], acc_ref)


def early_kernel(
    geo, meta_ref, tiles_ref, ao_ref, kernel_ref, weights_ref, acc_in, acc_ref
):
    odd = meta_ref[geo.odd_at] == 1
    for where in (zone(geo, odd, True), pl.ds(geo.early_at, geo.early), pl.ds(geo.spare, 1)):
        acc_ref[where] = jnp.zeros_like(acc_ref[where])
    refs = (meta_ref, tiles_ref, ao_ref, kernel_ref, weights_ref, acc_ref)
    for which, width in ((CROSS_MANY, geo.slots), (CROSS_FEW, 2)):
        each_group(
            geo, meta_ref, which, lambda chosen, width=width: add_own(geo, chosen, width, *refs)
        )


def near_kernel(
    geo, meta_ref, halo_a, halo_b, tiles_ref, ao_ref, kernel_ref, weights_ref, acc_in, acc_ref,
    early_out, out_a, out_b, halo_ref,
):
    outs = (out_a, out_b)
    for ref, (start, count) in zip((halo_a, halo_b), geo.pieces):
        halo_ref[pl.ds(start, count)] = ref[...]
    early_out[...] = acc_ref[pl.ds(geo.early_at, geo.early)].astype(early_out.dtype)
    refs = (meta_ref, tiles_ref, ao_ref, kernel_ref, weights_ref, acc_ref, halo_ref)
    for which, width in ((NEAR_MANY, geo.slots), (NEAR_FEW, 2)):
        each_group(
            geo, meta_ref, which, lambda chosen, width=width: add_whole(geo, chosen, width, *refs)
        )
    for out, (start, count) in zip(outs, geo.pieces):
        out[...] = acc_ref[pl.ds(geo.first_at + start, count)].astype(out.dtype)
    inner_part(geo, meta_ref, 0, refs[:-1])


def waiting_kernel(
    geo, meta_ref, tiles_ref, ao_ref, kernel_ref, weights_ref, acc_in, acc_ref, done_ref
):
    inner_part(geo, meta_ref, 1, (meta_ref, tiles_ref, ao_ref, kernel_ref, weights_ref, acc_ref))
    done_ref[0] = 1


def late_kernel(
    geo, meta_ref, done_ref, halo_ref, ao_ref, kernel_ref, weights_ref, h_ref, late_out, total_ref
):
    nb = ao_ref.shape[2]
    total_ref[...] = jnp.zeros_like(total_ref)

    def work(chosen):
        add_corner(
            geo, chosen, meta_ref, halo_ref, ao_ref, kernel_ref, weights_ref, h_ref, total_ref
        )

    groups = (meta_ref[geo.lengths_at + CROSS] + 1) // LATE_GROUP
    each_group(geo, meta_ref, CROSS, work, size=LATE_GROUP, end=groups)
    each_group(geo, meta_ref, CROSS, work, size=LATE_GROUP // 2, begin=2 * groups)
    for i in range(geo.reach):
        for j in range(geo.reach):
            late_out[i * geo.reach + j] = total_ref[
                i * nb : (i + 1) * nb, j * nb : (j + 1) * nb
            ].astype(late_out.dtype)


def inner_kernel(
    geo, meta_ref, first_a, first_b, tiles_ref, ao_ref, kernel_ref, weights_ref, h_ref, acc_in,
    acc_ref, out_ref, sems,
):
    odd = meta_ref[geo.odd_at] == 1
    refs = (meta_ref, tiles_ref, ao_ref, kernel_ref, weights_ref, acc_ref)
    inner_part(geo, meta_ref, 2, refs)

    def add_near(up, down):
        for piece, ref in enumerate((first_a, first_b)):
            for start, place, count in geo.near_packs(piece)[0 if up else 1]:
                acc_ref[pl.ds(start, count)] += ref[pl.ds(place, count)].astype(jnp.float32)

    by_parity(odd, add_near, True, False)
    done = zone(geo, odd, False)
    copy = pltpu.make_async_copy(acc_ref.at[done], out_ref.at[done], sems.at[0])
    copy.start()
    for which, width in ((CROSS_MANY, geo.slots), (CROSS_FEW, 2)):
        each_group(
            geo,
            meta_ref,
            which,
            lambda chosen, width=width: add_columns(
                geo, chosen, width, meta_ref, ao_ref, h_ref, acc_ref
            ),
        )

    def write_quiet(up, down):
        run_copies(
            [
                pltpu.make_async_copy(
                    acc_ref.at[pl.ds(start, count)], out_ref.at[pl.ds(start, count)], sems.at[1 + i]
                )
                for i, (start, count) in enumerate(geo.quiet[0 if up else 1])
            ]
        )

    by_parity(odd, write_quiet, True, False)
    copy.wait()


def finish_cross(geo, odd, parts, acc_ref, out_ref, total, sems):
    def add(up, down):
        copies = []
        for packs, ref in parts:
            for start, place, count in packs[0 if up else 1]:
                spot = pl.ds(len(copies) * geo.band, count)
                total[spot] = acc_ref[pl.ds(start, count)] + ref[pl.ds(place, count)].astype(
                    jnp.float32
                )
                copy = pltpu.make_async_copy(
                    total.at[spot], out_ref.at[pl.ds(start, count)], sems.at[len(copies)]
                )
                copy.start()
                copies.append(copy)
        for copy in copies:
            copy.wait()

    by_parity(odd, add, False, True)


def has_time(geo, meta_ref):
    left = [bounds[3] - bounds[2] for bounds in inner_share(geo, meta_ref)]
    return waits() & (left[0] + left[1] == 0)


def early_join_kernel(geo, meta_ref, early_ref, acc_ref, out_in, out_ref, total, sems):
    @pl.when(has_time(geo, meta_ref))
    def _():
        odd = meta_ref[geo.odd_at] == 1
        finish_cross(geo, odd, ((geo.early_packs, early_ref),), acc_ref, out_ref, total, sems)


def finish_kernel(geo, meta_ref, late_ref, early_ref, acc_ref, out_in, out_ref, total, sems):
    odd = meta_ref[geo.odd_at] == 1
    late = (geo.late_packs, late_ref)
    joined = has_time(geo, meta_ref)

    @pl.when(joined)
    def _():
        finish_cross(geo, odd, (late,), acc_ref, out_ref, total, sems)

    @pl.when(jnp.logical_not(joined))
    def _():
        parts = ((geo.early_packs, early_ref), late)
        finish_cross(geo, odd, parts, acc_ref, out_ref, total, sems)


def call(kernel, out_shape, in_specs, out_specs, scratch, aliases=None, cost=None):
    return pl.pallas_call(
        kernel,
        out_shape=out_shape,
        in_specs=in_specs,
        out_specs=out_specs,
        scratch_shapes=scratch,
        input_output_aliases=aliases or {},
        cost_estimate=cost,
        compiler_params=pltpu.CompilerParams(vmem_limit_bytes=16 * MIB),
    )


def to_first(x, size):
    pairs = [(i, i + 1) for i in range(0, size - 1, 2)]
    got = lax.ppermute(x, "blk", pairs + [(j, i) for i, j in pairs])
    return pltpu.with_memory_space_constraint(got, pltpu.VMEM)


def to_second(x, size):
    pairs = [(i, i + 1) for i in range(1, size - 1, 2)]
    got = lax.ppermute(x, "blk", pairs + [(j, i) for i, j in pairs])
    return pltpu.with_memory_space_constraint(got, pltpu.VMEM)


def local(density, ao_values, kernel, grid_weights, centre, sig_offsets, counts):
    rows, band, nb, _ = density.shape
    batches, slots, _, pts = ao_values.shape
    size = lax.axis_size("blk")
    geo = Geometry(rows, band, batches, slots)
    in_hbm = lambda x: pltpu.with_memory_space_constraint(x, pltpu.HBM)
    tiles = density.reshape(geo.own, nb, nb)
    pack = lambda count: pltpu.VMEM((count, nb, nb), jnp.bfloat16)
    dma = pltpu.SemaphoreType.DMA
    acc_type = pltpu.VMEM((geo.spare + 1, nb, nb), jnp.float32)

    pieces = tuple(pack(count) for _, count in geo.pieces)
    *near_halo, cross_halo, meta, acc = call(
        functools.partial(pack_kernel, geo),
        pieces + (pack(geo.halo),) + (pltpu.SMEM((geo.meta_size,), jnp.int32), acc_type),
        [ANY_SPEC] * 4,
        (VMEM_SPEC,) * 3 + (SMEM_SPEC, VMEM_SPEC),
        [
            pltpu.SMEM((batches,), jnp.int32),
            pltpu.SMEM((slots, batches), jnp.int32),
            pltpu.SMEM((batches,), jnp.int32),
            dma((4, max(2 * geo.reach, 3))),
        ],
        cost=pl.CostEstimate(flops=10**10, bytes_accessed=10**8, transcendentals=0),
    )(in_hbm(tiles), in_hbm(centre), in_hbm(sig_offsets.T), in_hbm(counts))
    cross_halo = to_second(cross_halo, size)
    near_halo = [to_first(piece, size) for piece in near_halo]

    panel = (tiles, ao_values, kernel, grid_weights)
    acc = call(
        functools.partial(early_kernel, geo),
        acc_type,
        [SMEM_SPEC] + [VMEM_SPEC] * 5,
        VMEM_SPEC,
        [],
        {5: 0},
    )(meta, *panel, acc)

    acc, early, *first = call(
        functools.partial(near_kernel, geo),
        (acc_type, pack(geo.early)) + pieces,
        [SMEM_SPEC] + [VMEM_SPEC] * 7,
        (VMEM_SPEC,) * 4,
        [pack(geo.halo)],
        {7: 0},
    )(meta, *near_halo, *panel, acc)
    early = to_second(early, size)
    first = [to_first(piece, size) for piece in first]

    acc, done = call(
        functools.partial(waiting_kernel, geo),
        (acc_type, pltpu.SMEM((1,), jnp.int32)),
        [SMEM_SPEC] + [VMEM_SPEC] * 5,
        (VMEM_SPEC, SMEM_SPEC),
        [],
        {5: 0},
    )(meta, *panel, acc)

    h_type = pltpu.VMEM((batches + 1, geo.reach * nb, pts), jnp.bfloat16)
    h, late = call(
        functools.partial(late_kernel, geo),
        (h_type, pack(geo.late)),
        [SMEM_SPEC] * 2 + [VMEM_SPEC] * 4,
        (VMEM_SPEC,) * 2,
        [pltpu.VMEM((geo.reach * nb, geo.reach * nb), jnp.float32)],
    )(meta, done, cross_halo, *panel[1:])
    late = to_second(late, size)

    whole = jax.ShapeDtypeStruct((geo.own, nb, nb), jnp.float32)
    acc, out = call(
        functools.partial(inner_kernel, geo),
        (acc_type, whole),
        [SMEM_SPEC] + [VMEM_SPEC] * 8,
        (VMEM_SPEC, ANY_SPEC),
        [dma((1 + max(len(runs) for runs in geo.quiet),))],
        {8: 0},
    )(meta, *first, *panel, h, acc)

    for kernel_of, got, parts in (
        (early_join_kernel, (early,), geo.reach),
        (finish_kernel, (late, early), 2 * geo.reach),
    ):
        out = call(
            functools.partial(kernel_of, geo),
            whole,
            [SMEM_SPEC] + [VMEM_SPEC] * (len(got) + 1) + [ANY_SPEC],
            ANY_SPEC,
            [pltpu.VMEM((parts * band, nb, nb), jnp.float32), dma((parts,))],
            {len(got) + 2: 0},
        )(meta, *got, acc, out)
    return out.reshape(rows, band, nb, nb)


def solution(mesh):
    placed = (
        P(("groups", "blk"), None, None, None),
        P(("groups", "blk"), None, None, None),
        P(("groups", "blk"), None, None),
        P(("groups", "blk"), None),
        P(("groups", "blk")),
        P(("groups", "blk"), None),
        P(("groups", "blk")),
    )
    return jax.shard_map(
        local,
        mesh=mesh,
        in_specs=placed,
        out_specs=P(("groups", "blk"), None, None, None),
        check_vma=False,
    )
```

```python
import functools

import jax
import jax.numpy as jnp
from jax import lax
from jax.experimental import pallas as pl
from jax.experimental.pallas import tpu as pltpu
from jax.sharding import PartitionSpec as P

MIB = 1 << 20
GROUP = 2
LATE_GROUP = 4
LISTS = 7
BUDGET = 41
WAIT = 8
COST = (10, 7)
SMEM_SPEC = pl.BlockSpec(memory_space=pltpu.SMEM)
VMEM_SPEC = pl.BlockSpec(memory_space=pltpu.VMEM)
ANY_SPEC = pl.BlockSpec(memory_space=pl.ANY)


class Geometry:
    def __init__(self, rows, band, batches, slots):
        self.rows, self.band, self.batches, self.slots = rows, band, batches, slots
        self.half = half = (band - 1) // 2
        self.reach = reach = half // 2
        self.own = rows * band
        low = [(-m, reach + m, band) for m in range(reach, 0, -1)]
        high = [(rows + m, 0, 3 * reach - m) for m in range(reach)]
        self.halo = sum(stop - start for _, start, stop in low)
        low_cut = [half - row for row, _, _ in low]
        high_cut = [rows - row + half for row, _, _ in high]
        early = (
            [(row, cut, stop) for (row, _, stop), cut in zip(low, low_cut)],
            [(row, start, cut) for (row, start, _), cut in zip(high, high_cut)],
        )
        late = (
            [(row, start, cut) for (row, start, _), cut in zip(low, low_cut)],
            [(row, cut, stop) for (row, _, stop), cut in zip(high, high_cut)],
        )
        self.early = sum(stop - start for _, start, stop in early[0])
        self.late = self.halo - self.early
        self.first_at = self.own
        self.early_at = self.own + self.halo
        self.spare = self.early_at + self.early
        cut = 6
        self.pieces = ((0, cut), (cut, self.halo - cut))
        self.halo_base = self.bases((low, high))
        self.early_base = self.bases(early)
        shifts = (rows, -rows)
        self.packs = [self.places(*pair) for pair in zip((low, high), shifts)]
        self.early_packs = [self.places(*pair) for pair in zip(early, shifts)]
        self.late_packs = [self.places(*pair) for pair in zip(late, shifts)]
        self.span = min(2 * reach, rows) * band
        self.quiet = [
            self.others(self.packs[1], 0, self.span),
            self.others(self.packs[0], self.own - self.span, self.own),
        ]
        self.list_size = batches + 2
        self.lengths_at = LISTS * self.list_size
        self.local_at = self.lengths_at + LISTS
        self.count_at = self.local_at + batches
        self.offsets_at = self.count_at + batches
        self.odd_at = self.offsets_at + slots * batches
        self.meta_size = self.odd_at + 1

    def bases(self, sides):
        found = {}
        for segments in sides:
            place = 0
            for row, start, stop in segments:
                found[row] = place - start
                place += stop - start
        return found

    def places(self, segments, shift):
        pack, place = ([], 0)
        for row, start, stop in segments:
            pack.append(((row + shift) * self.band + start, place, stop - start))
            place += stop - start
        return pack

    def others(self, pack, begin, end):
        touched = set()
        for start, _, count in pack:
            touched.update(range(start, start + count))
        runs = []
        for index in range(begin, end):
            if index in touched:
                continue
            if runs and sum(runs[-1]) == index:
                runs[-1] = (runs[-1][0], runs[-1][1] + 1)
            else:
                runs.append((index, 1))
        return runs

    def near_packs(self, piece):
        begin, count = self.pieces[piece]
        found = []
        for pack in self.packs:
            part = []
            for start, place, size in pack:
                low, high = max(place, begin), min(place + size, begin + count)
                if low < high:
                    part.append((start + low - place, low - begin, high - low))
            found.append(part)
        return found

    def pick(self, bases, shift, row, otherwise):
        value = otherwise
        for at, base in bases.items():
            value = jnp.where(row == at, base + shift, value)
        return value


def run_copies(copies):
    for copy in copies:
        copy.start()
    for copy in copies:
        copy.wait()


def by_parity(odd, body, first, second):
    @pl.when(jnp.logical_not(odd))
    def _():
        body(first, second)

    @pl.when(odd)
    def _():
        body(second, first)


CROSS_MANY, CROSS_FEW, NEAR_MANY, NEAR_FEW, INNER_MANY, INNER_FEW, CROSS = range(LISTS)


def build_lists(geo, index, centre_ref, offsets_ref, counts_ref, meta_ref):
    first = index * geo.rows
    odd = index % 2 == 1
    meta_ref[geo.odd_at] = odd.astype(jnp.int32)
    lengths = [jnp.int32(0)] * LISTS
    for b in range(geo.batches):
        local = centre_ref[b] - first
        count = counts_ref[b]
        meta_ref[geo.local_at + b] = local
        meta_ref[geo.count_at + b] = count
        low = high = jnp.bool_(False)
        for k in range(geo.slots):
            offset = offsets_ref[k, b]
            meta_ref[geo.offsets_at + k * geo.batches + b] = offset
            row = local + offset
            low = low | ((k < count) & (row < 0))
            high = high | ((k < count) & (row >= geo.rows))
        cross = (odd & high) | (jnp.logical_not(odd) & low)
        near = (odd & low) | (jnp.logical_not(odd) & high)
        inner = jnp.logical_not(low | high)
        many = count > 2
        few = (count > 0) & jnp.logical_not(many)
        kinds = [kind & size for kind in (cross, near, inner) for size in (many, few)]
        for which, member in enumerate(kinds + [cross]):
            meta_ref[which * geo.list_size + lengths[which]] = b
            lengths[which] = lengths[which] + member.astype(jnp.int32)
    for which in range(LISTS):
        meta_ref[which * geo.list_size + lengths[which]] = geo.batches
        meta_ref[geo.lengths_at + which] = lengths[which]


def zone(geo, odd, cross):
    span = geo.span if cross else geo.own - geo.span
    return pl.ds(jnp.where(odd == cross, geo.own - span, 0), span)


def pack_kernel(
    geo, density_ref, centre_in, offsets_in, counts_in,
    near_a, near_b, cross_ref, meta_ref, acc_ref,
    centre_ref, offsets_ref, counts_ref, sems,
):
    index = lax.axis_index("blk")
    odd = index % 2 == 1

    def copies(up, down):
        near = 0 if up else 1
        parts = [(cross_ref, geo.packs[1 - near])]
        parts += [(ref, geo.near_packs(i)[near]) for i, ref in enumerate((near_a, near_b))]
        return [
            pltpu.make_async_copy(
                density_ref.at[pl.ds(start, count)], ref.at[pl.ds(place, count)], sems.at[side, i]
            )
            for side, (ref, pack) in enumerate(parts)
            for i, (start, place, count) in enumerate(pack)
        ]

    def act(up, down, what):
        for copy in copies(up, down):
            what(copy)

    by_parity(odd, lambda up, down: act(up, down, lambda c: c.start()), True, False)
    scalars = [
        pltpu.make_async_copy(*pair, sems.at[3, i])
        for i, pair in enumerate(
            ((centre_in, centre_ref), (offsets_in, offsets_ref), (counts_in, counts_ref))
        )
    ]
    for copy in scalars:
        copy.start()
    for where in (zone(geo, odd, False), pl.ds(geo.first_at, geo.halo)):
        acc_ref[where] = jnp.zeros_like(acc_ref[where])
    for copy in scalars:
        copy.wait()
    build_lists(geo, index, centre_ref, offsets_ref, counts_ref, meta_ref)
    by_parity(odd, lambda up, down: act(up, down, lambda c: c.wait()), True, False)


def group_count(geo, meta_ref, which):
    return (meta_ref[geo.lengths_at + which] + GROUP - 1) // GROUP


def waits():
    return (lax.axis_index("blk") + 1) // 2 % 2 == 1


def inner_share(geo, meta_ref):
    before = BUDGET
    for which in (CROSS_MANY, CROSS_FEW, NEAR_MANY, NEAR_FEW):
        before = before - COST[which % 2] * group_count(geo, meta_ref, which)
    rounds = (meta_ref[geo.lengths_at + CROSS] + LATE_GROUP - 1) // LATE_GROUP
    waiting = jnp.where(waits(), WAIT - COST[0] * jnp.maximum(rounds - 1, 0), 0)
    share = []
    for which in (INNER_MANY, INNER_FEW):
        cost, count = COST[which % 2], group_count(geo, meta_ref, which)
        first = jnp.minimum(jnp.maximum(before, 0) // cost, count)
        second = jnp.minimum(jnp.maximum(waiting, 0) // cost, count - first)
        before = before - cost * first
        waiting = waiting - cost * second
        share.append((0, first, first + second, count))
    return share


def inner_part(geo, meta_ref, stage, refs):
    for which, width, bounds in zip(
        (INNER_MANY, INNER_FEW), (geo.slots, 2), inner_share(geo, meta_ref)
    ):
        each_group(
            geo,
            meta_ref,
            which,
            lambda chosen, width=width: add_whole(geo, chosen, width, *refs),
            begin=bounds[stage],
            end=bounds[stage + 1],
        )


def each_group(geo, meta_ref, which, body, size=GROUP, begin=0, end=None):
    length = meta_ref[geo.lengths_at + which]

    def step(i, carry):
        chosen = []
        for n in range(size):
            place = i * size + n
            there = place < length
            b = meta_ref[which * geo.list_size + jnp.minimum(place, length)]
            chosen.append((jnp.where(there, b, 0), there))
        body(chosen)
        return carry

    lax.fori_loop(begin, (length + size - 1) // size if end is None else end, step, 0)


class Slots:
    def __init__(self, geo, meta_ref, b, there, width):
        local = meta_ref[geo.local_at + b]
        count = jnp.where(there, meta_ref[geo.count_at + b], 0)
        self.offset = [meta_ref[geo.offsets_at + k * geo.batches + b] for k in range(width)]
        self.local = local
        self.row = [local + offset for offset in self.offset]
        self.live = [k < count for k in range(width)]
        self.own = [(row >= 0) & (row < geo.rows) for row in self.row]
        self.width = width


def panels(slots, ao_ref, b):
    return jnp.concatenate(
        [
            ao_ref[b, k] * jnp.where(slots.live[k], 1.0, 0.0).astype(ao_ref.dtype)
            for k in range(slots.width)
        ],
        axis=0,
    )


def gathered(tiles_ref, places):
    return jnp.concatenate(
        [jnp.concatenate([tiles_ref[place] for place in row], axis=1) for row in places], axis=0
    )


def potentials(xs, tiles, batches, kernel_ref):
    fs = [
        jnp.dot(t, x, preferred_element_type=jnp.float32).astype(jnp.bfloat16)
        for t, x in zip(tiles, xs)
    ]
    return [
        jnp.dot(f, kernel_ref[b], preferred_element_type=jnp.float32) for f, b in zip(fs, batches)
    ]


def outer_product(x, h):
    return lax.dot_general(x, h, (((1,), (1,)), ((), ())), preferred_element_type=jnp.float32)


def chain(xs, tiles, batches, kernel_ref, weights_ref):
    gs = potentials(xs, tiles, batches, kernel_ref)
    hs = [(g * weights_ref[pl.ds(b, 1), :]).astype(jnp.bfloat16) for g, b in zip(gs, batches)]
    return [outer_product(x, h) for x, h in zip(xs, hs)]


def scatter(part, target, nb, acc_ref):
    for k, row in enumerate(target):
        for j, place in enumerate(row):
            acc_ref[place] += part[k * nb : (k + 1) * nb, j * nb : (j + 1) * nb]


def add_whole(
    geo, chosen, width, meta_ref, tiles_ref, ao_ref, kernel_ref, weights_ref, acc_ref, halo_ref=None
):
    xs, tiles, targets = ([], [], [])
    for b, there in chosen:
        slots = Slots(geo, meta_ref, b, there, width)
        xs.append(panels(slots, ao_ref, b))
        rows, target = ([], [])
        for k in range(width):
            band = [slots.offset[j] - slots.offset[k] + geo.half for j in range(width)]
            own = slots.own[k]
            base = jnp.where(slots.live[k] & own, slots.row[k], 0) * geo.band
            row = jnp.concatenate([tiles_ref[base + o] for o in band], axis=1)
            if halo_ref is not None:
                away = slots.live[k] & jnp.logical_not(own)
                outside = jnp.where(away, geo.pick(geo.halo_base, 0, slots.row[k], 0), 0)
                other = [halo_ref[jnp.where(away, outside + o, 0)] for o in band]
                row = jnp.where(away, jnp.concatenate(other, axis=1), row)
                base = jnp.where(away, outside + geo.first_at, base)
            rows.append(row)
            target.append(
                [
                    jnp.where(slots.live[k] & slots.live[j], base + band[j], geo.spare)
                    for j in range(width)
                ]
            )
        tiles.append(jnp.concatenate(rows, axis=0))
        targets.append(target)
    parts = chain(xs, tiles, [b for b, _ in chosen], kernel_ref, weights_ref)
    for part, target in zip(parts, targets):
        scatter(part, target, ao_ref.shape[2], acc_ref)


def add_own(geo, chosen, width, meta_ref, tiles_ref, ao_ref, kernel_ref, weights_ref, acc_ref):
    xs, tiles, targets = ([], [], [])
    for b, there in chosen:
        slots = Slots(geo, meta_ref, b, there, width)
        xs.append(panels(slots, ao_ref, b))
        places, target = ([], [])
        for k in range(width):
            row = slots.row[k]
            band = [slots.offset[j] - slots.offset[k] + geo.half for j in range(width)]
            base = jnp.where(slots.own[k], row, 0) * geo.band
            places.append([base + o for o in band])
            base = geo.pick(geo.early_base, geo.early_at, row, base)
            target.append(
                [
                    jnp.where(
                        slots.live[k] & slots.live[j] & slots.own[j], base + band[j], geo.spare
                    )
                    for j in range(width)
                ]
            )
        tiles.append(gathered(tiles_ref, places))
        targets.append(target)
    parts = chain(xs, tiles, [b for b, _ in chosen], kernel_ref, weights_ref)
    for part, target in zip(parts, targets):
        scatter(part, target, ao_ref.shape[2], acc_ref)


def halo_rows(geo, meta_ref, slots):
    odd = meta_ref[geo.odd_at] == 1
    rows, places, present = ([], [], [])
    for i in range(geo.reach):
        row = jnp.where(odd, geo.rows + i, i - geo.reach)
        place, found = (jnp.int32(0), jnp.bool_(False))
        for k in range(slots.width):
            hit = slots.live[k] & (slots.row[k] == row)
            place = jnp.where(hit, k, place)
            found = found | hit
        rows.append(row)
        places.append(place)
        present.append(found)
    return rows, places, present


def add_corner(geo, chosen, meta_ref, halo_ref, ao_ref, kernel_ref, weights_ref, h_ref, total_ref):
    nb = ao_ref.shape[2]
    factor = lambda flag: jnp.where(flag, 1.0, 0.0)
    xs, sides, tiles, masks = ([], [], [], [])
    for b, there in chosen:
        slots = Slots(geo, meta_ref, b, there, geo.slots)
        rows, places, present = halo_rows(geo, meta_ref, slots)
        xs.append(panels(slots, ao_ref, b))
        sides.append(
            jnp.concatenate(
                [
                    ao_ref[b, place] * factor(found).astype(ao_ref.dtype)
                    for place, found in zip(places, present)
                ],
                axis=0,
            )
        )
        picked = []
        for row, found in zip(rows, present):
            base = geo.pick(geo.halo_base, 0, row, 0) - row + geo.half
            picked.append([jnp.where(found, base + column, 0) for column in slots.row])
        tiles.append(gathered(halo_ref, picked))
        masks.append([factor(found) for found in present])
    gs = potentials(xs, tiles, [b for b, _ in chosen], kernel_ref)
    hs = []
    for g, mask, (b, there) in zip(gs, masks, chosen):
        weights = weights_ref[pl.ds(b, 1), :]
        h = jnp.concatenate(
            [g[i * nb : (i + 1) * nb] * (weights * mask[i]) for i in range(geo.reach)], axis=0
        ).astype(jnp.bfloat16)
        h_ref[jnp.where(there, b, geo.batches)] = h
        hs.append(h)
    total_ref[...] += outer_product(
        jnp.concatenate(sides, axis=1), jnp.concatenate(hs, axis=1)
    )


def add_columns(geo, chosen, width, meta_ref, ao_ref, h_ref, acc_ref):
    parts, targets = ([], [])
    for b, there in chosen:
        slots = Slots(geo, meta_ref, b, there, width)
        rows, _, present = halo_rows(geo, meta_ref, slots)
        parts.append(outer_product(ao_ref[b, pl.ds(0, width)].reshape(-1, ao_ref.shape[3]), h_ref[b]))
        targets.append(
            [
                [
                    jnp.where(
                        slots.live[k] & slots.own[k] & found,
                        slots.row[k] * geo.band + row - slots.row[k] + geo.half,
                        geo.spare,
                    )
                    for row, found in zip(rows, present)
                ]
                for k in range(width)
            ]
        )
    for part, target in zip(parts, targets):
        scatter(part, target, ao_ref.shape[2], acc_ref)


def early_kernel(
    geo, meta_ref, tiles_ref, ao_ref, kernel_ref, weights_ref, acc_in, acc_ref
):
    odd = meta_ref[geo.odd_at] == 1
    for where in (zone(geo, odd, True), pl.ds(geo.early_at, geo.early), pl.ds(geo.spare, 1)):
        acc_ref[where] = jnp.zeros_like(acc_ref[where])
    refs = (meta_ref, tiles_ref, ao_ref, kernel_ref, weights_ref, acc_ref)
    for which, width in ((CROSS_MANY, geo.slots), (CROSS_FEW, 2)):
        each_group(
            geo, meta_ref, which, lambda chosen, width=width: add_own(geo, chosen, width, *refs)
        )


def near_kernel(
    geo, meta_ref, halo_a, halo_b, tiles_ref, ao_ref, kernel_ref, weights_ref, acc_in, acc_ref,
    early_out, out_a, out_b, halo_ref,
):
    outs = (out_a, out_b)
    for ref, (start, count) in zip((halo_a, halo_b), geo.pieces):
        halo_ref[pl.ds(start, count)] = ref[...]
    early_out[...] = acc_ref[pl.ds(geo.early_at, geo.early)].astype(early_out.dtype)
    refs = (meta_ref, tiles_ref, ao_ref, kernel_ref, weights_ref, acc_ref, halo_ref)
    for which, width in ((NEAR_MANY, geo.slots), (NEAR_FEW, 2)):
        each_group(
            geo, meta_ref, which, lambda chosen, width=width: add_whole(geo, chosen, width, *refs)
        )
    for out, (start, count) in zip(outs, geo.pieces):
        out[...] = acc_ref[pl.ds(geo.first_at + start, count)].astype(out.dtype)
    inner_part(geo, meta_ref, 0, refs[:-1])


def waiting_kernel(
    geo, meta_ref, tiles_ref, ao_ref, kernel_ref, weights_ref, acc_in, acc_ref, done_ref
):
    inner_part(geo, meta_ref, 1, (meta_ref, tiles_ref, ao_ref, kernel_ref, weights_ref, acc_ref))
    done_ref[0] = 1


def late_kernel(
    geo, meta_ref, done_ref, halo_ref, ao_ref, kernel_ref, weights_ref, h_ref, late_out, total_ref
):
    nb = ao_ref.shape[2]
    total_ref[...] = jnp.zeros_like(total_ref)

    def work(chosen):
        add_corner(
            geo, chosen, meta_ref, halo_ref, ao_ref, kernel_ref, weights_ref, h_ref, total_ref
        )

    groups = (meta_ref[geo.lengths_at + CROSS] + 1) // LATE_GROUP
    each_group(geo, meta_ref, CROSS, work, size=LATE_GROUP, end=groups)
    each_group(geo, meta_ref, CROSS, work, size=LATE_GROUP // 2, begin=2 * groups)
    for i in range(geo.reach):
        for j in range(geo.reach):
            late_out[i * geo.reach + j] = total_ref[
                i * nb : (i + 1) * nb, j * nb : (j + 1) * nb
            ].astype(late_out.dtype)


def inner_kernel(
    geo, meta_ref, first_a, first_b, tiles_ref, ao_ref, kernel_ref, weights_ref, h_ref, acc_in,
    acc_ref, out_ref, sems,
):
    odd = meta_ref[geo.odd_at] == 1
    refs = (meta_ref, tiles_ref, ao_ref, kernel_ref, weights_ref, acc_ref)
    inner_part(geo, meta_ref, 2, refs)

    def add_near(up, down):
        for piece, ref in enumerate((first_a, first_b)):
            for start, place, count in geo.near_packs(piece)[0 if up else 1]:
                acc_ref[pl.ds(start, count)] += ref[pl.ds(place, count)].astype(jnp.float32)

    by_parity(odd, add_near, True, False)
    done = zone(geo, odd, False)
    copy = pltpu.make_async_copy(acc_ref.at[done], out_ref.at[done], sems.at[0])
    copy.start()
    for which, width in ((CROSS_MANY, geo.slots), (CROSS_FEW, 2)):
        each_group(
            geo,
            meta_ref,
            which,
            lambda chosen, width=width: add_columns(
                geo, chosen, width, meta_ref, ao_ref, h_ref, acc_ref
            ),
        )

    def write_quiet(up, down):
        run_copies(
            [
                pltpu.make_async_copy(
                    acc_ref.at[pl.ds(start, count)], out_ref.at[pl.ds(start, count)], sems.at[1 + i]
                )
                for i, (start, count) in enumerate(geo.quiet[0 if up else 1])
            ]
        )

    by_parity(odd, write_quiet, True, False)
    copy.wait()


def finish_cross(geo, odd, parts, acc_ref, out_ref, total, sems):
    def add(up, down):
        copies = []
        for packs, ref in parts:
            for start, place, count in packs[0 if up else 1]:
                spot = pl.ds(len(copies) * geo.band, count)
                total[spot] = acc_ref[pl.ds(start, count)] + ref[pl.ds(place, count)].astype(
                    jnp.float32
                )
                copy = pltpu.make_async_copy(
                    total.at[spot], out_ref.at[pl.ds(start, count)], sems.at[len(copies)]
                )
                copy.start()
                copies.append(copy)
        for copy in copies:
            copy.wait()

    by_parity(odd, add, False, True)


def has_time(geo, meta_ref):
    left = [bounds[3] - bounds[2] for bounds in inner_share(geo, meta_ref)]
    return waits() & (left[0] + left[1] == 0)


def early_join_kernel(geo, meta_ref, early_ref, acc_ref, out_in, out_ref, total, sems):
    @pl.when(has_time(geo, meta_ref))
    def _():
        odd = meta_ref[geo.odd_at] == 1
        finish_cross(geo, odd, ((geo.early_packs, early_ref),), acc_ref, out_ref, total, sems)


def finish_kernel(geo, meta_ref, late_ref, early_ref, acc_ref, out_in, out_ref, total, sems):
    odd = meta_ref[geo.odd_at] == 1
    late = (geo.late_packs, late_ref)
    joined = has_time(geo, meta_ref)

    @pl.when(joined)
    def _():
        finish_cross(geo, odd, (late,), acc_ref, out_ref, total, sems)

    @pl.when(jnp.logical_not(joined))
    def _():
        parts = ((geo.early_packs, early_ref), late)
        finish_cross(geo, odd, parts, acc_ref, out_ref, total, sems)


def call(kernel, out_shape, in_specs, out_specs, scratch, aliases=None, cost=None):
    return pl.pallas_call(
        kernel,
        out_shape=out_shape,
        in_specs=in_specs,
        out_specs=out_specs,
        scratch_shapes=scratch,
        input_output_aliases=aliases or {},
        cost_estimate=cost,
        compiler_params=pltpu.CompilerParams(vmem_limit_bytes=16 * MIB),
    )


def to_first(x, size):
    pairs = [(i, i + 1) for i in range(0, size - 1, 2)]
    got = lax.ppermute(x, "blk", pairs + [(j, i) for i, j in pairs])
    return pltpu.with_memory_space_constraint(got, pltpu.VMEM)


def to_second(x, size):
    pairs = [(i, i + 1) for i in range(1, size - 1, 2)]
    got = lax.ppermute(x, "blk", pairs + [(j, i) for i, j in pairs])
    return pltpu.with_memory_space_constraint(got, pltpu.VMEM)


def local(density, ao_values, kernel, grid_weights, centre, sig_offsets, counts):
    rows, band, nb, _ = density.shape
    batches, slots, _, pts = ao_values.shape
    size = lax.axis_size("blk")
    geo = Geometry(rows, band, batches, slots)
    in_hbm = lambda x: pltpu.with_memory_space_constraint(x, pltpu.HBM)
    tiles = density.reshape(geo.own, nb, nb)
    pack = lambda count: pltpu.VMEM((count, nb, nb), jnp.bfloat16)
    dma = pltpu.SemaphoreType.DMA
    acc_type = pltpu.VMEM((geo.spare + 1, nb, nb), jnp.float32)

    pieces = tuple(pack(count) for _, count in geo.pieces)
    *near_halo, cross_halo, meta, acc = call(
        functools.partial(pack_kernel, geo),
        pieces + (pack(geo.halo),) + (pltpu.SMEM((geo.meta_size,), jnp.int32), acc_type),
        [ANY_SPEC] * 4,
        (VMEM_SPEC,) * 3 + (SMEM_SPEC, VMEM_SPEC),
        [
            pltpu.SMEM((batches,), jnp.int32),
            pltpu.SMEM((slots, batches), jnp.int32),
            pltpu.SMEM((batches,), jnp.int32),
            dma((4, max(2 * geo.reach, 3))),
        ],
        cost=pl.CostEstimate(flops=10**10, bytes_accessed=10**8, transcendentals=0),
    )(in_hbm(tiles), in_hbm(centre), in_hbm(sig_offsets.T), in_hbm(counts))
    cross_halo = to_second(cross_halo, size)
    near_halo = [to_first(piece, size) for piece in near_halo]

    panel = (tiles, ao_values, kernel, grid_weights)
    acc = call(
        functools.partial(early_kernel, geo),
        acc_type,
        [SMEM_SPEC] + [VMEM_SPEC] * 5,
        VMEM_SPEC,
        [],
        {5: 0},
    )(meta, *panel, acc)

    acc, early, *first = call(
        functools.partial(near_kernel, geo),
        (acc_type, pack(geo.early)) + pieces,
        [SMEM_SPEC] + [VMEM_SPEC] * 7,
        (VMEM_SPEC,) * 4,
        [pack(geo.halo)],
        {7: 0},
    )(meta, *near_halo, *panel, acc)
    early = to_second(early, size)
    first = [to_first(piece, size) for piece in first]

    acc, done = call(
        functools.partial(waiting_kernel, geo),
        (acc_type, pltpu.SMEM((1,), jnp.int32)),
        [SMEM_SPEC] + [VMEM_SPEC] * 5,
        (VMEM_SPEC, SMEM_SPEC),
        [],
        {5: 0},
    )(meta, *panel, acc)

    h_type = pltpu.VMEM((batches + 1, geo.reach * nb, pts), jnp.bfloat16)
    h, late = call(
        functools.partial(late_kernel, geo),
        (h_type, pack(geo.late)),
        [SMEM_SPEC] * 2 + [VMEM_SPEC] * 4,
        (VMEM_SPEC,) * 2,
        [pltpu.VMEM((geo.reach * nb, geo.reach * nb), jnp.float32)],
    )(meta, done, cross_halo, *panel[1:])
    late = to_second(late, size)

    whole = jax.ShapeDtypeStruct((geo.own, nb, nb), jnp.float32)
    acc, out = call(
        functools.partial(inner_kernel, geo),
        (acc_type, whole),
        [SMEM_SPEC] + [VMEM_SPEC] * 8,
        (VMEM_SPEC, ANY_SPEC),
        [dma((1 + max(len(runs) for runs in geo.quiet),))],
        {8: 0},
    )(meta, *first, *panel, h, acc)

    for kernel_of, got, parts in (
        (early_join_kernel, (early,), geo.reach),
        (finish_kernel, (late, early), 2 * geo.reach),
    ):
        out = call(
            functools.partial(kernel_of, geo),
            whole,
            [SMEM_SPEC] + [VMEM_SPEC] * (len(got) + 1) + [ANY_SPEC],
            ANY_SPEC,
            [pltpu.VMEM((parts * band, nb, nb), jnp.float32), dma((parts,))],
            {len(got) + 2: 0},
        )(meta, *got, acc, out)
    return out.reshape(rows, band, nb, nb)


def solution(mesh):
    placed = (
        P(("groups", "blk"), None, None, None),
        P(("groups", "blk"), None, None, None),
        P(("groups", "blk"), None, None),
        P(("groups", "blk"), None),
        P(("groups", "blk")),
        P(("groups", "blk"), None),
        P(("groups", "blk")),
    )
    return jax.shard_map(
        local,
        mesh=mesh,
        in_specs=placed,
        out_specs=P(("groups", "blk"), None, None, None),
        check_vma=False,
    )
```

```python
import functools

import jax
import jax.numpy as jnp
from jax import lax
from jax.experimental import pallas as pl
from jax.experimental.pallas import tpu as pltpu
from jax.sharding import PartitionSpec as P

MIB = 1 << 20
GROUP = 2
LATE_GROUP = 4
LISTS = 7
BUDGET = 43
WAIT = (24, 18)
COST = (10, 7)
SMEM_SPEC = pl.BlockSpec(memory_space=pltpu.SMEM)
VMEM_SPEC = pl.BlockSpec(memory_space=pltpu.VMEM)
ANY_SPEC = pl.BlockSpec(memory_space=pl.ANY)


class Geometry:
    def __init__(self, rows, band, batches, slots):
        self.rows, self.band, self.batches, self.slots = rows, band, batches, slots
        self.half = half = (band - 1) // 2
        self.reach = reach = half // 2
        self.own = rows * band
        low = [(-m, reach + m, band) for m in range(reach, 0, -1)]
        high = [(rows + m, 0, 3 * reach - m) for m in range(reach)]
        self.halo = sum(stop - start for _, start, stop in low)
        low_cut = [half - row for row, _, _ in low]
        high_cut = [rows - row + half for row, _, _ in high]
        early = (
            [(row, cut, stop) for (row, _, stop), cut in zip(low, low_cut)],
            [(row, start, cut) for (row, start, _), cut in zip(high, high_cut)],
        )
        late = (
            [(row, start, cut) for (row, start, _), cut in zip(low, low_cut)],
            [(row, cut, stop) for (row, _, stop), cut in zip(high, high_cut)],
        )
        self.early = sum(stop - start for _, start, stop in early[0])
        self.late = self.halo - self.early
        self.first_at = self.own
        self.early_at = self.own + self.halo
        self.spare = self.early_at + self.early
        self.halo_base = self.bases((low, high))
        self.early_base = self.bases(early)
        shifts = (rows, -rows)
        self.packs = [self.places(*pair) for pair in zip((low, high), shifts)]
        self.early_packs = [self.places(*pair) for pair in zip(early, shifts)]
        self.late_packs = [self.places(*pair) for pair in zip(late, shifts)]
        self.span = min(2 * reach, rows) * band
        self.quiet = [
            self.others(self.packs[1], 0, self.span),
            self.others(self.packs[0], self.own - self.span, self.own),
        ]
        self.list_size = batches + 2
        self.lengths_at = LISTS * self.list_size
        self.local_at = self.lengths_at + LISTS
        self.count_at = self.local_at + batches
        self.offsets_at = self.count_at + batches
        self.odd_at = self.offsets_at + slots * batches
        self.meta_size = self.odd_at + 1

    def bases(self, sides):
        found = {}
        for segments in sides:
            place = 0
            for row, start, stop in segments:
                found[row] = place - start
                place += stop - start
        return found

    def places(self, segments, shift):
        pack, place = ([], 0)
        for row, start, stop in segments:
            pack.append(((row + shift) * self.band + start, place, stop - start))
            place += stop - start
        return pack

    def others(self, pack, begin, end):
        touched = set()
        for start, _, count in pack:
            touched.update(range(start, start + count))
        runs = []
        for index in range(begin, end):
            if index in touched:
                continue
            if runs and sum(runs[-1]) == index:
                runs[-1] = (runs[-1][0], runs[-1][1] + 1)
            else:
                runs.append((index, 1))
        return runs

    def pick(self, bases, shift, row, otherwise):
        value = otherwise
        for at, base in bases.items():
            value = jnp.where(row == at, base + shift, value)
        return value


def run_copies(copies):
    for copy in copies:
        copy.start()
    for copy in copies:
        copy.wait()


def by_parity(odd, body, first, second):
    @pl.when(jnp.logical_not(odd))
    def _():
        body(first, second)

    @pl.when(odd)
    def _():
        body(second, first)


CROSS_MANY, CROSS_FEW, NEAR_MANY, NEAR_FEW, INNER_MANY, INNER_FEW, CROSS = range(LISTS)


def build_lists(geo, index, centre_ref, offsets_ref, counts_ref, meta_ref):
    first = index * geo.rows
    odd = index % 2 == 1
    meta_ref[geo.odd_at] = odd.astype(jnp.int32)
    lengths = [jnp.int32(0)] * LISTS
    for b in range(geo.batches):
        local = centre_ref[b] - first
        count = counts_ref[b]
        meta_ref[geo.local_at + b] = local
        meta_ref[geo.count_at + b] = count
        low = high = jnp.bool_(False)
        for k in range(geo.slots):
            offset = offsets_ref[k, b]
            meta_ref[geo.offsets_at + k * geo.batches + b] = offset
            row = local + offset
            low = low | ((k < count) & (row < 0))
            high = high | ((k < count) & (row >= geo.rows))
        cross = (odd & high) | (jnp.logical_not(odd) & low)
        near = (odd & low) | (jnp.logical_not(odd) & high)
        inner = jnp.logical_not(low | high)
        many = count > 2
        few = (count > 0) & jnp.logical_not(many)
        kinds = [kind & size for kind in (cross, near, inner) for size in (many, few)]
        for which, member in enumerate(kinds + [cross]):
            meta_ref[which * geo.list_size + lengths[which]] = b
            lengths[which] = lengths[which] + member.astype(jnp.int32)
    for which in range(LISTS):
        meta_ref[which * geo.list_size + lengths[which]] = geo.batches
        meta_ref[geo.lengths_at + which] = lengths[which]


def zone(geo, odd, cross):
    span = geo.span if cross else geo.own - geo.span
    return pl.ds(jnp.where(odd == cross, geo.own - span, 0), span)


def pack_kernel(
    geo, density_ref, centre_in, offsets_in, counts_in,
    near_ref, cross_ref, meta_ref, acc_ref,
    centre_ref, offsets_ref, counts_ref, sems,
):
    index = lax.axis_index("blk")
    odd = index % 2 == 1

    by_size = lambda pack: sorted(pack, key=lambda segment: segment[2])
    copies = []
    for side, (ref, upper) in enumerate(((cross_ref, odd), (near_ref, jnp.logical_not(odd)))):
        for i, (up, down) in enumerate(zip(*(by_size(pack) for pack in geo.packs))):
            start = jnp.where(upper, up[0], down[0])
            place = jnp.where(upper, up[1], down[1])
            copies.append(
                pltpu.make_async_copy(
                    density_ref.at[pl.ds(start, up[2])], ref.at[pl.ds(place, up[2])], sems.at[side, i]
                )
            )
    for copy in copies:
        copy.start()
    scalars = [
        pltpu.make_async_copy(*pair, sems.at[2, i])
        for i, pair in enumerate(
            ((centre_in, centre_ref), (offsets_in, offsets_ref), (counts_in, counts_ref))
        )
    ]
    for copy in scalars:
        copy.start()
    for where in (zone(geo, odd, False), pl.ds(geo.first_at, geo.halo)):
        acc_ref[where] = jnp.zeros_like(acc_ref[where])
    for copy in scalars:
        copy.wait()
    build_lists(geo, index, centre_ref, offsets_ref, counts_ref, meta_ref)
    for copy in copies:
        copy.wait()


def group_count(geo, meta_ref, which):
    return (meta_ref[geo.lengths_at + which] + GROUP - 1) // GROUP


def waits():
    return (lax.axis_index("blk") + 1) // 2 % 2 == 1


def inner_share(geo, meta_ref):
    before = BUDGET
    for which in (CROSS_MANY, CROSS_FEW, NEAR_MANY, NEAR_FEW):
        before = before - COST[which % 2] * group_count(geo, meta_ref, which)
    rounds = (meta_ref[geo.lengths_at + CROSS] + LATE_GROUP - 1) // LATE_GROUP
    room = jnp.where(meta_ref[geo.odd_at] == 1, WAIT[1], WAIT[0])
    waiting = jnp.where(waits(), room - COST[0] * jnp.maximum(rounds - 1, 0), 0)
    share = []
    for which in (INNER_MANY, INNER_FEW):
        cost, count = COST[which % 2], group_count(geo, meta_ref, which)
        first = jnp.minimum(jnp.maximum(before, 0) // cost, count)
        second = jnp.minimum(jnp.maximum(waiting, 0) // cost, count - first)
        before = before - cost * first
        waiting = waiting - cost * second
        share.append((0, first, first + second, count))
    return share


def inner_part(geo, meta_ref, stage, refs):
    for which, width, bounds in zip(
        (INNER_MANY, INNER_FEW), (geo.slots, 2), inner_share(geo, meta_ref)
    ):
        each_group(
            geo,
            meta_ref,
            which,
            lambda chosen, width=width: add_whole(geo, chosen, width, *refs),
            begin=bounds[stage],
            end=bounds[stage + 1],
        )


def each_group(geo, meta_ref, which, body, size=GROUP, begin=0, end=None):
    length = meta_ref[geo.lengths_at + which]

    def step(i, carry):
        chosen = []
        for n in range(size):
            place = i * size + n
            there = place < length
            b = meta_ref[which * geo.list_size + jnp.minimum(place, length)]
            chosen.append((jnp.where(there, b, 0), there))
        body(chosen)
        return carry

    lax.fori_loop(begin, (length + size - 1) // size if end is None else end, step, 0)


class Slots:
    def __init__(self, geo, meta_ref, b, there, width):
        local = meta_ref[geo.local_at + b]
        count = jnp.where(there, meta_ref[geo.count_at + b], 0)
        self.offset = [meta_ref[geo.offsets_at + k * geo.batches + b] for k in range(width)]
        self.local = local
        self.row = [local + offset for offset in self.offset]
        self.live = [k < count for k in range(width)]
        self.own = [(row >= 0) & (row < geo.rows) for row in self.row]
        self.width = width


def panels(slots, ao_ref, b):
    return jnp.concatenate(
        [
            ao_ref[b, k] * jnp.where(slots.live[k], 1.0, 0.0).astype(ao_ref.dtype)
            for k in range(slots.width)
        ],
        axis=0,
    )


def gathered(tiles_ref, places):
    return jnp.concatenate(
        [jnp.concatenate([tiles_ref[place] for place in row], axis=1) for row in places], axis=0
    )


def potentials(xs, tiles, batches, kernel_ref):
    fs = [
        jnp.dot(t, x, preferred_element_type=jnp.float32).astype(jnp.bfloat16)
        for t, x in zip(tiles, xs)
    ]
    return [
        jnp.dot(f, kernel_ref[b], preferred_element_type=jnp.float32) for f, b in zip(fs, batches)
    ]


def outer_product(x, h):
    return lax.dot_general(x, h, (((1,), (1,)), ((), ())), preferred_element_type=jnp.float32)


def chain(xs, tiles, batches, kernel_ref, weights_ref):
    gs = potentials(xs, tiles, batches, kernel_ref)
    hs = [(g * weights_ref[pl.ds(b, 1), :]).astype(jnp.bfloat16) for g, b in zip(gs, batches)]
    return [outer_product(x, h) for x, h in zip(xs, hs)]


def scatter(part, target, nb, acc_ref):
    for k, row in enumerate(target):
        for j, place in enumerate(row):
            acc_ref[place] += part[k * nb : (k + 1) * nb, j * nb : (j + 1) * nb]


def add_whole(
    geo, chosen, width, meta_ref, tiles_ref, ao_ref, kernel_ref, weights_ref, acc_ref, halo_ref=None
):
    xs, tiles, targets = ([], [], [])
    for b, there in chosen:
        slots = Slots(geo, meta_ref, b, there, width)
        xs.append(panels(slots, ao_ref, b))
        rows, target = ([], [])
        for k in range(width):
            band = [slots.offset[j] - slots.offset[k] + geo.half for j in range(width)]
            own = slots.own[k]
            base = jnp.where(slots.live[k] & own, slots.row[k], 0) * geo.band
            row = jnp.concatenate([tiles_ref[base + o] for o in band], axis=1)
            if halo_ref is not None:
                away = slots.live[k] & jnp.logical_not(own)
                outside = jnp.where(away, geo.pick(geo.halo_base, 0, slots.row[k], 0), 0)
                other = [halo_ref[jnp.where(away, outside + o, 0)] for o in band]
                row = jnp.where(away, jnp.concatenate(other, axis=1), row)
                base = jnp.where(away, outside + geo.first_at, base)
            rows.append(row)
            target.append(
                [
                    jnp.where(slots.live[k] & slots.live[j], base + band[j], geo.spare)
                    for j in range(width)
                ]
            )
        tiles.append(jnp.concatenate(rows, axis=0))
        targets.append(target)
    parts = chain(xs, tiles, [b for b, _ in chosen], kernel_ref, weights_ref)
    for part, target in zip(parts, targets):
        scatter(part, target, ao_ref.shape[2], acc_ref)


def add_own(geo, chosen, width, meta_ref, tiles_ref, ao_ref, kernel_ref, weights_ref, acc_ref):
    xs, tiles, targets = ([], [], [])
    for b, there in chosen:
        slots = Slots(geo, meta_ref, b, there, width)
        xs.append(panels(slots, ao_ref, b))
        places, target = ([], [])
        for k in range(width):
            row = slots.row[k]
            band = [slots.offset[j] - slots.offset[k] + geo.half for j in range(width)]
            base = jnp.where(slots.own[k], row, 0) * geo.band
            places.append([base + o for o in band])
            base = geo.pick(geo.early_base, geo.early_at, row, base)
            target.append(
                [
                    jnp.where(
                        slots.live[k] & slots.live[j] & slots.own[j], base + band[j], geo.spare
                    )
                    for j in range(width)
                ]
            )
        tiles.append(gathered(tiles_ref, places))
        targets.append(target)
    parts = chain(xs, tiles, [b for b, _ in chosen], kernel_ref, weights_ref)
    for part, target in zip(parts, targets):
        scatter(part, target, ao_ref.shape[2], acc_ref)


def halo_rows(geo, meta_ref, slots):
    odd = meta_ref[geo.odd_at] == 1
    rows, places, present = ([], [], [])
    for i in range(geo.reach):
        row = jnp.where(odd, geo.rows + i, i - geo.reach)
        place, found = (jnp.int32(0), jnp.bool_(False))
        for k in range(slots.width):
            hit = slots.live[k] & (slots.row[k] == row)
            place = jnp.where(hit, k, place)
            found = found | hit
        rows.append(row)
        places.append(place)
        present.append(found)
    return rows, places, present


def add_corner(geo, chosen, meta_ref, halo_ref, ao_ref, kernel_ref, weights_ref, h_ref, total_ref):
    nb = ao_ref.shape[2]
    factor = lambda flag: jnp.where(flag, 1.0, 0.0)
    xs, sides, tiles, masks = ([], [], [], [])
    for b, there in chosen:
        slots = Slots(geo, meta_ref, b, there, geo.slots)
        rows, places, present = halo_rows(geo, meta_ref, slots)
        xs.append(panels(slots, ao_ref, b))
        sides.append(
            jnp.concatenate(
                [
                    ao_ref[b, place] * factor(found).astype(ao_ref.dtype)
                    for place, found in zip(places, present)
                ],
                axis=0,
            )
        )
        picked = []
        for row, found in zip(rows, present):
            base = geo.pick(geo.halo_base, 0, row, 0) - row + geo.half
            picked.append([jnp.where(found, base + column, 0) for column in slots.row])
        tiles.append(gathered(halo_ref, picked))
        masks.append([factor(found) for found in present])
    gs = potentials(xs, tiles, [b for b, _ in chosen], kernel_ref)
    hs = []
    for g, mask, (b, there) in zip(gs, masks, chosen):
        weights = weights_ref[pl.ds(b, 1), :]
        h = jnp.concatenate(
            [g[i * nb : (i + 1) * nb] * (weights * mask[i]) for i in range(geo.reach)], axis=0
        ).astype(jnp.bfloat16)
        h_ref[jnp.where(there, b, geo.batches)] = h
        hs.append(h)
    total_ref[...] += outer_product(
        jnp.concatenate(sides, axis=1), jnp.concatenate(hs, axis=1)
    )


def add_columns(geo, chosen, width, meta_ref, ao_ref, h_ref, acc_ref):
    parts, targets = ([], [])
    for b, there in chosen:
        slots = Slots(geo, meta_ref, b, there, width)
        rows, _, present = halo_rows(geo, meta_ref, slots)
        parts.append(outer_product(ao_ref[b, pl.ds(0, width)].reshape(-1, ao_ref.shape[3]), h_ref[b]))
        targets.append(
            [
                [
                    jnp.where(
                        slots.live[k] & slots.own[k] & found,
                        slots.row[k] * geo.band + row - slots.row[k] + geo.half,
                        geo.spare,
                    )
                    for row, found in zip(rows, present)
                ]
                for k in range(width)
            ]
        )
    for part, target in zip(parts, targets):
        scatter(part, target, ao_ref.shape[2], acc_ref)


def early_kernel(
    geo, meta_ref, tiles_ref, ao_ref, kernel_ref, weights_ref, acc_in, acc_ref, early_out
):
    odd = meta_ref[geo.odd_at] == 1
    for where in (zone(geo, odd, True), pl.ds(geo.early_at, geo.early), pl.ds(geo.spare, 1)):
        acc_ref[where] = jnp.zeros_like(acc_ref[where])
    refs = (meta_ref, tiles_ref, ao_ref, kernel_ref, weights_ref, acc_ref)
    for which, width in ((CROSS_MANY, geo.slots), (CROSS_FEW, 2)):
        each_group(
            geo, meta_ref, which, lambda chosen, width=width: add_own(geo, chosen, width, *refs)
        )
    early_out[...] = acc_ref[pl.ds(geo.early_at, geo.early)].astype(early_out.dtype)


def near_kernel(
    geo, meta_ref, halo_ref, tiles_ref, ao_ref, kernel_ref, weights_ref, acc_in, acc_ref, first_out
):
    refs = (meta_ref, tiles_ref, ao_ref, kernel_ref, weights_ref, acc_ref, halo_ref)
    for which, width in ((NEAR_MANY, geo.slots), (NEAR_FEW, 2)):
        each_group(
            geo, meta_ref, which, lambda chosen, width=width: add_whole(geo, chosen, width, *refs)
        )
    first_out[...] = acc_ref[pl.ds(geo.first_at, geo.halo)].astype(first_out.dtype)
    inner_part(geo, meta_ref, 0, refs[:-1])


def waiting_kernel(
    geo, meta_ref, tiles_ref, ao_ref, kernel_ref, weights_ref, acc_in, acc_ref, done_ref
):
    inner_part(geo, meta_ref, 1, (meta_ref, tiles_ref, ao_ref, kernel_ref, weights_ref, acc_ref))
    done_ref[0] = 1


def late_kernel(
    geo, meta_ref, done_ref, halo_ref, ao_ref, kernel_ref, weights_ref, h_ref, late_out, total_ref
):
    nb = ao_ref.shape[2]
    total_ref[...] = jnp.zeros_like(total_ref)

    def work(chosen):
        add_corner(
            geo, chosen, meta_ref, halo_ref, ao_ref, kernel_ref, weights_ref, h_ref, total_ref
        )

    groups = (meta_ref[geo.lengths_at + CROSS] + 1) // LATE_GROUP
    each_group(geo, meta_ref, CROSS, work, size=LATE_GROUP, end=groups)
    each_group(geo, meta_ref, CROSS, work, size=LATE_GROUP // 2, begin=2 * groups)
    for i in range(geo.reach):
        for j in range(geo.reach):
            late_out[i * geo.reach + j] = total_ref[
                i * nb : (i + 1) * nb, j * nb : (j + 1) * nb
            ].astype(late_out.dtype)


def inner_kernel(
    geo, meta_ref, first_ref, tiles_ref, ao_ref, kernel_ref, weights_ref, h_ref, acc_in,
    acc_ref, out_ref, sems,
):
    odd = meta_ref[geo.odd_at] == 1
    refs = (meta_ref, tiles_ref, ao_ref, kernel_ref, weights_ref, acc_ref)
    inner_part(geo, meta_ref, 2, refs)

    def add_near(up, down):
        for start, place, count in geo.packs[0 if up else 1]:
            acc_ref[pl.ds(start, count)] += first_ref[pl.ds(place, count)].astype(jnp.float32)

    by_parity(odd, add_near, True, False)
    done = zone(geo, odd, False)
    copy = pltpu.make_async_copy(acc_ref.at[done], out_ref.at[done], sems.at[0])
    copy.start()
    for which, width in ((CROSS_MANY, geo.slots), (CROSS_FEW, 2)):
        each_group(
            geo,
            meta_ref,
            which,
            lambda chosen, width=width: add_columns(
                geo, chosen, width, meta_ref, ao_ref, h_ref, acc_ref
            ),
        )

    def write_quiet(up, down):
        run_copies(
            [
                pltpu.make_async_copy(
                    acc_ref.at[pl.ds(start, count)], out_ref.at[pl.ds(start, count)], sems.at[1 + i]
                )
                for i, (start, count) in enumerate(geo.quiet[0 if up else 1])
            ]
        )

    by_parity(odd, write_quiet, True, False)
    copy.wait()


def finish_cross(geo, odd, parts, acc_ref, out_ref, total, sems):
    def add(up, down):
        copies = []
        for packs, ref in parts:
            for start, place, count in packs[0 if up else 1]:
                spot = pl.ds(len(copies) * geo.band, count)
                total[spot] = acc_ref[pl.ds(start, count)] + ref[pl.ds(place, count)].astype(
                    jnp.float32
                )
                copy = pltpu.make_async_copy(
                    total.at[spot], out_ref.at[pl.ds(start, count)], sems.at[len(copies)]
                )
                copy.start()
                copies.append(copy)
        for copy in copies:
            copy.wait()

    by_parity(odd, add, False, True)


def has_time(geo, meta_ref):
    left = [bounds[3] - bounds[2] for bounds in inner_share(geo, meta_ref)]
    return waits() & (left[0] + left[1] == 0)


def early_join_kernel(geo, meta_ref, early_ref, acc_ref, out_in, out_ref, total, sems):
    @pl.when(has_time(geo, meta_ref))
    def _():
        odd = meta_ref[geo.odd_at] == 1
        finish_cross(geo, odd, ((geo.early_packs, early_ref),), acc_ref, out_ref, total, sems)


def finish_kernel(geo, meta_ref, late_ref, early_ref, acc_ref, out_in, out_ref, total, sems):
    odd = meta_ref[geo.odd_at] == 1
    late = (geo.late_packs, late_ref)
    joined = has_time(geo, meta_ref)

    @pl.when(joined)
    def _():
        finish_cross(geo, odd, (late,), acc_ref, out_ref, total, sems)

    @pl.when(jnp.logical_not(joined))
    def _():
        parts = ((geo.early_packs, early_ref), late)
        finish_cross(geo, odd, parts, acc_ref, out_ref, total, sems)


def call(kernel, out_shape, in_specs, out_specs, scratch, aliases=None, cost=None):
    return pl.pallas_call(
        kernel,
        out_shape=out_shape,
        in_specs=in_specs,
        out_specs=out_specs,
        scratch_shapes=scratch,
        input_output_aliases=aliases or {},
        cost_estimate=cost,
        compiler_params=pltpu.CompilerParams(vmem_limit_bytes=16 * MIB),
    )


def to_first(x, size):
    pairs = [(i, i + 1) for i in range(0, size - 1, 2)]
    got = lax.ppermute(x, "blk", pairs + [(j, i) for i, j in pairs])
    return pltpu.with_memory_space_constraint(got, pltpu.VMEM)


def to_second(x, size):
    pairs = [(i, i + 1) for i in range(1, size - 1, 2)]
    got = lax.ppermute(x, "blk", pairs + [(j, i) for i, j in pairs])
    return pltpu.with_memory_space_constraint(got, pltpu.VMEM)


def local(density, ao_values, kernel, grid_weights, centre, sig_offsets, counts):
    rows, band, nb, _ = density.shape
    batches, slots, _, pts = ao_values.shape
    size = lax.axis_size("blk")
    geo = Geometry(rows, band, batches, slots)
    in_hbm = lambda x: pltpu.with_memory_space_constraint(x, pltpu.HBM)
    tiles = density.reshape(geo.own, nb, nb)
    pack = lambda count: pltpu.VMEM((count, nb, nb), jnp.bfloat16)
    dma = pltpu.SemaphoreType.DMA
    acc_type = pltpu.VMEM((geo.spare + 1, nb, nb), jnp.float32)

    near_halo, cross_halo, meta, acc = call(
        functools.partial(pack_kernel, geo),
        (pack(geo.halo),) * 2 + (pltpu.SMEM((geo.meta_size,), jnp.int32), acc_type),
        [ANY_SPEC] * 4,
        (VMEM_SPEC,) * 2 + (SMEM_SPEC, VMEM_SPEC),
        [
            pltpu.SMEM((batches,), jnp.int32),
            pltpu.SMEM((slots, batches), jnp.int32),
            pltpu.SMEM((batches,), jnp.int32),
            dma((3, max(geo.reach, 3))),
        ],
        cost=pl.CostEstimate(flops=10**10, bytes_accessed=10**8, transcendentals=0),
    )(in_hbm(tiles), in_hbm(centre), in_hbm(sig_offsets.T), in_hbm(counts))
    cross_halo = to_second(cross_halo, size)
    near_halo = to_first(near_halo, size)

    panel = (tiles, ao_values, kernel, grid_weights)
    acc, early = call(
        functools.partial(early_kernel, geo),
        (acc_type, pack(geo.early)),
        [SMEM_SPEC] + [VMEM_SPEC] * 5,
        (VMEM_SPEC,) * 2,
        [],
        {5: 0},
    )(meta, *panel, acc)
    early = to_second(early, size)

    acc, first = call(
        functools.partial(near_kernel, geo),
        (acc_type, pack(geo.halo)),
        [SMEM_SPEC] + [VMEM_SPEC] * 6,
        (VMEM_SPEC,) * 2,
        [],
        {6: 0},
    )(meta, near_halo, *panel, acc)
    first = to_first(first, size)

    acc, done = call(
        functools.partial(waiting_kernel, geo),
        (acc_type, pltpu.SMEM((1,), jnp.int32)),
        [SMEM_SPEC] + [VMEM_SPEC] * 5,
        (VMEM_SPEC, SMEM_SPEC),
        [],
        {5: 0},
    )(meta, *panel, acc)

    h_type = pltpu.VMEM((batches + 1, geo.reach * nb, pts), jnp.bfloat16)
    h, late = call(
        functools.partial(late_kernel, geo),
        (h_type, pack(geo.late)),
        [SMEM_SPEC] * 2 + [VMEM_SPEC] * 4,
        (VMEM_SPEC,) * 2,
        [pltpu.VMEM((geo.reach * nb, geo.reach * nb), jnp.float32)],
    )(meta, done, cross_halo, *panel[1:])
    late = to_second(late, size)

    whole = jax.ShapeDtypeStruct((geo.own, nb, nb), jnp.float32)
    acc, out = call(
        functools.partial(inner_kernel, geo),
        (acc_type, whole),
        [SMEM_SPEC] + [VMEM_SPEC] * 7,
        (VMEM_SPEC, ANY_SPEC),
        [dma((1 + max(len(runs) for runs in geo.quiet),))],
        {7: 0},
    )(meta, first, *panel, h, acc)

    for kernel_of, got, parts in (
        (early_join_kernel, (early,), geo.reach),
        (finish_kernel, (late, early), 2 * geo.reach),
    ):
        out = call(
            functools.partial(kernel_of, geo),
            whole,
            [SMEM_SPEC] + [VMEM_SPEC] * (len(got) + 1) + [ANY_SPEC],
            ANY_SPEC,
            [pltpu.VMEM((parts * band, nb, nb), jnp.float32), dma((parts,))],
            {len(got) + 2: 0},
        )(meta, *got, acc, out)
    return out.reshape(rows, band, nb, nb)


def solution(mesh):
    placed = (
        P(("groups", "blk"), None, None, None),
        P(("groups", "blk"), None, None, None),
        P(("groups", "blk"), None, None),
        P(("groups", "blk"), None),
        P(("groups", "blk")),
        P(("groups", "blk"), None),
        P(("groups", "blk")),
    )
    return jax.shard_map(
        local,
        mesh=mesh,
        in_specs=placed,
        out_specs=P(("groups", "blk"), None, None, None),
        check_vma=False,
    )
```

```python
import functools

import jax
import jax.numpy as jnp
from jax import lax
from jax.experimental import pallas as pl
from jax.experimental.pallas import tpu as pltpu
from jax.sharding import PartitionSpec as P

MIB = 1 << 20
GROUP = 2
LATE_GROUP = 4
LISTS = 7
BUDGET = 45
WAIT = 18
COST = (10, 7)
SMEM_SPEC = pl.BlockSpec(memory_space=pltpu.SMEM)
VMEM_SPEC = pl.BlockSpec(memory_space=pltpu.VMEM)
ANY_SPEC = pl.BlockSpec(memory_space=pl.ANY)


class Geometry:
    def __init__(self, rows, band, batches, slots):
        self.rows, self.band, self.batches, self.slots = rows, band, batches, slots
        self.half = half = (band - 1) // 2
        self.reach = reach = half // 2
        self.own = rows * band
        low = [(-m, reach + m, band) for m in range(reach, 0, -1)]
        high = [(rows + m, 0, 3 * reach - m) for m in range(reach)]
        self.halo = sum(stop - start for _, start, stop in low)
        low_cut = [half - row for row, _, _ in low]
        high_cut = [rows - row + half for row, _, _ in high]
        early = (
            [(row, cut, stop) for (row, _, stop), cut in zip(low, low_cut)],
            [(row, start, cut) for (row, start, _), cut in zip(high, high_cut)],
        )
        late = (
            [(row, start, cut) for (row, start, _), cut in zip(low, low_cut)],
            [(row, cut, stop) for (row, _, stop), cut in zip(high, high_cut)],
        )
        self.early = sum(stop - start for _, start, stop in early[0])
        self.late = self.halo - self.early
        self.first_at = self.own
        self.early_at = self.own + self.halo
        self.spare = self.early_at + self.early
        self.halo_base = self.bases((low, high))
        self.early_base = self.bases(early)
        shifts = (rows, -rows)
        self.packs = [self.places(*pair) for pair in zip((low, high), shifts)]
        self.early_packs = [self.places(*pair) for pair in zip(early, shifts)]
        self.late_packs = [self.places(*pair) for pair in zip(late, shifts)]
        self.span = min(2 * reach, rows) * band
        self.quiet = [
            self.others(self.packs[1], 0, self.span),
            self.others(self.packs[0], self.own - self.span, self.own),
        ]
        self.list_size = batches + 2
        self.lengths_at = LISTS * self.list_size
        self.local_at = self.lengths_at + LISTS
        self.count_at = self.local_at + batches
        self.offsets_at = self.count_at + batches
        self.odd_at = self.offsets_at + slots * batches
        self.meta_size = self.odd_at + 1

    def bases(self, sides):
        found = {}
        for segments in sides:
            place = 0
            for row, start, stop in segments:
                found[row] = place - start
                place += stop - start
        return found

    def places(self, segments, shift):
        pack, place = ([], 0)
        for row, start, stop in segments:
            pack.append(((row + shift) * self.band + start, place, stop - start))
            place += stop - start
        return pack

    def others(self, pack, begin, end):
        touched = set()
        for start, _, count in pack:
            touched.update(range(start, start + count))
        runs = []
        for index in range(begin, end):
            if index in touched:
                continue
            if runs and sum(runs[-1]) == index:
                runs[-1] = (runs[-1][0], runs[-1][1] + 1)
            else:
                runs.append((index, 1))
        return runs

    def pick(self, bases, shift, row, otherwise):
        value = otherwise
        for at, base in bases.items():
            value = jnp.where(row == at, base + shift, value)
        return value


def run_copies(copies):
    for copy in copies:
        copy.start()
    for copy in copies:
        copy.wait()


def by_parity(odd, body, first, second):
    @pl.when(jnp.logical_not(odd))
    def _():
        body(first, second)

    @pl.when(odd)
    def _():
        body(second, first)


CROSS_MANY, CROSS_FEW, NEAR_MANY, NEAR_FEW, INNER_MANY, INNER_FEW, CROSS = range(LISTS)


def build_lists(geo, index, centre_ref, offsets_ref, counts_ref, meta_ref):
    first = index * geo.rows
    odd = index % 2 == 1
    meta_ref[geo.odd_at] = odd.astype(jnp.int32)
    lengths = [jnp.int32(0)] * LISTS
    for b in range(geo.batches):
        local = centre_ref[b] - first
        count = counts_ref[b]
        meta_ref[geo.local_at + b] = local
        meta_ref[geo.count_at + b] = count
        low = high = jnp.bool_(False)
        for k in range(geo.slots):
            offset = offsets_ref[k, b]
            meta_ref[geo.offsets_at + k * geo.batches + b] = offset
            row = local + offset
            low = low | ((k < count) & (row < 0))
            high = high | ((k < count) & (row >= geo.rows))
        cross = (odd & high) | (jnp.logical_not(odd) & low)
        near = (odd & low) | (jnp.logical_not(odd) & high)
        inner = jnp.logical_not(low | high)
        many = count > 2
        few = (count > 0) & jnp.logical_not(many)
        kinds = [kind & size for kind in (cross, near, inner) for size in (many, few)]
        for which, member in enumerate(kinds + [cross]):
            meta_ref[which * geo.list_size + lengths[which]] = b
            lengths[which] = lengths[which] + member.astype(jnp.int32)
    for which in range(LISTS):
        meta_ref[which * geo.list_size + lengths[which]] = geo.batches
        meta_ref[geo.lengths_at + which] = lengths[which]


def zone(geo, odd, cross):
    span = geo.span if cross else geo.own - geo.span
    return pl.ds(jnp.where(odd == cross, geo.own - span, 0), span)


def pack_kernel(
    geo, density_ref, centre_in, offsets_in, counts_in,
    near_ref, cross_ref, meta_ref, acc_ref,
    centre_ref, offsets_ref, counts_ref, sems,
):
    index = lax.axis_index("blk")
    odd = index % 2 == 1

    by_size = lambda pack: sorted(pack, key=lambda segment: segment[2])
    copies = []
    for side, (ref, upper) in enumerate(((cross_ref, odd), (near_ref, jnp.logical_not(odd)))):
        for i, (up, down) in enumerate(zip(*(by_size(pack) for pack in geo.packs))):
            start = jnp.where(upper, up[0], down[0])
            place = jnp.where(upper, up[1], down[1])
            copies.append(
                pltpu.make_async_copy(
                    density_ref.at[pl.ds(start, up[2])], ref.at[pl.ds(place, up[2])], sems.at[side, i]
                )
            )
    for copy in copies:
        copy.start()
    scalars = [
        pltpu.make_async_copy(*pair, sems.at[2, i])
        for i, pair in enumerate(
            ((centre_in, centre_ref), (offsets_in, offsets_ref), (counts_in, counts_ref))
        )
    ]
    for copy in scalars:
        copy.start()
    for where in (zone(geo, odd, False), pl.ds(geo.first_at, geo.halo)):
        acc_ref[where] = jnp.zeros_like(acc_ref[where])
    for copy in scalars:
        copy.wait()
    build_lists(geo, index, centre_ref, offsets_ref, counts_ref, meta_ref)
    for copy in copies:
        copy.wait()


def group_count(geo, meta_ref, which):
    return (meta_ref[geo.lengths_at + which] + GROUP - 1) // GROUP


def waits():
    return (lax.axis_index("blk") + 1) // 2 % 2 == 1


def inner_share(geo, meta_ref):
    before = BUDGET
    for which in (CROSS_MANY, CROSS_FEW, NEAR_MANY, NEAR_FEW):
        before = before - COST[which % 2] * group_count(geo, meta_ref, which)
    rounds = (meta_ref[geo.lengths_at + CROSS] + LATE_GROUP - 1) // LATE_GROUP
    waiting = jnp.where(waits(), WAIT - COST[0] * jnp.maximum(rounds - 1, 0), 0)
    share = []
    for which in (INNER_MANY, INNER_FEW):
        cost, count = COST[which % 2], group_count(geo, meta_ref, which)
        first = jnp.minimum(jnp.maximum(before, 0) // cost, count)
        second = jnp.minimum(jnp.maximum(waiting, 0) // cost, count - first)
        before = before - cost * first
        waiting = waiting - cost * second
        share.append((0, first, first + second, count))
    return share


def inner_part(geo, meta_ref, stage, refs):
    for which, width, bounds in zip(
        (INNER_MANY, INNER_FEW), (geo.slots, 2), inner_share(geo, meta_ref)
    ):
        each_group(
            geo,
            meta_ref,
            which,
            lambda chosen, width=width: add_whole(geo, chosen, width, *refs),
            begin=bounds[stage],
            end=bounds[stage + 1],
        )


def each_group(geo, meta_ref, which, body, size=GROUP, begin=0, end=None):
    length = meta_ref[geo.lengths_at + which]

    def step(i, carry):
        chosen = []
        for n in range(size):
            place = i * size + n
            there = place < length
            b = meta_ref[which * geo.list_size + jnp.minimum(place, length)]
            chosen.append((jnp.where(there, b, 0), there))
        body(chosen)
        return carry

    lax.fori_loop(begin, (length + size - 1) // size if end is None else end, step, 0)


class Slots:
    def __init__(self, geo, meta_ref, b, there, width):
        local = meta_ref[geo.local_at + b]
        count = jnp.where(there, meta_ref[geo.count_at + b], 0)
        self.offset = [meta_ref[geo.offsets_at + k * geo.batches + b] for k in range(width)]
        self.local = local
        self.row = [local + offset for offset in self.offset]
        self.live = [k < count for k in range(width)]
        self.own = [(row >= 0) & (row < geo.rows) for row in self.row]
        self.width = width


def panels(slots, ao_ref, b):
    return jnp.concatenate(
        [
            ao_ref[b, k] * jnp.where(slots.live[k], 1.0, 0.0).astype(ao_ref.dtype)
            for k in range(slots.width)
        ],
        axis=0,
    )


def gathered(tiles_ref, places):
    return jnp.concatenate(
        [jnp.concatenate([tiles_ref[place] for place in row], axis=1) for row in places], axis=0
    )


def potentials(xs, tiles, batches, kernel_ref):
    fs = [
        jnp.dot(t, x, preferred_element_type=jnp.float32).astype(jnp.bfloat16)
        for t, x in zip(tiles, xs)
    ]
    return [
        jnp.dot(f, kernel_ref[b], preferred_element_type=jnp.float32) for f, b in zip(fs, batches)
    ]


def outer_product(x, h):
    return lax.dot_general(x, h, (((1,), (1,)), ((), ())), preferred_element_type=jnp.float32)


def chain(xs, tiles, batches, kernel_ref, weights_ref):
    gs = potentials(xs, tiles, batches, kernel_ref)
    hs = [(g * weights_ref[pl.ds(b, 1), :]).astype(jnp.bfloat16) for g, b in zip(gs, batches)]
    return [outer_product(x, h) for x, h in zip(xs, hs)]


def scatter(part, target, nb, acc_ref):
    for k, row in enumerate(target):
        for j, place in enumerate(row):
            acc_ref[place] += part[k * nb : (k + 1) * nb, j * nb : (j + 1) * nb]


def add_whole(
    geo, chosen, width, meta_ref, tiles_ref, ao_ref, kernel_ref, weights_ref, acc_ref, halo_ref=None
):
    xs, tiles, targets = ([], [], [])
    for b, there in chosen:
        slots = Slots(geo, meta_ref, b, there, width)
        xs.append(panels(slots, ao_ref, b))
        rows, target = ([], [])
        for k in range(width):
            band = [slots.offset[j] - slots.offset[k] + geo.half for j in range(width)]
            own = slots.own[k]
            base = jnp.where(slots.live[k] & own, slots.row[k], 0) * geo.band
            row = jnp.concatenate([tiles_ref[base + o] for o in band], axis=1)
            if halo_ref is not None:
                away = slots.live[k] & jnp.logical_not(own)
                outside = jnp.where(away, geo.pick(geo.halo_base, 0, slots.row[k], 0), 0)
                other = [halo_ref[jnp.where(away, outside + o, 0)] for o in band]
                row = jnp.where(away, jnp.concatenate(other, axis=1), row)
                base = jnp.where(away, outside + geo.first_at, base)
            rows.append(row)
            target.append(
                [
                    jnp.where(slots.live[k] & slots.live[j], base + band[j], geo.spare)
                    for j in range(width)
                ]
            )
        tiles.append(jnp.concatenate(rows, axis=0))
        targets.append(target)
    parts = chain(xs, tiles, [b for b, _ in chosen], kernel_ref, weights_ref)
    for part, target in zip(parts, targets):
        scatter(part, target, ao_ref.shape[2], acc_ref)


def add_own(geo, chosen, width, meta_ref, tiles_ref, ao_ref, kernel_ref, weights_ref, acc_ref):
    xs, tiles, targets = ([], [], [])
    for b, there in chosen:
        slots = Slots(geo, meta_ref, b, there, width)
        xs.append(panels(slots, ao_ref, b))
        places, target = ([], [])
        for k in range(width):
            row = slots.row[k]
            band = [slots.offset[j] - slots.offset[k] + geo.half for j in range(width)]
            base = jnp.where(slots.own[k], row, 0) * geo.band
            places.append([base + o for o in band])
            base = geo.pick(geo.early_base, geo.early_at, row, base)
            target.append(
                [
                    jnp.where(
                        slots.live[k] & slots.live[j] & slots.own[j], base + band[j], geo.spare
                    )
                    for j in range(width)
                ]
            )
        tiles.append(gathered(tiles_ref, places))
        targets.append(target)
    parts = chain(xs, tiles, [b for b, _ in chosen], kernel_ref, weights_ref)
    for part, target in zip(parts, targets):
        scatter(part, target, ao_ref.shape[2], acc_ref)


def halo_rows(geo, meta_ref, slots):
    odd = meta_ref[geo.odd_at] == 1
    rows, places, present = ([], [], [])
    for i in range(geo.reach):
        row = jnp.where(odd, geo.rows + i, i - geo.reach)
        place, found = (jnp.int32(0), jnp.bool_(False))
        for k in range(slots.width):
            hit = slots.live[k] & (slots.row[k] == row)
            place = jnp.where(hit, k, place)
            found = found | hit
        rows.append(row)
        places.append(place)
        present.append(found)
    return rows, places, present


def add_corner(geo, chosen, meta_ref, halo_ref, ao_ref, kernel_ref, weights_ref, h_ref, total_ref):
    nb = ao_ref.shape[2]
    factor = lambda flag: jnp.where(flag, 1.0, 0.0)
    xs, sides, tiles, masks = ([], [], [], [])
    for b, there in chosen:
        slots = Slots(geo, meta_ref, b, there, geo.slots)
        rows, places, present = halo_rows(geo, meta_ref, slots)
        xs.append(panels(slots, ao_ref, b))
        sides.append(
            jnp.concatenate(
                [
                    ao_ref[b, place] * factor(found).astype(ao_ref.dtype)
                    for place, found in zip(places, present)
                ],
                axis=0,
            )
        )
        picked = []
        for row, found in zip(rows, present):
            base = geo.pick(geo.halo_base, 0, row, 0) - row + geo.half
            picked.append([jnp.where(found, base + column, 0) for column in slots.row])
        tiles.append(gathered(halo_ref, picked))
        masks.append([factor(found) for found in present])
    gs = potentials(xs, tiles, [b for b, _ in chosen], kernel_ref)
    hs = []
    for g, mask, (b, there) in zip(gs, masks, chosen):
        weights = weights_ref[pl.ds(b, 1), :]
        h = jnp.concatenate(
            [g[i * nb : (i + 1) * nb] * (weights * mask[i]) for i in range(geo.reach)], axis=0
        ).astype(jnp.bfloat16)
        h_ref[jnp.where(there, b, geo.batches)] = h
        hs.append(h)
    total_ref[...] += outer_product(
        jnp.concatenate(sides, axis=1), jnp.concatenate(hs, axis=1)
    )


def add_columns(geo, chosen, width, meta_ref, ao_ref, h_ref, acc_ref):
    parts, targets = ([], [])
    for b, there in chosen:
        slots = Slots(geo, meta_ref, b, there, width)
        rows, _, present = halo_rows(geo, meta_ref, slots)
        parts.append(outer_product(ao_ref[b, pl.ds(0, width)].reshape(-1, ao_ref.shape[3]), h_ref[b]))
        targets.append(
            [
                [
                    jnp.where(
                        slots.live[k] & slots.own[k] & found,
                        slots.row[k] * geo.band + row - slots.row[k] + geo.half,
                        geo.spare,
                    )
                    for row, found in zip(rows, present)
                ]
                for k in range(width)
            ]
        )
    for part, target in zip(parts, targets):
        scatter(part, target, ao_ref.shape[2], acc_ref)


def early_kernel(
    geo, meta_ref, tiles_ref, ao_ref, kernel_ref, weights_ref, acc_in, acc_ref, early_out
):
    odd = meta_ref[geo.odd_at] == 1
    for where in (zone(geo, odd, True), pl.ds(geo.early_at, geo.early), pl.ds(geo.spare, 1)):
        acc_ref[where] = jnp.zeros_like(acc_ref[where])
    refs = (meta_ref, tiles_ref, ao_ref, kernel_ref, weights_ref, acc_ref)
    for which, width in ((CROSS_MANY, geo.slots), (CROSS_FEW, 2)):
        each_group(
            geo, meta_ref, which, lambda chosen, width=width: add_own(geo, chosen, width, *refs)
        )
    early_out[...] = acc_ref[pl.ds(geo.early_at, geo.early)].astype(early_out.dtype)


def near_kernel(
    geo, meta_ref, halo_ref, tiles_ref, ao_ref, kernel_ref, weights_ref, acc_in, acc_ref, first_out
):
    refs = (meta_ref, tiles_ref, ao_ref, kernel_ref, weights_ref, acc_ref, halo_ref)
    for which, width in ((NEAR_MANY, geo.slots), (NEAR_FEW, 2)):
        each_group(
            geo, meta_ref, which, lambda chosen, width=width: add_whole(geo, chosen, width, *refs)
        )
    first_out[...] = acc_ref[pl.ds(geo.first_at, geo.halo)].astype(first_out.dtype)
    inner_part(geo, meta_ref, 0, refs[:-1])


def waiting_kernel(
    geo, meta_ref, tiles_ref, ao_ref, kernel_ref, weights_ref, acc_in, acc_ref, done_ref
):
    inner_part(geo, meta_ref, 1, (meta_ref, tiles_ref, ao_ref, kernel_ref, weights_ref, acc_ref))
    done_ref[0] = 1


def late_kernel(
    geo, meta_ref, done_ref, halo_ref, ao_ref, kernel_ref, weights_ref, h_ref, late_out, total_ref
):
    nb = ao_ref.shape[2]
    total_ref[...] = jnp.zeros_like(total_ref)

    def work(chosen):
        add_corner(
            geo, chosen, meta_ref, halo_ref, ao_ref, kernel_ref, weights_ref, h_ref, total_ref
        )

    groups = (meta_ref[geo.lengths_at + CROSS] + 1) // LATE_GROUP
    each_group(geo, meta_ref, CROSS, work, size=LATE_GROUP, end=groups)
    each_group(geo, meta_ref, CROSS, work, size=LATE_GROUP // 2, begin=2 * groups)
    for i in range(geo.reach):
        for j in range(geo.reach):
            late_out[i * geo.reach + j] = total_ref[
                i * nb : (i + 1) * nb, j * nb : (j + 1) * nb
            ].astype(late_out.dtype)


def inner_kernel(
    geo, meta_ref, first_ref, tiles_ref, ao_ref, kernel_ref, weights_ref, h_ref, acc_in,
    acc_ref, out_ref, sems,
):
    odd = meta_ref[geo.odd_at] == 1
    refs = (meta_ref, tiles_ref, ao_ref, kernel_ref, weights_ref, acc_ref)
    inner_part(geo, meta_ref, 2, refs)

    def add_near(up, down):
        for start, place, count in geo.packs[0 if up else 1]:
            acc_ref[pl.ds(start, count)] += first_ref[pl.ds(place, count)].astype(jnp.float32)

    by_parity(odd, add_near, True, False)
    done = zone(geo, odd, False)
    copy = pltpu.make_async_copy(acc_ref.at[done], out_ref.at[done], sems.at[0])
    copy.start()
    for which, width in ((CROSS_MANY, geo.slots), (CROSS_FEW, 2)):
        each_group(
            geo,
            meta_ref,
            which,
            lambda chosen, width=width: add_columns(
                geo, chosen, width, meta_ref, ao_ref, h_ref, acc_ref
            ),
        )

    def write_quiet(up, down):
        run_copies(
            [
                pltpu.make_async_copy(
                    acc_ref.at[pl.ds(start, count)], out_ref.at[pl.ds(start, count)], sems.at[1 + i]
                )
                for i, (start, count) in enumerate(geo.quiet[0 if up else 1])
            ]
        )

    by_parity(odd, write_quiet, True, False)
    copy.wait()


def finish_cross(geo, odd, parts, acc_ref, out_ref, total, sems):
    def add(up, down):
        copies = []
        for packs, ref in parts:
            for start, place, count in packs[0 if up else 1]:
                spot = pl.ds(len(copies) * geo.band, count)
                total[spot] = acc_ref[pl.ds(start, count)] + ref[pl.ds(place, count)].astype(
                    jnp.float32
                )
                copy = pltpu.make_async_copy(
                    total.at[spot], out_ref.at[pl.ds(start, count)], sems.at[len(copies)]
                )
                copy.start()
                copies.append(copy)
        for copy in copies:
            copy.wait()

    by_parity(odd, add, False, True)


def has_time(geo, meta_ref):
    left = [bounds[3] - bounds[2] for bounds in inner_share(geo, meta_ref)]
    return waits() & (left[0] + left[1] == 0)


def early_join_kernel(geo, meta_ref, early_ref, acc_ref, out_in, out_ref, total, sems):
    @pl.when(has_time(geo, meta_ref))
    def _():
        odd = meta_ref[geo.odd_at] == 1
        finish_cross(geo, odd, ((geo.early_packs, early_ref),), acc_ref, out_ref, total, sems)


def finish_kernel(geo, meta_ref, late_ref, early_ref, acc_ref, out_in, out_ref, total, sems):
    odd = meta_ref[geo.odd_at] == 1
    late = (geo.late_packs, late_ref)
    joined = has_time(geo, meta_ref)

    @pl.when(joined)
    def _():
        finish_cross(geo, odd, (late,), acc_ref, out_ref, total, sems)

    @pl.when(jnp.logical_not(joined))
    def _():
        parts = ((geo.early_packs, early_ref), late)
        finish_cross(geo, odd, parts, acc_ref, out_ref, total, sems)


def call(kernel, out_shape, in_specs, out_specs, scratch, aliases=None, cost=None):
    return pl.pallas_call(
        kernel,
        out_shape=out_shape,
        in_specs=in_specs,
        out_specs=out_specs,
        scratch_shapes=scratch,
        input_output_aliases=aliases or {},
        cost_estimate=cost,
        compiler_params=pltpu.CompilerParams(vmem_limit_bytes=16 * MIB),
    )


def to_first(x, size):
    pairs = [(i, i + 1) for i in range(0, size - 1, 2)]
    got = lax.ppermute(x, "blk", pairs + [(j, i) for i, j in pairs])
    return pltpu.with_memory_space_constraint(got, pltpu.VMEM)


def to_second(x, size):
    pairs = [(i, i + 1) for i in range(1, size - 1, 2)]
    got = lax.ppermute(x, "blk", pairs + [(j, i) for i, j in pairs])
    return pltpu.with_memory_space_constraint(got, pltpu.VMEM)


def local(density, ao_values, kernel, grid_weights, centre, sig_offsets, counts):
    rows, band, nb, _ = density.shape
    batches, slots, _, pts = ao_values.shape
    size = lax.axis_size("blk")
    geo = Geometry(rows, band, batches, slots)
    in_hbm = lambda x: pltpu.with_memory_space_constraint(x, pltpu.HBM)
    tiles = density.reshape(geo.own, nb, nb)
    pack = lambda count: pltpu.VMEM((count, nb, nb), jnp.bfloat16)
    dma = pltpu.SemaphoreType.DMA
    acc_type = pltpu.VMEM((geo.spare + 1, nb, nb), jnp.float32)

    near_halo, cross_halo, meta, acc = call(
        functools.partial(pack_kernel, geo),
        (pack(geo.halo),) * 2 + (pltpu.SMEM((geo.meta_size,), jnp.int32), acc_type),
        [ANY_SPEC] * 4,
        (VMEM_SPEC,) * 2 + (SMEM_SPEC, VMEM_SPEC),
        [
            pltpu.SMEM((batches,), jnp.int32),
            pltpu.SMEM((slots, batches), jnp.int32),
            pltpu.SMEM((batches,), jnp.int32),
            dma((3, max(geo.reach, 3))),
        ],
        cost=pl.CostEstimate(flops=10**10, bytes_accessed=10**8, transcendentals=0),
    )(in_hbm(tiles), in_hbm(centre), in_hbm(sig_offsets.T), in_hbm(counts))
    cross_halo = to_second(cross_halo, size)
    near_halo = to_first(near_halo, size)

    panel = (tiles, ao_values, kernel, grid_weights)
    acc, early = call(
        functools.partial(early_kernel, geo),
        (acc_type, pack(geo.early)),
        [SMEM_SPEC] + [VMEM_SPEC] * 5,
        (VMEM_SPEC,) * 2,
        [],
        {5: 0},
    )(meta, *panel, acc)
    early = to_second(early, size)

    acc, first = call(
        functools.partial(near_kernel, geo),
        (acc_type, pack(geo.halo)),
        [SMEM_SPEC] + [VMEM_SPEC] * 6,
        (VMEM_SPEC,) * 2,
        [],
        {6: 0},
    )(meta, near_halo, *panel, acc)
    first = to_first(first, size)

    acc, done = call(
        functools.partial(waiting_kernel, geo),
        (acc_type, pltpu.SMEM((1,), jnp.int32)),
        [SMEM_SPEC] + [VMEM_SPEC] * 5,
        (VMEM_SPEC, SMEM_SPEC),
        [],
        {5: 0},
    )(meta, *panel, acc)

    h_type = pltpu.VMEM((batches + 1, geo.reach * nb, pts), jnp.bfloat16)
    h, late = call(
        functools.partial(late_kernel, geo),
        (h_type, pack(geo.late)),
        [SMEM_SPEC] * 2 + [VMEM_SPEC] * 4,
        (VMEM_SPEC,) * 2,
        [pltpu.VMEM((geo.reach * nb, geo.reach * nb), jnp.float32)],
    )(meta, done, cross_halo, *panel[1:])
    late = to_second(late, size)

    whole = jax.ShapeDtypeStruct((geo.own, nb, nb), jnp.float32)
    acc, out = call(
        functools.partial(inner_kernel, geo),
        (acc_type, whole),
        [SMEM_SPEC] + [VMEM_SPEC] * 7,
        (VMEM_SPEC, ANY_SPEC),
        [dma((1 + max(len(runs) for runs in geo.quiet),))],
        {7: 0},
    )(meta, first, *panel, h, acc)

    for kernel_of, got, parts in (
        (early_join_kernel, (early,), geo.reach),
        (finish_kernel, (late, early), 2 * geo.reach),
    ):
        out = call(
            functools.partial(kernel_of, geo),
            whole,
            [SMEM_SPEC] + [VMEM_SPEC] * (len(got) + 1) + [ANY_SPEC],
            ANY_SPEC,
            [pltpu.VMEM((parts * band, nb, nb), jnp.float32), dma((parts,))],
            {len(got) + 2: 0},
        )(meta, *got, acc, out)
    return out.reshape(rows, band, nb, nb)


def solution(mesh):
    placed = (
        P(("groups", "blk"), None, None, None),
        P(("groups", "blk"), None, None, None),
        P(("groups", "blk"), None, None),
        P(("groups", "blk"), None),
        P(("groups", "blk")),
        P(("groups", "blk"), None),
        P(("groups", "blk")),
    )
    return jax.shard_map(
        local,
        mesh=mesh,
        in_specs=placed,
        out_specs=P(("groups", "blk"), None, None, None),
        check_vma=False,
    )
```
